32 devices in a mesh: dp: 8 (over y, x, core), expert: 4 (over z).
Axes of the slice: x: 2, y: 2, z: 4, core: 2. Of those that a mesh axis runs over, the one named last changes fastest.
Arguments:
- tokens: bfloat16 [4096, 2048], P(('dp', 'expert')), may hold values from -6 to 6
- routes: int32 [4096, 2], P(('dp', 'expert')), may hold values from 0 to 3, all different within a row; in each aligned block of 128 rows (0 to 127, 128 to 255, ...) at most 64 rows name the same one
- route_scores: float32 [4096, 2], P(('dp', 'expert')), may hold values from -4 to 4
- out_grad: bfloat16 [4096, 2048], P(('dp', 'expert')), may hold values from -6 to 6
- gate_up: bfloat16 [4, 2048, 1024], P('expert'), may hold values from -0.125 to 0.125
- down_weight: bfloat16 [4, 2048, 512], P('expert'), may hold values from -0.25 to 0.25
Outputs:
- mixed_out: bfloat16 [4096, 2048], P(('dp', 'expert'))
- token_grad: bfloat16 [4096, 2048], P(('dp', 'expert'))
- grad_gate_up: float32 [4, 2048, 1024], P('expert', 'dp')
- grad_down: float32 [4, 2048, 512], P('expert', 'dp')
The draws below stay inside these ranges and needn't reach their ends.
Inputs may be any that keep to these rules, and one draw needn't show every extreme that they name: `routes`: the 2 experts of a token differ. Among the 128 tokens of one device no expert is named more than 64 times, and in some device's tokens an expert is named exactly 64 times.
All inputs are finite; a program needn't handle non-finite values.
Results may differ from the reference program's by a relative error of at most 0.015.
Values may be sent and summed in bfloat16 or wider, within the bound.
No kernel may reach another device: no remote copies, remote signals or barrier semaphores. Data moves between devices by JAX's collectives and lax.ppermute only.
A program may use at most 64 MiB of HBM per device.

```python
import math
import jax
import jax.numpy as jnp
import numpy as np
from jax import lax

D = 2048
H = 512
TOP = 2
TOK_DEV = 128
EXPERTS = 4
CAP = 64
TOKENS = 4096
N_DP = 8
N_EXPERT = 4


def with_spikes(array, key, source, target, parts, factor):
    owner, partner = [(jnp.arange(array.shape[dim]) // (array.shape[dim] // parts)).reshape([-1 if axis == dim else 1 for axis in range(array.ndim)]) for dim in (source, target)]
    chosen = jax.random.permutation(key, parts)[partner]
    strong = (owner == chosen) | (owner == (partner + parts // 2) % parts)
    return jnp.where(strong, factor * array, array)


def shard_levels(rng, extent, pieces, smallest, top_value):
    loudness, own = 1.0, jax.random.fold_in(rng, 6)
    for dim, shards_of in pieces:
        draws = jnp.exp(jax.random.uniform(jax.random.fold_in(own, dim), (shards_of,), jnp.float32, smallest / len(pieces), top_value / len(pieces)))
        loudness = loudness * jnp.repeat(draws, extent[dim] // shards_of).reshape([-1 if axis == dim else 1 for axis in range(len(extent))])
    return loudness


def shared_out(own_key, own, number, rows, number_of, top, reach, lean):
    ranking = jax.random.permutation(own_key, number_of)
    packed, common = shares(number_of, rows * top, reach, lean, True), shares(number_of, rows * top, reach, lean, False)
    places = jnp.arange(number_of)

    def named(tallies, rotation):
        used = int((tallies > 0).sum())
        fixed = max(1, used // 4)
        passed = fixed + (places - fixed + rotation * (used - fixed)) % max(1, number_of - fixed)
        return jnp.zeros((number_of,), jnp.int32).at[ranking[jnp.where(places < fixed, places, passed)]].set(jnp.asarray(tallies, jnp.int32))

    tallies = jnp.where(number % 4 == 0, named(packed, number // 4), named(common, number - number // 4 - 1))
    mixed = jax.random.permutation(jax.random.fold_in(own, 3), number_of)
    source_of, sink = mixed[0:number_of // 2 * 2:2], mixed[1:number_of // 2 * 2:2]
    margin = jnp.minimum(tallies[source_of] - 1, reach - tallies[sink]) // 2
    margin = jnp.where((source_of == ranking[0]) | (sink == ranking[0]) | (tallies[sink] == 0), 0, jnp.maximum(margin, 0))
    passed = jax.random.randint(jax.random.fold_in(own, 4), (number_of // 2,), 0, 1 << 20) % (margin + 1)
    tallies = tallies.at[source_of].add(-passed).at[sink].add(passed)
    items = jnp.searchsorted(jnp.cumsum(tallies), jnp.arange(rows * top), side="right").astype(jnp.int32)
    grid = items.reshape(top, rows).T
    grid = grid[jax.random.permutation(jax.random.fold_in(own, 1), rows)]
    rotation = jax.random.randint(jax.random.fold_in(own, 2), (rows, 1), 0, top)
    return jnp.take_along_axis(grid, (jnp.arange(top)[None, :] + rotation) % top, axis=1)


def shares(number_of, total, reach, skew, full):
    portions = [(1 << 20) // math.isqrt(rank ** skew) + 1 for rank in range(1, number_of + 1)]
    largest = reach if full else min(reach, max(-(-total // number_of), total * portions[0] // sum(portions)))
    least = 1 if total - largest >= number_of - 1 else 0
    given, spare = [largest] + [least] * (number_of - 1), total - largest - least * (number_of - 1)
    while spare > 0:
        candidates = [i for i in range(1, number_of) if given[i] < largest] or [i for i in range(1, number_of) if given[i] < reach]
        whole, remaining = sum([portions[i] for i in candidates]), spare
        for i in candidates:
            addition = min(reach - given[i], max(1, remaining * portions[i] // whole), spare)
            given[i] = given[i] + addition
            spare = spare - addition
    return np.array(given)


def gaussian(key, extent, deviation, reach, cuts=(), held_as=jnp.bfloat16):
    entries = deviation * jax.random.normal(key, extent, jnp.float32)
    if cuts:
        entries = entries * shard_levels(key, extent, cuts, -0.22, 0.18)
    return jnp.clip(entries, -reach, reach).astype(held_as)


def heavy_noise(own_key, extent, deviation, bound, cuts, heavy, kind=jnp.bfloat16):
    array = deviation * jax.random.normal(own_key, extent, jnp.float32)
    if cuts:
        array = array * shard_levels(own_key, extent, cuts, -0.22, 0.18)
    return jnp.clip(with_spikes(array, jax.random.fold_in(own_key, 3), *heavy), -bound, bound).astype(kind)


def setup_inputs(seed: int = 0) -> dict:
    key_of = jax.random.split(jax.random.key(seed), 7)
    tokens = heavy_noise(key_of[0], (TOKENS, D), 1.0, 6.0, ((0, 32),), (0, 1, 32, 2.75))
    routes_keys = jax.random.split(jax.random.fold_in(key_of[1], 1), TOKENS // TOK_DEV)
    routes_turns = jax.random.permutation(jax.random.fold_in(key_of[1], 3), TOKENS // TOK_DEV)
    routes = jax.vmap(lambda own, number: shared_out(jax.random.fold_in(key_of[1], 2), own, number, TOK_DEV, EXPERTS, TOP, CAP, 2))(routes_keys, routes_turns).reshape((TOKENS, TOP))
    route_scores = gaussian(key_of[2], (TOKENS, TOP), 1.0, 4.0, ((0, 32),), jnp.float32)
    out_grad = gaussian(key_of[3], (TOKENS, D), 1.0, 6.0, ((0, 32),))
    gate_up = gaussian(key_of[4], (EXPERTS, D, 2 * H), D ** -0.5, 0.125, ((0, 4),))
    down_weight = gaussian(key_of[5], (EXPERTS, D, H), H ** -0.5, 0.25, ((0, 4),))
    return {"tokens": tokens, "routes": routes, "route_scores": route_scores, "out_grad": out_grad, "gate_up": gate_up, "down_weight": down_weight}


def expert_pass(row_block, grad_block, w_in, w_out):
    hidden_units = w_out.shape[1]
    preact = jnp.dot(row_block, w_in, preferred_element_type=jnp.float32)
    gate_pre = preact[:, :hidden_units]
    up_pre = preact[:, hidden_units:]
    hidden = (jax.nn.silu(gate_pre) * up_pre).astype(jnp.bfloat16)
    produced = jnp.dot(hidden, w_out.T, preferred_element_type=jnp.float32).astype(jnp.bfloat16)
    hidden_grad = jnp.dot(grad_block, w_out, preferred_element_type=jnp.float32)
    sigmoid_gate = jax.nn.sigmoid(gate_pre)
    gate_grad = hidden_grad * up_pre * sigmoid_gate * (1.0 + gate_pre * (1.0 - sigmoid_gate))
    up_grad = hidden_grad * gate_pre * sigmoid_gate
    pre_grad = jnp.concatenate([gate_grad, up_grad], axis=1).astype(jnp.bfloat16)
    input_grad = jnp.dot(pre_grad, w_in.T, preferred_element_type=jnp.float32).astype(jnp.bfloat16)
    term_in = jnp.dot(row_block.T, pre_grad, preferred_element_type=jnp.float32)
    term_down = jnp.dot(grad_block.T, hidden, preferred_element_type=jnp.float32)
    return produced, input_grad, term_in, term_down


def reference(tokens, routes, route_scores, out_grad, gate_up, down_weight):
    group_tokens = TOK_DEV * N_EXPERT
    group_routes = group_tokens * TOP
    group_slots = N_EXPERT * CAP
    scores_exp = jnp.exp(route_scores)
    weights = scores_exp / jnp.sum(scores_exp, axis=1, keepdims=True)
    route_grad = (weights[:, :, None] * out_grad[:, None, :].astype(jnp.float32)).astype(jnp.bfloat16)

    def per_group(totals, group_data):
        total_in, total_down = totals
        tok_group, route_group, weight_group, grad_group = group_data
        flat_routes = route_group.reshape(group_routes)
        expert_ids = lax.broadcasted_iota(jnp.int32, (group_routes, EXPERTS), 1)
        chosen = (flat_routes[:, None] == expert_ids).astype(jnp.int32)
        position = jnp.sum((jnp.cumsum(chosen, axis=0) - chosen) * chosen, axis=1).astype(jnp.int32)
        slot_table = jnp.full((EXPERTS, group_slots), group_routes, jnp.int32)
        slot_table = slot_table.at[flat_routes, position].set(jnp.arange(group_routes, dtype=jnp.int32))
        zero_row = jnp.zeros((1, D), tok_group.dtype)
        rows_source = jnp.concatenate([jnp.repeat(tok_group, TOP, axis=0), zero_row], axis=0)
        grads_source = jnp.concatenate([grad_group.reshape(group_routes, D), zero_row], axis=0)
        row_blocks = rows_source[slot_table]
        grad_blocks = grads_source[slot_table]

        def per_expert(expert_item):
            return expert_pass(*expert_item)

        produced, input_grad, term_in, term_down = lax.map(per_expert, (row_blocks, grad_blocks, gate_up, down_weight))
        total_in = total_in + lax.optimization_barrier(term_in.astype(jnp.bfloat16)).astype(jnp.float32)
        total_down = total_down + lax.optimization_barrier(term_down.astype(jnp.bfloat16)).astype(jnp.float32)
        lookup = (flat_routes * group_slots + position).astype(jnp.int32)
        picked = produced.reshape(EXPERTS * group_slots, D)[lookup].astype(jnp.float32).reshape(group_tokens, TOP, D)
        mixed_group = jnp.sum(weight_group[:, :, None] * picked, axis=1).astype(jnp.bfloat16)
        back_grads = input_grad.reshape(EXPERTS * group_slots, D)[lookup].astype(jnp.float32).reshape(group_tokens, TOP, D)
        token_group = jnp.sum(back_grads, axis=1).astype(jnp.bfloat16)
        return (total_in, total_down), (mixed_group, token_group)

    start_totals = (jnp.zeros((EXPERTS, D, 2 * H), jnp.float32), jnp.zeros((EXPERTS, D, H), jnp.float32))
    group_inputs = (tokens.reshape(N_DP, group_tokens, D), routes.reshape(N_DP, group_tokens, TOP), weights.reshape(N_DP, group_tokens, TOP), route_grad.reshape(N_DP, group_tokens, TOP, D))
    totals, outputs = lax.scan(per_group, start_totals, group_inputs)
    mixed_out = outputs[0].reshape(TOKENS, D)
    token_grad = outputs[1].reshape(TOKENS, D)
    return mixed_out, token_grad, totals[0] / N_DP, totals[1] / N_DP
```

```python
import functools

import jax
import jax.numpy as jnp
from jax import lax
from jax.experimental import pallas as pl
from jax.experimental.pallas import tpu as pltpu
from jax.sharding import PartitionSpec as P

F32 = jnp.float32
BF16 = jnp.bfloat16


def contract(left, right):
    return lax.dot_general(left, right, (((0,), (0,)), ((), ())), preferred_element_type=F32)


def slot_rows(first, routes, experts, capacity):
    tops, toks = routes.shape
    padded = -(-experts // 8) * 8
    rows = lax.broadcasted_iota(jnp.int32, (padded, toks), 0)
    ids = rows + first
    ids = jnp.where(ids >= experts, ids - experts, ids)
    ids = jnp.where(rows < experts, ids, -1)
    hits = [routes[k : k + 1, :] == ids for k in range(tops)]
    named = functools.reduce(jnp.logical_or, hits)
    before = lax.broadcasted_iota(jnp.int32, (toks, toks), 0) < lax.broadcasted_iota(
        jnp.int32, (toks, toks), 1
    )
    position = jnp.dot(
        named.astype(F32).astype(BF16),
        before.astype(F32).astype(BF16),
        preferred_element_type=F32,
    )
    slot = position + (rows * capacity).astype(F32)
    return [jnp.sum(jnp.where(hit, slot, 0.0), axis=0, keepdims=True) for hit in hits]


def weight_rows(scores):
    grown = jnp.exp(scores)
    return grown / jnp.sum(grown, axis=0, keepdims=True)


def to_column(row):
    toks = row.shape[1]
    same = lax.broadcasted_iota(jnp.int32, (toks, toks), 0) == lax.broadcasted_iota(
        jnp.int32, (toks, toks), 1
    )
    return jnp.sum(jnp.where(same, row, 0.0), axis=1, keepdims=True)


def put_blocks(outs, rows, columns):
    start = 0
    for out in outs:
        size = out.shape[0]
        out[:, columns] = rows[start : start + size]
        start += size


def column_steps(width):
    step = 512 if width % 512 == 0 else width
    return [slice(at, at + step) for at in range(0, width, step)]


def dispatch_kernel(experts, capacity, weighted, first, routes, *refs):
    scores = refs[0] if weighted else None
    values, outs = refs[weighted], refs[weighted + 1 :]
    slots, toks = experts * capacity, values.shape[0]
    places = lax.broadcasted_iota(jnp.int32, (slots, toks), 0).astype(F32)
    hits = [places == row for row in slot_rows(first[0], routes[...], experts, capacity)]
    picker = functools.reduce(jnp.logical_or, hits).astype(F32).astype(BF16)
    if weighted:
        weights = weight_rows(scores[...])
        scale = sum(
            jnp.sum(jnp.where(hit, weights[k : k + 1, :], 0.0), axis=1, keepdims=True)
            for k, hit in enumerate(hits)
        )
    for columns in column_steps(values.shape[1]):
        rows = jnp.dot(picker, values[:, columns], preferred_element_type=F32)
        if weighted:
            rows = rows * scale
        put_blocks(outs, rows.astype(BF16), columns)


def combine_kernel(experts, capacity, weighted, first, routes, *refs):
    scores = refs[0] if weighted else None
    blocks, out = refs[weighted:-1], refs[-1]
    slots, toks = experts * capacity, out.shape[0]
    places = lax.broadcasted_iota(jnp.int32, (toks, slots), 1).astype(F32)
    hits = [
        places == to_column(row) for row in slot_rows(first[0], routes[...], experts, capacity)
    ]
    if weighted:
        weights = weight_rows(scores[...])
        scales = [to_column(weights[k : k + 1, :]) for k in range(len(hits))]
        pickers = [hit.astype(F32).astype(BF16) for hit in hits]
    else:
        pickers = [functools.reduce(jnp.logical_or, hits).astype(F32).astype(BF16)]
    for columns in column_steps(out.shape[1]):
        rows = [block[:, columns] for block in blocks]
        rows = rows[0] if len(rows) == 1 else jnp.concatenate(rows, axis=0)
        picked = [jnp.dot(picker, rows, preferred_element_type=F32) for picker in pickers]
        if weighted:
            picked = [scale * part for scale, part in zip(scales, picked)]
        out[:, columns] = sum(picked).astype(out.dtype)


def call(kernel, out_shape, inputs, flops, moved):
    return pl.pallas_call(
        kernel,
        out_shape=out_shape,
        in_specs=[pl.BlockSpec(memory_space=pltpu.SMEM)]
        + [pl.BlockSpec(memory_space=pltpu.VMEM)] * (len(inputs) - 1),
        compiler_params=pltpu.CompilerParams(vmem_limit_bytes=32 * 1024 * 1024),
        cost_estimate=pl.CostEstimate(flops=flops, bytes_accessed=moved, transcendentals=0),
    )(*inputs)


def body(tokens, routes, route_scores, out_grad, gate_up, down_weight):
    experts = lax.axis_size("expert")
    groups = lax.axis_size("dp")
    toks, width = tokens.shape
    tops = routes.shape[1]
    units = down_weight.shape[2]
    capacity = (toks * tops + experts - 1) // experts
    slots = experts * capacity
    share = width // groups
    direct = experts <= 8 and capacity % 16 == 0
    w_in, w_out = gate_up[0], down_weight[0]
    routes_t, scores_t = routes.T, route_scores.T
    me = lax.axis_index("expert") if direct else jnp.int32(0)
    first = me.astype(jnp.int32).reshape(1)
    sizes = [capacity] * experts if direct else [slots]
    block_shapes = [jax.ShapeDtypeStruct((size, width), BF16) for size in sizes]
    cost = (2 * slots * toks * width, 2 * (slots + toks) * width)

    def exchange(blocks, sign):
        if not direct:
            block = blocks[0].reshape(experts, capacity, width)
            moved = lax.all_to_all(block, "expert", split_axis=0, concat_axis=0, tiled=True)
            return [moved.reshape(slots, width)]
        out = [blocks[0]]
        for step in range(1, experts):
            pairs = [(at, (at + sign * step) % experts) for at in range(experts)]
            out.append(lax.ppermute(blocks[step], "expert", pairs))
        return out

    def joined(blocks):
        return blocks[0] if len(blocks) == 1 else jnp.concatenate(blocks, axis=0)

    def split(rows):
        return [rows[at : at + sizes[0]] for at in range(0, slots, sizes[0])]

    sent_rows = call(
        functools.partial(dispatch_kernel, experts, capacity, False),
        block_shapes,
        (first, routes_t, tokens),
        *cost,
    )
    token_rows = joined(exchange(sent_rows, 1))
    sent_grads = call(
        functools.partial(dispatch_kernel, experts, capacity, True),
        block_shapes,
        (first, routes_t, scores_t, out_grad),
        *cost,
    )
    grad_rows = joined(exchange(sent_grads, 1))

    preact = jnp.dot(token_rows, w_in, preferred_element_type=F32)
    gate, up = preact[:, :units], preact[:, units:]
    hidden = (jax.nn.silu(gate) * up).astype(BF16)
    produced = jnp.dot(hidden, w_out.T, preferred_element_type=F32).astype(BF16)
    returned = exchange(split(produced), -1)

    hidden_grad = jnp.dot(grad_rows, w_out, preferred_element_type=F32)
    sigmoid = jax.nn.sigmoid(gate)
    gate_grad = hidden_grad * up * sigmoid * (1.0 + gate * (1.0 - sigmoid))
    up_grad = hidden_grad * gate * sigmoid
    pre_grad = jnp.concatenate([gate_grad, up_grad], axis=1).astype(BF16)
    input_grad = jnp.dot(pre_grad, w_in.T, preferred_element_type=F32).astype(BF16)
    sent_back = exchange(split(input_grad), -1)

    def summed(left, right):
        part = contract(left, right).astype(BF16)
        return lax.psum_scatter(part, "dp", scatter_dimension=0, tiled=True).astype(F32) / groups

    grad_in = summed(token_rows, pre_grad).reshape(1, share, 2 * units)
    grad_down = summed(grad_rows, hidden).reshape(1, share, units)

    out_shape = jax.ShapeDtypeStruct((toks, width), BF16)
    mixed_out = call(
        functools.partial(combine_kernel, experts, capacity, True),
        out_shape,
        (first, routes_t, scores_t, *returned),
        *cost,
    )
    token_grad = call(
        functools.partial(combine_kernel, experts, capacity, False),
        out_shape,
        (first, routes_t, *sent_back),
        *cost,
    )
    return (mixed_out, token_grad, grad_in, grad_down)


def solution(mesh):
    in_specs = (
        P(("dp", "expert"), None),
        P(("dp", "expert"), None),
        P(("dp", "expert"), None),
        P(("dp", "expert"), None),
        P("expert", None, None),
        P("expert", None, None),
    )
    out_specs = (
        P(("dp", "expert"), None),
        P(("dp", "expert"), None),
        P("expert", "dp", None),
        P("expert", "dp", None),
    )
    return jax.shard_map(body, mesh=mesh, in_specs=in_specs, out_specs=out_specs, check_vma=False)
```

```python
import functools

import jax
import jax.numpy as jnp
from jax import lax
from jax.experimental import pallas as pl
from jax.experimental.pallas import tpu as pltpu
from jax.sharding import PartitionSpec as P

F32 = jnp.float32
BF16 = jnp.bfloat16
BRIEF = pl.CostEstimate(flops=1024, bytes_accessed=1024, transcendentals=0)


def contract(left, right):
    return lax.dot_general(left, right, (((0,), (0,)), ((), ())), preferred_element_type=F32)


def slot_rows(first, routes, experts, capacity):
    tops, toks = routes.shape
    padded = -(-experts // 8) * 8
    rows = lax.broadcasted_iota(jnp.int32, (padded, toks), 0)
    ids = rows + first
    ids = jnp.where(ids >= experts, ids - experts, ids)
    ids = jnp.where(rows < experts, ids, -1)
    hits = [routes[k : k + 1, :] == ids for k in range(tops)]
    named = functools.reduce(jnp.logical_or, hits)
    before = lax.broadcasted_iota(jnp.int32, (toks, toks), 0) < lax.broadcasted_iota(
        jnp.int32, (toks, toks), 1
    )
    position = jnp.dot(
        named.astype(F32).astype(BF16),
        before.astype(F32).astype(BF16),
        preferred_element_type=F32,
    )
    slot = position + (rows * capacity).astype(F32)
    return [jnp.sum(jnp.where(hit, slot, 0.0), axis=0, keepdims=True) for hit in hits]


def weight_rows(scores):
    grown = jnp.exp(scores)
    return grown / jnp.sum(grown, axis=0, keepdims=True)


def to_column(row):
    toks = row.shape[1]
    same = lax.broadcasted_iota(jnp.int32, (toks, toks), 0) == lax.broadcasted_iota(
        jnp.int32, (toks, toks), 1
    )
    return jnp.sum(jnp.where(same, row, 0.0), axis=1, keepdims=True)


def put_blocks(outs, rows, columns):
    start = 0
    for out in outs:
        size = out.shape[0]
        out[:, columns] = rows[start : start + size]
        start += size


def column_steps(width):
    step = 512 if width % 512 == 0 else width
    return [slice(at, at + step) for at in range(0, width, step)]


def dispatch_kernel(experts, capacity, weighted, first, routes, *refs):
    scores = refs[0] if weighted else None
    values, outs = refs[weighted], refs[weighted + 1 :]
    slots, toks = experts * capacity, values.shape[0]
    places = lax.broadcasted_iota(jnp.int32, (slots, toks), 0).astype(F32)
    hits = [places == row for row in slot_rows(first[0], routes[...], experts, capacity)]
    picker = functools.reduce(jnp.logical_or, hits).astype(F32).astype(BF16)
    if weighted:
        weights = weight_rows(scores[...])
        scale = sum(
            jnp.sum(jnp.where(hit, weights[k : k + 1, :], 0.0), axis=1, keepdims=True)
            for k, hit in enumerate(hits)
        )
    for columns in column_steps(values.shape[1]):
        rows = jnp.dot(picker, values[:, columns], preferred_element_type=F32)
        if weighted:
            rows = rows * scale
        put_blocks(outs, rows.astype(BF16), columns)


def combine_kernel(experts, capacity, weighted, first, routes, *refs):
    scores = refs[0] if weighted else None
    blocks, out = refs[weighted:-1], refs[-1]
    slots, toks = experts * capacity, out.shape[0]
    places = lax.broadcasted_iota(jnp.int32, (toks, slots), 1).astype(F32)
    hits = [
        places == to_column(row) for row in slot_rows(first[0], routes[...], experts, capacity)
    ]
    if weighted:
        weights = weight_rows(scores[...])
        scales = [to_column(weights[k : k + 1, :]) for k in range(len(hits))]
        pickers = [hit.astype(F32).astype(BF16) for hit in hits]
    else:
        pickers = [functools.reduce(jnp.logical_or, hits).astype(F32).astype(BF16)]
    for columns in column_steps(out.shape[1]):
        rows = [block[:, columns] for block in blocks]
        rows = rows[0] if len(rows) == 1 else jnp.concatenate(rows, axis=0)
        picked = [jnp.dot(picker, rows, preferred_element_type=F32) for picker in pickers]
        if weighted:
            picked = [scale * part for scale, part in zip(scales, picked)]
        out[:, columns] = sum(picked).astype(out.dtype)


def gradient_kernel(shares, halves, rows, grads, pre_grad, hidden, out):
    wide = pre_grad.shape[1]
    out[0, :, :wide] = contract(rows[...], pre_grad[...]).astype(out.dtype)
    out[0, :, wide:] = contract(grads[...], hidden[...]).astype(out.dtype)


def gradient_shares(tasks, me, share, rows, grads, pre_grad, hidden):
    slots, width = rows.shape
    wide, narrow = pre_grad.shape[1] // 2, hidden.shape[1] // 2
    shares = jnp.stack([jnp.bitwise_xor(me, j) for j, _ in tasks]).astype(jnp.int32)
    halves = jnp.array([half for _, half in tasks], jnp.int32)
    count = len(tasks)
    return pl.pallas_call(
        gradient_kernel,
        out_shape=jax.ShapeDtypeStruct((count, share, wide + narrow), BF16),
        grid_spec=pltpu.PrefetchScalarGridSpec(
            num_scalar_prefetch=2,
            grid=(count,),
            in_specs=[
                pl.BlockSpec((slots, share), lambda t, at, half: (0, at[t])),
                pl.BlockSpec((slots, share), lambda t, at, half: (0, at[t])),
                pl.BlockSpec((slots, wide), lambda t, at, half: (0, half[t])),
                pl.BlockSpec((slots, narrow), lambda t, at, half: (0, half[t])),
            ],
            out_specs=pl.BlockSpec((1, share, wide + narrow), lambda t, at, half: (t, 0, 0)),
        ),
        compiler_params=pltpu.CompilerParams(vmem_limit_bytes=32 * 1024 * 1024),
        cost_estimate=BRIEF,
    )(shares, halves, rows, grads, pre_grad, hidden)


def mean_kernel(count, left, left_last, right, right_last, wide_out, narrow_out):
    wide = wide_out.shape[1] // 2
    narrow = narrow_out.shape[1] // 2
    for at, (own, last) in enumerate(((left, left_last), (right, right_last))):
        total = (own[...] + last[...].astype(F32)) / count
        wide_out[:, at * wide : (at + 1) * wide] = total[:, :wide]
        narrow_out[:, at * narrow : (at + 1) * narrow] = total[:, wide:]


def add(left, right):
    return left.astype(F32) + right.astype(F32)


def cube_shares(me, share, rows, grads, pre_grad, hidden):
    size = lax.axis_size("dp")
    make = functools.partial(gradient_shares, me=me, share=share)
    operands = dict(rows=rows, grads=grads, pre_grad=pre_grad, hidden=hidden)

    def swap(block, bit):
        return lax.ppermute(block, "dp", [(at, at ^ bit) for at in range(size)])

    first = make([(3, 0), (7, 0), (5, 1), (7, 1)], **operands)
    first_in = swap(first, 1)
    later = make([(1, 0), (5, 0), (1, 1), (3, 1)], **operands)
    later_in = swap(later, 1)
    keep_first = make([(2, 0), (6, 0), (4, 1), (6, 1)], **operands)
    keep_later = make([(0, 0), (4, 0), (0, 1), (2, 1)], **operands)
    sent = add(keep_first, first_in).astype(BF16)
    left_in = swap(sent[:2], 2)
    right_in = swap(sent[2:], 4)
    kept = add(keep_later, later_in)
    left, right = kept[:2] + left_in.astype(F32), kept[2:] + right_in.astype(F32)
    left_last = swap(left[1].astype(BF16), 4)
    right_last = swap(right[1].astype(BF16), 2)
    wide, narrow = pre_grad.shape[1], hidden.shape[1]
    return pl.pallas_call(
        functools.partial(mean_kernel, size),
        out_shape=(
            jax.ShapeDtypeStruct((share, wide), F32),
            jax.ShapeDtypeStruct((share, narrow), F32),
        ),
        in_specs=[pl.BlockSpec(memory_space=pltpu.VMEM)] * 4,
        compiler_params=pltpu.CompilerParams(vmem_limit_bytes=32 * 1024 * 1024),
        cost_estimate=BRIEF,
    )(left[0], left_last, right[0], right_last)


def after(value, *others):
    return lax.optimization_barrier((value, *others))[0]


def call(kernel, out_shape, inputs):
    return pl.pallas_call(
        kernel,
        out_shape=out_shape,
        in_specs=[pl.BlockSpec(memory_space=pltpu.SMEM)]
        + [pl.BlockSpec(memory_space=pltpu.VMEM)] * (len(inputs) - 1),
        compiler_params=pltpu.CompilerParams(vmem_limit_bytes=32 * 1024 * 1024),
        cost_estimate=BRIEF,
    )(*inputs)


def body(tokens, routes, route_scores, out_grad, gate_up, down_weight):
    experts = lax.axis_size("expert")
    groups = lax.axis_size("dp")
    toks, width = tokens.shape
    tops = routes.shape[1]
    units = down_weight.shape[2]
    capacity = (toks * tops + experts - 1) // experts
    slots = experts * capacity
    share = width // groups
    direct = experts <= 8 and capacity % 16 == 0
    w_in, w_out = gate_up[0], down_weight[0]
    routes_t, scores_t = routes.T, route_scores.T
    me = lax.axis_index("expert") if direct else jnp.int32(0)
    first = me.astype(jnp.int32).reshape(1)
    sizes = [capacity] * experts if direct else [slots]
    block_shapes = [jax.ShapeDtypeStruct((size, width), BF16) for size in sizes]

    def exchange(blocks, sign):
        if not direct:
            block = blocks[0].reshape(experts, capacity, width)
            moved = lax.all_to_all(block, "expert", split_axis=0, concat_axis=0, tiled=True)
            return [moved.reshape(slots, width)]
        out = [blocks[0]]
        for step in range(1, experts):
            pairs = [(at, (at + sign * step) % experts) for at in range(experts)]
            out.append(lax.ppermute(blocks[step], "expert", pairs))
        return out

    def joined(blocks):
        return blocks[0] if len(blocks) == 1 else jnp.concatenate(blocks, axis=0)

    def split(rows):
        return [rows[at : at + sizes[0]] for at in range(0, slots, sizes[0])]

    sent_rows = call(
        functools.partial(dispatch_kernel, experts, capacity, False),
        block_shapes,
        (first, routes_t, tokens),
    )
    got_rows = exchange(sent_rows, 1)
    token_rows = joined(got_rows)
    sent_grads = call(
        functools.partial(dispatch_kernel, experts, capacity, True),
        block_shapes,
        (first, routes_t, scores_t, out_grad),
    )
    if direct:
        sent_grads = after(sent_grads, got_rows[1])
    got_grads = exchange(sent_grads, 1)
    grad_rows = joined(got_grads)

    preact = jnp.dot(token_rows, w_in, preferred_element_type=F32)
    gate, up = preact[:, :units], preact[:, units:]
    hidden = (jax.nn.silu(gate) * up).astype(BF16)
    produced = jnp.dot(hidden, w_out.T, preferred_element_type=F32).astype(BF16)
    if direct:
        grad_rows = after(grad_rows, produced)
        produced = after(produced, got_grads[1])
    returned = exchange(split(produced), -1)

    hidden_grad = jnp.dot(grad_rows, w_out, preferred_element_type=F32)
    sigmoid = jax.nn.sigmoid(gate)
    gate_grad = hidden_grad * up * sigmoid * (1.0 + gate * (1.0 - sigmoid))
    up_grad = hidden_grad * gate * sigmoid
    pre_grad = jnp.concatenate([gate_grad, up_grad], axis=1).astype(BF16)
    input_grad = jnp.dot(pre_grad, w_in.T, preferred_element_type=F32).astype(BF16)
    if direct:
        input_grad = after(input_grad, returned[1])
    sent_back = exchange(split(input_grad), -1)

    if groups == 8 and share % 128 == 0:
        grad_in, grad_down = cube_shares(
            lax.axis_index("dp"), share, token_rows, grad_rows, pre_grad, hidden
        )
    else:

        def summed(left, right):
            part = contract(left, right).astype(BF16)
            whole = lax.psum_scatter(part, "dp", scatter_dimension=0, tiled=True)
            return whole.astype(F32) / groups

        grad_in = summed(token_rows, pre_grad)
        grad_down = summed(grad_rows, hidden)
    grad_in = grad_in.reshape(1, share, 2 * units)
    grad_down = grad_down.reshape(1, share, units)

    out_shape = jax.ShapeDtypeStruct((toks, width), BF16)
    mixed_out = call(
        functools.partial(combine_kernel, experts, capacity, True),
        out_shape,
        (first, routes_t, scores_t, *returned),
    )
    token_grad = call(
        functools.partial(combine_kernel, experts, capacity, False),
        out_shape,
        (first, routes_t, *sent_back),
    )
    return (mixed_out, token_grad, grad_in, grad_down)


def solution(mesh):
    in_specs = (
        P(("dp", "expert"), None),
        P(("dp", "expert"), None),
        P(("dp", "expert"), None),
        P(("dp", "expert"), None),
        P("expert", None, None),
        P("expert", None, None),
    )
    out_specs = (
        P(("dp", "expert"), None),
        P(("dp", "expert"), None),
        P("expert", "dp", None),
        P("expert", "dp", None),
    )
    return jax.shard_map(body, mesh=mesh, in_specs=in_specs, out_specs=out_specs, check_vma=False)
```

```python
import functools

import jax
import jax.numpy as jnp
from jax import lax
from jax.experimental import pallas as pl
from jax.experimental.pallas import tpu as pltpu
from jax.sharding import PartitionSpec as P

F32 = jnp.float32
BF16 = jnp.bfloat16
BRIEF = pl.CostEstimate(flops=1024, bytes_accessed=1024, transcendentals=0)


def contract(left, right):
    return lax.dot_general(left, right, (((0,), (0,)), ((), ())), preferred_element_type=F32)


def slot_rows(first, routes, experts, capacity):
    tops, toks = routes.shape
    padded = -(-experts // 8) * 8
    rows = lax.broadcasted_iota(jnp.int32, (padded, toks), 0)
    ids = rows + first
    ids = jnp.where(ids >= experts, ids - experts, ids)
    ids = jnp.where(rows < experts, ids, -1)
    hits = [routes[k : k + 1, :] == ids for k in range(tops)]
    named = functools.reduce(jnp.logical_or, hits)
    before = lax.broadcasted_iota(jnp.int32, (toks, toks), 0) < lax.broadcasted_iota(
        jnp.int32, (toks, toks), 1
    )
    position = jnp.dot(
        named.astype(F32).astype(BF16),
        before.astype(F32).astype(BF16),
        preferred_element_type=F32,
    )
    slot = position + (rows * capacity).astype(F32)
    return [jnp.sum(jnp.where(hit, slot, 0.0), axis=0, keepdims=True) for hit in hits]


def weight_rows(scores):
    grown = jnp.exp(scores)
    return grown / jnp.sum(grown, axis=0, keepdims=True)


def to_column(row):
    toks = row.shape[1]
    same = lax.broadcasted_iota(jnp.int32, (toks, toks), 0) == lax.broadcasted_iota(
        jnp.int32, (toks, toks), 1
    )
    return jnp.sum(jnp.where(same, row, 0.0), axis=1, keepdims=True)


def put_blocks(outs, rows, columns):
    start = 0
    for out in outs:
        size = out.shape[0]
        out[:, columns] = rows[start : start + size]
        start += size


def column_steps(width):
    step = 512 if width % 512 == 0 else width
    return [slice(at, at + step) for at in range(0, width, step)]


def dispatch_kernel(experts, capacity, weighted, first, routes, *refs):
    scores = refs[0] if weighted else None
    values, outs = refs[weighted], refs[weighted + 1 :]
    slots, toks = experts * capacity, values.shape[0]
    places = lax.broadcasted_iota(jnp.int32, (slots, toks), 0).astype(F32)
    hits = [places == row for row in slot_rows(first[0], routes[...], experts, capacity)]
    picker = functools.reduce(jnp.logical_or, hits).astype(F32).astype(BF16)
    if weighted:
        weights = weight_rows(scores[...])
        scale = sum(
            jnp.sum(jnp.where(hit, weights[k : k + 1, :], 0.0), axis=1, keepdims=True)
            for k, hit in enumerate(hits)
        )
    for columns in column_steps(values.shape[1]):
        rows = jnp.dot(picker, values[:, columns], preferred_element_type=F32)
        if weighted:
            rows = rows * scale
        put_blocks(outs, rows.astype(BF16), columns)


def combine_kernel(experts, capacity, weighted, first, routes, *refs):
    scores = refs[0] if weighted else None
    blocks, out = refs[weighted:-1], refs[-1]
    slots, toks = experts * capacity, out.shape[0]
    places = lax.broadcasted_iota(jnp.int32, (toks, slots), 1).astype(F32)
    hits = [
        places == to_column(row) for row in slot_rows(first[0], routes[...], experts, capacity)
    ]
    if weighted:
        weights = weight_rows(scores[...])
        scales = [to_column(weights[k : k + 1, :]) for k in range(len(hits))]
        pickers = [hit.astype(F32).astype(BF16) for hit in hits]
    else:
        pickers = [functools.reduce(jnp.logical_or, hits).astype(F32).astype(BF16)]
    for columns in column_steps(out.shape[1]):
        rows = [block[:, columns] for block in blocks]
        rows = rows[0] if len(rows) == 1 else jnp.concatenate(rows, axis=0)
        picked = [jnp.dot(picker, rows, preferred_element_type=F32) for picker in pickers]
        if weighted:
            picked = [scale * part for scale, part in zip(scales, picked)]
        out[:, columns] = sum(picked).astype(out.dtype)


def whole(count):
    return [pl.BlockSpec(memory_space=pltpu.VMEM)] * count


ROOMY = pltpu.CompilerParams(vmem_limit_bytes=40 * 1024 * 1024)


def write_shares(at, rows, grads, pre_grad, hidden, out):
    share = out.shape[1]
    wide, narrow = pre_grad.shape[1] // 2, hidden.shape[1] // 2

    def write(t, half):
        own = pl.ds(pl.multiple_of(at[t] * share, share), share)
        out[t, :, :wide] = contract(
            rows[:, own], pre_grad[:, half * wide : (half + 1) * wide]
        ).astype(out.dtype)
        out[t, :, wide:] = contract(
            grads[:, own], hidden[:, half * narrow : (half + 1) * narrow]
        ).astype(out.dtype)

    for half in range(2):

        @pl.loop(0, out.shape[0] // 2)
        def _(n):
            write(n // 2 * 4 + half * 2 + n % 2, half)


def join_blocks(blocks, rows):
    start = 0
    for block in blocks:
        rows[start : start + block.shape[0], :] = block[...]
        start += block.shape[0]


def forward_kernel(count, *refs):
    blocks, (w_in, down), (rows, preact, hidden) = (
        refs[:count],
        refs[count : count + 2],
        refs[count + 2 : count + 5],
    )
    outs = refs[count + 5 :]
    join_blocks(blocks, rows)
    width, units = down.shape
    step = 256 if units % 256 == 0 else units
    for begin in range(0, units, step):
        gate_at, up_at = slice(begin, begin + step), slice(units + begin, units + begin + step)
        gate = jnp.dot(rows[...], w_in[:, gate_at], preferred_element_type=F32)
        up = jnp.dot(rows[...], w_in[:, up_at], preferred_element_type=F32)
        preact[:, gate_at] = gate
        preact[:, up_at] = up
        hidden[:, gate_at] = (gate / (1.0 + jnp.exp(-gate)) * up).astype(BF16)
    step = 512 if width % 512 == 0 else width

    @pl.loop(0, width // step)
    def _(c):
        own = pl.ds(pl.multiple_of(c * step, step), step)
        part = lax.dot_general(
            hidden[...], down[own, :], (((1,), (1,)), ((), ())), preferred_element_type=F32
        )
        put_blocks(outs, part.astype(BF16), own)


def forward(blocks, w_in, down):
    width, units = down.shape
    slots = sum(block.shape[0] for block in blocks)
    rows, preact, hidden, *outs = pl.pallas_call(
        functools.partial(forward_kernel, len(blocks)),
        out_shape=(
            jax.ShapeDtypeStruct((slots, width), BF16),
            jax.ShapeDtypeStruct((slots, 2 * units), F32),
            jax.ShapeDtypeStruct((slots, units), BF16),
            *[jax.ShapeDtypeStruct(block.shape, BF16) for block in blocks],
        ),
        in_specs=whole(2 + len(blocks)),
        out_specs=whole(3 + len(blocks)),
        compiler_params=ROOMY,
        cost_estimate=BRIEF,
    )(*blocks, w_in, down)
    return rows, preact, hidden, outs


def backward_kernel(at, preact, hidden, rows, down, *refs):
    blocks, (pre_grad, grads, out) = refs[:-3], refs[-3:]
    join_blocks(blocks, grads)
    units = hidden.shape[1]
    step = 256 if units % 256 == 0 else units
    for begin in range(0, units, step):
        gate = preact[:, begin : begin + step]
        up = preact[:, units + begin : units + begin + step]
        hidden_grad = jnp.dot(
            grads[...], down[:, begin : begin + step], preferred_element_type=F32
        )
        sigmoid = 1.0 / (1.0 + jnp.exp(-gate))
        gate_grad = hidden_grad * up * sigmoid * (1.0 + gate * (1.0 - sigmoid))
        up_grad = hidden_grad * gate * sigmoid
        pre_grad[:, begin : begin + step] = gate_grad.astype(BF16)
        pre_grad[:, units + begin : units + begin + step] = up_grad.astype(BF16)
    write_shares(at, rows, grads, pre_grad, hidden, out)


def backward(at, share, preact, hidden, rows, down, blocks):
    slots, width = rows.shape
    units = hidden.shape[1]
    return pl.pallas_call(
        backward_kernel,
        out_shape=(
            jax.ShapeDtypeStruct((slots, 2 * units), BF16),
            jax.ShapeDtypeStruct((slots, width), BF16),
            jax.ShapeDtypeStruct((at.shape[0], share, 3 * units // 2), BF16),
        ),
        in_specs=[pl.BlockSpec(memory_space=pltpu.SMEM)] + whole(4 + len(blocks)),
        out_specs=whole(3),
        compiler_params=ROOMY,
        cost_estimate=BRIEF,
    )(at, preact, hidden, rows, down, *blocks)


def rest_kernel(at, rows, grads, pre_grad, hidden, w_in, *outs):
    write_shares(at, rows, grads, pre_grad, hidden, outs[0])
    width = rows.shape[1]
    step = 512 if width % 512 == 0 else width

    @pl.loop(0, width // step)
    def _(c):
        own = pl.ds(pl.multiple_of(c * step, step), step)
        part = lax.dot_general(
            pre_grad[...], w_in[own, :], (((1,), (1,)), ((), ())), preferred_element_type=F32
        )
        put_blocks(outs[1:], part.astype(BF16), own)


def rest(at, share, rows, grads, pre_grad, hidden, w_in, sizes):
    width, units = rows.shape[1], hidden.shape[1]
    return pl.pallas_call(
        rest_kernel,
        out_shape=(
            jax.ShapeDtypeStruct((at.shape[0], share, 3 * units // 2), BF16),
            *[jax.ShapeDtypeStruct((size, width), BF16) for size in sizes],
        ),
        in_specs=[pl.BlockSpec(memory_space=pltpu.SMEM)] + whole(5),
        out_specs=whole(1 + len(sizes)),
        compiler_params=ROOMY,
        cost_estimate=BRIEF,
    )(at, rows, grads, pre_grad, hidden, w_in)


def add_kernel(kept, got, left, right, later):
    half = left.shape[0]
    left[...] = add(kept[:half], got[:half]).astype(BF16)
    right[...] = add(kept[half : 2 * half], got[half : 2 * half]).astype(BF16)
    later[...] = add(kept[2 * half :], got[2 * half :])


def next_kernel(later, left_in, right_in, left_send, right_send, left, right):
    left[...] = add(later[0], left_in[0])
    left_send[...] = add(later[1], left_in[1]).astype(BF16)
    right[...] = add(later[2], right_in[0])
    right_send[...] = add(later[3], right_in[1]).astype(BF16)


def mean_kernel(count, left, left_last, right, right_last, wide_out, narrow_out):
    wide = wide_out.shape[1] // 2
    narrow = narrow_out.shape[1] // 2
    for at, (own, last) in enumerate(((left, left_last), (right, right_last))):
        total = (own[...] + last[...].astype(F32)) / count
        wide_out[:, at * wide : (at + 1) * wide] = total[:, :wide]
        narrow_out[:, at * narrow : (at + 1) * narrow] = total[:, wide:]


def add(left, right):
    return left.astype(F32) + right.astype(F32)


CUBE_SEND = (3, 7, 5, 7, 1, 5, 1, 3)


def cube_sum(sent, kept, earlier):
    size = lax.axis_size("dp")
    _, share, columns = sent.shape

    def swap(block, bit):
        return lax.ppermute(block, "dp", [(at, at ^ bit) for at in range(size)])

    half = jax.ShapeDtypeStruct((2, share, columns), BF16)
    one = jax.ShapeDtypeStruct((share, columns), BF16)
    own = jax.ShapeDtypeStruct((share, columns), F32)
    left, right, later = pl.pallas_call(
        add_kernel,
        out_shape=(half, half, jax.ShapeDtypeStruct((4, share, columns), F32)),
        in_specs=whole(2),
        out_specs=whole(3),
        compiler_params=ROOMY,
        cost_estimate=BRIEF,
    )(kept, swap(sent, 1))
    left_send, right_send, left, right = pl.pallas_call(
        next_kernel,
        out_shape=(one, one, own, own),
        in_specs=whole(3),
        out_specs=whole(4),
        compiler_params=ROOMY,
        cost_estimate=BRIEF,
    )(*after((later, swap(left, 2), swap(right, 4)), *earlier))
    wide, narrow = 4 * columns // 3, 2 * columns // 3
    return pl.pallas_call(
        functools.partial(mean_kernel, size),
        out_shape=(
            jax.ShapeDtypeStruct((share, wide), F32),
            jax.ShapeDtypeStruct((share, narrow), F32),
        ),
        in_specs=whole(4),
        compiler_params=ROOMY,
        cost_estimate=BRIEF,
    )(left, swap(left_send, 4), right, swap(right_send, 2))


def after(value, *others):
    return lax.optimization_barrier((value, *others))[0]


def call(kernel, out_shape, inputs):
    return pl.pallas_call(
        kernel,
        out_shape=out_shape,
        in_specs=[pl.BlockSpec(memory_space=pltpu.SMEM)]
        + [pl.BlockSpec(memory_space=pltpu.VMEM)] * (len(inputs) - 1),
        compiler_params=pltpu.CompilerParams(vmem_limit_bytes=32 * 1024 * 1024),
        cost_estimate=BRIEF,
    )(*inputs)


def body(tokens, routes, route_scores, out_grad, gate_up, down_weight):
    experts = lax.axis_size("expert")
    groups = lax.axis_size("dp")
    toks, width = tokens.shape
    tops = routes.shape[1]
    units = down_weight.shape[2]
    capacity = (toks * tops + experts - 1) // experts
    slots = experts * capacity
    share = width // groups
    direct = experts <= 8 and capacity % 16 == 0
    w_in, w_out = gate_up[0], down_weight[0]
    routes_t, scores_t = routes.T, route_scores.T
    me = lax.axis_index("expert") if direct else jnp.int32(0)
    first = me.astype(jnp.int32).reshape(1)
    sizes = [capacity] * experts if direct else [slots]
    block_shapes = [jax.ShapeDtypeStruct((size, width), BF16) for size in sizes]

    def exchange(blocks, sign):
        if not direct:
            block = blocks[0].reshape(experts, capacity, width)
            moved = lax.all_to_all(block, "expert", split_axis=0, concat_axis=0, tiled=True)
            return [moved.reshape(slots, width)]
        out = [blocks[0]]
        for step in range(1, experts):
            pairs = [(at, (at + sign * step) % experts) for at in range(experts)]
            out.append(lax.ppermute(blocks[step], "expert", pairs))
        return out

    def joined(blocks):
        return blocks[0] if len(blocks) == 1 else jnp.concatenate(blocks, axis=0)

    def split(rows):
        return [rows[at : at + sizes[0]] for at in range(0, slots, sizes[0])]

    sent_rows = call(
        functools.partial(dispatch_kernel, experts, capacity, False),
        block_shapes,
        (first, routes_t, tokens),
    )
    got_rows = exchange(sent_rows, 1)
    sent_grads = call(
        functools.partial(dispatch_kernel, experts, capacity, True),
        block_shapes,
        (first, routes_t, scores_t, out_grad),
    )
    cube = direct and groups == 8 and share % 256 == 0
    if cube:
        sent_grads = after(sent_grads, got_rows[1])
        got_grads = exchange(sent_grads, 1)
        token_rows, preact, hidden, produced = forward(got_rows, w_in, w_out)
        returned = exchange(produced, -1)
        got_grads = after(got_grads, returned[1], returned[-1])
        own = lax.axis_index("dp")
        send_at = jnp.stack([jnp.bitwise_xor(own, j) for j in CUBE_SEND]).astype(jnp.int32)
        pre_grad, grad_rows, sent = backward(
            send_at, share, preact, hidden, token_rows, w_out, got_grads
        )
        kept, *input_grads = rest(
            jnp.bitwise_xor(send_at, 1),
            share,
            token_rows,
            grad_rows,
            pre_grad,
            hidden,
            w_in,
            sizes,
        )
        sent_back = exchange(input_grads, -1)
    else:
        token_rows = joined(got_rows)
        grad_rows = joined(exchange(sent_grads, 1))
        preact = jnp.dot(token_rows, w_in, preferred_element_type=F32)
        gate, up = preact[:, :units], preact[:, units:]
        hidden = (jax.nn.silu(gate) * up).astype(BF16)
        produced = jnp.dot(hidden, w_out.T, preferred_element_type=F32).astype(BF16)
        returned = exchange(split(produced), -1)
        hidden_grad = jnp.dot(grad_rows, w_out, preferred_element_type=F32)
        sigmoid = jax.nn.sigmoid(gate)
        gate_grad = hidden_grad * up * sigmoid * (1.0 + gate * (1.0 - sigmoid))
        up_grad = hidden_grad * gate * sigmoid
        pre_grad = jnp.concatenate([gate_grad, up_grad], axis=1).astype(BF16)
        input_grad = jnp.dot(pre_grad, w_in.T, preferred_element_type=F32).astype(BF16)
        sent_back = exchange(split(input_grad), -1)

    out_shape = jax.ShapeDtypeStruct((toks, width), BF16)
    mixed_out = call(
        functools.partial(combine_kernel, experts, capacity, True),
        out_shape,
        (first, routes_t, scores_t, *returned),
    )
    if cube:
        grad_in, grad_down = cube_sum(sent, kept, (mixed_out, sent_back[1]))
    else:

        def summed(left, right):
            part = contract(left, right).astype(BF16)
            total = lax.psum_scatter(part, "dp", scatter_dimension=0, tiled=True)
            return total.astype(F32) / groups

        grad_in = summed(token_rows, pre_grad)
        grad_down = summed(grad_rows, hidden)
    grad_in = grad_in.reshape(1, share, 2 * units)
    grad_down = grad_down.reshape(1, share, units)

    token_grad = call(
        functools.partial(combine_kernel, experts, capacity, False),
        out_shape,
        (first, routes_t, *sent_back),
    )
    return (mixed_out, token_grad, grad_in, grad_down)


def solution(mesh):
    in_specs = (
        P(("dp", "expert"), None),
        P(("dp", "expert"), None),
        P(("dp", "expert"), None),
        P(("dp", "expert"), None),
        P("expert", None, None),
        P("expert", None, None),
    )
    out_specs = (
        P(("dp", "expert"), None),
        P(("dp", "expert"), None),
        P("expert", "dp", None),
        P("expert", "dp", None),
    )
    return jax.shard_map(body, mesh=mesh, in_specs=in_specs, out_specs=out_specs, check_vma=False)
```

```python
import functools

import jax
import jax.numpy as jnp
from jax import lax
from jax.experimental import pallas as pl
from jax.experimental.pallas import tpu as pltpu
from jax.sharding import PartitionSpec as P

F32 = jnp.float32
BF16 = jnp.bfloat16
BRIEF = pl.CostEstimate(flops=1024, bytes_accessed=1024, transcendentals=0)


def contract(left, right):
    return lax.dot_general(left, right, (((0,), (0,)), ((), ())), preferred_element_type=F32)


def slot_rows(first, routes, experts, capacity):
    tops, toks = routes.shape
    padded = -(-experts // 8) * 8
    rows = lax.broadcasted_iota(jnp.int32, (padded, toks), 0)
    ids = rows + first
    ids = jnp.where(ids >= experts, ids - experts, ids)
    ids = jnp.where(rows < experts, ids, -1)
    hits = [routes[k : k + 1, :] == ids for k in range(tops)]
    named = functools.reduce(jnp.logical_or, hits)
    before = lax.broadcasted_iota(jnp.int32, (toks, toks), 0) < lax.broadcasted_iota(
        jnp.int32, (toks, toks), 1
    )
    position = jnp.dot(
        named.astype(F32).astype(BF16),
        before.astype(F32).astype(BF16),
        preferred_element_type=F32,
    )
    slot = position + (rows * capacity).astype(F32)
    return [jnp.sum(jnp.where(hit, slot, 0.0), axis=0, keepdims=True) for hit in hits]


def weight_rows(scores):
    grown = jnp.exp(scores)
    return grown / jnp.sum(grown, axis=0, keepdims=True)


def to_column(row):
    toks = row.shape[1]
    same = lax.broadcasted_iota(jnp.int32, (toks, toks), 0) == lax.broadcasted_iota(
        jnp.int32, (toks, toks), 1
    )
    return jnp.sum(jnp.where(same, row, 0.0), axis=1, keepdims=True)


def put_blocks(outs, rows, columns):
    start = 0
    for out in outs:
        size = out.shape[0]
        out[:, columns] = rows[start : start + size]
        start += size


def column_steps(width):
    step = 512 if width % 512 == 0 else width
    return [slice(at, at + step) for at in range(0, width, step)]


def dispatch_kernel(experts, capacity, weighted, first, routes, *refs):
    scores = refs[0] if weighted else None
    values, outs = refs[weighted], refs[weighted + 1 :]
    slots, toks = experts * capacity, values.shape[0]
    places = lax.broadcasted_iota(jnp.int32, (slots, toks), 0).astype(F32)
    hits = [places == row for row in slot_rows(first[0], routes[...], experts, capacity)]
    picker = functools.reduce(jnp.logical_or, hits).astype(F32).astype(BF16)
    if weighted:
        weights = weight_rows(scores[...])
        scale = sum(
            jnp.sum(jnp.where(hit, weights[k : k + 1, :], 0.0), axis=1, keepdims=True)
            for k, hit in enumerate(hits)
        )
    for columns in column_steps(values.shape[1]):
        rows = jnp.dot(picker, values[:, columns], preferred_element_type=F32)
        if weighted:
            rows = rows * scale
        put_blocks(outs, rows.astype(BF16), columns)


def combine_kernel(experts, capacity, weighted, first, routes, *refs):
    scores = refs[0] if weighted else None
    blocks, out = refs[weighted:-1], refs[-1]
    slots, toks = experts * capacity, out.shape[0]
    places = lax.broadcasted_iota(jnp.int32, (toks, slots), 1).astype(F32)
    hits = [
        places == to_column(row) for row in slot_rows(first[0], routes[...], experts, capacity)
    ]
    if weighted:
        weights = weight_rows(scores[...])
        scales = [to_column(weights[k : k + 1, :]) for k in range(len(hits))]
        pickers = [hit.astype(F32).astype(BF16) for hit in hits]
    else:
        pickers = [functools.reduce(jnp.logical_or, hits).astype(F32).astype(BF16)]
    for columns in column_steps(out.shape[1]):
        rows = [block[:, columns] for block in blocks]
        rows = rows[0] if len(rows) == 1 else jnp.concatenate(rows, axis=0)
        picked = [jnp.dot(picker, rows, preferred_element_type=F32) for picker in pickers]
        if weighted:
            picked = [scale * part for scale, part in zip(scales, picked)]
        out[:, columns] = sum(picked).astype(out.dtype)


def whole(count):
    return [pl.BlockSpec(memory_space=pltpu.VMEM)] * count


ROOMY = pltpu.CompilerParams(vmem_limit_bytes=16 * 1024 * 1024)


def write_shares(at, rows_t, grads_t, pre_grad, hidden, out):
    share = out.shape[1]
    wide, narrow = pre_grad.shape[1] // 2, hidden.shape[1] // 2

    def write(t, half):
        own = pl.ds(pl.multiple_of(at[t] * share, share), share)
        out[t, :, :wide] = jnp.dot(
            rows_t[own, :],
            pre_grad[:, half * wide : (half + 1) * wide],
            preferred_element_type=F32,
        ).astype(out.dtype)
        out[t, :, wide:] = jnp.dot(
            grads_t[own, :],
            hidden[:, half * narrow : (half + 1) * narrow],
            preferred_element_type=F32,
        ).astype(out.dtype)

    for half in range(2):

        @pl.loop(0, out.shape[0] // 2)
        def _(n):
            write(n // 2 * 4 + half * 2 + n % 2, half)


def join_blocks(blocks, rows):
    start = 0
    for block in blocks:
        rows[start : start + block.shape[0], :] = block[...]
        start += block.shape[0]


def transpose_into(rows, rows_t):
    width = rows.shape[1]
    step = 256 if width % 256 == 0 else width

    @pl.loop(0, width // step)
    def _(c):
        own = pl.ds(pl.multiple_of(c * step, step), step)
        rows_t[own, :] = rows[:, own].T


def forward_kernel(count, *refs):
    blocks, (w_in, down), (rows_t, preact, hidden), outs, rows = (
        refs[:count],
        refs[count : count + 2],
        refs[count + 2 : count + 5],
        refs[count + 5 : -1],
        refs[-1],
    )
    join_blocks(blocks, rows)
    width, units = down.shape
    step = 256 if units % 256 == 0 else units
    for begin in range(0, units, step):
        gate_at, up_at = slice(begin, begin + step), slice(units + begin, units + begin + step)
        gate = jnp.dot(rows[...], w_in[:, gate_at], preferred_element_type=F32)
        up = jnp.dot(rows[...], w_in[:, up_at], preferred_element_type=F32)
        preact[:, gate_at] = gate
        preact[:, up_at] = up
        hidden[:, gate_at] = (gate / (1.0 + jnp.exp(-gate)) * up).astype(BF16)
    step = 512 if width % 512 == 0 else width

    @pl.loop(0, width // step)
    def _(c):
        own = pl.ds(pl.multiple_of(c * step, step), step)
        part = lax.dot_general(
            hidden[...], down[own, :], (((1,), (1,)), ((), ())), preferred_element_type=F32
        )
        put_blocks(outs, part.astype(BF16), own)

    transpose_into(rows, rows_t)


def forward(blocks, w_in, down):
    width, units = down.shape
    slots = sum(block.shape[0] for block in blocks)
    rows_t, preact, hidden, *outs = pl.pallas_call(
        functools.partial(forward_kernel, len(blocks)),
        out_shape=(
            jax.ShapeDtypeStruct((width, slots), BF16),
            jax.ShapeDtypeStruct((slots, 2 * units), F32),
            jax.ShapeDtypeStruct((slots, units), BF16),
            *[jax.ShapeDtypeStruct(block.shape, BF16) for block in blocks],
        ),
        in_specs=whole(2 + len(blocks)),
        out_specs=whole(3 + len(blocks)),
        scratch_shapes=[pltpu.VMEM((slots, width), BF16)],
        compiler_params=ROOMY,
        cost_estimate=BRIEF,
    )(*blocks, w_in, down)
    return rows_t, preact, hidden, outs


def backward_kernel(preact, down, *refs):
    blocks, (pre_grad, grads_t, grads) = refs[:-3], refs[-3:]
    join_blocks(blocks, grads)
    transpose_into(grads, grads_t)
    units = down.shape[1]
    step = 256 if units % 256 == 0 else units
    for begin in range(0, units, step):
        gate = preact[:, begin : begin + step]
        up = preact[:, units + begin : units + begin + step]
        hidden_grad = jnp.dot(
            grads[...], down[:, begin : begin + step], preferred_element_type=F32
        )
        sigmoid = 1.0 / (1.0 + jnp.exp(-gate))
        gate_grad = hidden_grad * up * sigmoid * (1.0 + gate * (1.0 - sigmoid))
        up_grad = hidden_grad * gate * sigmoid
        pre_grad[:, begin : begin + step] = gate_grad.astype(BF16)
        pre_grad[:, units + begin : units + begin + step] = up_grad.astype(BF16)


def backward(preact, down, blocks):
    width, units = down.shape
    slots = preact.shape[0]
    return pl.pallas_call(
        backward_kernel,
        out_shape=(
            jax.ShapeDtypeStruct((slots, 2 * units), BF16),
            jax.ShapeDtypeStruct((width, slots), BF16),
        ),
        in_specs=whole(2 + len(blocks)),
        out_specs=whole(2),
        scratch_shapes=[pltpu.VMEM((slots, width), BF16)],
        compiler_params=ROOMY,
        cost_estimate=BRIEF,
    )(preact, down, *blocks)


def shares(at, share, rows_t, grads_t, pre_grad, hidden):
    units = hidden.shape[1]
    return pl.pallas_call(
        write_shares,
        out_shape=jax.ShapeDtypeStruct((at.shape[0], share, 3 * units // 2), BF16),
        in_specs=[pl.BlockSpec(memory_space=pltpu.SMEM)] + whole(4),
        out_specs=whole(1)[0],
        compiler_params=ROOMY,
        cost_estimate=BRIEF,
    )(at, rows_t, grads_t, pre_grad, hidden)


def input_kernel(pre_grad, w_in, *outs):
    width = w_in.shape[0]
    step = 512 if width % 512 == 0 else width

    @pl.loop(0, width // step)
    def _(c):
        own = pl.ds(pl.multiple_of(c * step, step), step)
        part = lax.dot_general(
            pre_grad[...], w_in[own, :], (((1,), (1,)), ((), ())), preferred_element_type=F32
        )
        put_blocks(outs, part.astype(BF16), own)


def input_gradients(pre_grad, w_in, sizes):
    return pl.pallas_call(
        input_kernel,
        out_shape=[jax.ShapeDtypeStruct((size, w_in.shape[0]), BF16) for size in sizes],
        in_specs=whole(2),
        out_specs=whole(len(sizes)),
        compiler_params=ROOMY,
        cost_estimate=BRIEF,
    )(pre_grad, w_in)


def add_kernel(kept, got, left, right, later):
    half = left.shape[0]
    left[...] = add(kept[:half], got[:half]).astype(BF16)
    right[...] = add(kept[half : 2 * half], got[half : 2 * half]).astype(BF16)
    later[...] = add(kept[2 * half :], got[2 * half :])


def next_kernel(later, left_in, right_in, left_send, right_send, left, right):
    left[...] = add(later[0], left_in[0])
    left_send[...] = add(later[1], left_in[1]).astype(BF16)
    right[...] = add(later[2], right_in[0])
    right_send[...] = add(later[3], right_in[1]).astype(BF16)


def mean_kernel(count, left, left_last, right, right_last, wide_out, narrow_out):
    wide = wide_out.shape[1] // 2
    narrow = narrow_out.shape[1] // 2
    for at, (own, last) in enumerate(((left, left_last), (right, right_last))):
        total = (own[...] + last[...].astype(F32)) / count
        wide_out[:, at * wide : (at + 1) * wide] = total[:, :wide]
        narrow_out[:, at * narrow : (at + 1) * narrow] = total[:, wide:]


def add(left, right):
    return left.astype(F32) + right.astype(F32)


CUBE_SEND = (3, 7, 5, 7, 1, 5, 1, 3)


def cube_sum(sent, kept, earlier):
    size = lax.axis_size("dp")
    _, share, columns = sent.shape

    def swap(block, bit):
        return lax.ppermute(block, "dp", [(at, at ^ bit) for at in range(size)])

    half = jax.ShapeDtypeStruct((2, share, columns), BF16)
    one = jax.ShapeDtypeStruct((share, columns), BF16)
    own = jax.ShapeDtypeStruct((share, columns), F32)
    left, right, later = pl.pallas_call(
        add_kernel,
        out_shape=(half, half, jax.ShapeDtypeStruct((4, share, columns), F32)),
        in_specs=whole(2),
        out_specs=whole(3),
        compiler_params=ROOMY,
        cost_estimate=BRIEF,
    )(kept, swap(sent, 1))
    left_send, right_send, left, right = pl.pallas_call(
        next_kernel,
        out_shape=(one, one, own, own),
        in_specs=whole(3),
        out_specs=whole(4),
        compiler_params=ROOMY,
        cost_estimate=BRIEF,
    )(*after((later, swap(left, 2), swap(right, 4)), *earlier))
    wide, narrow = 4 * columns // 3, 2 * columns // 3
    return pl.pallas_call(
        functools.partial(mean_kernel, size),
        out_shape=(
            jax.ShapeDtypeStruct((share, wide), F32),
            jax.ShapeDtypeStruct((share, narrow), F32),
        ),
        in_specs=whole(4),
        compiler_params=ROOMY,
        cost_estimate=BRIEF,
    )(left, swap(left_send, 4), right, swap(right_send, 2))


def after(value, *others):
    return lax.optimization_barrier((value, *others))[0]


def call(kernel, out_shape, inputs):
    return pl.pallas_call(
        kernel,
        out_shape=out_shape,
        in_specs=[pl.BlockSpec(memory_space=pltpu.SMEM)]
        + [pl.BlockSpec(memory_space=pltpu.VMEM)] * (len(inputs) - 1),
        compiler_params=ROOMY,
        cost_estimate=BRIEF,
    )(*inputs)


def body(tokens, routes, route_scores, out_grad, gate_up, down_weight):
    experts = lax.axis_size("expert")
    groups = lax.axis_size("dp")
    toks, width = tokens.shape
    tops = routes.shape[1]
    units = down_weight.shape[2]
    capacity = (toks * tops + experts - 1) // experts
    slots = experts * capacity
    share = width // groups
    direct = experts <= 8 and capacity % 16 == 0
    w_in, w_out = gate_up[0], down_weight[0]
    routes_t, scores_t = routes.T, route_scores.T
    me = lax.axis_index("expert") if direct else jnp.int32(0)
    first = me.astype(jnp.int32).reshape(1)
    sizes = [capacity] * experts if direct else [slots]
    block_shapes = [jax.ShapeDtypeStruct((size, width), BF16) for size in sizes]

    def exchange(blocks, sign):
        if not direct:
            block = blocks[0].reshape(experts, capacity, width)
            moved = lax.all_to_all(block, "expert", split_axis=0, concat_axis=0, tiled=True)
            return [moved.reshape(slots, width)]
        out = [blocks[0]]
        for step in range(1, experts):
            pairs = [(at, (at + sign * step) % experts) for at in range(experts)]
            out.append(lax.ppermute(blocks[step], "expert", pairs))
        return out

    def joined(blocks):
        return blocks[0] if len(blocks) == 1 else jnp.concatenate(blocks, axis=0)

    def split(rows):
        return [rows[at : at + sizes[0]] for at in range(0, slots, sizes[0])]

    sent_rows = call(
        functools.partial(dispatch_kernel, experts, capacity, False),
        block_shapes,
        (first, routes_t, tokens),
    )
    got_rows = exchange(sent_rows, 1)
    sent_grads = call(
        functools.partial(dispatch_kernel, experts, capacity, True),
        block_shapes,
        (first, routes_t, scores_t, out_grad),
    )
    cube = direct and groups == 8 and share % 256 == 0
    if cube:
        sent_grads = after(sent_grads, got_rows[1])
        got_grads = exchange(sent_grads, 1)
        rows_t, preact, hidden, produced = forward(got_rows, w_in, w_out)
        got_grads = after(got_grads, *produced)
        returned = exchange(produced, -1)
        own = lax.axis_index("dp")
        send_at = jnp.stack([jnp.bitwise_xor(own, j) for j in CUBE_SEND]).astype(jnp.int32)
        keep_at = jnp.bitwise_xor(send_at, 1)
        pre_grad, grads_t = backward(preact, w_out, got_grads)
        send_at, keep_at = after((send_at, keep_at), returned[1])
        sent = shares(send_at, share, rows_t, grads_t, pre_grad, hidden)
        kept = shares(keep_at, share, rows_t, grads_t, pre_grad, hidden)
        input_grads = input_gradients(after(pre_grad, kept, returned[-1]), w_in, sizes)
        sent_back = exchange(input_grads, -1)
        kept = after(kept, *input_grads)
    else:
        token_rows = joined(got_rows)
        grad_rows = joined(exchange(sent_grads, 1))
        preact = jnp.dot(token_rows, w_in, preferred_element_type=F32)
        gate, up = preact[:, :units], preact[:, units:]
        hidden = (jax.nn.silu(gate) * up).astype(BF16)
        produced = jnp.dot(hidden, w_out.T, preferred_element_type=F32).astype(BF16)
        returned = exchange(split(produced), -1)
        hidden_grad = jnp.dot(grad_rows, w_out, preferred_element_type=F32)
        sigmoid = jax.nn.sigmoid(gate)
        gate_grad = hidden_grad * up * sigmoid * (1.0 + gate * (1.0 - sigmoid))
        up_grad = hidden_grad * gate * sigmoid
        pre_grad = jnp.concatenate([gate_grad, up_grad], axis=1).astype(BF16)
        input_grad = jnp.dot(pre_grad, w_in.T, preferred_element_type=F32).astype(BF16)
        sent_back = exchange(split(input_grad), -1)

    out_shape = jax.ShapeDtypeStruct((toks, width), BF16)
    mixed_out = call(
        functools.partial(combine_kernel, experts, capacity, True),
        out_shape,
        (first, routes_t, scores_t, *returned),
    )
    if cube:
        grad_in, grad_down = cube_sum(sent, kept, (mixed_out, sent_back[1]))
    else:

        def summed(left, right):
            part = contract(left, right).astype(BF16)
            total = lax.psum_scatter(part, "dp", scatter_dimension=0, tiled=True)
            return total.astype(F32) / groups

        grad_in = summed(token_rows, pre_grad)
        grad_down = summed(grad_rows, hidden)
    grad_in = grad_in.reshape(1, share, 2 * units)
    grad_down = grad_down.reshape(1, share, units)

    token_grad = call(
        functools.partial(combine_kernel, experts, capacity, False),
        out_shape,
        (first, routes_t, *sent_back),
    )
    return (mixed_out, token_grad, grad_in, grad_down)


def solution(mesh):
    in_specs = (
        P(("dp", "expert"), None),
        P(("dp", "expert"), None),
        P(("dp", "expert"), None),
        P(("dp", "expert"), None),
        P("expert", None, None),
        P("expert", None, None),
    )
    out_specs = (
        P(("dp", "expert"), None),
        P(("dp", "expert"), None),
        P("expert", "dp", None),
        P("expert", "dp", None),
    )
    return jax.shard_map(body, mesh=mesh, in_specs=in_specs, out_specs=out_specs, check_vma=False)
```

```python
import functools

import jax
import jax.numpy as jnp
from jax import lax
from jax.experimental import pallas as pl
from jax.experimental.pallas import tpu as pltpu
from jax.sharding import PartitionSpec as P

F32 = jnp.float32
BF16 = jnp.bfloat16
BRIEF = pl.CostEstimate(flops=1024, bytes_accessed=1024, transcendentals=0)
COVER = pl.CostEstimate(flops=10**11, bytes_accessed=10**8, transcendentals=0)
ROOMY = pltpu.CompilerParams(vmem_limit_bytes=16 * 1024 * 1024)


def contract(left, right):
    return lax.dot_general(left, right, (((0,), (0,)), ((), ())), preferred_element_type=F32)


def slot_rows(first, routes, experts, capacity):
    tops, toks = routes.shape
    padded = -(-experts // 8) * 8
    rows = lax.broadcasted_iota(jnp.int32, (padded, toks), 0)
    ids = rows + first
    ids = jnp.where(ids >= experts, ids - experts, ids)
    ids = jnp.where(rows < experts, ids, -1)
    hits = [routes[k : k + 1, :] == ids for k in range(tops)]
    named = functools.reduce(jnp.logical_or, hits)
    before = lax.broadcasted_iota(jnp.int32, (toks, toks), 0) < lax.broadcasted_iota(
        jnp.int32, (toks, toks), 1
    )
    position = jnp.dot(
        named.astype(F32).astype(BF16),
        before.astype(F32).astype(BF16),
        preferred_element_type=F32,
    )
    slot = position + (rows * capacity).astype(F32)
    return [jnp.sum(jnp.where(hit, slot, 0.0), axis=0, keepdims=True) for hit in hits]


def weight_rows(scores):
    grown = jnp.exp(scores)
    return grown / jnp.sum(grown, axis=0, keepdims=True)


def to_column(row):
    toks = row.shape[1]
    same = lax.broadcasted_iota(jnp.int32, (toks, toks), 0) == lax.broadcasted_iota(
        jnp.int32, (toks, toks), 1
    )
    return jnp.sum(jnp.where(same, row, 0.0), axis=1, keepdims=True)


def put_blocks(outs, rows, columns):
    start = 0
    for out in outs:
        size = out.shape[0]
        out[:, columns] = rows[start : start + size]
        start += size


def column_steps(width):
    step = 512 if width % 512 == 0 else width
    return [slice(at, at + step) for at in range(0, width, step)]


def dispatch_kernel(experts, capacity, weighted, first, routes, *refs):
    scores = refs[0] if weighted else None
    values, outs = refs[weighted], refs[weighted + 1 :]
    slots, toks = experts * capacity, values.shape[0]
    places = lax.broadcasted_iota(jnp.int32, (slots, toks), 0).astype(F32)
    hits = [places == row for row in slot_rows(first[0], routes[...], experts, capacity)]
    picker = functools.reduce(jnp.logical_or, hits).astype(F32).astype(BF16)
    if weighted:
        weights = weight_rows(scores[...])
        scale = sum(
            jnp.sum(jnp.where(hit, weights[k : k + 1, :], 0.0), axis=1, keepdims=True)
            for k, hit in enumerate(hits)
        )
    for columns in column_steps(values.shape[1]):
        rows = jnp.dot(picker, values[:, columns], preferred_element_type=F32)
        if weighted:
            rows = rows * scale
        put_blocks(outs, rows.astype(BF16), columns)


def combine_kernel(experts, capacity, weighted, first, routes, *refs):
    scores = refs[0] if weighted else None
    blocks, out = refs[weighted:-1], refs[-1]
    slots, toks = experts * capacity, out.shape[0]
    places = lax.broadcasted_iota(jnp.int32, (toks, slots), 1).astype(F32)
    hits = [
        places == to_column(row) for row in slot_rows(first[0], routes[...], experts, capacity)
    ]
    if weighted:
        weights = weight_rows(scores[...])
        scales = [to_column(weights[k : k + 1, :]) for k in range(len(hits))]
        pickers = [hit.astype(F32).astype(BF16) for hit in hits]
    else:
        pickers = [functools.reduce(jnp.logical_or, hits).astype(F32).astype(BF16)]
    for columns in column_steps(out.shape[1]):
        rows = [block[:, columns] for block in blocks]
        rows = rows[0] if len(rows) == 1 else jnp.concatenate(rows, axis=0)
        picked = [jnp.dot(picker, rows, preferred_element_type=F32) for picker in pickers]
        if weighted:
            picked = [scale * part for scale, part in zip(scales, picked)]
        out[:, columns] = sum(picked).astype(out.dtype)


def whole(count):
    return [pl.BlockSpec(memory_space=pltpu.VMEM)] * count


def write_shares(at, rows_t, grads_t, pre_grad, hidden, out):
    share = out.shape[1]
    wide, narrow = pre_grad.shape[1] // 2, hidden.shape[1] // 2

    def write(t, half):
        own = pl.ds(pl.multiple_of(at[t] * share, share), share)
        out[t, :, :wide] = jnp.dot(
            rows_t[own, :],
            pre_grad[:, half * wide : (half + 1) * wide],
            preferred_element_type=F32,
        ).astype(out.dtype)
        out[t, :, wide:] = jnp.dot(
            grads_t[own, :],
            hidden[:, half * narrow : (half + 1) * narrow],
            preferred_element_type=F32,
        ).astype(out.dtype)

    for t in range(out.shape[0]):
        write(t, t // 2 % 2)


def join_blocks(blocks, rows):
    start = 0
    for block in blocks:
        rows[start : start + block.shape[0], :] = block[...]
        start += block.shape[0]


def transpose_into(rows, rows_t):
    width = rows.shape[1]
    step = 256 if width % 256 == 0 else width

    @pl.loop(0, width // step)
    def _(c):
        own = pl.ds(pl.multiple_of(c * step, step), step)
        rows_t[own, :] = rows[:, own].T


def forward_kernel(count, *refs):
    blocks, (w_in, down), (rows_t, preact, hidden), outs, rows = (
        refs[:count],
        refs[count : count + 2],
        refs[count + 2 : count + 5],
        refs[count + 5 : -1],
        refs[-1],
    )
    join_blocks(blocks, rows)
    width, units = down.shape
    step = 256 if units % 256 == 0 else units
    for begin in range(0, units, step):
        gate_at, up_at = slice(begin, begin + step), slice(units + begin, units + begin + step)
        gate = jnp.dot(rows[...], w_in[:, gate_at], preferred_element_type=F32)
        up = jnp.dot(rows[...], w_in[:, up_at], preferred_element_type=F32)
        preact[:, gate_at] = gate
        preact[:, up_at] = up
        hidden[:, gate_at] = (gate / (1.0 + jnp.exp(-gate)) * up).astype(BF16)
    step = 512 if width % 512 == 0 else width

    @pl.loop(0, width // step)
    def _(c):
        own = pl.ds(pl.multiple_of(c * step, step), step)
        part = lax.dot_general(
            hidden[...], down[own, :], (((1,), (1,)), ((), ())), preferred_element_type=F32
        )
        put_blocks(outs, part.astype(BF16), own)

    transpose_into(rows, rows_t)


def forward(blocks, w_in, down):
    width, units = down.shape
    slots = sum(block.shape[0] for block in blocks)
    rows_t, preact, hidden, *outs = pl.pallas_call(
        functools.partial(forward_kernel, len(blocks)),
        out_shape=(
            jax.ShapeDtypeStruct((width, slots), BF16),
            jax.ShapeDtypeStruct((slots, 2 * units), F32),
            jax.ShapeDtypeStruct((slots, units), BF16),
            *[jax.ShapeDtypeStruct(block.shape, BF16) for block in blocks],
        ),
        in_specs=whole(2 + len(blocks)),
        out_specs=whole(3 + len(blocks)),
        scratch_shapes=[pltpu.VMEM((slots, width), BF16)],
        compiler_params=ROOMY,
        cost_estimate=BRIEF,
    )(*blocks, w_in, down)
    return rows_t, preact, hidden, outs


def backward_kernel(preact_hbm, down, *refs):
    blocks, (pre_grad, grads_t, grads, preact, block_sems, sem) = refs[:-6], refs[-6:]
    fetch = pltpu.make_async_copy(preact_hbm, preact, sem)
    fetch.start()
    size = blocks[0].shape[0]
    joins = [
        pltpu.make_async_copy(block, grads.at[pl.ds(n * size, size)], block_sems.at[n])
        for n, block in enumerate(blocks)
    ]
    for join in joins:
        join.start()
    for join in joins:
        join.wait()
    fetch.wait()
    units = down.shape[1]
    step = 256 if units % 256 == 0 else units
    for begin in range(0, units, step):
        gate = preact[:, begin : begin + step]
        up = preact[:, units + begin : units + begin + step]
        hidden_grad = jnp.dot(
            grads[...], down[:, begin : begin + step], preferred_element_type=F32
        )
        sigmoid = 1.0 / (1.0 + jnp.exp(-gate))
        gate_grad = hidden_grad * up * sigmoid * (1.0 + gate * (1.0 - sigmoid))
        up_grad = hidden_grad * gate * sigmoid
        pre_grad[:, begin : begin + step] = gate_grad.astype(BF16)
        pre_grad[:, units + begin : units + begin + step] = up_grad.astype(BF16)
    transpose_into(grads, grads_t)


def anywhere(count):
    return [pl.BlockSpec(memory_space=pl.ANY)] * count


def backward(preact, down, blocks):
    width, units = down.shape
    slots = preact.shape[0]
    return pl.pallas_call(
        backward_kernel,
        out_shape=(
            jax.ShapeDtypeStruct((slots, 2 * units), BF16),
            jax.ShapeDtypeStruct((width, slots), BF16),
        ),
        in_specs=anywhere(1) + whole(1) + anywhere(len(blocks)),
        out_specs=whole(2),
        scratch_shapes=[
            pltpu.VMEM((slots, width), BF16),
            pltpu.VMEM((slots, 2 * units), F32),
            pltpu.SemaphoreType.DMA((len(blocks),)),
            pltpu.SemaphoreType.DMA,
        ],
        compiler_params=ROOMY,
        cost_estimate=BRIEF,
    )(preact, down, *blocks)


def shares(at, share, rows_t, grads_t, pre_grad, hidden, cost):
    units = hidden.shape[1]
    return pl.pallas_call(
        write_shares,
        out_shape=jax.ShapeDtypeStruct((at.shape[0], share, 3 * units // 2), BF16),
        in_specs=[pl.BlockSpec(memory_space=pltpu.SMEM)] + whole(4),
        out_specs=whole(1)[0],
        compiler_params=ROOMY,
        cost_estimate=cost,
    )(at, rows_t, grads_t, pre_grad, hidden)


def input_kernel(count, pre_grad, w_in, *refs):
    blocks, outs, sems = refs[:count], refs[count : 2 * count], refs[-1]
    width, size = w_in.shape[0], blocks[0].shape[0]
    copies = [
        pltpu.make_async_copy(block, out.at[pl.ds(0, size)], sems.at[n])
        for n, (block, out) in enumerate(zip(blocks, outs))
    ]
    for copy in copies:
        copy.start()
    step = 512 if width % 512 == 0 else width
    for begin in range(0, width, step):
        part = lax.dot_general(
            pre_grad[...],
            w_in[begin : begin + step, :],
            (((1,), (1,)), ((), ())),
            preferred_element_type=F32,
        ).astype(BF16)
        for n, out in enumerate(outs):
            out[size:, begin : begin + step] = part[n * size : (n + 1) * size]
    for copy in copies:
        copy.wait()


def both_returns(pre_grad, w_in, produced):
    count = len(produced)
    size, width = produced[0].shape
    return pl.pallas_call(
        functools.partial(input_kernel, count),
        out_shape=[jax.ShapeDtypeStruct((2 * size, width), BF16)] * count,
        in_specs=whole(2) + anywhere(count),
        out_specs=whole(count),
        scratch_shapes=[pltpu.SemaphoreType.DMA((count,))],
        compiler_params=ROOMY,
        cost_estimate=BRIEF,
    )(pre_grad, w_in, *produced)


def add_kernel(kept, got, left, right):
    half = left.shape[0]
    left[...] = add(kept[:half], got[:half]).astype(BF16)
    right[...] = add(kept[half:], got[half : 2 * half]).astype(BF16)


def next_kernel(kept, got, left_in, right_in, left_send, right_send):
    first = got.shape[0] // 2
    left_send[...] = (add(kept[1], got[first + 1]) + left_in[1].astype(F32)).astype(BF16)
    right_send[...] = (add(kept[3], got[first + 3]) + right_in[1].astype(F32)).astype(BF16)


def own_kernel(kept, got, left_in, right_in, left, right):
    first = got.shape[0] // 2
    left[...] = add(kept[0], got[first]) + left_in[0].astype(F32)
    right[...] = add(kept[2], got[first + 2]) + right_in[0].astype(F32)


def mean_kernel(count, left, left_last, right, right_last, wide_out, narrow_out):
    wide = wide_out.shape[1] // 2
    narrow = narrow_out.shape[1] // 2
    for at, (own, last) in enumerate(((left, left_last), (right, right_last))):
        total = (own[...] + last[...].astype(F32)) / count
        wide_out[:, at * wide : (at + 1) * wide] = total[:, :wide]
        narrow_out[:, at * narrow : (at + 1) * narrow] = total[:, wide:]


def add(left, right):
    return left.astype(F32) + right.astype(F32)


CUBE_SEND = (3, 7, 5, 7, 1, 5, 1, 3)


def cube_sum(sent, kept_first, kept_later):
    size = lax.axis_size("dp")
    _, share, columns = sent.shape

    def swap(block, bit):
        return lax.ppermute(block, "dp", [(at, at ^ bit) for at in range(size)])

    def run(kernel, out_shape, inputs, cost=BRIEF):
        return pl.pallas_call(
            kernel,
            out_shape=out_shape,
            in_specs=whole(len(inputs)),
            out_specs=whole(len(out_shape)),
            compiler_params=ROOMY,
            cost_estimate=cost,
        )(*inputs)

    half = jax.ShapeDtypeStruct((2, share, columns), BF16)
    one = jax.ShapeDtypeStruct((share, columns), BF16)
    own = jax.ShapeDtypeStruct((share, columns), F32)
    got = swap(sent, 1)
    left, right = run(add_kernel, (half, half), (kept_first, got))
    parts = (kept_later, got, swap(left, 2), swap(right, 4))
    left_send, right_send = run(next_kernel, (one, one), parts)
    left, right = run(own_kernel, (own, own), parts, COVER)
    wide, narrow = 4 * columns // 3, 2 * columns // 3
    means = run(
        functools.partial(mean_kernel, size),
        (
            jax.ShapeDtypeStruct((share, wide), F32),
            jax.ShapeDtypeStruct((share, narrow), F32),
        ),
        (left, swap(left_send, 4), right, swap(right_send, 2)),
    )
    return means, left


def after(value, *others):
    return lax.optimization_barrier((value, *others))[0]


def finish_kernel(experts, capacity, first, routes, scores, *refs):
    blocks, (mixed, back) = refs[:-2], refs[-2:]
    slots, toks = experts * capacity, mixed.shape[0]
    places = lax.broadcasted_iota(jnp.int32, (toks, slots), 1).astype(F32)
    hits = [
        places == to_column(row) for row in slot_rows(first[0], routes[...], experts, capacity)
    ]
    weights = weight_rows(scores[...])
    scales = [to_column(weights[k : k + 1, :]) for k in range(len(hits))]
    pickers = [hit.astype(F32).astype(BF16) for hit in hits]
    either = functools.reduce(jnp.logical_or, hits).astype(F32).astype(BF16)
    for columns in column_steps(mixed.shape[1]):
        rows = jnp.concatenate([block[:capacity, columns] for block in blocks], axis=0)
        picked = [jnp.dot(picker, rows, preferred_element_type=F32) for picker in pickers]
        mixed[:, columns] = sum(
            scale * part for scale, part in zip(scales, picked)
        ).astype(mixed.dtype)
        rows = jnp.concatenate([block[capacity:, columns] for block in blocks], axis=0)
        back[:, columns] = jnp.dot(either, rows, preferred_element_type=F32).astype(back.dtype)


def call(kernel, out_shape, inputs):
    return pl.pallas_call(
        kernel,
        out_shape=out_shape,
        in_specs=[pl.BlockSpec(memory_space=pltpu.SMEM)]
        + [pl.BlockSpec(memory_space=pltpu.VMEM)] * (len(inputs) - 1),
        compiler_params=ROOMY,
        cost_estimate=BRIEF,
    )(*inputs)


def body(tokens, routes, route_scores, out_grad, gate_up, down_weight):
    experts = lax.axis_size("expert")
    groups = lax.axis_size("dp")
    toks, width = tokens.shape
    tops = routes.shape[1]
    units = down_weight.shape[2]
    capacity = (toks * tops + experts - 1) // experts
    slots = experts * capacity
    share = width // groups
    direct = experts <= 8 and capacity % 16 == 0
    w_in, w_out = gate_up[0], down_weight[0]
    routes_t, scores_t = routes.T, route_scores.T
    me = lax.axis_index("expert") if direct else jnp.int32(0)
    first = me.astype(jnp.int32).reshape(1)
    sizes = [capacity] * experts if direct else [slots]
    block_shapes = [jax.ShapeDtypeStruct((size, width), BF16) for size in sizes]

    def exchange(blocks, sign):
        if not direct:
            block = blocks[0].reshape(experts, capacity, width)
            moved = lax.all_to_all(block, "expert", split_axis=0, concat_axis=0, tiled=True)
            return [moved.reshape(slots, width)]
        out = [blocks[0]]
        for step in range(1, experts):
            pairs = [(at, (at + sign * step) % experts) for at in range(experts)]
            out.append(lax.ppermute(blocks[step], "expert", pairs))
        return out

    def joined(blocks):
        return blocks[0] if len(blocks) == 1 else jnp.concatenate(blocks, axis=0)

    def split(rows):
        return [rows[at : at + sizes[0]] for at in range(0, slots, sizes[0])]

    sent_rows = call(
        functools.partial(dispatch_kernel, experts, capacity, False),
        block_shapes,
        (first, routes_t, tokens),
    )
    got_rows = exchange(sent_rows, 1)
    sent_grads = call(
        functools.partial(dispatch_kernel, experts, capacity, True),
        block_shapes,
        (first, routes_t, scores_t, out_grad),
    )
    out_shape = jax.ShapeDtypeStruct((toks, width), BF16)
    cube = direct and groups == 8 and share % 256 == 0
    if cube:
        sent_grads = after(sent_grads, got_rows[1], got_rows[-1])
        got_grads = exchange(sent_grads, 1)
        rows_t, preact, hidden, produced = forward(got_rows, w_in, w_out)
        got_grads = after(got_grads, hidden)
        own = lax.axis_index("dp")
        send_at = jnp.stack([jnp.bitwise_xor(own, j) for j in CUBE_SEND]).astype(jnp.int32)
        keep_at = jnp.bitwise_xor(send_at, 1)
        pre_grad, grads_t = backward(preact, w_out, got_grads)
        both = both_returns(pre_grad, w_in, produced)
        returned = exchange(both, -1)
        operands = (share, rows_t, grads_t, pre_grad, hidden)
        sent = shares(after(send_at, both[0]), *operands, BRIEF)
        half = len(CUBE_SEND) // 2
        kept_first = shares(keep_at[:half], *operands, COVER)
        kept_later = shares(after(keep_at[half:], kept_first), *operands, COVER)
        (grad_in, grad_down), nearly = cube_sum(sent, kept_first, kept_later)
        mixed_out, token_grad = call(
            functools.partial(finish_kernel, experts, capacity),
            (out_shape, out_shape),
            (after(first, nearly), routes_t, scores_t, *returned),
        )
    else:
        token_rows = joined(got_rows)
        grad_rows = joined(exchange(sent_grads, 1))
        preact = jnp.dot(token_rows, w_in, preferred_element_type=F32)
        gate, up = preact[:, :units], preact[:, units:]
        hidden = (jax.nn.silu(gate) * up).astype(BF16)
        produced = jnp.dot(hidden, w_out.T, preferred_element_type=F32).astype(BF16)
        returned = exchange(split(produced), -1)
        hidden_grad = jnp.dot(grad_rows, w_out, preferred_element_type=F32)
        sigmoid = jax.nn.sigmoid(gate)
        gate_grad = hidden_grad * up * sigmoid * (1.0 + gate * (1.0 - sigmoid))
        up_grad = hidden_grad * gate * sigmoid
        pre_grad = jnp.concatenate([gate_grad, up_grad], axis=1).astype(BF16)
        input_grad = jnp.dot(pre_grad, w_in.T, preferred_element_type=F32).astype(BF16)
        sent_back = exchange(split(input_grad), -1)

        def summed(left, right):
            part = contract(left, right).astype(BF16)
            total = lax.psum_scatter(part, "dp", scatter_dimension=0, tiled=True)
            return total.astype(F32) / groups

        grad_in = summed(token_rows, pre_grad)
        grad_down = summed(grad_rows, hidden)
        mixed_out = call(
            functools.partial(combine_kernel, experts, capacity, True),
            out_shape,
            (first, routes_t, scores_t, *returned),
        )
        token_grad = call(
            functools.partial(combine_kernel, experts, capacity, False),
            out_shape,
            (first, routes_t, *sent_back),
        )
    grad_in = grad_in.reshape(1, share, 2 * units)
    grad_down = grad_down.reshape(1, share, units)
    return (mixed_out, token_grad, grad_in, grad_down)


def solution(mesh):
    in_specs = (
        P(("dp", "expert"), None),
        P(("dp", "expert"), None),
        P(("dp", "expert"), None),
        P(("dp", "expert"), None),
        P("expert", None, None),
        P("expert", None, None),
    )
    out_specs = (
        P(("dp", "expert"), None),
        P(("dp", "expert"), None),
        P("expert", "dp", None),
        P("expert", "dp", None),
    )
    return jax.shard_map(body, mesh=mesh, in_specs=in_specs, out_specs=out_specs, check_vma=False)
```

```python
import functools

import jax
import jax.numpy as jnp
from jax import lax
from jax.experimental import pallas as pl
from jax.experimental.pallas import tpu as pltpu
from jax.sharding import PartitionSpec as P

F32 = jnp.float32
BF16 = jnp.bfloat16
BRIEF = pl.CostEstimate(flops=1024, bytes_accessed=1024, transcendentals=0)
COVER = pl.CostEstimate(flops=10**11, bytes_accessed=10**8, transcendentals=0)
ROOMY = pltpu.CompilerParams(vmem_limit_bytes=16 * 1024 * 1024)
ALONE = pltpu.CompilerParams(vmem_limit_bytes=60 * 1024 * 1024)


def contract(left, right):
    return lax.dot_general(left, right, (((0,), (0,)), ((), ())), preferred_element_type=F32)


def slot_rows(first, routes, experts, capacity):
    tops, toks = routes.shape
    padded = -(-experts // 8) * 8
    rows = lax.broadcasted_iota(jnp.int32, (padded, toks), 0)
    ids = rows + first
    ids = jnp.where(ids >= experts, ids - experts, ids)
    ids = jnp.where(rows < experts, ids, -1)
    hits = [routes[k : k + 1, :] == ids for k in range(tops)]
    named = functools.reduce(jnp.logical_or, hits)
    before = lax.broadcasted_iota(jnp.int32, (toks, toks), 0) < lax.broadcasted_iota(
        jnp.int32, (toks, toks), 1
    )
    position = jnp.dot(
        named.astype(F32).astype(BF16),
        before.astype(F32).astype(BF16),
        preferred_element_type=F32,
    )
    slot = position + (rows * capacity).astype(F32)
    return [jnp.sum(jnp.where(hit, slot, 0.0), axis=0, keepdims=True) for hit in hits]


def weight_rows(scores):
    grown = jnp.exp(scores)
    return grown / jnp.sum(grown, axis=0, keepdims=True)


def to_column(row):
    toks = row.shape[1]
    same = lax.broadcasted_iota(jnp.int32, (toks, toks), 0) == lax.broadcasted_iota(
        jnp.int32, (toks, toks), 1
    )
    return jnp.sum(jnp.where(same, row, 0.0), axis=1, keepdims=True)


def put_blocks(outs, rows, columns):
    start = 0
    for out in outs:
        size = out.shape[0]
        out[:, columns] = rows[start : start + size]
        start += size


def column_steps(width):
    step = 512 if width % 512 == 0 else width
    return [slice(at, at + step) for at in range(0, width, step)]


def dispatch_kernel(experts, capacity, weighted, first, *refs):
    count = 2 + weighted
    sources, outs = refs[:count], refs[count : -count - 1]
    held, sems = refs[-count - 1 : -1], refs[-1]
    copies = [
        pltpu.make_async_copy(source, place, sems.at[n])
        for n, (source, place) in enumerate(zip(sources, held))
    ]
    for copy in copies:
        copy.start()
    routes, values = held[0], held[-1]
    scores = held[1] if weighted else None
    for copy in copies[:-1]:
        copy.wait()
    slots, toks = experts * capacity, values.shape[0]
    places = lax.broadcasted_iota(jnp.int32, (slots, toks), 0).astype(F32)
    hits = [places == row for row in slot_rows(first[0], routes[...], experts, capacity)]
    picker = functools.reduce(jnp.logical_or, hits).astype(F32).astype(BF16)
    if weighted:
        weights = weight_rows(scores[...])
        scale = sum(
            jnp.sum(jnp.where(hit, weights[k : k + 1, :], 0.0), axis=1, keepdims=True)
            for k, hit in enumerate(hits)
        )
    copies[-1].wait()
    for columns in column_steps(values.shape[1]):
        rows = jnp.dot(picker, values[:, columns], preferred_element_type=F32)
        if weighted:
            rows = rows * scale
        put_blocks(outs, rows.astype(BF16), columns)


def combine_kernel(experts, capacity, weighted, first, routes, *refs):
    scores = refs[0] if weighted else None
    blocks, out = refs[weighted:-1], refs[-1]
    slots, toks = experts * capacity, out.shape[0]
    places = lax.broadcasted_iota(jnp.int32, (toks, slots), 1).astype(F32)
    hits = [
        places == to_column(row) for row in slot_rows(first[0], routes[...], experts, capacity)
    ]
    if weighted:
        weights = weight_rows(scores[...])
        scales = [to_column(weights[k : k + 1, :]) for k in range(len(hits))]
        pickers = [hit.astype(F32).astype(BF16) for hit in hits]
    else:
        pickers = [functools.reduce(jnp.logical_or, hits).astype(F32).astype(BF16)]
    for columns in column_steps(out.shape[1]):
        rows = [block[:, columns] for block in blocks]
        rows = rows[0] if len(rows) == 1 else jnp.concatenate(rows, axis=0)
        picked = [jnp.dot(picker, rows, preferred_element_type=F32) for picker in pickers]
        if weighted:
            picked = [scale * part for scale, part in zip(scales, picked)]
        out[:, columns] = sum(picked).astype(out.dtype)


def whole(count):
    return [pl.BlockSpec(memory_space=pltpu.VMEM)] * count


def write_shares(at, rows_t, grads_t, pre_grad, hidden, out):
    share = out.shape[1]
    wide, narrow = pre_grad.shape[1] // 2, hidden.shape[1] // 2

    def write(t, half):
        own = pl.ds(pl.multiple_of(at[t] * share, share), share)
        out[t, :, :wide] = jnp.dot(
            rows_t[own, :],
            pre_grad[:, half * wide : (half + 1) * wide],
            preferred_element_type=F32,
        ).astype(out.dtype)
        out[t, :, wide:] = jnp.dot(
            grads_t[own, :],
            hidden[:, half * narrow : (half + 1) * narrow],
            preferred_element_type=F32,
        ).astype(out.dtype)

    for t in range(out.shape[0]):
        write(t, t // 2 % 2)


def transpose_into(rows, rows_t):
    width = rows.shape[1]
    step = 256 if width % 256 == 0 else width

    @pl.loop(0, width // step)
    def _(c):
        own = pl.ds(pl.multiple_of(c * step, step), step)
        rows_t[own, :] = rows[:, own].T


def join_copies(blocks, rows, sems):
    size = blocks[0].shape[0]
    joins = [
        pltpu.make_async_copy(block, rows.at[pl.ds(n * size, size)], sems.at[n])
        for n, block in enumerate(blocks)
    ]
    for join in joins:
        join.start()
    return joins


def forward_kernel(count, *refs):
    blocks, (w_in_hbm, down_hbm), (rows_t, preact, hidden), outs, scratch = (
        refs[:count],
        refs[count : count + 2],
        refs[count + 2 : count + 5],
        refs[count + 5 : 2 * count + 5],
        refs[2 * count + 5 :],
    )
    rows, w_in, down, block_sems, weight_sems, down_sem = scratch
    joins = join_copies(blocks, rows, block_sems)
    width, units = down.shape
    step = 256 if units % 256 == 0 else units
    loads = []
    for n in range(2 * units // step):
        begin = (n % 2) * units + n // 2 * step
        loads.append(
            pltpu.make_async_copy(
                w_in_hbm.at[:, pl.ds(begin, step)],
                w_in.at[:, pl.ds(begin, step)],
                weight_sems.at[n],
            )
        )
        loads[-1].start()
    load_down = pltpu.make_async_copy(down_hbm, down, down_sem)
    load_down.start()
    for join in joins:
        join.wait()
    for n in range(units // step):
        begin = n * step
        gate_at, up_at = slice(begin, begin + step), slice(units + begin, units + begin + step)
        loads[2 * n].wait()
        gate = jnp.dot(rows[...], w_in[:, gate_at], preferred_element_type=F32)
        loads[2 * n + 1].wait()
        up = jnp.dot(rows[...], w_in[:, up_at], preferred_element_type=F32)
        preact[:, gate_at] = gate
        preact[:, up_at] = up
        hidden[:, gate_at] = (gate / (1.0 + jnp.exp(-gate)) * up).astype(BF16)
    load_down.wait()
    for columns in column_steps(width):
        part = lax.dot_general(
            hidden[...], down[columns, :], (((1,), (1,)), ((), ())), preferred_element_type=F32
        )
        put_blocks(outs, part.astype(BF16), columns)
    transpose_into(rows, rows_t)


def forward(blocks, w_in, down):
    width, units = down.shape
    slots = sum(block.shape[0] for block in blocks)
    count = len(blocks)
    rows_t, preact, hidden, *outs = pl.pallas_call(
        functools.partial(forward_kernel, count),
        out_shape=(
            jax.ShapeDtypeStruct((width, slots), BF16),
            jax.ShapeDtypeStruct((slots, 2 * units), F32),
            jax.ShapeDtypeStruct((slots, units), BF16),
            *[jax.ShapeDtypeStruct(block.shape, BF16) for block in blocks],
        ),
        in_specs=anywhere(count) + in_hbm(2),
        out_specs=whole(3 + count),
        scratch_shapes=[
            pltpu.VMEM((slots, width), BF16),
            pltpu.VMEM(w_in.shape, BF16),
            pltpu.VMEM(down.shape, BF16),
            pltpu.SemaphoreType.DMA((count,)),
            pltpu.SemaphoreType.DMA((2 * units // min(units, 256),)),
            pltpu.SemaphoreType.DMA,
        ],
        compiler_params=pltpu.CompilerParams(vmem_limit_bytes=46 * 1024 * 1024),
        cost_estimate=BRIEF,
    )(*blocks, w_in, down)
    return rows_t, preact, hidden, outs


def backward_kernel(preact_hbm, down, *refs):
    blocks, (pre_grad, grads_t, grads, preact, block_sems, sem) = refs[:-6], refs[-6:]
    fetch = pltpu.make_async_copy(preact_hbm, preact, sem)
    fetch.start()
    joins = join_copies(blocks, grads, block_sems)
    for join in joins:
        join.wait()
    fetch.wait()
    units = down.shape[1]
    step = 256 if units % 256 == 0 else units
    for begin in range(0, units, step):
        gate = preact[:, begin : begin + step]
        up = preact[:, units + begin : units + begin + step]
        hidden_grad = jnp.dot(
            grads[...], down[:, begin : begin + step], preferred_element_type=F32
        )
        sigmoid = 1.0 / (1.0 + jnp.exp(-gate))
        gate_grad = hidden_grad * up * sigmoid * (1.0 + gate * (1.0 - sigmoid))
        up_grad = hidden_grad * gate * sigmoid
        pre_grad[:, begin : begin + step] = gate_grad.astype(BF16)
        pre_grad[:, units + begin : units + begin + step] = up_grad.astype(BF16)
    transpose_into(grads, grads_t)


def anywhere(count):
    return [pl.BlockSpec(memory_space=pl.ANY)] * count


def in_hbm(count):
    return [pl.BlockSpec(memory_space=pltpu.HBM)] * count


def backward(preact, down, blocks):
    width, units = down.shape
    slots = preact.shape[0]
    return pl.pallas_call(
        backward_kernel,
        out_shape=(
            jax.ShapeDtypeStruct((slots, 2 * units), BF16),
            jax.ShapeDtypeStruct((width, slots), BF16),
        ),
        in_specs=anywhere(1) + whole(1) + anywhere(len(blocks)),
        out_specs=whole(2),
        scratch_shapes=[
            pltpu.VMEM((slots, width), BF16),
            pltpu.VMEM((slots, 2 * units), F32),
            pltpu.SemaphoreType.DMA((len(blocks),)),
            pltpu.SemaphoreType.DMA,
        ],
        compiler_params=ROOMY,
        cost_estimate=BRIEF,
    )(preact, down, *blocks)


def shares(at, share, rows_t, grads_t, pre_grad, hidden, cost):
    units = hidden.shape[1]
    return pl.pallas_call(
        write_shares,
        out_shape=jax.ShapeDtypeStruct((at.shape[0], share, 3 * units // 2), BF16),
        in_specs=[pl.BlockSpec(memory_space=pltpu.SMEM)] + whole(4),
        out_specs=whole(1)[0],
        compiler_params=ROOMY,
        cost_estimate=cost,
    )(at, rows_t, grads_t, pre_grad, hidden)


def input_kernel(count, pre_grad, w_in, *refs):
    blocks, outs, sems = refs[:count], refs[count : 2 * count], refs[-1]
    width, size = w_in.shape[0], blocks[0].shape[0]
    copies = [
        pltpu.make_async_copy(block, out.at[pl.ds(0, size)], sems.at[n])
        for n, (block, out) in enumerate(zip(blocks, outs))
        if out.shape[0] > size
    ]
    for copy in copies:
        copy.start()
    for columns in column_steps(width):
        part = lax.dot_general(
            pre_grad[...], w_in[columns, :], (((1,), (1,)), ((), ())), preferred_element_type=F32
        ).astype(BF16)
        for n, out in enumerate(outs):
            out[out.shape[0] - size :, columns] = part[n * size : (n + 1) * size]
    for copy in copies:
        copy.wait()


def input_gradients(pre_grad, w_in, produced, alone):
    count = len(produced)
    size, width = produced[0].shape
    return pl.pallas_call(
        functools.partial(input_kernel, count),
        out_shape=[
            jax.ShapeDtypeStruct((size if n == alone else 2 * size, width), BF16)
            for n in range(count)
        ],
        in_specs=whole(2) + anywhere(count),
        out_specs=whole(count),
        scratch_shapes=[pltpu.SemaphoreType.DMA((count,))],
        compiler_params=ROOMY,
        cost_estimate=BRIEF,
    )(pre_grad, w_in, *produced)


def add_kernel(kept, got, left, right):
    half = left.shape[0]
    left[...] = add(kept[:half], got[:half]).astype(BF16)
    right[...] = add(kept[half:], got[half : 2 * half]).astype(BF16)


def next_kernel(kept, got, left_in, right_in, left_send, right_send):
    first = got.shape[0] // 2
    left_send[...] = (add(kept[1], got[first + 1]) + left_in[1].astype(F32)).astype(BF16)
    right_send[...] = (add(kept[3], got[first + 3]) + right_in[1].astype(F32)).astype(BF16)


def own_kernel(kept, got, left_in, right_in, left, right):
    first = got.shape[0] // 2
    left[...] = add(kept[0], got[first]) + left_in[0].astype(F32)
    right[...] = add(kept[2], got[first + 2]) + right_in[0].astype(F32)


def mean_kernel(count, left, left_last, right, right_last, wide_out, narrow_out):
    wide = wide_out.shape[1] // 2
    narrow = narrow_out.shape[1] // 2
    for at, (own, last) in enumerate(((left, left_last), (right, right_last))):
        total = (own[...] + last[...].astype(F32)) / count
        wide_out[:, at * wide : (at + 1) * wide] = total[:, :wide]
        narrow_out[:, at * narrow : (at + 1) * narrow] = total[:, wide:]


def add(left, right):
    return left.astype(F32) + right.astype(F32)


CUBE_SEND = (3, 7, 5, 7, 1, 5, 1, 3)


def cube_sum(sent, kept_first, kept_later):
    size = lax.axis_size("dp")
    _, share, columns = sent.shape

    def swap(block, bit):
        return lax.ppermute(block, "dp", [(at, at ^ bit) for at in range(size)])

    def run(kernel, out_shape, inputs, cost=BRIEF):
        return pl.pallas_call(
            kernel,
            out_shape=out_shape,
            in_specs=whole(len(inputs)),
            out_specs=whole(len(out_shape)),
            compiler_params=ROOMY,
            cost_estimate=cost,
        )(*inputs)

    half = jax.ShapeDtypeStruct((2, share, columns), BF16)
    one = jax.ShapeDtypeStruct((share, columns), BF16)
    own = jax.ShapeDtypeStruct((share, columns), F32)
    got = swap(sent, 1)
    left, right = run(add_kernel, (half, half), (kept_first, got))
    parts = (kept_later, got, swap(left, 2), swap(right, 4))
    left_send, right_send = run(next_kernel, (one, one), parts)
    left, right = run(own_kernel, (own, own), parts, COVER)
    wide, narrow = 4 * columns // 3, 2 * columns // 3
    means = run(
        functools.partial(mean_kernel, size),
        (
            jax.ShapeDtypeStruct((share, wide), F32),
            jax.ShapeDtypeStruct((share, narrow), F32),
        ),
        (left, swap(left_send, 4), right, swap(right_send, 2)),
    )
    return means, left


def after(value, *others):
    return lax.optimization_barrier((value, *others))[0]


def partial_kernel(experts, capacity, first, routes, scores, *refs):
    blocks, (mixed, back, pickers, scales) = refs[:-4], refs[-4:]
    slots, toks = experts * capacity, mixed.shape[0]
    places = lax.broadcasted_iota(jnp.int32, (toks, slots), 1).astype(F32)
    hits = [
        places == to_column(row) for row in slot_rows(first[0], routes[...], experts, capacity)
    ]
    weights = weight_rows(scores[...])
    for k, hit in enumerate(hits):
        pickers[k] = hit.astype(F32).astype(BF16)
        scales[k] = jnp.broadcast_to(to_column(weights[k : k + 1, :]), scales.shape[1:])
    pickers[len(hits)] = functools.reduce(jnp.logical_or, hits).astype(F32).astype(BF16)
    outputs = [(0, blocks[0], 0), (experts // 2, blocks[1], 0)]
    gradients = [(0, blocks[0], capacity), (experts // 2, blocks[2], 0)]
    sum_blocks(capacity, pickers, scales, outputs, gradients, None, mixed, back)


def final_kernel(capacity, pickers, scales, mixed_part, back_part, *refs):
    blocks, (mixed, back) = refs[:-2], refs[-2:]
    places = [n for n in range(1, len(blocks) + 2) if 2 * n != len(blocks) + 2]
    outputs = [(n, block, 0) for n, block in zip(places, blocks)]
    gradients = [(n, block, capacity) for n, block in zip(places, blocks)]
    parts = (mixed_part, back_part)
    sum_blocks(capacity, pickers, scales, outputs, gradients, parts, mixed, back)


def sum_blocks(capacity, pickers, scales, outputs, gradients, parts, mixed, back):
    tops = scales.shape[0]

    def select(terms, k, columns):
        slots = [slice(n * capacity, (n + 1) * capacity) for n, _, _ in terms]
        picker = jnp.concatenate([pickers[k, :, at] for at in slots], axis=1)
        rows = [block[start : start + capacity, columns] for _, block, start in terms]
        return jnp.dot(picker, jnp.concatenate(rows, axis=0), preferred_element_type=F32)

    for columns in column_steps(mixed.shape[1]):
        total = sum(scales[k, :, :1] * select(outputs, k, columns) for k in range(tops))
        grad = select(gradients, tops, columns)
        if parts is not None:
            total, grad = total + parts[0][:, columns], grad + parts[1][:, columns]
        mixed[:, columns] = total.astype(mixed.dtype)
        back[:, columns] = grad.astype(back.dtype)


def dispatch(experts, capacity, out_shape, first, *sources):
    weighted = len(sources) > 2
    return pl.pallas_call(
        functools.partial(dispatch_kernel, experts, capacity, weighted),
        out_shape=out_shape,
        in_specs=[pl.BlockSpec(memory_space=pltpu.SMEM)] + in_hbm(len(sources)),
        out_specs=whole(len(out_shape)),
        scratch_shapes=[pltpu.VMEM(source.shape, source.dtype) for source in sources]
        + [pltpu.SemaphoreType.DMA((len(sources),))],
        compiler_params=ALONE,
        cost_estimate=BRIEF,
    )(first, *sources)


def call(kernel, out_shape, inputs):
    return pl.pallas_call(
        kernel,
        out_shape=out_shape,
        in_specs=[pl.BlockSpec(memory_space=pltpu.SMEM)]
        + [pl.BlockSpec(memory_space=pltpu.VMEM)] * (len(inputs) - 1),
        compiler_params=ROOMY,
        cost_estimate=BRIEF,
    )(*inputs)


def body(tokens, routes, route_scores, out_grad, gate_up, down_weight):
    experts = lax.axis_size("expert")
    groups = lax.axis_size("dp")
    toks, width = tokens.shape
    tops = routes.shape[1]
    units = down_weight.shape[2]
    capacity = (toks * tops + experts - 1) // experts
    slots = experts * capacity
    share = width // groups
    direct = experts <= 8 and capacity % 16 == 0
    w_in, w_out = gate_up[0], down_weight[0]
    routes_t, scores_t = routes.T, route_scores.T
    me = lax.axis_index("expert") if direct else jnp.int32(0)
    first = me.astype(jnp.int32).reshape(1)
    sizes = [capacity] * experts if direct else [slots]
    block_shapes = [jax.ShapeDtypeStruct((size, width), BF16) for size in sizes]

    def travel(block, step, sign):
        pairs = [(at, (at + sign * step) % experts) for at in range(experts)]
        return lax.ppermute(block, "expert", pairs)

    def exchange(blocks, sign):
        if not direct:
            block = blocks[0].reshape(experts, capacity, width)
            moved = lax.all_to_all(block, "expert", split_axis=0, concat_axis=0, tiled=True)
            return [moved.reshape(slots, width)]
        return [blocks[0]] + [travel(blocks[step], step, sign) for step in range(1, experts)]

    def joined(blocks):
        return blocks[0] if len(blocks) == 1 else jnp.concatenate(blocks, axis=0)

    def split(rows):
        return [rows[at : at + sizes[0]] for at in range(0, slots, sizes[0])]

    sent_rows = dispatch(experts, capacity, block_shapes, first, routes_t, tokens)
    got_rows = exchange(sent_rows, 1)
    sent_grads = dispatch(experts, capacity, block_shapes, first, routes_t, scores_t, out_grad)
    out_shape = jax.ShapeDtypeStruct((toks, width), BF16)
    cube = direct and experts == 4 and groups == 8 and share % 256 == 0
    if cube:
        sent_grads = after(sent_grads, got_rows[1], got_rows[-1])
        got_grads = exchange(sent_grads, 1)
        rows_t, preact, hidden, produced = forward(got_rows, w_in, w_out)
        got_grads = after(got_grads, hidden)
        own = lax.axis_index("dp")
        send_at = jnp.stack([jnp.bitwise_xor(own, j) for j in CUBE_SEND]).astype(jnp.int32)
        keep_at = jnp.bitwise_xor(send_at, 1)
        far = experts // 2
        far_out = travel(produced[far], far, -1)
        pre_grad, grads_t = backward(preact, w_out, got_grads)
        operands = (share, rows_t, grads_t, pre_grad, hidden)
        sent = shares(send_at, *operands, BRIEF)
        blocks = input_gradients(after(pre_grad, sent), w_in, produced, far)
        returned = exchange(blocks, -1)
        half = len(CUBE_SEND) // 2
        kept_first = shares(after(keep_at[:half], blocks[0]), *operands, COVER)
        kept_later = shares(after(keep_at[half:], kept_first, far_out), *operands, COVER)
        (grad_in, grad_down), nearly = cube_sum(sent, kept_first, kept_later)
        mixed_part, back_part, pickers, scales = call(
            functools.partial(partial_kernel, experts, capacity),
            (
                jax.ShapeDtypeStruct((toks, width), F32),
                jax.ShapeDtypeStruct((toks, width), F32),
                jax.ShapeDtypeStruct((tops + 1, toks, slots), BF16),
                jax.ShapeDtypeStruct((tops, toks, 128), F32),
            ),
            (after(first, nearly), routes_t, scores_t, returned[0], far_out, returned[far]),
        )
        pickers = after(pickers, grad_in)
        near = [block for n, block in enumerate(returned) if n not in (0, far)]
        mixed_out, token_grad = pl.pallas_call(
            functools.partial(final_kernel, capacity),
            out_shape=(out_shape, out_shape),
            in_specs=whole(4 + len(near)),
            out_specs=whole(2),
            compiler_params=ROOMY,
            cost_estimate=BRIEF,
        )(pickers, scales, mixed_part, back_part, *near)
    else:
        token_rows = joined(got_rows)
        grad_rows = joined(exchange(sent_grads, 1))
        preact = jnp.dot(token_rows, w_in, preferred_element_type=F32)
        gate, up = preact[:, :units], preact[:, units:]
        hidden = (jax.nn.silu(gate) * up).astype(BF16)
        produced = jnp.dot(hidden, w_out.T, preferred_element_type=F32).astype(BF16)
        returned = exchange(split(produced), -1)
        hidden_grad = jnp.dot(grad_rows, w_out, preferred_element_type=F32)
        sigmoid = jax.nn.sigmoid(gate)
        gate_grad = hidden_grad * up * sigmoid * (1.0 + gate * (1.0 - sigmoid))
        up_grad = hidden_grad * gate * sigmoid
        pre_grad = jnp.concatenate([gate_grad, up_grad], axis=1).astype(BF16)
        input_grad = jnp.dot(pre_grad, w_in.T, preferred_element_type=F32).astype(BF16)
        sent_back = exchange(split(input_grad), -1)

        def summed(left, right):
            part = contract(left, right).astype(BF16)
            total = lax.psum_scatter(part, "dp", scatter_dimension=0, tiled=True)
            return total.astype(F32) / groups

        grad_in = summed(token_rows, pre_grad)
        grad_down = summed(grad_rows, hidden)
        mixed_out = call(
            functools.partial(combine_kernel, experts, capacity, True),
            out_shape,
            (first, routes_t, scores_t, *returned),
        )
        token_grad = call(
            functools.partial(combine_kernel, experts, capacity, False),
            out_shape,
            (first, routes_t, *sent_back),
        )
    grad_in = grad_in.reshape(1, share, 2 * units)
    grad_down = grad_down.reshape(1, share, units)
    return (mixed_out, token_grad, grad_in, grad_down)


def solution(mesh):
    in_specs = (
        P(("dp", "expert"), None),
        P(("dp", "expert"), None),
        P(("dp", "expert"), None),
        P(("dp", "expert"), None),
        P("expert", None, None),
        P("expert", None, None),
    )
    out_specs = (
        P(("dp", "expert"), None),
        P(("dp", "expert"), None),
        P("expert", "dp", None),
        P("expert", "dp", None),
    )
    return jax.shard_map(body, mesh=mesh, in_specs=in_specs, out_specs=out_specs, check_vma=False)
```

```python
import functools

import jax
import jax.numpy as jnp
from jax import lax
from jax.experimental import pallas as pl
from jax.experimental.pallas import tpu as pltpu
from jax.sharding import PartitionSpec as P

F32 = jnp.float32
BF16 = jnp.bfloat16
BRIEF = pl.CostEstimate(flops=1024, bytes_accessed=1024, transcendentals=0)
COVER = pl.CostEstimate(flops=10**11, bytes_accessed=10**8, transcendentals=0)
ROOMY = pltpu.CompilerParams(vmem_limit_bytes=16 * 1024 * 1024)
ALONE = pltpu.CompilerParams(vmem_limit_bytes=60 * 1024 * 1024)


def contract(left, right):
    return lax.dot_general(left, right, (((0,), (0,)), ((), ())), preferred_element_type=F32)


def slot_rows(first, routes, experts, capacity):
    tops, toks = routes.shape
    padded = -(-experts // 8) * 8
    rows = lax.broadcasted_iota(jnp.int32, (padded, toks), 0)
    ids = rows + first
    ids = jnp.where(ids >= experts, ids - experts, ids)
    ids = jnp.where(rows < experts, ids, -1)
    hits = [routes[k : k + 1, :] == ids for k in range(tops)]
    named = functools.reduce(jnp.logical_or, hits)
    before = lax.broadcasted_iota(jnp.int32, (toks, toks), 0) < lax.broadcasted_iota(
        jnp.int32, (toks, toks), 1
    )
    position = jnp.dot(
        named.astype(F32).astype(BF16),
        before.astype(F32).astype(BF16),
        preferred_element_type=F32,
    )
    slot = position + (rows * capacity).astype(F32)
    return [jnp.sum(jnp.where(hit, slot, 0.0), axis=0, keepdims=True) for hit in hits]


def weight_rows(scores):
    grown = jnp.exp(scores)
    return grown / jnp.sum(grown, axis=0, keepdims=True)


def to_column(row):
    toks = row.shape[1]
    same = lax.broadcasted_iota(jnp.int32, (toks, toks), 0) == lax.broadcasted_iota(
        jnp.int32, (toks, toks), 1
    )
    return jnp.sum(jnp.where(same, row, 0.0), axis=1, keepdims=True)


def put_blocks(outs, rows, columns):
    start = 0
    for out in outs:
        size = out.shape[0]
        out[:, columns] = rows[start : start + size]
        start += size


def column_steps(width):
    step = 512 if width % 512 == 0 else width
    return [slice(at, at + step) for at in range(0, width, step)]


def dispatch_kernel(experts, capacity, weighted, first, *refs):
    count = 2 + weighted
    sources, outs = refs[:count], refs[count : -count - 1]
    held, sems = refs[-count - 1 : -1], refs[-1]
    copies = [
        pltpu.make_async_copy(source, place, sems.at[n])
        for n, (source, place) in enumerate(zip(sources, held))
    ]
    for copy in copies:
        copy.start()
    routes, values = held[0], held[-1]
    scores = held[1] if weighted else None
    for copy in copies[:-1]:
        copy.wait()
    slots, toks = experts * capacity, values.shape[0]
    places = lax.broadcasted_iota(jnp.int32, (slots, toks), 0).astype(F32)
    hits = [places == row for row in slot_rows(first[0], routes[...], experts, capacity)]
    picker = functools.reduce(jnp.logical_or, hits).astype(F32).astype(BF16)
    if weighted:
        weights = weight_rows(scores[...])
        scale = sum(
            jnp.sum(jnp.where(hit, weights[k : k + 1, :], 0.0), axis=1, keepdims=True)
            for k, hit in enumerate(hits)
        )
    copies[-1].wait()
    for columns in column_steps(values.shape[1]):
        rows = jnp.dot(picker, values[:, columns], preferred_element_type=F32)
        if weighted:
            rows = rows * scale
        put_blocks(outs, rows.astype(BF16), columns)


def combine_kernel(experts, capacity, weighted, first, routes, *refs):
    scores = refs[0] if weighted else None
    blocks, out = refs[weighted:-1], refs[-1]
    slots, toks = experts * capacity, out.shape[0]
    places = lax.broadcasted_iota(jnp.int32, (toks, slots), 1).astype(F32)
    hits = [
        places == to_column(row) for row in slot_rows(first[0], routes[...], experts, capacity)
    ]
    if weighted:
        weights = weight_rows(scores[...])
        scales = [to_column(weights[k : k + 1, :]) for k in range(len(hits))]
        pickers = [hit.astype(F32).astype(BF16) for hit in hits]
    else:
        pickers = [functools.reduce(jnp.logical_or, hits).astype(F32).astype(BF16)]
    for columns in column_steps(out.shape[1]):
        rows = [block[:, columns] for block in blocks]
        rows = rows[0] if len(rows) == 1 else jnp.concatenate(rows, axis=0)
        picked = [jnp.dot(picker, rows, preferred_element_type=F32) for picker in pickers]
        if weighted:
            picked = [scale * part for scale, part in zip(scales, picked)]
        out[:, columns] = sum(picked).astype(out.dtype)


def whole(count):
    return [pl.BlockSpec(memory_space=pltpu.VMEM)] * count


def write_shares(at, rows_t, grads_t, pre_grad, hidden, out):
    share = out.shape[1]
    wide, narrow = pre_grad.shape[1] // 2, hidden.shape[1] // 2

    def write(t, half):
        own = pl.ds(pl.multiple_of(at[t] * share, share), share)
        out[t, :, :wide] = jnp.dot(
            rows_t[own, :],
            pre_grad[:, half * wide : (half + 1) * wide],
            preferred_element_type=F32,
        ).astype(out.dtype)
        out[t, :, wide:] = jnp.dot(
            grads_t[own, :],
            hidden[:, half * narrow : (half + 1) * narrow],
            preferred_element_type=F32,
        ).astype(out.dtype)

    for t in range(out.shape[0]):
        write(t, t // 2 % 2)


def transpose_into(rows, rows_t):
    width = rows.shape[1]
    step = 256 if width % 256 == 0 else width

    @pl.loop(0, width // step)
    def _(c):
        own = pl.ds(pl.multiple_of(c * step, step), step)
        rows_t[own, :] = rows[:, own].T


def join_copies(blocks, rows, sems):
    size = blocks[0].shape[0]
    joins = [
        pltpu.make_async_copy(block, rows.at[pl.ds(n * size, size)], sems.at[n])
        for n, block in enumerate(blocks)
    ]
    for join in joins:
        join.start()
    return joins


def forward_kernel(count, *refs):
    blocks, (w_in_hbm, down_hbm), (rows_t, preact, hidden), outs, scratch = (
        refs[:count],
        refs[count : count + 2],
        refs[count + 2 : count + 5],
        refs[count + 5 : 2 * count + 5],
        refs[2 * count + 5 :],
    )
    rows, w_in, down, block_sems, weight_sems, down_sem = scratch
    joins = join_copies(blocks, rows, block_sems)
    width, units = down.shape
    step = 256 if units % 256 == 0 else units
    loads = []
    for n in range(2 * units // step):
        begin = (n % 2) * units + n // 2 * step
        loads.append(
            pltpu.make_async_copy(
                w_in_hbm.at[:, pl.ds(begin, step)],
                w_in.at[:, pl.ds(begin, step)],
                weight_sems.at[n],
            )
        )
        loads[-1].start()
    load_down = pltpu.make_async_copy(down_hbm, down, down_sem)
    load_down.start()
    for join in joins:
        join.wait()
    for n in range(units // step):
        begin = n * step
        gate_at, up_at = slice(begin, begin + step), slice(units + begin, units + begin + step)
        loads[2 * n].wait()
        gate = jnp.dot(rows[...], w_in[:, gate_at], preferred_element_type=F32)
        loads[2 * n + 1].wait()
        up = jnp.dot(rows[...], w_in[:, up_at], preferred_element_type=F32)
        preact[:, gate_at] = gate
        preact[:, up_at] = up
        hidden[:, gate_at] = (gate / (1.0 + jnp.exp(-gate)) * up).astype(BF16)
    load_down.wait()
    for columns in column_steps(width):
        part = lax.dot_general(
            hidden[...], down[columns, :], (((1,), (1,)), ((), ())), preferred_element_type=F32
        )
        put_blocks(outs, part.astype(BF16), columns)
    transpose_into(rows, rows_t)


def forward(blocks, w_in, down):
    width, units = down.shape
    slots = sum(block.shape[0] for block in blocks)
    count = len(blocks)
    rows_t, preact, hidden, *outs = pl.pallas_call(
        functools.partial(forward_kernel, count),
        out_shape=(
            jax.ShapeDtypeStruct((width, slots), BF16),
            jax.ShapeDtypeStruct((slots, 2 * units), F32),
            jax.ShapeDtypeStruct((slots, units), BF16),
            *[jax.ShapeDtypeStruct(block.shape, BF16) for block in blocks],
        ),
        in_specs=anywhere(count) + in_hbm(2),
        out_specs=whole(3 + count),
        scratch_shapes=[
            pltpu.VMEM((slots, width), BF16),
            pltpu.VMEM(w_in.shape, BF16),
            pltpu.VMEM(down.shape, BF16),
            pltpu.SemaphoreType.DMA((count,)),
            pltpu.SemaphoreType.DMA((2 * units // min(units, 256),)),
            pltpu.SemaphoreType.DMA,
        ],
        compiler_params=pltpu.CompilerParams(vmem_limit_bytes=46 * 1024 * 1024),
        cost_estimate=BRIEF,
    )(*blocks, w_in, down)
    return rows_t, preact, hidden, outs


def backward_kernel(preact_hbm, down, *refs):
    blocks, (pre_grad, grads_t, grads, preact, block_sems, sem) = refs[:-6], refs[-6:]
    fetch = pltpu.make_async_copy(preact_hbm, preact, sem)
    fetch.start()
    joins = join_copies(blocks, grads, block_sems)
    for join in joins:
        join.wait()
    fetch.wait()
    units = down.shape[1]
    step = 256 if units % 256 == 0 else units
    for begin in range(0, units, step):
        gate = preact[:, begin : begin + step]
        up = preact[:, units + begin : units + begin + step]
        hidden_grad = jnp.dot(
            grads[...], down[:, begin : begin + step], preferred_element_type=F32
        )
        sigmoid = 1.0 / (1.0 + jnp.exp(-gate))
        gate_grad = hidden_grad * up * sigmoid * (1.0 + gate * (1.0 - sigmoid))
        up_grad = hidden_grad * gate * sigmoid
        pre_grad[:, begin : begin + step] = gate_grad.astype(BF16)
        pre_grad[:, units + begin : units + begin + step] = up_grad.astype(BF16)
    transpose_into(grads, grads_t)


def anywhere(count):
    return [pl.BlockSpec(memory_space=pl.ANY)] * count


def in_hbm(count):
    return [pl.BlockSpec(memory_space=pltpu.HBM)] * count


def backward(preact, down, blocks):
    width, units = down.shape
    slots = preact.shape[0]
    return pl.pallas_call(
        backward_kernel,
        out_shape=(
            jax.ShapeDtypeStruct((slots, 2 * units), BF16),
            jax.ShapeDtypeStruct((width, slots), BF16),
        ),
        in_specs=anywhere(1) + whole(1) + anywhere(len(blocks)),
        out_specs=whole(2),
        scratch_shapes=[
            pltpu.VMEM((slots, width), BF16),
            pltpu.VMEM((slots, 2 * units), F32),
            pltpu.SemaphoreType.DMA((len(blocks),)),
            pltpu.SemaphoreType.DMA,
        ],
        compiler_params=ROOMY,
        cost_estimate=BRIEF,
    )(preact, down, *blocks)


def shares(at, share, rows_t, grads_t, pre_grad, hidden, cost):
    units = hidden.shape[1]
    return pl.pallas_call(
        write_shares,
        out_shape=jax.ShapeDtypeStruct((at.shape[0], share, 3 * units // 2), BF16),
        in_specs=[pl.BlockSpec(memory_space=pltpu.SMEM)] + whole(4),
        out_specs=whole(1)[0],
        compiler_params=ROOMY,
        cost_estimate=cost,
    )(at, rows_t, grads_t, pre_grad, hidden)


def input_kernel(count, pre_grad, w_in, *refs):
    blocks, outs, sems = refs[:count], refs[count : 2 * count], refs[-1]
    width, size = w_in.shape[0], blocks[0].shape[0]
    copies = [
        pltpu.make_async_copy(block, out.at[pl.ds(0, size)], sems.at[n])
        for n, (block, out) in enumerate(zip(blocks, outs))
        if out.shape[0] > size
    ]
    for copy in copies:
        copy.start()
    for columns in column_steps(width):
        part = lax.dot_general(
            pre_grad[...], w_in[columns, :], (((1,), (1,)), ((), ())), preferred_element_type=F32
        ).astype(BF16)
        for n, out in enumerate(outs):
            out[out.shape[0] - size :, columns] = part[n * size : (n + 1) * size]
    for copy in copies:
        copy.wait()


def input_gradients(pre_grad, w_in, produced, alone):
    count = len(produced)
    size, width = produced[0].shape
    return pl.pallas_call(
        functools.partial(input_kernel, count),
        out_shape=[
            jax.ShapeDtypeStruct((size if n == alone else 2 * size, width), BF16)
            for n in range(count)
        ],
        in_specs=whole(2) + anywhere(count),
        out_specs=whole(count),
        scratch_shapes=[pltpu.SemaphoreType.DMA((count,))],
        compiler_params=ROOMY,
        cost_estimate=BRIEF,
    )(pre_grad, w_in, *produced)


def add_kernel(kept, got, left, right):
    half = left.shape[0]
    left[...] = add(kept[:half], got[:half]).astype(BF16)
    right[...] = add(kept[half:], got[half : 2 * half]).astype(BF16)


def next_kernel(kept, got, left_in, right_in, left_send, right_send):
    first = got.shape[0] // 2
    left_send[...] = (add(kept[1], got[first + 1]) + left_in[1].astype(F32)).astype(BF16)
    right_send[...] = (add(kept[3], got[first + 3]) + right_in[1].astype(F32)).astype(BF16)


def own_kernel(kept, got, left_in, right_in, left, right):
    first = got.shape[0] // 2
    left[...] = add(kept[0], got[first]) + left_in[0].astype(F32)
    right[...] = add(kept[2], got[first + 2]) + right_in[0].astype(F32)


def add(left, right):
    return left.astype(F32) + right.astype(F32)


CUBE_SEND = (3, 7, 5, 7, 1, 5, 1, 3)


def cube_sum(sent, kept_first, kept_later):
    size = lax.axis_size("dp")
    _, share, columns = sent.shape

    def swap(block, bit):
        return lax.ppermute(block, "dp", [(at, at ^ bit) for at in range(size)])

    def run(kernel, out_shape, inputs, cost=BRIEF):
        return pl.pallas_call(
            kernel,
            out_shape=out_shape,
            in_specs=whole(len(inputs)),
            out_specs=whole(len(out_shape)),
            compiler_params=ROOMY,
            cost_estimate=cost,
        )(*inputs)

    half = jax.ShapeDtypeStruct((2, share, columns), BF16)
    one = jax.ShapeDtypeStruct((share, columns), BF16)
    own = jax.ShapeDtypeStruct((share, columns), F32)
    got = swap(sent, 1)
    left, right = run(add_kernel, (half, half), (kept_first, got))
    parts = (kept_later, got, swap(left, 2), swap(right, 4))
    left_send, right_send = run(next_kernel, (one, one), parts)
    left, right = run(own_kernel, (own, own), parts, COVER)
    return left, swap(left_send, 4), right, swap(right_send, 2)


def after(value, *others):
    return lax.optimization_barrier((value, *others))[0]


def partial_kernel(experts, capacity, alone, first, routes, scores, *refs):
    blocks, (mixed, back, pickers, scales) = refs[:-4], refs[-4:]
    slots, toks = experts * capacity, mixed.shape[0]
    places = lax.broadcasted_iota(jnp.int32, (toks, slots), 1).astype(F32)
    hits = [
        places == to_column(row) for row in slot_rows(first[0], routes[...], experts, capacity)
    ]
    weights = weight_rows(scores[...])
    for k, hit in enumerate(hits):
        pickers[k] = hit.astype(F32).astype(BF16)
        scales[k] = jnp.broadcast_to(to_column(weights[k : k + 1, :]), scales.shape[1:])
    pickers[len(hits)] = functools.reduce(jnp.logical_or, hits).astype(F32).astype(BF16)
    outputs = [(0, blocks[0], 0), (alone, blocks[1], 0)]
    gradients = [(0, blocks[0], capacity), (alone, blocks[2], 0)]
    for columns in column_steps(mixed.shape[1]):
        total, grad = sum_blocks(capacity, pickers, scales, outputs, gradients, columns)
        mixed[:, columns] = total
        back[:, columns] = grad


def sum_blocks(capacity, pickers, scales, outputs, gradients, columns):
    tops = scales.shape[0]

    def select(terms, k):
        slots = [slice(n * capacity, (n + 1) * capacity) for n, _, _ in terms]
        picker = jnp.concatenate([pickers[k, :, at] for at in slots], axis=1)
        rows = [block[start : start + capacity, columns] for _, block, start in terms]
        return jnp.dot(picker, jnp.concatenate(rows, axis=0), preferred_element_type=F32)

    total = sum(scales[k, :, :1] * select(outputs, k) for k in range(tops))
    return total, select(gradients, tops)


def last_kernel(capacity, count, places, *refs):
    number = len(places)
    pickers, scales, mixed_part, back_part, left, left_last, right, right_last = refs[:8]
    sources, (mixed, back, wide, narrow) = refs[8 : 8 + number], refs[8 + number : 12 + number]
    scratch = refs[12 + number :]
    held, scratch = scratch[:number], scratch[number:]
    mixed_vmem, back_vmem, wide_vmem, narrow_vmem, in_sems, out_sems = scratch
    loads = [
        pltpu.make_async_copy(source, block, in_sems.at[n])
        for n, (source, block) in enumerate(zip(sources, held))
    ]
    for load in loads:
        load.start()
    stores = []

    def store(source, target, columns):
        stores.append(
            pltpu.make_async_copy(
                source.at[:, columns], target.at[:, columns], out_sems.at[len(stores)]
            )
        )
        stores[-1].start()

    middle, edge = wide.shape[1] // 2, narrow.shape[1] // 2
    for at, (own, last) in enumerate(((left, left_last), (right, right_last))):
        total = (own[...] + last[...].astype(F32)) / count
        columns = slice(at * middle, (at + 1) * middle)
        wide_vmem[:, columns] = total[:, :middle]
        store(wide_vmem, wide, columns)
        columns = slice(at * edge, (at + 1) * edge)
        narrow_vmem[:, columns] = total[:, middle:]
        store(narrow_vmem, narrow, columns)
    for load in loads:
        load.wait()
    outputs = [(n, block, 0) for n, block in zip(places, held)]
    gradients = [(n, block, capacity) for n, block in zip(places, held)]
    for columns in column_steps(mixed.shape[1]):
        total, grad = sum_blocks(capacity, pickers, scales, outputs, gradients, columns)
        mixed_vmem[:, columns] = (total + mixed_part[:, columns]).astype(BF16)
        store(mixed_vmem, mixed, columns)
        back_vmem[:, columns] = (grad + back_part[:, columns]).astype(BF16)
        store(back_vmem, back, columns)
    for stored in stores:
        stored.wait()


def last(capacity, count, places, parts, sums, blocks):
    toks, width = parts[-1].shape
    share, columns = sums[0].shape
    wide, narrow = 4 * columns // 3, 2 * columns // 3
    shapes = [
        ((toks, width), BF16),
        ((toks, width), BF16),
        ((share, wide), F32),
        ((share, narrow), F32),
    ]
    return pl.pallas_call(
        functools.partial(last_kernel, capacity, count, places),
        out_shape=[jax.ShapeDtypeStruct(*shape) for shape in shapes],
        in_specs=whole(8) + anywhere(len(blocks)),
        out_specs=anywhere(4),
        scratch_shapes=[pltpu.VMEM(block.shape, BF16) for block in blocks]
        + [pltpu.VMEM(*shape) for shape in shapes]
        + [
            pltpu.SemaphoreType.DMA((len(blocks),)),
            pltpu.SemaphoreType.DMA((4 + 2 * len(column_steps(width)),)),
        ],
        compiler_params=ROOMY,
        cost_estimate=BRIEF,
    )(*parts, *sums, *blocks)


def dispatch(experts, capacity, out_shape, first, *sources):
    weighted = len(sources) > 2
    return pl.pallas_call(
        functools.partial(dispatch_kernel, experts, capacity, weighted),
        out_shape=out_shape,
        in_specs=[pl.BlockSpec(memory_space=pltpu.SMEM)] + in_hbm(len(sources)),
        out_specs=whole(len(out_shape)),
        scratch_shapes=[pltpu.VMEM(source.shape, source.dtype) for source in sources]
        + [pltpu.SemaphoreType.DMA((len(sources),))],
        compiler_params=ALONE,
        cost_estimate=BRIEF,
    )(first, *sources)


def call(kernel, out_shape, inputs):
    return pl.pallas_call(
        kernel,
        out_shape=out_shape,
        in_specs=[pl.BlockSpec(memory_space=pltpu.SMEM)]
        + [pl.BlockSpec(memory_space=pltpu.VMEM)] * (len(inputs) - 1),
        compiler_params=ROOMY,
        cost_estimate=BRIEF,
    )(*inputs)


def body(tokens, routes, route_scores, out_grad, gate_up, down_weight):
    experts = lax.axis_size("expert")
    groups = lax.axis_size("dp")
    toks, width = tokens.shape
    tops = routes.shape[1]
    units = down_weight.shape[2]
    capacity = (toks * tops + experts - 1) // experts
    slots = experts * capacity
    share = width // groups
    direct = experts <= 8 and capacity % 16 == 0
    w_in, w_out = gate_up[0], down_weight[0]
    routes_t, scores_t = routes.T, route_scores.T
    me = lax.axis_index("expert") if direct else jnp.int32(0)
    first = me.astype(jnp.int32).reshape(1)
    sizes = [capacity] * experts if direct else [slots]
    block_shapes = [jax.ShapeDtypeStruct((size, width), BF16) for size in sizes]

    def travel(block, step, sign):
        pairs = [(at, (at + sign * step) % experts) for at in range(experts)]
        return lax.ppermute(block, "expert", pairs)

    def exchange(blocks, sign):
        if not direct:
            block = blocks[0].reshape(experts, capacity, width)
            moved = lax.all_to_all(block, "expert", split_axis=0, concat_axis=0, tiled=True)
            return [moved.reshape(slots, width)]
        return [blocks[0]] + [travel(blocks[step], step, sign) for step in range(1, experts)]

    def joined(blocks):
        return blocks[0] if len(blocks) == 1 else jnp.concatenate(blocks, axis=0)

    def split(rows):
        return [rows[at : at + sizes[0]] for at in range(0, slots, sizes[0])]

    sent_rows = dispatch(experts, capacity, block_shapes, first, routes_t, tokens)
    got_rows = exchange(sent_rows, 1)
    sent_grads = dispatch(experts, capacity, block_shapes, first, routes_t, scores_t, out_grad)
    out_shape = jax.ShapeDtypeStruct((toks, width), BF16)
    cube = direct and experts == 4 and groups == 8 and share % 256 == 0
    if cube:
        sent_grads = after(sent_grads, got_rows[1], got_rows[-1])
        got_grads = exchange(sent_grads, 1)
        rows_t, preact, hidden, produced = forward(got_rows, w_in, w_out)
        got_grads = after(got_grads, hidden)
        own = lax.axis_index("dp")
        send_at = jnp.stack([jnp.bitwise_xor(own, j) for j in CUBE_SEND]).astype(jnp.int32)
        keep_at = jnp.bitwise_xor(send_at, 1)
        early = 1
        early_out = travel(produced[early], early, -1)
        pre_grad, grads_t = backward(preact, w_out, got_grads)
        operands = (share, rows_t, grads_t, pre_grad, hidden)
        sent = shares(send_at, *operands, BRIEF)
        blocks = input_gradients(after(pre_grad, sent), w_in, produced, early)
        returned = exchange(blocks, -1)
        half = len(CUBE_SEND) // 2
        kept_first = shares(after(keep_at[:half], blocks[0]), *operands, COVER)
        kept_later = shares(after(keep_at[half:], kept_first, early_out), *operands, COVER)
        sums = cube_sum(sent, kept_first, kept_later)
        mixed_part, back_part, pickers, scales = call(
            functools.partial(partial_kernel, experts, capacity, early),
            (
                jax.ShapeDtypeStruct((toks, width), F32),
                jax.ShapeDtypeStruct((toks, width), F32),
                jax.ShapeDtypeStruct((tops + 1, toks, slots), BF16),
                jax.ShapeDtypeStruct((tops, toks, 128), F32),
            ),
            (after(first, sums[0]), routes_t, scores_t, returned[0], early_out, returned[early]),
        )
        places = [n for n in range(1, experts) if n != early]
        parts = (pickers, scales, mixed_part, back_part)
        near = [returned[n] for n in places]
        mixed_out, token_grad, grad_in, grad_down = last(
            capacity, groups, places, parts, sums, near
        )
    else:
        token_rows = joined(got_rows)
        grad_rows = joined(exchange(sent_grads, 1))
        preact = jnp.dot(token_rows, w_in, preferred_element_type=F32)
        gate, up = preact[:, :units], preact[:, units:]
        hidden = (jax.nn.silu(gate) * up).astype(BF16)
        produced = jnp.dot(hidden, w_out.T, preferred_element_type=F32).astype(BF16)
        returned = exchange(split(produced), -1)
        hidden_grad = jnp.dot(grad_rows, w_out, preferred_element_type=F32)
        sigmoid = jax.nn.sigmoid(gate)
        gate_grad = hidden_grad * up * sigmoid * (1.0 + gate * (1.0 - sigmoid))
        up_grad = hidden_grad * gate * sigmoid
        pre_grad = jnp.concatenate([gate_grad, up_grad], axis=1).astype(BF16)
        input_grad = jnp.dot(pre_grad, w_in.T, preferred_element_type=F32).astype(BF16)
        sent_back = exchange(split(input_grad), -1)

        def summed(left, right):
            part = contract(left, right).astype(BF16)
            total = lax.psum_scatter(part, "dp", scatter_dimension=0, tiled=True)
            return total.astype(F32) / groups

        grad_in = summed(token_rows, pre_grad)
        grad_down = summed(grad_rows, hidden)
        mixed_out = call(
            functools.partial(combine_kernel, experts, capacity, True),
            out_shape,
            (first, routes_t, scores_t, *returned),
        )
        token_grad = call(
            functools.partial(combine_kernel, experts, capacity, False),
            out_shape,
            (first, routes_t, *sent_back),
        )
    grad_in = grad_in.reshape(1, share, 2 * units)
    grad_down = grad_down.reshape(1, share, units)
    return (mixed_out, token_grad, grad_in, grad_down)


def solution(mesh):
    in_specs = (
        P(("dp", "expert"), None),
        P(("dp", "expert"), None),
        P(("dp", "expert"), None),
        P(("dp", "expert"), None),
        P("expert", None, None),
        P("expert", None, None),
    )
    out_specs = (
        P(("dp", "expert"), None),
        P(("dp", "expert"), None),
        P("expert", "dp", None),
        P("expert", "dp", None),
    )
    return jax.shard_map(body, mesh=mesh, in_specs=in_specs, out_specs=out_specs, check_vma=False)
```

```python
import functools

import jax
import jax.numpy as jnp
from jax import lax
from jax.experimental import pallas as pl
from jax.experimental.pallas import tpu as pltpu
from jax.sharding import PartitionSpec as P

F32 = jnp.float32
BF16 = jnp.bfloat16
BRIEF = pl.CostEstimate(flops=1024, bytes_accessed=1024, transcendentals=0)
COVER = pl.CostEstimate(flops=10**11, bytes_accessed=10**8, transcendentals=0)
ROOMY = pltpu.CompilerParams(vmem_limit_bytes=16 * 1024 * 1024)
ALONE = pltpu.CompilerParams(vmem_limit_bytes=60 * 1024 * 1024)


def contract(left, right):
    return lax.dot_general(left, right, (((0,), (0,)), ((), ())), preferred_element_type=F32)


def slot_rows(first, routes, experts, capacity):
    tops, toks = routes.shape
    padded = -(-experts // 8) * 8
    rows = lax.broadcasted_iota(jnp.int32, (padded, toks), 0)
    ids = rows + first
    ids = jnp.where(ids >= experts, ids - experts, ids)
    ids = jnp.where(rows < experts, ids, -1)
    hits = [routes[k : k + 1, :] == ids for k in range(tops)]
    named = functools.reduce(jnp.logical_or, hits)
    before = lax.broadcasted_iota(jnp.int32, (toks, toks), 0) < lax.broadcasted_iota(
        jnp.int32, (toks, toks), 1
    )
    position = jnp.dot(
        named.astype(F32).astype(BF16),
        before.astype(F32).astype(BF16),
        preferred_element_type=F32,
    )
    slot = position + (rows * capacity).astype(F32)
    return [jnp.sum(jnp.where(hit, slot, 0.0), axis=0, keepdims=True) for hit in hits]


def weight_rows(scores):
    grown = jnp.exp(scores)
    return grown / jnp.sum(grown, axis=0, keepdims=True)


def to_column(row):
    toks = row.shape[1]
    same = lax.broadcasted_iota(jnp.int32, (toks, toks), 0) == lax.broadcasted_iota(
        jnp.int32, (toks, toks), 1
    )
    return jnp.sum(jnp.where(same, row, 0.0), axis=1, keepdims=True)


def put_blocks(outs, rows, columns):
    start = 0
    for out in outs:
        size = out.shape[0]
        out[:, columns] = rows[start : start + size]
        start += size


def column_steps(width):
    step = 512 if width % 512 == 0 else width
    return [slice(at, at + step) for at in range(0, width, step)]


def dispatch_kernel(experts, capacity, weighted, first, *refs):
    count = 2 + weighted
    sources, outs = refs[:count], refs[count : -count - 1]
    held, sems = refs[-count - 1 : -1], refs[-1]
    copies = [
        pltpu.make_async_copy(source, place, sems.at[n])
        for n, (source, place) in enumerate(zip(sources, held))
    ]
    for copy in copies:
        copy.start()
    routes, values = held[0], held[-1]
    scores = held[1] if weighted else None
    for copy in copies[:-1]:
        copy.wait()
    slots, toks = experts * capacity, values.shape[0]
    places = lax.broadcasted_iota(jnp.int32, (slots, toks), 0).astype(F32)
    hits = [places == row for row in slot_rows(first[0], routes[...], experts, capacity)]
    picker = functools.reduce(jnp.logical_or, hits).astype(F32).astype(BF16)
    if weighted:
        weights = weight_rows(scores[...])
        scale = sum(
            jnp.sum(jnp.where(hit, weights[k : k + 1, :], 0.0), axis=1, keepdims=True)
            for k, hit in enumerate(hits)
        )
    copies[-1].wait()
    for columns in column_steps(values.shape[1]):
        rows = jnp.dot(picker, values[:, columns], preferred_element_type=F32)
        if weighted:
            rows = rows * scale
        put_blocks(outs, rows.astype(BF16), columns)


def combine_kernel(experts, capacity, weighted, first, routes, *refs):
    scores = refs[0] if weighted else None
    blocks, out = refs[weighted:-1], refs[-1]
    slots, toks = experts * capacity, out.shape[0]
    places = lax.broadcasted_iota(jnp.int32, (toks, slots), 1).astype(F32)
    hits = [
        places == to_column(row) for row in slot_rows(first[0], routes[...], experts, capacity)
    ]
    if weighted:
        weights = weight_rows(scores[...])
        scales = [to_column(weights[k : k + 1, :]) for k in range(len(hits))]
        pickers = [hit.astype(F32).astype(BF16) for hit in hits]
    else:
        pickers = [functools.reduce(jnp.logical_or, hits).astype(F32).astype(BF16)]
    for columns in column_steps(out.shape[1]):
        rows = [block[:, columns] for block in blocks]
        rows = rows[0] if len(rows) == 1 else jnp.concatenate(rows, axis=0)
        picked = [jnp.dot(picker, rows, preferred_element_type=F32) for picker in pickers]
        if weighted:
            picked = [scale * part for scale, part in zip(scales, picked)]
        out[:, columns] = sum(picked).astype(out.dtype)


def whole(count):
    return [pl.BlockSpec(memory_space=pltpu.VMEM)] * count


def write_shares(at, rows_t, grads_t, pre_grad, hidden, out):
    share = out.shape[1]
    wide, narrow = pre_grad.shape[1] // 2, hidden.shape[1] // 2

    def write(t, half):
        own = pl.ds(pl.multiple_of(at[t] * share, share), share)
        out[t, :, :wide] = jnp.dot(
            rows_t[own, :],
            pre_grad[:, half * wide : (half + 1) * wide],
            preferred_element_type=F32,
        ).astype(out.dtype)
        out[t, :, wide:] = jnp.dot(
            grads_t[own, :],
            hidden[:, half * narrow : (half + 1) * narrow],
            preferred_element_type=F32,
        ).astype(out.dtype)

    for t in range(out.shape[0]):
        write(t, t // 2 % 2)


def transpose_into(rows, rows_t):
    width = rows.shape[1]
    step = 256 if width % 256 == 0 else width

    @pl.loop(0, width // step)
    def _(c):
        own = pl.ds(pl.multiple_of(c * step, step), step)
        rows_t[own, :] = rows[:, own].T


def join_copies(blocks, rows, sems):
    size = blocks[0].shape[0]
    joins = [
        pltpu.make_async_copy(block, rows.at[pl.ds(n * size, size)], sems.at[n])
        for n, block in enumerate(blocks)
    ]
    for join in joins:
        join.start()
    return joins


def forward_kernel(count, *refs):
    blocks, w_in_hbm, (rows_t, preact, hidden), outs, scratch = (
        refs[:count],
        refs[count],
        refs[count + 1 : count + 4],
        refs[count + 4 : 2 * count + 4],
        refs[2 * count + 4 :],
    )
    rows, w_in, block_sems, weight_sems = scratch
    joins = join_copies(blocks, rows, block_sems)
    units = hidden.shape[1]
    step = 256 if units % 256 == 0 else units
    loads = []
    for n in range(2 * units // step):
        begin = (n % 2) * units + n // 2 * step
        loads.append(
            pltpu.make_async_copy(
                w_in_hbm.at[:, pl.ds(begin, step)],
                w_in.at[:, pl.ds(begin, step)],
                weight_sems.at[n],
            )
        )
        loads[-1].start()
    for join in joins:
        join.wait()
    for n in range(units // step):
        begin = n * step
        gate_at, up_at = slice(begin, begin + step), slice(units + begin, units + begin + step)
        loads[2 * n].wait()
        gate = jnp.dot(rows[...], w_in[:, gate_at], preferred_element_type=F32)
        loads[2 * n + 1].wait()
        up = jnp.dot(rows[...], w_in[:, up_at], preferred_element_type=F32)
        preact[:, gate_at] = gate
        preact[:, up_at] = up
        value = (gate / (1.0 + jnp.exp(-gate)) * up).astype(BF16)
        hidden[:, gate_at] = value
        put_blocks(outs, value, gate_at)
    transpose_into(rows, rows_t)


def forward(blocks, w_in):
    width, units = w_in.shape[0], w_in.shape[1] // 2
    slots = sum(block.shape[0] for block in blocks)
    count = len(blocks)
    rows_t, preact, hidden, *outs = pl.pallas_call(
        functools.partial(forward_kernel, count),
        out_shape=(
            jax.ShapeDtypeStruct((width, slots), BF16),
            jax.ShapeDtypeStruct((slots, 2 * units), F32),
            jax.ShapeDtypeStruct((slots, units), BF16),
            *[jax.ShapeDtypeStruct((block.shape[0], units), BF16) for block in blocks],
        ),
        in_specs=anywhere(count) + in_hbm(1),
        out_specs=whole(3 + count),
        scratch_shapes=[
            pltpu.VMEM((slots, width), BF16),
            pltpu.VMEM(w_in.shape, BF16),
            pltpu.SemaphoreType.DMA((count,)),
            pltpu.SemaphoreType.DMA((2 * units // min(units, 256),)),
        ],
        compiler_params=pltpu.CompilerParams(vmem_limit_bytes=46 * 1024 * 1024),
        cost_estimate=BRIEF,
    )(*blocks, w_in)
    return rows_t, preact, hidden, outs


def backward_kernel(preact_hbm, down, *refs):
    blocks, (pre_grad, grads_t, grads, preact, block_sems, sem) = refs[:-6], refs[-6:]
    fetch = pltpu.make_async_copy(preact_hbm, preact, sem)
    fetch.start()
    joins = join_copies(blocks, grads, block_sems)
    for join in joins:
        join.wait()
    fetch.wait()
    units = down.shape[1]
    step = 256 if units % 256 == 0 else units
    for begin in range(0, units, step):
        gate = preact[:, begin : begin + step]
        up = preact[:, units + begin : units + begin + step]
        hidden_grad = jnp.dot(
            grads[...], down[:, begin : begin + step], preferred_element_type=F32
        )
        sigmoid = 1.0 / (1.0 + jnp.exp(-gate))
        gate_grad = hidden_grad * up * sigmoid * (1.0 + gate * (1.0 - sigmoid))
        up_grad = hidden_grad * gate * sigmoid
        pre_grad[:, begin : begin + step] = gate_grad.astype(BF16)
        pre_grad[:, units + begin : units + begin + step] = up_grad.astype(BF16)
    transpose_into(grads, grads_t)


def anywhere(count):
    return [pl.BlockSpec(memory_space=pl.ANY)] * count


def in_hbm(count):
    return [pl.BlockSpec(memory_space=pltpu.HBM)] * count


def backward(preact, down, blocks):
    width, units = down.shape
    slots = preact.shape[0]
    return pl.pallas_call(
        backward_kernel,
        out_shape=(
            jax.ShapeDtypeStruct((slots, 2 * units), BF16),
            jax.ShapeDtypeStruct((width, slots), BF16),
        ),
        in_specs=anywhere(1) + whole(1) + anywhere(len(blocks)),
        out_specs=whole(2),
        scratch_shapes=[
            pltpu.VMEM((slots, width), BF16),
            pltpu.VMEM((slots, 2 * units), F32),
            pltpu.SemaphoreType.DMA((len(blocks),)),
            pltpu.SemaphoreType.DMA,
        ],
        compiler_params=ROOMY,
        cost_estimate=BRIEF,
    )(preact, down, *blocks)


def shares(at, share, rows_t, grads_t, pre_grad, hidden, cost):
    units = hidden.shape[1]
    return pl.pallas_call(
        write_shares,
        out_shape=jax.ShapeDtypeStruct((at.shape[0], share, 3 * units // 2), BF16),
        in_specs=[pl.BlockSpec(memory_space=pltpu.SMEM)] + whole(4),
        out_specs=whole(1)[0],
        compiler_params=ROOMY,
        cost_estimate=cost,
    )(at, rows_t, grads_t, pre_grad, hidden)


def input_kernel(pre_grad, w_in, *outs):
    for columns in column_steps(w_in.shape[0]):
        part = lax.dot_general(
            pre_grad[...], w_in[columns, :], (((1,), (1,)), ((), ())), preferred_element_type=F32
        )
        put_blocks(outs, part.astype(BF16), columns)


def input_gradients(pre_grad, w_in, sizes):
    return pl.pallas_call(
        input_kernel,
        out_shape=[jax.ShapeDtypeStruct((size, w_in.shape[0]), BF16) for size in sizes],
        in_specs=whole(2),
        out_specs=whole(len(sizes)),
        compiler_params=ROOMY,
        cost_estimate=BRIEF,
    )(pre_grad, w_in)


def add_kernel(kept, got, left, right):
    half = left.shape[0]
    left[...] = add(kept[:half], got[:half]).astype(BF16)
    right[...] = add(kept[half:], got[half : 2 * half]).astype(BF16)


def next_kernel(kept, got, left_in, right_in, left_send, right_send):
    first = got.shape[0] // 2
    left_send[...] = (add(kept[1], got[first + 1]) + left_in[1].astype(F32)).astype(BF16)
    right_send[...] = (add(kept[3], got[first + 3]) + right_in[1].astype(F32)).astype(BF16)


def own_kernel(kept, got, left_in, right_in, left, right):
    first = got.shape[0] // 2
    left[...] = add(kept[0], got[first]) + left_in[0].astype(F32)
    right[...] = add(kept[2], got[first + 2]) + right_in[0].astype(F32)


def add(left, right):
    return left.astype(F32) + right.astype(F32)


CUBE_SEND = (3, 7, 5, 7, 1, 5, 1, 3)


def cube_sum(sent, kept_first, keep_later):
    size = lax.axis_size("dp")
    _, share, columns = sent.shape

    def swap(block, bit):
        return lax.ppermute(block, "dp", [(at, at ^ bit) for at in range(size)])

    def run(kernel, out_shape, inputs, cost=BRIEF):
        return pl.pallas_call(
            kernel,
            out_shape=out_shape,
            in_specs=whole(len(inputs)),
            out_specs=whole(len(out_shape)),
            compiler_params=ROOMY,
            cost_estimate=cost,
        )(*inputs)

    half = jax.ShapeDtypeStruct((2, share, columns), BF16)
    one = jax.ShapeDtypeStruct((share, columns), BF16)
    own = jax.ShapeDtypeStruct((share, columns), F32)
    got = swap(sent, 1)
    left, right = run(add_kernel, (half, half), (kept_first, got))
    parts = (keep_later(got), got, swap(left, 2), swap(right, 4))
    left_send, right_send = run(next_kernel, (one, one), parts)
    left, right = run(own_kernel, (own, own), parts, COVER)
    return left, swap(left_send, 4), right, swap(right_send, 2)


def after(value, *others):
    return lax.optimization_barrier((value, *others))[0]


def mixed_kernel(experts, capacity, first, routes, scores, down_hbm, *refs):
    blocks, (mixed, either, outputs, down, sems) = refs[:experts], refs[experts:]
    toks, width = mixed.shape
    slots = experts * capacity

    def load(n):
        expert = first[0] + n
        expert = jnp.where(expert >= experts, expert - experts, expert)
        rows = pl.ds(pl.multiple_of(expert * width, width), width)
        return pltpu.make_async_copy(down_hbm.at[rows], down.at[n % 2], sems.at[n % 2])

    load(0).start()
    for n in range(experts):
        if n + 1 < experts:
            load(n + 1).start()
        load(n).wait()
        for columns in column_steps(width):
            part = lax.dot_general(
                blocks[n][...],
                down[n % 2, columns, :],
                (((1,), (1,)), ((), ())),
                preferred_element_type=F32,
            )
            outputs[n * capacity : (n + 1) * capacity, columns] = part.astype(BF16)
    places = lax.broadcasted_iota(jnp.int32, (toks, slots), 1).astype(F32)
    hits = [
        places == to_column(row) for row in slot_rows(first[0], routes[...], experts, capacity)
    ]
    either[...] = functools.reduce(jnp.logical_or, hits).astype(F32).astype(BF16)
    weights = weight_rows(scores[...])
    scales = [to_column(weights[k : k + 1, :]) for k in range(len(hits))]
    pickers = [hit.astype(F32).astype(BF16) for hit in hits]
    for columns in column_steps(width):
        picked = [
            jnp.dot(picker, outputs[:, columns], preferred_element_type=F32) for picker in pickers
        ]
        mixed[:, columns] = sum(scale * part for scale, part in zip(scales, picked)).astype(BF16)


def mix(experts, capacity, first, routes, scores, down, blocks, toks, width):
    slots = experts * capacity
    return pl.pallas_call(
        functools.partial(mixed_kernel, experts, capacity),
        out_shape=(
            jax.ShapeDtypeStruct((toks, width), BF16),
            jax.ShapeDtypeStruct((toks, slots), BF16),
        ),
        in_specs=[pl.BlockSpec(memory_space=pltpu.SMEM)]
        + whole(2)
        + anywhere(1)
        + whole(len(blocks)),
        out_specs=whole(2),
        scratch_shapes=[
            pltpu.VMEM((slots, width), BF16),
            pltpu.VMEM((2, width, down.shape[1]), BF16),
            pltpu.SemaphoreType.DMA((2,)),
        ],
        compiler_params=ROOMY,
        cost_estimate=COVER,
    )(first, routes, scores, down, *blocks)


def last_kernel(count, number, *refs):
    either, left, left_last, right, right_last = refs[:5]
    sources, (back, wide, narrow) = refs[5 : 5 + number], refs[5 + number : 8 + number]
    rows, back_vmem, wide_vmem, narrow_vmem, in_sems, out_sems = refs[8 + number :]
    joins = join_copies(sources, rows, in_sems)
    stores = []

    def store(source, target, columns):
        stores.append(
            pltpu.make_async_copy(
                source.at[:, columns], target.at[:, columns], out_sems.at[len(stores)]
            )
        )
        stores[-1].start()

    middle, edge = wide.shape[1] // 2, narrow.shape[1] // 2
    for at, (own, last) in enumerate(((left, left_last), (right, right_last))):
        total = (own[...] + last[...].astype(F32)) / count
        columns = slice(at * middle, (at + 1) * middle)
        wide_vmem[:, columns] = total[:, :middle]
        store(wide_vmem, wide, columns)
        columns = slice(at * edge, (at + 1) * edge)
        narrow_vmem[:, columns] = total[:, middle:]
        store(narrow_vmem, narrow, columns)
    for join in joins:
        join.wait()
    for columns in column_steps(back.shape[1]):
        back_vmem[:, columns] = jnp.dot(
            either[...], rows[:, columns], preferred_element_type=F32
        ).astype(BF16)
        store(back_vmem, back, columns)
    for stored in stores:
        stored.wait()


def last(count, either, sums, blocks):
    toks, slots = either.shape
    width = blocks[0].shape[1]
    share, columns = sums[0].shape
    shapes = [
        ((toks, width), BF16),
        ((share, 4 * columns // 3), F32),
        ((share, 2 * columns // 3), F32),
    ]
    return pl.pallas_call(
        functools.partial(last_kernel, count, len(blocks)),
        out_shape=[jax.ShapeDtypeStruct(*shape) for shape in shapes],
        in_specs=whole(5) + anywhere(len(blocks)),
        out_specs=anywhere(3),
        scratch_shapes=[pltpu.VMEM((slots, width), BF16)]
        + [pltpu.VMEM(*shape) for shape in shapes]
        + [
            pltpu.SemaphoreType.DMA((len(blocks),)),
            pltpu.SemaphoreType.DMA((4 + len(column_steps(width)),)),
        ],
        compiler_params=ROOMY,
        cost_estimate=BRIEF,
    )(either, *sums, *blocks)


def dispatch(experts, capacity, out_shape, first, *sources):
    weighted = len(sources) > 2
    return pl.pallas_call(
        functools.partial(dispatch_kernel, experts, capacity, weighted),
        out_shape=out_shape,
        in_specs=[pl.BlockSpec(memory_space=pltpu.SMEM)] + in_hbm(len(sources)),
        out_specs=whole(len(out_shape)),
        scratch_shapes=[pltpu.VMEM(source.shape, source.dtype) for source in sources]
        + [pltpu.SemaphoreType.DMA((len(sources),))],
        compiler_params=ALONE,
        cost_estimate=BRIEF,
    )(first, *sources)


def call(kernel, out_shape, inputs):
    return pl.pallas_call(
        kernel,
        out_shape=out_shape,
        in_specs=[pl.BlockSpec(memory_space=pltpu.SMEM)]
        + [pl.BlockSpec(memory_space=pltpu.VMEM)] * (len(inputs) - 1),
        compiler_params=ROOMY,
        cost_estimate=BRIEF,
    )(*inputs)


def body(tokens, routes, route_scores, out_grad, gate_up, down_weight):
    experts = lax.axis_size("expert")
    groups = lax.axis_size("dp")
    toks, width = tokens.shape
    tops = routes.shape[1]
    units = down_weight.shape[2]
    capacity = (toks * tops + experts - 1) // experts
    slots = experts * capacity
    share = width // groups
    direct = experts <= 8 and capacity % 16 == 0
    w_in, w_out = gate_up[0], down_weight[0]
    routes_t, scores_t = routes.T, route_scores.T
    me = lax.axis_index("expert") if direct else jnp.int32(0)
    first = me.astype(jnp.int32).reshape(1)
    sizes = [capacity] * experts if direct else [slots]
    block_shapes = [jax.ShapeDtypeStruct((size, width), BF16) for size in sizes]

    def travel(block, step, sign):
        pairs = [(at, (at + sign * step) % experts) for at in range(experts)]
        return lax.ppermute(block, "expert", pairs)

    def exchange(blocks, sign):
        if not direct:
            block = blocks[0].reshape(experts, capacity, width)
            moved = lax.all_to_all(block, "expert", split_axis=0, concat_axis=0, tiled=True)
            return [moved.reshape(slots, width)]
        return [blocks[0]] + [travel(blocks[step], step, sign) for step in range(1, experts)]

    def joined(blocks):
        return blocks[0] if len(blocks) == 1 else jnp.concatenate(blocks, axis=0)

    def split(rows):
        return [rows[at : at + sizes[0]] for at in range(0, slots, sizes[0])]

    sent_rows = dispatch(experts, capacity, block_shapes, first, routes_t, tokens)
    got_rows = exchange(sent_rows, 1)
    sent_grads = dispatch(experts, capacity, block_shapes, first, routes_t, scores_t, out_grad)
    out_shape = jax.ShapeDtypeStruct((toks, width), BF16)
    cube = direct and experts == 4 and groups == 8 and share % 256 == 0
    if cube:
        sent_grads = after(sent_grads, got_rows[1], got_rows[-1])
        got_grads = exchange(sent_grads, 1)
        own = lax.axis_index("dp")
        down_piece = lax.dynamic_slice_in_dim(w_out, own * share, share, 0)
        all_down = lax.all_gather(down_piece, ("expert", "dp"), axis=0, tiled=True)
        rows_t, preact, hidden, hidden_blocks = forward(got_rows, w_in)
        got_grads = after(got_grads, hidden)
        hidden_back = exchange(hidden_blocks, -1)
        send_at = jnp.stack([jnp.bitwise_xor(own, j) for j in CUBE_SEND]).astype(jnp.int32)
        keep_at = jnp.bitwise_xor(send_at, 1)
        pre_grad, grads_t = backward(preact, w_out, got_grads)
        operands = (share, rows_t, grads_t, pre_grad, hidden)
        sent = shares(after(send_at, *hidden_back[1:]), *operands, BRIEF)
        blocks = input_gradients(after(pre_grad, sent), w_in, sizes)
        returned = exchange(blocks, -1)
        half = len(CUBE_SEND) // 2
        kept_first = shares(after(keep_at[:half], blocks[0]), *operands, COVER)

        def keep_later(got):
            return shares(after(keep_at[half:], kept_first, got), *operands, COVER)

        sums = cube_sum(sent, kept_first, keep_later)
        mixed_out, either = mix(
            experts,
            capacity,
            after(first, sums[0]),
            routes_t,
            scores_t,
            all_down,
            hidden_back,
            toks,
            width,
        )
        token_grad, grad_in, grad_down = last(groups, either, sums, returned)
    else:
        token_rows = joined(got_rows)
        grad_rows = joined(exchange(sent_grads, 1))
        preact = jnp.dot(token_rows, w_in, preferred_element_type=F32)
        gate, up = preact[:, :units], preact[:, units:]
        hidden = (jax.nn.silu(gate) * up).astype(BF16)
        produced = jnp.dot(hidden, w_out.T, preferred_element_type=F32).astype(BF16)
        returned = exchange(split(produced), -1)
        hidden_grad = jnp.dot(grad_rows, w_out, preferred_element_type=F32)
        sigmoid = jax.nn.sigmoid(gate)
        gate_grad = hidden_grad * up * sigmoid * (1.0 + gate * (1.0 - sigmoid))
        up_grad = hidden_grad * gate * sigmoid
        pre_grad = jnp.concatenate([gate_grad, up_grad], axis=1).astype(BF16)
        input_grad = jnp.dot(pre_grad, w_in.T, preferred_element_type=F32).astype(BF16)
        sent_back = exchange(split(input_grad), -1)

        def summed(left, right):
            part = contract(left, right).astype(BF16)
            total = lax.psum_scatter(part, "dp", scatter_dimension=0, tiled=True)
            return total.astype(F32) / groups

        grad_in = summed(token_rows, pre_grad)
        grad_down = summed(grad_rows, hidden)
        mixed_out = call(
            functools.partial(combine_kernel, experts, capacity, True),
            out_shape,
            (first, routes_t, scores_t, *returned),
        )
        token_grad = call(
            functools.partial(combine_kernel, experts, capacity, False),
            out_shape,
            (first, routes_t, *sent_back),
        )
    grad_in = grad_in.reshape(1, share, 2 * units)
    grad_down = grad_down.reshape(1, share, units)
    return (mixed_out, token_grad, grad_in, grad_down)


def solution(mesh):
    in_specs = (
        P(("dp", "expert"), None),
        P(("dp", "expert"), None),
        P(("dp", "expert"), None),
        P(("dp", "expert"), None),
        P("expert", None, None),
        P("expert", None, None),
    )
    out_specs = (
        P(("dp", "expert"), None),
        P(("dp", "expert"), None),
        P("expert", "dp", None),
        P("expert", "dp", None),
    )
    return jax.shard_map(body, mesh=mesh, in_specs=in_specs, out_specs=out_specs, check_vma=False)
```

```python
import functools

import jax
import jax.numpy as jnp
from jax import lax
from jax.experimental import pallas as pl
from jax.experimental.pallas import tpu as pltpu
from jax.sharding import PartitionSpec as P

F32 = jnp.float32
BF16 = jnp.bfloat16
BRIEF = pl.CostEstimate(flops=1024, bytes_accessed=1024, transcendentals=0)
COVER = pl.CostEstimate(flops=10**11, bytes_accessed=10**8, transcendentals=0)
ROOMY = pltpu.CompilerParams(vmem_limit_bytes=16 * 1024 * 1024)
ALONE = pltpu.CompilerParams(vmem_limit_bytes=60 * 1024 * 1024)


def contract(left, right):
    return lax.dot_general(left, right, (((0,), (0,)), ((), ())), preferred_element_type=F32)


def slot_rows(first, routes, experts, capacity):
    tops, toks = routes.shape
    padded = -(-experts // 8) * 8
    rows = lax.broadcasted_iota(jnp.int32, (padded, toks), 0)
    ids = rows + first
    ids = jnp.where(ids >= experts, ids - experts, ids)
    ids = jnp.where(rows < experts, ids, -1)
    hits = [routes[k : k + 1, :] == ids for k in range(tops)]
    named = functools.reduce(jnp.logical_or, hits)
    before = lax.broadcasted_iota(jnp.int32, (toks, toks), 0) < lax.broadcasted_iota(
        jnp.int32, (toks, toks), 1
    )
    position = jnp.dot(
        named.astype(F32).astype(BF16),
        before.astype(F32).astype(BF16),
        preferred_element_type=F32,
    )
    slot = position + (rows * capacity).astype(F32)
    return [jnp.sum(jnp.where(hit, slot, 0.0), axis=0, keepdims=True) for hit in hits]


def weight_rows(scores):
    grown = jnp.exp(scores)
    return grown / jnp.sum(grown, axis=0, keepdims=True)


def to_column(row):
    toks = row.shape[1]
    same = lax.broadcasted_iota(jnp.int32, (toks, toks), 0) == lax.broadcasted_iota(
        jnp.int32, (toks, toks), 1
    )
    return jnp.sum(jnp.where(same, row, 0.0), axis=1, keepdims=True)


def put_blocks(outs, rows, columns):
    start = 0
    for out in outs:
        size = out.shape[0]
        out[:, columns] = rows[start : start + size]
        start += size


def column_steps(width):
    step = 512 if width % 512 == 0 else width
    return [slice(at, at + step) for at in range(0, width, step)]


def dispatch_kernel(experts, capacity, weighted, first, *refs):
    count = 2 + weighted
    sources, outs = refs[:count], refs[count : -count - 1]
    held, sems = refs[-count - 1 : -1], refs[-1]
    copies = [
        pltpu.make_async_copy(source, place, sems.at[n])
        for n, (source, place) in enumerate(zip(sources, held))
    ]
    for copy in copies:
        copy.start()
    routes, values = held[0], held[-1]
    scores = held[1] if weighted else None
    for copy in copies[:-1]:
        copy.wait()
    slots, toks = experts * capacity, values.shape[0]
    places = lax.broadcasted_iota(jnp.int32, (slots, toks), 0).astype(F32)
    hits = [places == row for row in slot_rows(first[0], routes[...], experts, capacity)]
    picker = functools.reduce(jnp.logical_or, hits).astype(F32).astype(BF16)
    if weighted:
        weights = weight_rows(scores[...])
        scale = sum(
            jnp.sum(jnp.where(hit, weights[k : k + 1, :], 0.0), axis=1, keepdims=True)
            for k, hit in enumerate(hits)
        )
    copies[-1].wait()
    for columns in column_steps(values.shape[1]):
        rows = jnp.dot(picker, values[:, columns], preferred_element_type=F32)
        if weighted:
            rows = rows * scale
        put_blocks(outs, rows.astype(BF16), columns)


def combine_kernel(experts, capacity, weighted, first, routes, *refs):
    scores = refs[0] if weighted else None
    blocks, out = refs[weighted:-1], refs[-1]
    slots, toks = experts * capacity, out.shape[0]
    places = lax.broadcasted_iota(jnp.int32, (toks, slots), 1).astype(F32)
    hits = [
        places == to_column(row) for row in slot_rows(first[0], routes[...], experts, capacity)
    ]
    if weighted:
        weights = weight_rows(scores[...])
        scales = [to_column(weights[k : k + 1, :]) for k in range(len(hits))]
        pickers = [hit.astype(F32).astype(BF16) for hit in hits]
    else:
        pickers = [functools.reduce(jnp.logical_or, hits).astype(F32).astype(BF16)]
    for columns in column_steps(out.shape[1]):
        rows = [block[:, columns] for block in blocks]
        rows = rows[0] if len(rows) == 1 else jnp.concatenate(rows, axis=0)
        picked = [jnp.dot(picker, rows, preferred_element_type=F32) for picker in pickers]
        if weighted:
            picked = [scale * part for scale, part in zip(scales, picked)]
        out[:, columns] = sum(picked).astype(out.dtype)


def whole(count):
    return [pl.BlockSpec(memory_space=pltpu.VMEM)] * count


def write_shares(at, rows_t, grads_t, pre_grad, hidden, out):
    share = out.shape[1]
    wide, narrow = pre_grad.shape[1] // 2, hidden.shape[1] // 2

    def write(t, half):
        own = pl.ds(pl.multiple_of(at[t] * share, share), share)
        out[t, :, :wide] = jnp.dot(
            rows_t[own, :],
            pre_grad[:, half * wide : (half + 1) * wide],
            preferred_element_type=F32,
        ).astype(out.dtype)
        out[t, :, wide:] = jnp.dot(
            grads_t[own, :],
            hidden[:, half * narrow : (half + 1) * narrow],
            preferred_element_type=F32,
        ).astype(out.dtype)

    for t in range(out.shape[0]):
        write(t, t // 2 % 2)


def transpose_into(rows, rows_t):
    width = rows.shape[1]
    step = 256 if width % 256 == 0 else width

    @pl.loop(0, width // step)
    def _(c):
        own = pl.ds(pl.multiple_of(c * step, step), step)
        rows_t[own, :] = rows[:, own].T


def join_copies(blocks, rows, sems):
    size = blocks[0].shape[0]
    joins = [
        pltpu.make_async_copy(block, rows.at[pl.ds(n * size, size)], sems.at[n])
        for n, block in enumerate(blocks)
    ]
    for join in joins:
        join.start()
    return joins


def forward_kernel(count, *refs):
    blocks, (w_in_hbm, down_hbm), (rows_t, preact, hidden), outs, scratch = (
        refs[:count],
        refs[count : count + 2],
        refs[count + 2 : count + 5],
        refs[count + 5 : 2 * count + 5],
        refs[2 * count + 5 :],
    )
    rows, w_in, down, block_sems, weight_sems, down_sem = scratch
    joins = join_copies(blocks, rows, block_sems)
    width, units = down.shape
    step = 256 if units % 256 == 0 else units
    loads = []
    for n in range(2 * units // step):
        begin = (n % 2) * units + n // 2 * step
        loads.append(
            pltpu.make_async_copy(
                w_in_hbm.at[:, pl.ds(begin, step)],
                w_in.at[:, pl.ds(begin, step)],
                weight_sems.at[n],
            )
        )
        loads[-1].start()
    load_down = pltpu.make_async_copy(down_hbm, down, down_sem)
    load_down.start()
    for join in joins:
        join.wait()
    for n in range(units // step):
        begin = n * step
        gate_at, up_at = slice(begin, begin + step), slice(units + begin, units + begin + step)
        loads[2 * n].wait()
        gate = jnp.dot(rows[...], w_in[:, gate_at], preferred_element_type=F32)
        loads[2 * n + 1].wait()
        up = jnp.dot(rows[...], w_in[:, up_at], preferred_element_type=F32)
        preact[:, gate_at] = gate
        preact[:, up_at] = up
        hidden[:, gate_at] = (gate / (1.0 + jnp.exp(-gate)) * up).astype(BF16)
    load_down.wait()
    for columns in column_steps(width):
        part = lax.dot_general(
            hidden[...], down[columns, :], (((1,), (1,)), ((), ())), preferred_element_type=F32
        )
        put_blocks(outs, part.astype(BF16), columns)
    transpose_into(rows, rows_t)


def forward(blocks, w_in, down):
    width, units = down.shape
    slots = sum(block.shape[0] for block in blocks)
    count = len(blocks)
    rows_t, preact, hidden, *outs = pl.pallas_call(
        functools.partial(forward_kernel, count),
        out_shape=(
            jax.ShapeDtypeStruct((width, slots), BF16),
            jax.ShapeDtypeStruct((slots, 2 * units), F32),
            jax.ShapeDtypeStruct((slots, units), BF16),
            *[jax.ShapeDtypeStruct(block.shape, BF16) for block in blocks],
        ),
        in_specs=anywhere(count) + in_hbm(2),
        out_specs=whole(3 + count),
        scratch_shapes=[
            pltpu.VMEM((slots, width), BF16),
            pltpu.VMEM(w_in.shape, BF16),
            pltpu.VMEM(down.shape, BF16),
            pltpu.SemaphoreType.DMA((count,)),
            pltpu.SemaphoreType.DMA((2 * units // min(units, 256),)),
            pltpu.SemaphoreType.DMA,
        ],
        compiler_params=pltpu.CompilerParams(vmem_limit_bytes=46 * 1024 * 1024),
        cost_estimate=BRIEF,
    )(*blocks, w_in, down)
    return rows_t, preact, hidden, outs


def backward_kernel(preact_hbm, down, *refs):
    blocks, (pre_grad, grads_t, grads, preact, block_sems, sem) = refs[:-6], refs[-6:]
    fetch = pltpu.make_async_copy(preact_hbm, preact, sem)
    fetch.start()
    joins = join_copies(blocks, grads, block_sems)
    for join in joins:
        join.wait()
    fetch.wait()
    units = down.shape[1]
    step = 256 if units % 256 == 0 else units
    for begin in range(0, units, step):
        gate = preact[:, begin : begin + step]
        up = preact[:, units + begin : units + begin + step]
        hidden_grad = jnp.dot(
            grads[...], down[:, begin : begin + step], preferred_element_type=F32
        )
        sigmoid = 1.0 / (1.0 + jnp.exp(-gate))
        gate_grad = hidden_grad * up * sigmoid * (1.0 + gate * (1.0 - sigmoid))
        up_grad = hidden_grad * gate * sigmoid
        pre_grad[:, begin : begin + step] = gate_grad.astype(BF16)
        pre_grad[:, units + begin : units + begin + step] = up_grad.astype(BF16)
    transpose_into(grads, grads_t)


def anywhere(count):
    return [pl.BlockSpec(memory_space=pl.ANY)] * count


def in_hbm(count):
    return [pl.BlockSpec(memory_space=pltpu.HBM)] * count


def backward(preact, down, blocks):
    width, units = down.shape
    slots = preact.shape[0]
    return pl.pallas_call(
        backward_kernel,
        out_shape=(
            jax.ShapeDtypeStruct((slots, 2 * units), BF16),
            jax.ShapeDtypeStruct((width, slots), BF16),
        ),
        in_specs=anywhere(1) + whole(1) + anywhere(len(blocks)),
        out_specs=whole(2),
        scratch_shapes=[
            pltpu.VMEM((slots, width), BF16),
            pltpu.VMEM((slots, 2 * units), F32),
            pltpu.SemaphoreType.DMA((len(blocks),)),
            pltpu.SemaphoreType.DMA,
        ],
        compiler_params=ROOMY,
        cost_estimate=BRIEF,
    )(preact, down, *blocks)


def shares(at, share, rows_t, grads_t, pre_grad, hidden, cost):
    units = hidden.shape[1]
    return pl.pallas_call(
        write_shares,
        out_shape=jax.ShapeDtypeStruct((at.shape[0], share, 3 * units // 2), BF16),
        in_specs=[pl.BlockSpec(memory_space=pltpu.SMEM)] + whole(4),
        out_specs=whole(1)[0],
        compiler_params=ROOMY,
        cost_estimate=cost,
    )(at, rows_t, grads_t, pre_grad, hidden)


def input_kernel(count, pre_grad, w_in, *refs):
    blocks, outs, sems = refs[:count], refs[count : 2 * count], refs[-1]
    width, size = w_in.shape[0], blocks[0].shape[0]
    copies = [
        pltpu.make_async_copy(block, out.at[pl.ds(0, size)], sems.at[n])
        for n, (block, out) in enumerate(zip(blocks, outs))
        if out.shape[0] > size
    ]
    for copy in copies:
        copy.start()
    for columns in column_steps(width):
        part = lax.dot_general(
            pre_grad[...], w_in[columns, :], (((1,), (1,)), ((), ())), preferred_element_type=F32
        ).astype(BF16)
        for n, out in enumerate(outs):
            out[out.shape[0] - size :, columns] = part[n * size : (n + 1) * size]
    for copy in copies:
        copy.wait()


def input_gradients(pre_grad, w_in, produced, alone):
    count = len(produced)
    size, width = produced[0].shape
    return pl.pallas_call(
        functools.partial(input_kernel, count),
        out_shape=[
            jax.ShapeDtypeStruct((size if n == alone else 2 * size, width), BF16)
            for n in range(count)
        ],
        in_specs=whole(2) + anywhere(count),
        out_specs=whole(count),
        scratch_shapes=[pltpu.SemaphoreType.DMA((count,))],
        compiler_params=ROOMY,
        cost_estimate=BRIEF,
    )(pre_grad, w_in, *produced)


def add_kernel(kept, got, left, right):
    half = left.shape[0]
    left[...] = add(kept[:half], got[:half]).astype(BF16)
    right[...] = add(kept[half:], got[half : 2 * half]).astype(BF16)


def next_kernel(kept, got, left_in, right_in, left_send, right_send):
    first = got.shape[0] // 2
    left_send[...] = (add(kept[1], got[first + 1]) + left_in[1].astype(F32)).astype(BF16)
    right_send[...] = (add(kept[3], got[first + 3]) + right_in[1].astype(F32)).astype(BF16)


def own_kernel(kept, got, left_in, right_in, left, right):
    first = got.shape[0] // 2
    left[...] = add(kept[0], got[first]) + left_in[0].astype(F32)
    right[...] = add(kept[2], got[first + 2]) + right_in[0].astype(F32)


def add(left, right):
    return left.astype(F32) + right.astype(F32)


CUBE_SEND = (3, 7, 5, 7, 1, 5, 1, 3)


def cube_sum(sent, kept_first, kept_later):
    size = lax.axis_size("dp")
    _, share, columns = sent.shape

    def swap(block, bit):
        return lax.ppermute(block, "dp", [(at, at ^ bit) for at in range(size)])

    def run(kernel, out_shape, inputs, cost=BRIEF):
        return pl.pallas_call(
            kernel,
            out_shape=out_shape,
            in_specs=whole(len(inputs)),
            out_specs=whole(len(out_shape)),
            compiler_params=ROOMY,
            cost_estimate=cost,
        )(*inputs)

    half = jax.ShapeDtypeStruct((2, share, columns), BF16)
    one = jax.ShapeDtypeStruct((share, columns), BF16)
    own = jax.ShapeDtypeStruct((share, columns), F32)
    got = swap(sent, 1)
    left, right = run(add_kernel, (half, half), (kept_first, got))
    parts = (kept_later, got, swap(left, 2), swap(right, 4))
    left_send, right_send = run(next_kernel, (one, one), parts)
    left, right = run(own_kernel, (own, own), parts, COVER)
    return left, swap(left_send, 4), right, swap(right_send, 2)


def after(value, *others):
    return lax.optimization_barrier((value, *others))[0]


def partial_kernel(experts, capacity, alone, first, routes, scores, *refs):
    blocks, (mixed, back, pickers, scales) = refs[:-4], refs[-4:]
    slots, toks = experts * capacity, mixed.shape[0]
    places = lax.broadcasted_iota(jnp.int32, (toks, slots), 1).astype(F32)
    hits = [
        places == to_column(row) for row in slot_rows(first[0], routes[...], experts, capacity)
    ]
    weights = weight_rows(scores[...])
    for k, hit in enumerate(hits):
        pickers[k] = hit.astype(F32).astype(BF16)
        scales[k] = jnp.broadcast_to(to_column(weights[k : k + 1, :]), scales.shape[1:])
    pickers[len(hits)] = functools.reduce(jnp.logical_or, hits).astype(F32).astype(BF16)
    outputs = [(0, blocks[0], 0), (alone, blocks[1], 0)]
    gradients = [(0, blocks[0], capacity), (alone, blocks[2], 0)]
    for columns in column_steps(mixed.shape[1]):
        total, grad = sum_blocks(capacity, pickers, scales, outputs, gradients, columns)
        mixed[:, columns] = total
        back[:, columns] = grad


def sum_blocks(capacity, pickers, scales, outputs, gradients, columns):
    tops = scales.shape[0]

    def select(terms, k):
        slots = [slice(n * capacity, (n + 1) * capacity) for n, _, _ in terms]
        picker = jnp.concatenate([pickers[k, :, at] for at in slots], axis=1)
        rows = [block[start : start + capacity, columns] for _, block, start in terms]
        return jnp.dot(picker, jnp.concatenate(rows, axis=0), preferred_element_type=F32)

    total = sum(scales[k, :, :1] * select(outputs, k) for k in range(tops))
    return total, select(gradients, tops)


def mean_kernel(count, left, left_last, right, right_last, wide, narrow):
    middle, edge = wide.shape[1] // 2, narrow.shape[1] // 2
    for at, (own, last) in enumerate(((left, left_last), (right, right_last))):
        total = (own[...] + last[...].astype(F32)) / count
        wide[:, at * middle : (at + 1) * middle] = total[:, :middle]
        narrow[:, at * edge : (at + 1) * edge] = total[:, middle:]


def means(count, sums):
    share, columns = sums[0].shape
    return pl.pallas_call(
        functools.partial(mean_kernel, count),
        out_shape=(
            jax.ShapeDtypeStruct((share, 4 * columns // 3), F32),
            jax.ShapeDtypeStruct((share, 2 * columns // 3), F32),
        ),
        in_specs=whole(4),
        out_specs=whole(2),
        compiler_params=ROOMY,
        cost_estimate=BRIEF,
    )(*sums)


def last_kernel(capacity, places, pickers, scales, mixed_part, back_part, *refs):
    number = len(places)
    sources, (mixed, back), held = refs[:number], refs[number : number + 2], refs[number + 2 :]
    held, (mixed_vmem, back_vmem, in_sems, out_sems) = held[:number], held[number:]
    pieces = column_steps(mixed.shape[1])
    loads = [
        [
            pltpu.make_async_copy(source.at[:, columns], block.at[:, columns], in_sems.at[c, n])
            for n, (source, block) in enumerate(zip(sources, held))
        ]
        for c, columns in enumerate(pieces)
    ]
    for piece in loads:
        for load in piece:
            load.start()
    outputs = [(n, block, 0) for n, block in zip(places, held)]
    gradients = [(n, block, capacity) for n, block in zip(places, held)]
    stores = []
    for c, columns in enumerate(pieces):
        for load in loads[c]:
            load.wait()
        total, grad = sum_blocks(capacity, pickers, scales, outputs, gradients, columns)
        mixed_vmem[:, columns] = (total + mixed_part[:, columns]).astype(BF16)
        back_vmem[:, columns] = (grad + back_part[:, columns]).astype(BF16)
        for n, (source, target) in enumerate(((mixed_vmem, mixed), (back_vmem, back))):
            stores.append(
                pltpu.make_async_copy(
                    source.at[:, columns], target.at[:, columns], out_sems.at[c, n]
                )
            )
            stores[-1].start()
    for stored in stores:
        stored.wait()


def last(capacity, places, parts, blocks):
    toks, width = parts[-1].shape
    out_shape = jax.ShapeDtypeStruct((toks, width), BF16)
    pieces = len(column_steps(width))
    return pl.pallas_call(
        functools.partial(last_kernel, capacity, places),
        out_shape=(out_shape, out_shape),
        in_specs=whole(4) + anywhere(len(blocks)),
        out_specs=anywhere(2),
        scratch_shapes=[pltpu.VMEM(block.shape, BF16) for block in blocks]
        + [pltpu.VMEM((toks, width), BF16)] * 2
        + [
            pltpu.SemaphoreType.DMA((pieces, len(blocks))),
            pltpu.SemaphoreType.DMA((pieces, 2)),
        ],
        compiler_params=ROOMY,
        cost_estimate=BRIEF,
    )(*parts, *blocks)


def dispatch(experts, capacity, out_shape, first, *sources):
    weighted = len(sources) > 2
    return pl.pallas_call(
        functools.partial(dispatch_kernel, experts, capacity, weighted),
        out_shape=out_shape,
        in_specs=[pl.BlockSpec(memory_space=pltpu.SMEM)] + in_hbm(len(sources)),
        out_specs=whole(len(out_shape)),
        scratch_shapes=[pltpu.VMEM(source.shape, source.dtype) for source in sources]
        + [pltpu.SemaphoreType.DMA((len(sources),))],
        compiler_params=ALONE,
        cost_estimate=BRIEF,
    )(first, *sources)


def call(kernel, out_shape, inputs):
    return pl.pallas_call(
        kernel,
        out_shape=out_shape,
        in_specs=[pl.BlockSpec(memory_space=pltpu.SMEM)]
        + [pl.BlockSpec(memory_space=pltpu.VMEM)] * (len(inputs) - 1),
        compiler_params=ROOMY,
        cost_estimate=BRIEF,
    )(*inputs)


def body(tokens, routes, route_scores, out_grad, gate_up, down_weight):
    experts = lax.axis_size("expert")
    groups = lax.axis_size("dp")
    toks, width = tokens.shape
    tops = routes.shape[1]
    units = down_weight.shape[2]
    capacity = (toks * tops + experts - 1) // experts
    slots = experts * capacity
    share = width // groups
    direct = experts <= 8 and capacity % 16 == 0
    w_in, w_out = gate_up[0], down_weight[0]
    routes_t, scores_t = routes.T, route_scores.T
    me = lax.axis_index("expert") if direct else jnp.int32(0)
    first = me.astype(jnp.int32).reshape(1)
    sizes = [capacity] * experts if direct else [slots]
    block_shapes = [jax.ShapeDtypeStruct((size, width), BF16) for size in sizes]

    def travel(block, step, sign):
        pairs = [(at, (at + sign * step) % experts) for at in range(experts)]
        return lax.ppermute(block, "expert", pairs)

    def exchange(blocks, sign):
        if not direct:
            block = blocks[0].reshape(experts, capacity, width)
            moved = lax.all_to_all(block, "expert", split_axis=0, concat_axis=0, tiled=True)
            return [moved.reshape(slots, width)]
        steps = range(1, experts) if sign > 0 else range(experts - 1, 0, -1)
        moved = {step: travel(blocks[step], step, sign) for step in steps}
        return [blocks[0]] + [moved[step] for step in range(1, experts)]

    def joined(blocks):
        return blocks[0] if len(blocks) == 1 else jnp.concatenate(blocks, axis=0)

    def split(rows):
        return [rows[at : at + sizes[0]] for at in range(0, slots, sizes[0])]

    sent_rows = dispatch(experts, capacity, block_shapes, first, routes_t, tokens)
    got_rows = exchange(sent_rows, 1)
    sent_grads = dispatch(experts, capacity, block_shapes, first, routes_t, scores_t, out_grad)
    out_shape = jax.ShapeDtypeStruct((toks, width), BF16)
    cube = direct and experts == 4 and groups == 8 and share % 256 == 0
    if cube:
        sent_grads = after(sent_grads, got_rows[1], got_rows[-1])
        got_grads = exchange(sent_grads, 1)
        rows_t, preact, hidden, produced = forward(got_rows, w_in, w_out)
        got_grads = after(got_grads, hidden)
        own = lax.axis_index("dp")
        send_at = jnp.stack([jnp.bitwise_xor(own, j) for j in CUBE_SEND]).astype(jnp.int32)
        keep_at = jnp.bitwise_xor(send_at, 1)
        early = experts - 1
        early_out = travel(produced[early], early, -1)
        pre_grad, grads_t = backward(preact, w_out, got_grads)
        operands = (share, rows_t, grads_t, pre_grad, hidden)
        sent = shares(send_at, *operands, BRIEF)
        blocks = input_gradients(after(pre_grad, sent), w_in, produced, early)
        returned = exchange(blocks, -1)
        half = len(CUBE_SEND) // 2
        kept_first = shares(after(keep_at[:half], blocks[0]), *operands, COVER)
        kept_later = shares(after(keep_at[half:], kept_first, early_out), *operands, COVER)
        sums = cube_sum(sent, kept_first, kept_later)
        mixed_part, back_part, pickers, scales = call(
            functools.partial(partial_kernel, experts, capacity, early),
            (
                jax.ShapeDtypeStruct((toks, width), F32),
                jax.ShapeDtypeStruct((toks, width), F32),
                jax.ShapeDtypeStruct((tops + 1, toks, slots), BF16),
                jax.ShapeDtypeStruct((tops, toks, 128), F32),
            ),
            (after(first, sums[0]), routes_t, scores_t, returned[0], early_out, returned[early]),
        )
        places = [n for n in range(experts - 1, 0, -1) if n != early]
        grad_in, grad_down = means(groups, sums)
        parts = (after(pickers, grad_in), scales, mixed_part, back_part)
        mixed_out, token_grad = last(capacity, places, parts, [returned[n] for n in places])
    else:
        token_rows = joined(got_rows)
        grad_rows = joined(exchange(sent_grads, 1))
        preact = jnp.dot(token_rows, w_in, preferred_element_type=F32)
        gate, up = preact[:, :units], preact[:, units:]
        hidden = (jax.nn.silu(gate) * up).astype(BF16)
        produced = jnp.dot(hidden, w_out.T, preferred_element_type=F32).astype(BF16)
        returned = exchange(split(produced), -1)
        hidden_grad = jnp.dot(grad_rows, w_out, preferred_element_type=F32)
        sigmoid = jax.nn.sigmoid(gate)
        gate_grad = hidden_grad * up * sigmoid * (1.0 + gate * (1.0 - sigmoid))
        up_grad = hidden_grad * gate * sigmoid
        pre_grad = jnp.concatenate([gate_grad, up_grad], axis=1).astype(BF16)
        input_grad = jnp.dot(pre_grad, w_in.T, preferred_element_type=F32).astype(BF16)
        sent_back = exchange(split(input_grad), -1)

        def summed(left, right):
            part = contract(left, right).astype(BF16)
            total = lax.psum_scatter(part, "dp", scatter_dimension=0, tiled=True)
            return total.astype(F32) / groups

        grad_in = summed(token_rows, pre_grad)
        grad_down = summed(grad_rows, hidden)
        mixed_out = call(
            functools.partial(combine_kernel, experts, capacity, True),
            out_shape,
            (first, routes_t, scores_t, *returned),
        )
        token_grad = call(
            functools.partial(combine_kernel, experts, capacity, False),
            out_shape,
            (first, routes_t, *sent_back),
        )
    grad_in = grad_in.reshape(1, share, 2 * units)
    grad_down = grad_down.reshape(1, share, units)
    return (mixed_out, token_grad, grad_in, grad_down)


def solution(mesh):
    in_specs = (
        P(("dp", "expert"), None),
        P(("dp", "expert"), None),
        P(("dp", "expert"), None),
        P(("dp", "expert"), None),
        P("expert", None, None),
        P("expert", None, None),
    )
    out_specs = (
        P(("dp", "expert"), None),
        P(("dp", "expert"), None),
        P("expert", "dp", None),
        P("expert", "dp", None),
    )
    return jax.shard_map(body, mesh=mesh, in_specs=in_specs, out_specs=out_specs, check_vma=False)
```

```python
import functools

import jax
import jax.numpy as jnp
from jax import lax
from jax.experimental import pallas as pl
from jax.experimental.pallas import tpu as pltpu
from jax.sharding import PartitionSpec as P

F32 = jnp.float32
BF16 = jnp.bfloat16
BRIEF = pl.CostEstimate(flops=1024, bytes_accessed=1024, transcendentals=0)
COVER = pl.CostEstimate(flops=10**11, bytes_accessed=10**8, transcendentals=0)
ROOMY = pltpu.CompilerParams(vmem_limit_bytes=16 * 1024 * 1024)
BIG = pltpu.CompilerParams(vmem_limit_bytes=28 * 1024 * 1024)
ALONE = pltpu.CompilerParams(vmem_limit_bytes=60 * 1024 * 1024)


def contract(left, right):
    return lax.dot_general(left, right, (((0,), (0,)), ((), ())), preferred_element_type=F32)


def slot_rows(first, routes, experts, capacity):
    tops, toks = routes.shape
    padded = -(-experts // 8) * 8
    rows = lax.broadcasted_iota(jnp.int32, (padded, toks), 0)
    ids = rows + first
    ids = jnp.where(ids >= experts, ids - experts, ids)
    ids = jnp.where(rows < experts, ids, -1)
    hits = [routes[k : k + 1, :] == ids for k in range(tops)]
    named = functools.reduce(jnp.logical_or, hits)
    before = lax.broadcasted_iota(jnp.int32, (toks, toks), 0) < lax.broadcasted_iota(
        jnp.int32, (toks, toks), 1
    )
    position = jnp.dot(
        named.astype(F32).astype(BF16),
        before.astype(F32).astype(BF16),
        preferred_element_type=F32,
    )
    slot = position + (rows * capacity).astype(F32)
    return [jnp.sum(jnp.where(hit, slot, 0.0), axis=0, keepdims=True) for hit in hits]


def weight_rows(scores):
    grown = jnp.exp(scores)
    return grown / jnp.sum(grown, axis=0, keepdims=True)


def to_column(row):
    toks = row.shape[1]
    same = lax.broadcasted_iota(jnp.int32, (toks, toks), 0) == lax.broadcasted_iota(
        jnp.int32, (toks, toks), 1
    )
    return jnp.sum(jnp.where(same, row, 0.0), axis=1, keepdims=True)


def put_blocks(outs, rows, columns):
    start = 0
    for out in outs:
        size = out.shape[0]
        out[:, columns] = rows[start : start + size]
        start += size


def column_steps(width):
    step = 512 if width % 512 == 0 else width
    return [slice(at, at + step) for at in range(0, width, step)]


def dispatch_kernel(experts, capacity, weighted, first, *refs):
    count = 2 + weighted
    sources, refs = refs[:count], refs[count:]
    number = (len(refs) - count - 2) // 2
    outs, ready, (*held, sems, out_sems) = refs[:number], refs[number : 2 * number], refs[2 * number :]
    copies = [
        pltpu.make_async_copy(source, place, sems.at[n])
        for n, (source, place) in enumerate(zip(sources, held))
    ]
    for copy in copies:
        copy.start()
    routes, values = held[0], held[-1]
    scores = held[1] if weighted else None
    for copy in copies[:-1]:
        copy.wait()
    slots, toks = experts * capacity, values.shape[0]
    places = lax.broadcasted_iota(jnp.int32, (slots, toks), 0).astype(F32)
    hits = [places == row for row in slot_rows(first[0], routes[...], experts, capacity)]
    picker = functools.reduce(jnp.logical_or, hits).astype(F32).astype(BF16)
    if weighted:
        weights = weight_rows(scores[...])
        scale = sum(
            jnp.sum(jnp.where(hit, weights[k : k + 1, :], 0.0), axis=1, keepdims=True)
            for k, hit in enumerate(hits)
        )
    copies[-1].wait()
    stores = []
    for c, columns in enumerate(column_steps(values.shape[1])):
        rows = jnp.dot(picker, values[:, columns], preferred_element_type=F32)
        if weighted:
            rows = rows * scale
        put_blocks(ready, rows.astype(BF16), columns)
        for n, (block, out) in enumerate(zip(ready, outs)):
            stores.append(
                pltpu.make_async_copy(block.at[:, columns], out.at[:, columns], out_sems.at[c, n])
            )
            stores[-1].start()
    for store in stores:
        store.wait()


def combine_kernel(experts, capacity, weighted, first, routes, *refs):
    scores = refs[0] if weighted else None
    blocks, out = refs[weighted:-1], refs[-1]
    slots, toks = experts * capacity, out.shape[0]
    places = lax.broadcasted_iota(jnp.int32, (toks, slots), 1).astype(F32)
    hits = [
        places == to_column(row) for row in slot_rows(first[0], routes[...], experts, capacity)
    ]
    if weighted:
        weights = weight_rows(scores[...])
        scales = [to_column(weights[k : k + 1, :]) for k in range(len(hits))]
        pickers = [hit.astype(F32).astype(BF16) for hit in hits]
    else:
        pickers = [functools.reduce(jnp.logical_or, hits).astype(F32).astype(BF16)]
    for columns in column_steps(out.shape[1]):
        rows = [block[:, columns] for block in blocks]
        rows = rows[0] if len(rows) == 1 else jnp.concatenate(rows, axis=0)
        picked = [jnp.dot(picker, rows, preferred_element_type=F32) for picker in pickers]
        if weighted:
            picked = [scale * part for scale, part in zip(scales, picked)]
        out[:, columns] = sum(picked).astype(out.dtype)


def whole(count):
    return [pl.BlockSpec(memory_space=pltpu.VMEM)] * count


def write_shares(at, rows_t, grads_t, pre_grad, hidden, out):
    share = out.shape[1]
    wide, narrow = pre_grad.shape[1] // 2, hidden.shape[1] // 2

    def write(t, half):
        own = pl.ds(pl.multiple_of(at[t] * share, share), share)
        out[t, :, :wide] = jnp.dot(
            rows_t[own, :],
            pre_grad[:, half * wide : (half + 1) * wide],
            preferred_element_type=F32,
        ).astype(out.dtype)
        out[t, :, wide:] = jnp.dot(
            grads_t[own, :],
            hidden[:, half * narrow : (half + 1) * narrow],
            preferred_element_type=F32,
        ).astype(out.dtype)

    for t in range(out.shape[0]):
        write(t, t // 2 % 2)


def transpose_into(rows, rows_t):
    width = rows.shape[1]
    step = 256 if width % 256 == 0 else width

    @pl.loop(0, width // step)
    def _(c):
        own = pl.ds(pl.multiple_of(c * step, step), step)
        rows_t[own, :] = rows[:, own].T


def join_copies(blocks, rows, sems):
    size = blocks[0].shape[0]
    joins = [
        pltpu.make_async_copy(block, rows.at[pl.ds(n * size, size)], sems.at[n])
        for n, block in enumerate(blocks)
    ]
    for join in joins:
        join.start()
    return joins


def forward_kernel(count, *refs):
    blocks, (w_in_hbm, down_hbm), (rows_t, preact, hidden), outs, scratch = (
        refs[:count],
        refs[count : count + 2],
        refs[count + 2 : count + 5],
        refs[count + 5 : 2 * count + 5],
        refs[2 * count + 5 :],
    )
    rows, w_in, down, block_sems, weight_sems, down_sem = scratch
    joins = join_copies(blocks, rows, block_sems)
    width, units = down.shape
    step = 256 if units % 256 == 0 else units
    loads = []
    for n in range(2 * units // step):
        begin = (n % 2) * units + n // 2 * step
        loads.append(
            pltpu.make_async_copy(
                w_in_hbm.at[:, pl.ds(begin, step)],
                w_in.at[:, pl.ds(begin, step)],
                weight_sems.at[n],
            )
        )
        loads[-1].start()
    load_down = pltpu.make_async_copy(down_hbm, down, down_sem)
    load_down.start()
    for join in joins:
        join.wait()
    for n in range(units // step):
        begin = n * step
        gate_at, up_at = slice(begin, begin + step), slice(units + begin, units + begin + step)
        loads[2 * n].wait()
        gate = jnp.dot(rows[...], w_in[:, gate_at], preferred_element_type=F32)
        loads[2 * n + 1].wait()
        up = jnp.dot(rows[...], w_in[:, up_at], preferred_element_type=F32)
        preact[:, gate_at] = gate
        preact[:, up_at] = up
        hidden[:, gate_at] = (gate / (1.0 + jnp.exp(-gate)) * up).astype(BF16)
    load_down.wait()
    for columns in column_steps(width):
        part = lax.dot_general(
            hidden[...], down[columns, :], (((1,), (1,)), ((), ())), preferred_element_type=F32
        )
        put_blocks(outs, part.astype(BF16), columns)
    transpose_into(rows, rows_t)


def forward(blocks, w_in, down):
    width, units = down.shape
    slots = sum(block.shape[0] for block in blocks)
    count = len(blocks)
    rows_t, preact, hidden, *outs = pl.pallas_call(
        functools.partial(forward_kernel, count),
        out_shape=(
            jax.ShapeDtypeStruct((width, slots), BF16),
            jax.ShapeDtypeStruct((slots, 2 * units), F32),
            jax.ShapeDtypeStruct((slots, units), BF16),
            *[jax.ShapeDtypeStruct(block.shape, BF16) for block in blocks],
        ),
        in_specs=anywhere(count) + in_hbm(2),
        out_specs=whole(3 + count),
        scratch_shapes=[
            pltpu.VMEM((slots, width), BF16),
            pltpu.VMEM(w_in.shape, BF16),
            pltpu.VMEM(down.shape, BF16),
            pltpu.SemaphoreType.DMA((count,)),
            pltpu.SemaphoreType.DMA((2 * units // min(units, 256),)),
            pltpu.SemaphoreType.DMA,
        ],
        compiler_params=pltpu.CompilerParams(vmem_limit_bytes=46 * 1024 * 1024),
        cost_estimate=BRIEF,
    )(*blocks, w_in, down)
    return rows_t, preact, hidden, outs


def backward_kernel(count, at, preact_hbm, w_in_hbm, rows_t, hidden, down, *refs):
    blocks, (pre_grad, grads_t, sent, w_in, *refs) = refs[:count], refs[count:]
    grads, preact, block_sems, load_sem, sem = refs
    joins = join_copies(blocks, grads, block_sems)
    fetch = pltpu.make_async_copy(preact_hbm, preact, sem)
    fetch.start()
    load = pltpu.make_async_copy(w_in_hbm, w_in, load_sem)
    load.start()
    units = down.shape[1]
    for join in joins:
        join.wait()
    fetch.wait()
    step = 256 if units % 256 == 0 else units
    for begin in range(0, units, step):
        gate = preact[:, begin : begin + step]
        up = preact[:, units + begin : units + begin + step]
        hidden_grad = jnp.dot(
            grads[...], down[:, begin : begin + step], preferred_element_type=F32
        )
        sigmoid = 1.0 / (1.0 + jnp.exp(-gate))
        gate_grad = hidden_grad * up * sigmoid * (1.0 + gate * (1.0 - sigmoid))
        up_grad = hidden_grad * gate * sigmoid
        pre_grad[:, begin : begin + step] = gate_grad.astype(BF16)
        pre_grad[:, units + begin : units + begin + step] = up_grad.astype(BF16)
    transpose_into(grads, grads_t)
    write_shares(at, rows_t, grads_t, pre_grad, hidden, sent)
    load.wait()


def return_kernel(count, alone, pre_grad, w_in, *refs):
    blocks, outs, sems = refs[:count], refs[count : 2 * count], refs[-1]
    size = blocks[0].shape[0]
    copies = [
        pltpu.make_async_copy(block, out.at[pl.ds(0, size)], sems.at[n])
        for n, (block, out) in enumerate(zip(blocks, outs))
        if n != alone
    ]
    for copy in copies:
        copy.start()
    for columns in column_steps(w_in.shape[0]):
        part = lax.dot_general(
            pre_grad[...], w_in[columns, :], (((1,), (1,)), ((), ())), preferred_element_type=F32
        ).astype(BF16)
        for n, out in enumerate(outs):
            out[out.shape[0] - size :, columns] = part[n * size : (n + 1) * size]
    for copy in copies:
        copy.wait()


def returns(pre_grad, w_in, produced, alone):
    count = len(produced)
    size, width = produced[0].shape
    return pl.pallas_call(
        functools.partial(return_kernel, count, alone),
        out_shape=[
            jax.ShapeDtypeStruct((size if n == alone else 2 * size, width), BF16)
            for n in range(count)
        ],
        in_specs=whole(2) + anywhere(count),
        out_specs=whole(count),
        scratch_shapes=[pltpu.SemaphoreType.DMA((count,))],
        compiler_params=ROOMY,
        cost_estimate=BRIEF,
    )(pre_grad, w_in, *produced)


def anywhere(count):
    return [pl.BlockSpec(memory_space=pl.ANY)] * count


def in_hbm(count):
    return [pl.BlockSpec(memory_space=pltpu.HBM)] * count


def backward(at, share, preact, w_in, rows_t, hidden, down, blocks):
    width, units = down.shape
    slots = preact.shape[0]
    count = len(blocks)
    return pl.pallas_call(
        functools.partial(backward_kernel, count),
        out_shape=(
            jax.ShapeDtypeStruct((slots, 2 * units), BF16),
            jax.ShapeDtypeStruct((width, slots), BF16),
            jax.ShapeDtypeStruct((at.shape[0], share, 3 * units // 2), BF16),
            jax.ShapeDtypeStruct(w_in.shape, BF16),
        ),
        in_specs=[pl.BlockSpec(memory_space=pltpu.SMEM)]
        + anywhere(2)
        + whole(3)
        + anywhere(count),
        out_specs=whole(4),
        scratch_shapes=[
            pltpu.VMEM((slots, width), BF16),
            pltpu.VMEM((slots, 2 * units), F32),
            pltpu.SemaphoreType.DMA((count,)),
            pltpu.SemaphoreType.DMA,
            pltpu.SemaphoreType.DMA,
        ],
        compiler_params=BIG,
        cost_estimate=BRIEF,
    )(at, preact, w_in, rows_t, hidden, down, *blocks)


def shares(at, share, rows_t, grads_t, pre_grad, hidden, cost):
    units = hidden.shape[1]
    return pl.pallas_call(
        write_shares,
        out_shape=jax.ShapeDtypeStruct((at.shape[0], share, 3 * units // 2), BF16),
        in_specs=[pl.BlockSpec(memory_space=pltpu.SMEM)] + whole(4),
        out_specs=whole(1)[0],
        compiler_params=ROOMY,
        cost_estimate=cost,
    )(at, rows_t, grads_t, pre_grad, hidden)


def add_kernel(kept, got, left, right):
    half = left.shape[0]
    left[...] = add(kept[:half], got[:half]).astype(BF16)
    right[...] = add(kept[half:], got[half : 2 * half]).astype(BF16)


def next_kernel(kept, got, left_in, right_in, left_send, right_send):
    first = got.shape[0] // 2
    left_send[...] = (add(kept[1], got[first + 1]) + left_in[1].astype(F32)).astype(BF16)
    right_send[...] = (add(kept[3], got[first + 3]) + right_in[1].astype(F32)).astype(BF16)


def own_kernel(kept, got, left_in, right_in, left, right):
    first = got.shape[0] // 2
    left[...] = add(kept[0], got[first]) + left_in[0].astype(F32)
    right[...] = add(kept[2], got[first + 2]) + right_in[0].astype(F32)


def add(left, right):
    return left.astype(F32) + right.astype(F32)


CUBE_SEND = (3, 7, 5, 7, 1, 5, 1, 3)


def swap(block, bit):
    return lax.ppermute(block, "dp", [(at, at ^ bit) for at in range(lax.axis_size("dp"))])


def cube_sum(got, kept_first, kept_later):
    _, share, columns = got.shape

    def run(kernel, out_shape, inputs, cost=BRIEF):
        return pl.pallas_call(
            kernel,
            out_shape=out_shape,
            in_specs=whole(len(inputs)),
            out_specs=whole(len(out_shape)),
            compiler_params=ROOMY,
            cost_estimate=cost,
        )(*inputs)

    half = jax.ShapeDtypeStruct((2, share, columns), BF16)
    one = jax.ShapeDtypeStruct((share, columns), BF16)
    own = jax.ShapeDtypeStruct((share, columns), F32)
    left, right = run(add_kernel, (half, half), (kept_first, got))
    parts = (kept_later, got, swap(left, 2), swap(right, 4))
    left_send, right_send = run(next_kernel, (one, one), parts)
    left, right = run(own_kernel, (own, own), parts, COVER)
    return left, swap(left_send, 4), right, swap(right_send, 2)


def after(value, *others):
    return lax.optimization_barrier((value, *others))[0]


def partial_kernel(experts, capacity, alone, late, first, routes, scores, *refs):
    (own, early, back_early), (mixed, back, late_picker, scales) = refs[:-4], refs[-4:]
    slots, toks = experts * capacity, mixed.shape[0]
    places = lax.broadcasted_iota(jnp.int32, (toks, slots), 1).astype(F32)
    hits = [
        places == to_column(row) for row in slot_rows(first[0], routes[...], experts, capacity)
    ]
    hits.append(functools.reduce(jnp.logical_or, hits))
    picker = jnp.concatenate([hit.astype(F32).astype(BF16) for hit in hits], axis=0)
    weights = weight_rows(scores[...])
    for k in range(scales.shape[0]):
        scales[k] = jnp.broadcast_to(to_column(weights[k : k + 1, :]), scales.shape[1:])

    def slots_of(blocks):
        parts = [picker[:, n * capacity : (n + 1) * capacity] for n in blocks]
        return jnp.concatenate(parts, axis=1)

    late_picker[...] = slots_of(late)
    now = slots_of((0, alone))
    for columns in column_steps(mixed.shape[1]):
        outputs = jnp.concatenate([own[:capacity, columns], early[:, columns]], axis=0)
        gradients = jnp.concatenate([own[capacity:, columns], back_early[:, columns]], axis=0)
        total, grad = sum_rows(now, scales, outputs, gradients)
        mixed[:, columns] = total
        back[:, columns] = grad


def sum_rows(picker, scales, outputs, gradients):
    tops, toks = scales.shape[:2]
    picked = jnp.dot(picker[: tops * toks], outputs, preferred_element_type=F32)
    total = sum(scales[k, :, :1] * picked[k * toks : (k + 1) * toks] for k in range(tops))
    return total, jnp.dot(picker[tops * toks :], gradients, preferred_element_type=F32)


def mean_kernel(count, left, left_last, right, right_last, wide, narrow):
    middle, edge = wide.shape[1] // 2, narrow.shape[1] // 2
    for at, (own, last) in enumerate(((left, left_last), (right, right_last))):
        total = (own[...] + last[...].astype(F32)) / count
        wide[:, at * middle : (at + 1) * middle] = total[:, :middle]
        narrow[:, at * edge : (at + 1) * edge] = total[:, middle:]


def means(count, sums):
    share, columns = sums[0].shape
    return pl.pallas_call(
        functools.partial(mean_kernel, count),
        out_shape=(
            jax.ShapeDtypeStruct((share, 4 * columns // 3), F32),
            jax.ShapeDtypeStruct((share, 2 * columns // 3), F32),
        ),
        in_specs=whole(4),
        out_specs=whole(2),
        compiler_params=ROOMY,
        cost_estimate=BRIEF,
    )(*sums)


def last_kernel(capacity, number, picker, scales, mixed_part, back_part, *refs):
    sources, (mixed, back), refs = refs[:number], refs[number : number + 2], refs[number + 2 :]
    outputs, gradients, mixed_vmem, back_vmem, in_sems, out_sems = refs
    pieces = column_steps(mixed.shape[1])
    loads = [
        [
            pltpu.make_async_copy(
                source.at[pl.ds(half * capacity, capacity), columns],
                held.at[pl.ds(n * capacity, capacity), columns],
                in_sems.at[c, 2 * n + half],
            )
            for n, source in enumerate(sources)
            for half, held in enumerate((outputs, gradients))
        ]
        for c, columns in enumerate(pieces)
    ]
    for piece in loads:
        for load in piece:
            load.start()
    stores = []
    for c, columns in enumerate(pieces):
        for load in loads[c]:
            load.wait()
        total, grad = sum_rows(picker[...], scales, outputs[:, columns], gradients[:, columns])
        mixed_vmem[:, columns] = (total + mixed_part[:, columns]).astype(BF16)
        back_vmem[:, columns] = (grad + back_part[:, columns]).astype(BF16)
        for n, (source, target) in enumerate(((mixed_vmem, mixed), (back_vmem, back))):
            stores.append(
                pltpu.make_async_copy(
                    source.at[:, columns], target.at[:, columns], out_sems.at[c, n]
                )
            )
            stores[-1].start()
    for stored in stores:
        stored.wait()


def last(capacity, parts, blocks):
    toks, width = parts[-1].shape
    out_shape = jax.ShapeDtypeStruct((toks, width), BF16)
    pieces = len(column_steps(width))
    return pl.pallas_call(
        functools.partial(last_kernel, capacity, len(blocks)),
        out_shape=(out_shape, out_shape),
        in_specs=whole(4) + anywhere(len(blocks)),
        out_specs=anywhere(2),
        scratch_shapes=[pltpu.VMEM((len(blocks) * capacity, width), BF16)] * 2
        + [pltpu.VMEM((toks, width), BF16)] * 2
        + [
            pltpu.SemaphoreType.DMA((pieces, 2 * len(blocks))),
            pltpu.SemaphoreType.DMA((pieces, 2)),
        ],
        compiler_params=ROOMY,
        cost_estimate=BRIEF,
    )(*parts, *blocks)


def dispatch(experts, capacity, out_shape, first, *sources):
    weighted = len(sources) > 2
    return pl.pallas_call(
        functools.partial(dispatch_kernel, experts, capacity, weighted),
        out_shape=out_shape,
        in_specs=[pl.BlockSpec(memory_space=pltpu.SMEM)] + in_hbm(len(sources)),
        out_specs=anywhere(len(out_shape)),
        scratch_shapes=[pltpu.VMEM(out.shape, out.dtype) for out in out_shape]
        + [pltpu.VMEM(source.shape, source.dtype) for source in sources]
        + [
            pltpu.SemaphoreType.DMA((len(sources),)),
            pltpu.SemaphoreType.DMA((len(column_steps(out_shape[0].shape[1])), len(out_shape))),
        ],
        compiler_params=ALONE,
        cost_estimate=BRIEF,
    )(first, *sources)


def call(kernel, out_shape, inputs):
    return pl.pallas_call(
        kernel,
        out_shape=out_shape,
        in_specs=[pl.BlockSpec(memory_space=pltpu.SMEM)]
        + [pl.BlockSpec(memory_space=pltpu.VMEM)] * (len(inputs) - 1),
        compiler_params=ROOMY,
        cost_estimate=BRIEF,
    )(*inputs)


def body(tokens, routes, route_scores, out_grad, gate_up, down_weight):
    experts = lax.axis_size("expert")
    groups = lax.axis_size("dp")
    toks, width = tokens.shape
    tops = routes.shape[1]
    units = down_weight.shape[2]
    capacity = (toks * tops + experts - 1) // experts
    slots = experts * capacity
    share = width // groups
    direct = experts <= 8 and capacity % 16 == 0
    w_in, w_out = gate_up[0], down_weight[0]
    routes_t, scores_t = routes.T, route_scores.T
    me = lax.axis_index("expert") if direct else jnp.int32(0)
    first = me.astype(jnp.int32).reshape(1)
    sizes = [capacity] * experts if direct else [slots]
    block_shapes = [jax.ShapeDtypeStruct((size, width), BF16) for size in sizes]

    def travel(block, step, sign):
        pairs = [(at, (at + sign * step) % experts) for at in range(experts)]
        return lax.ppermute(block, "expert", pairs)

    def exchange(blocks, sign):
        if not direct:
            block = blocks[0].reshape(experts, capacity, width)
            moved = lax.all_to_all(block, "expert", split_axis=0, concat_axis=0, tiled=True)
            return [moved.reshape(slots, width)]
        steps = range(1, experts) if sign > 0 else range(experts - 1, 0, -1)
        moved = {step: travel(blocks[step], step, sign) for step in steps}
        return [blocks[0]] + [moved[step] for step in range(1, experts)]

    def joined(blocks):
        return blocks[0] if len(blocks) == 1 else jnp.concatenate(blocks, axis=0)

    def split(rows):
        return [rows[at : at + sizes[0]] for at in range(0, slots, sizes[0])]

    sent_rows = dispatch(experts, capacity, block_shapes, first, routes_t, tokens)
    got_rows = exchange(sent_rows, 1)
    sent_grads = dispatch(experts, capacity, block_shapes, first, routes_t, scores_t, out_grad)
    out_shape = jax.ShapeDtypeStruct((toks, width), BF16)
    cube = direct and experts == 4 and groups == 8 and share % 256 == 0
    if cube:
        sent_grads = after(sent_grads, got_rows[1], got_rows[-1])
        got_grads = exchange(sent_grads, 1)
        rows_t, preact, hidden, produced = forward(got_rows, w_in, w_out)
        got_grads = after(got_grads, hidden)
        own = lax.axis_index("dp")
        send_at = jnp.stack([jnp.bitwise_xor(own, j) for j in CUBE_SEND]).astype(jnp.int32)
        keep_at = jnp.bitwise_xor(send_at, 1)
        early = experts - 1
        early_out = travel(produced[early], early, -1)
        pre_grad, grads_t, sent, w_in_here = backward(
            send_at, share, preact, w_in, rows_t, hidden, w_out, got_grads
        )
        operands = (share, rows_t, grads_t, pre_grad, hidden)
        got = swap(sent, 1)
        blocks = returns(after(pre_grad, sent), w_in_here, produced, early)
        returned = exchange(blocks, -1)
        half = len(CUBE_SEND) // 2
        kept_first = shares(after(keep_at[:half], blocks[0]), *operands, COVER)
        kept_later = shares(after(keep_at[half:], kept_first, early_out, got), *operands, COVER)
        sums = cube_sum(got, kept_first, kept_later)
        late = [n for n in range(experts - 1, 0, -1) if n != early]
        mixed_part, back_part, picker, scales = call(
            functools.partial(partial_kernel, experts, capacity, early, late),
            (
                jax.ShapeDtypeStruct((toks, width), F32),
                jax.ShapeDtypeStruct((toks, width), F32),
                jax.ShapeDtypeStruct(((tops + 1) * toks, len(late) * capacity), BF16),
                jax.ShapeDtypeStruct((tops, toks, 128), F32),
            ),
            (after(first, sums[0]), routes_t, scores_t, returned[0], early_out, returned[early]),
        )
        grad_in, grad_down = means(groups, sums)
        parts = (after(picker, grad_in), scales, mixed_part, back_part)
        mixed_out, token_grad = last(capacity, parts, [returned[n] for n in late])
    else:
        token_rows = joined(got_rows)
        grad_rows = joined(exchange(sent_grads, 1))
        preact = jnp.dot(token_rows, w_in, preferred_element_type=F32)
        gate, up = preact[:, :units], preact[:, units:]
        hidden = (jax.nn.silu(gate) * up).astype(BF16)
        produced = jnp.dot(hidden, w_out.T, preferred_element_type=F32).astype(BF16)
        returned = exchange(split(produced), -1)
        hidden_grad = jnp.dot(grad_rows, w_out, preferred_element_type=F32)
        sigmoid = jax.nn.sigmoid(gate)
        gate_grad = hidden_grad * up * sigmoid * (1.0 + gate * (1.0 - sigmoid))
        up_grad = hidden_grad * gate * sigmoid
        pre_grad = jnp.concatenate([gate_grad, up_grad], axis=1).astype(BF16)
        input_grad = jnp.dot(pre_grad, w_in.T, preferred_element_type=F32).astype(BF16)
        sent_back = exchange(split(input_grad), -1)

        def summed(left, right):
            part = contract(left, right).astype(BF16)
            total = lax.psum_scatter(part, "dp", scatter_dimension=0, tiled=True)
            return total.astype(F32) / groups

        grad_in = summed(token_rows, pre_grad)
        grad_down = summed(grad_rows, hidden)
        mixed_out = call(
            functools.partial(combine_kernel, experts, capacity, True),
            out_shape,
            (first, routes_t, scores_t, *returned),
        )
        token_grad = call(
            functools.partial(combine_kernel, experts, capacity, False),
            out_shape,
            (first, routes_t, *sent_back),
        )
    grad_in = grad_in.reshape(1, share, 2 * units)
    grad_down = grad_down.reshape(1, share, units)
    return (mixed_out, token_grad, grad_in, grad_down)


def solution(mesh):
    in_specs = (
        P(("dp", "expert"), None),
        P(("dp", "expert"), None),
        P(("dp", "expert"), None),
        P(("dp", "expert"), None),
        P("expert", None, None),
        P("expert", None, None),
    )
    out_specs = (
        P(("dp", "expert"), None),
        P(("dp", "expert"), None),
        P("expert", "dp", None),
        P("expert", "dp", None),
    )
    return jax.shard_map(body, mesh=mesh, in_specs=in_specs, out_specs=out_specs, check_vma=False)
```

```python
import functools

import jax
import jax.numpy as jnp
from jax import lax
from jax.experimental import pallas as pl
from jax.experimental.pallas import tpu as pltpu
from jax.sharding import PartitionSpec as P

F32 = jnp.float32
BF16 = jnp.bfloat16
BRIEF = pl.CostEstimate(flops=1024, bytes_accessed=1024, transcendentals=0)
COVER = pl.CostEstimate(flops=4 * 10**10, bytes_accessed=1024, transcendentals=0)
ROOMY = pltpu.CompilerParams(vmem_limit_bytes=16 * 1024 * 1024)
BIG = pltpu.CompilerParams(vmem_limit_bytes=28 * 1024 * 1024)
ALONE = pltpu.CompilerParams(vmem_limit_bytes=60 * 1024 * 1024)


def contract(left, right):
    return lax.dot_general(left, right, (((0,), (0,)), ((), ())), preferred_element_type=F32)


def slot_rows(first, routes, experts, capacity):
    tops, toks = routes.shape
    padded = -(-experts // 8) * 8
    rows = lax.broadcasted_iota(jnp.int32, (padded, toks), 0)
    ids = rows + first
    ids = jnp.where(ids >= experts, ids - experts, ids)
    ids = jnp.where(rows < experts, ids, -1)
    hits = [routes[k : k + 1, :] == ids for k in range(tops)]
    named = functools.reduce(jnp.logical_or, hits)
    before = lax.broadcasted_iota(jnp.int32, (toks, toks), 0) < lax.broadcasted_iota(
        jnp.int32, (toks, toks), 1
    )
    position = jnp.dot(
        named.astype(F32).astype(BF16),
        before.astype(F32).astype(BF16),
        preferred_element_type=F32,
    )
    slot = position + (rows * capacity).astype(F32)
    return [jnp.sum(jnp.where(hit, slot, 0.0), axis=0, keepdims=True) for hit in hits]


def weight_rows(scores):
    grown = jnp.exp(scores)
    return grown / jnp.sum(grown, axis=0, keepdims=True)


def to_column(row):
    toks = row.shape[1]
    same = lax.broadcasted_iota(jnp.int32, (toks, toks), 0) == lax.broadcasted_iota(
        jnp.int32, (toks, toks), 1
    )
    return jnp.sum(jnp.where(same, row, 0.0), axis=1, keepdims=True)


def put_blocks(outs, rows, columns):
    start = 0
    for out in outs:
        size = out.shape[0]
        out[:, columns] = rows[start : start + size]
        start += size


def column_steps(width):
    step = 512 if width % 512 == 0 else width
    return [slice(at, at + step) for at in range(0, width, step)]


def dispatch_kernel(experts, capacity, weighted, first, *refs):
    count = 2 + weighted
    sources, refs = refs[:count], refs[count:]
    number = (len(refs) - count - 2) // 2
    outs, ready, (*held, sems, out_sems) = refs[:number], refs[number : 2 * number], refs[2 * number :]
    copies = [
        pltpu.make_async_copy(source, place, sems.at[n])
        for n, (source, place) in enumerate(zip(sources, held))
    ]
    for copy in copies:
        copy.start()
    routes, values = held[0], held[-1]
    scores = held[1] if weighted else None
    for copy in copies[:-1]:
        copy.wait()
    slots, toks = experts * capacity, values.shape[0]
    places = lax.broadcasted_iota(jnp.int32, (slots, toks), 0).astype(F32)
    hits = [places == row for row in slot_rows(first[0], routes[...], experts, capacity)]
    picker = functools.reduce(jnp.logical_or, hits).astype(F32).astype(BF16)
    if weighted:
        weights = weight_rows(scores[...])
        scale = sum(
            jnp.sum(jnp.where(hit, weights[k : k + 1, :], 0.0), axis=1, keepdims=True)
            for k, hit in enumerate(hits)
        )
    copies[-1].wait()
    stores = []
    for c, columns in enumerate(column_steps(values.shape[1])):
        rows = jnp.dot(picker, values[:, columns], preferred_element_type=F32)
        if weighted:
            rows = rows * scale
        put_blocks(ready, rows.astype(BF16), columns)
        for n, (block, out) in enumerate(zip(ready, outs)):
            stores.append(
                pltpu.make_async_copy(block.at[:, columns], out.at[:, columns], out_sems.at[c, n])
            )
            stores[-1].start()
    for store in stores:
        store.wait()


def combine_kernel(experts, capacity, weighted, first, routes, *refs):
    scores = refs[0] if weighted else None
    blocks, out = refs[weighted:-1], refs[-1]
    slots, toks = experts * capacity, out.shape[0]
    places = lax.broadcasted_iota(jnp.int32, (toks, slots), 1).astype(F32)
    hits = [
        places == to_column(row) for row in slot_rows(first[0], routes[...], experts, capacity)
    ]
    if weighted:
        weights = weight_rows(scores[...])
        scales = [to_column(weights[k : k + 1, :]) for k in range(len(hits))]
        pickers = [hit.astype(F32).astype(BF16) for hit in hits]
    else:
        pickers = [functools.reduce(jnp.logical_or, hits).astype(F32).astype(BF16)]
    for columns in column_steps(out.shape[1]):
        rows = [block[:, columns] for block in blocks]
        rows = rows[0] if len(rows) == 1 else jnp.concatenate(rows, axis=0)
        picked = [jnp.dot(picker, rows, preferred_element_type=F32) for picker in pickers]
        if weighted:
            picked = [scale * part for scale, part in zip(scales, picked)]
        out[:, columns] = sum(picked).astype(out.dtype)


def whole(count):
    return [pl.BlockSpec(memory_space=pltpu.VMEM)] * count


def write_shares(at, rows_t, grads_t, pre_grad, hidden, out):
    share = out.shape[1]
    wide, narrow = pre_grad.shape[1] // 2, hidden.shape[1] // 2

    def write(t, half):
        own = pl.ds(pl.multiple_of(at[t] * share, share), share)
        out[t, :, :wide] = jnp.dot(
            rows_t[own, :],
            pre_grad[:, half * wide : (half + 1) * wide],
            preferred_element_type=F32,
        ).astype(out.dtype)
        out[t, :, wide:] = jnp.dot(
            grads_t[own, :],
            hidden[:, half * narrow : (half + 1) * narrow],
            preferred_element_type=F32,
        ).astype(out.dtype)

    for t in range(out.shape[0]):
        write(t, t // 2 % 2)


def transpose_into(rows, rows_t):
    width = rows.shape[1]
    step = 256 if width % 256 == 0 else width

    @pl.loop(0, width // step)
    def _(c):
        own = pl.ds(pl.multiple_of(c * step, step), step)
        rows_t[own, :] = rows[:, own].T


def join_copies(blocks, rows, sems):
    size = blocks[0].shape[0]
    joins = [
        pltpu.make_async_copy(block, rows.at[pl.ds(n * size, size)], sems.at[n])
        for n, block in enumerate(blocks)
    ]
    for join in joins:
        join.start()
    return joins


def forward_kernel(count, *refs):
    blocks, (w_in_hbm, down_hbm), (rows_t, preact, hidden), outs, scratch = (
        refs[:count],
        refs[count : count + 2],
        refs[count + 2 : count + 5],
        refs[count + 5 : 2 * count + 5],
        refs[2 * count + 5 :],
    )
    rows, w_in, down, block_sems, weight_sems, down_sem = scratch
    joins = join_copies(blocks, rows, block_sems)
    width, units = down.shape
    step = 256 if units % 256 == 0 else units
    loads = []
    for n in range(2 * units // step):
        begin = (n % 2) * units + n // 2 * step
        loads.append(
            pltpu.make_async_copy(
                w_in_hbm.at[:, pl.ds(begin, step)],
                w_in.at[:, pl.ds(begin, step)],
                weight_sems.at[n],
            )
        )
        loads[-1].start()
    load_down = pltpu.make_async_copy(down_hbm, down, down_sem)
    load_down.start()
    for join in joins:
        join.wait()
    for n in range(units // step):
        begin = n * step
        gate_at, up_at = slice(begin, begin + step), slice(units + begin, units + begin + step)
        loads[2 * n].wait()
        gate = jnp.dot(rows[...], w_in[:, gate_at], preferred_element_type=F32)
        loads[2 * n + 1].wait()
        up = jnp.dot(rows[...], w_in[:, up_at], preferred_element_type=F32)
        preact[:, gate_at] = gate
        preact[:, up_at] = up
        hidden[:, gate_at] = (gate / (1.0 + jnp.exp(-gate)) * up).astype(BF16)
    load_down.wait()
    for columns in column_steps(width):
        part = lax.dot_general(
            hidden[...], down[columns, :], (((1,), (1,)), ((), ())), preferred_element_type=F32
        )
        put_blocks(outs, part.astype(BF16), columns)
    transpose_into(rows, rows_t)


def forward(blocks, w_in, down):
    width, units = down.shape
    slots = sum(block.shape[0] for block in blocks)
    count = len(blocks)
    rows_t, preact, hidden, *outs = pl.pallas_call(
        functools.partial(forward_kernel, count),
        out_shape=(
            jax.ShapeDtypeStruct((width, slots), BF16),
            jax.ShapeDtypeStruct((slots, 2 * units), F32),
            jax.ShapeDtypeStruct((slots, units), BF16),
            *[jax.ShapeDtypeStruct(block.shape, BF16) for block in blocks],
        ),
        in_specs=anywhere(count) + in_hbm(2),
        out_specs=whole(3 + count),
        scratch_shapes=[
            pltpu.VMEM((slots, width), BF16),
            pltpu.VMEM(w_in.shape, BF16),
            pltpu.VMEM(down.shape, BF16),
            pltpu.SemaphoreType.DMA((count,)),
            pltpu.SemaphoreType.DMA((2 * units // min(units, 256),)),
            pltpu.SemaphoreType.DMA,
        ],
        compiler_params=pltpu.CompilerParams(vmem_limit_bytes=46 * 1024 * 1024),
        cost_estimate=BRIEF,
    )(*blocks, w_in, down)
    return rows_t, preact, hidden, outs


def backward_kernel(count, at, preact_hbm, w_in_hbm, rows_t, hidden, down, *refs):
    blocks, (pre_grad, grads_t, sent, w_in, *refs) = refs[:count], refs[count:]
    grads, preact, block_sems, load_sem, sem = refs
    joins = join_copies(blocks, grads, block_sems)
    fetch = pltpu.make_async_copy(preact_hbm, preact, sem)
    fetch.start()
    load = pltpu.make_async_copy(w_in_hbm, w_in, load_sem)
    load.start()
    units = down.shape[1]
    for join in joins:
        join.wait()
    fetch.wait()
    step = 256 if units % 256 == 0 else units
    for begin in range(0, units, step):
        gate = preact[:, begin : begin + step]
        up = preact[:, units + begin : units + begin + step]
        hidden_grad = jnp.dot(
            grads[...], down[:, begin : begin + step], preferred_element_type=F32
        )
        sigmoid = 1.0 / (1.0 + jnp.exp(-gate))
        gate_grad = hidden_grad * up * sigmoid * (1.0 + gate * (1.0 - sigmoid))
        up_grad = hidden_grad * gate * sigmoid
        pre_grad[:, begin : begin + step] = gate_grad.astype(BF16)
        pre_grad[:, units + begin : units + begin + step] = up_grad.astype(BF16)
    transpose_into(grads, grads_t)
    write_shares(at, rows_t, grads_t, pre_grad, hidden, sent)
    load.wait()


def return_kernel(count, alone, pre_grad, w_in, *refs):
    blocks, outs, sems = refs[:count], refs[count : 2 * count], refs[-1]
    size = blocks[0].shape[0]
    copies = [
        pltpu.make_async_copy(block, out.at[pl.ds(0, size)], sems.at[n])
        for n, (block, out) in enumerate(zip(blocks, outs))
        if n != alone
    ]
    for copy in copies:
        copy.start()
    for columns in column_steps(w_in.shape[0]):
        part = lax.dot_general(
            pre_grad[...], w_in[columns, :], (((1,), (1,)), ((), ())), preferred_element_type=F32
        ).astype(BF16)
        for n, out in enumerate(outs):
            out[out.shape[0] - size :, columns] = part[n * size : (n + 1) * size]
    for copy in copies:
        copy.wait()


def returns(pre_grad, w_in, produced, alone):
    count = len(produced)
    size, width = produced[0].shape
    return pl.pallas_call(
        functools.partial(return_kernel, count, alone),
        out_shape=[
            jax.ShapeDtypeStruct((size if n == alone else 2 * size, width), BF16)
            for n in range(count)
        ],
        in_specs=whole(2) + anywhere(count),
        out_specs=whole(count),
        scratch_shapes=[pltpu.SemaphoreType.DMA((count,))],
        compiler_params=ROOMY,
        cost_estimate=BRIEF,
    )(pre_grad, w_in, *produced)


def anywhere(count):
    return [pl.BlockSpec(memory_space=pl.ANY)] * count


def in_hbm(count):
    return [pl.BlockSpec(memory_space=pltpu.HBM)] * count


def backward(at, share, preact, w_in, rows_t, hidden, down, blocks):
    width, units = down.shape
    slots = preact.shape[0]
    count = len(blocks)
    return pl.pallas_call(
        functools.partial(backward_kernel, count),
        out_shape=(
            jax.ShapeDtypeStruct((slots, 2 * units), BF16),
            jax.ShapeDtypeStruct((width, slots), BF16),
            jax.ShapeDtypeStruct((at.shape[0], share, 3 * units // 2), BF16),
            jax.ShapeDtypeStruct(w_in.shape, BF16),
        ),
        in_specs=[pl.BlockSpec(memory_space=pltpu.SMEM)]
        + anywhere(2)
        + whole(3)
        + anywhere(count),
        out_specs=whole(4),
        scratch_shapes=[
            pltpu.VMEM((slots, width), BF16),
            pltpu.VMEM((slots, 2 * units), F32),
            pltpu.SemaphoreType.DMA((count,)),
            pltpu.SemaphoreType.DMA,
            pltpu.SemaphoreType.DMA,
        ],
        compiler_params=BIG,
        cost_estimate=BRIEF,
    )(at, preact, w_in, rows_t, hidden, down, *blocks)


def shares(at, share, rows_t, grads_t, pre_grad, hidden, cost):
    units = hidden.shape[1]
    return pl.pallas_call(
        write_shares,
        out_shape=jax.ShapeDtypeStruct((at.shape[0], share, 3 * units // 2), BF16),
        in_specs=[pl.BlockSpec(memory_space=pltpu.SMEM)] + whole(4),
        out_specs=whole(1)[0],
        compiler_params=ROOMY,
        cost_estimate=cost,
    )(at, rows_t, grads_t, pre_grad, hidden)


def add_kernel(kept, got, left, right):
    half = left.shape[0]
    left[...] = add(kept[:half], got[:half]).astype(BF16)
    right[...] = add(kept[half:], got[half : 2 * half]).astype(BF16)


def next_kernel(kept, got, left_in, right_in, left_send, right_send):
    first = got.shape[0] // 2
    left_send[...] = (add(kept[1], got[first + 1]) + left_in[1].astype(F32)).astype(BF16)
    right_send[...] = (add(kept[3], got[first + 3]) + right_in[1].astype(F32)).astype(BF16)


def own_kernel(kept, got, left_in, right_in, left, right):
    first = got.shape[0] // 2
    left[...] = add(kept[0], got[first]) + left_in[0].astype(F32)
    right[...] = add(kept[2], got[first + 2]) + right_in[0].astype(F32)


def add(left, right):
    return left.astype(F32) + right.astype(F32)


CUBE_SEND = (3, 7, 5, 7, 1, 5, 1, 3)


def swap(block, bit):
    return lax.ppermute(block, "dp", [(at, at ^ bit) for at in range(lax.axis_size("dp"))])


def cube_sum(got, kept_first, kept_later):
    _, share, columns = got.shape

    def run(kernel, out_shape, inputs, cost=BRIEF):
        return pl.pallas_call(
            kernel,
            out_shape=out_shape,
            in_specs=whole(len(inputs)),
            out_specs=whole(len(out_shape)),
            compiler_params=ROOMY,
            cost_estimate=cost,
        )(*inputs)

    half = jax.ShapeDtypeStruct((2, share, columns), BF16)
    one = jax.ShapeDtypeStruct((share, columns), BF16)
    own = jax.ShapeDtypeStruct((share, columns), F32)
    left, right = run(add_kernel, (half, half), (kept_first, got))
    parts = (kept_later, got, swap(left, 2), swap(right, 4))
    left_send, right_send = run(next_kernel, (one, one), parts)
    left, right = run(own_kernel, (own, own), parts, COVER)
    return left, swap(left_send, 4), right, swap(right_send, 2)


def after(value, *others):
    return lax.optimization_barrier((value, *others))[0]


def partial_kernel(experts, capacity, alone, late, first, routes, scores, *refs):
    (own, early, back_early), (mixed, back, late_picker, scales) = refs[:-4], refs[-4:]
    slots, toks = experts * capacity, mixed.shape[0]
    places = lax.broadcasted_iota(jnp.int32, (toks, slots), 1).astype(F32)
    hits = [
        places == to_column(row) for row in slot_rows(first[0], routes[...], experts, capacity)
    ]
    hits.append(functools.reduce(jnp.logical_or, hits))
    picker = jnp.concatenate([hit.astype(F32).astype(BF16) for hit in hits], axis=0)
    weights = weight_rows(scores[...])
    for k in range(scales.shape[0]):
        scales[k] = jnp.broadcast_to(to_column(weights[k : k + 1, :]), scales.shape[1:])

    def slots_of(blocks):
        parts = [picker[:, n * capacity : (n + 1) * capacity] for n in blocks]
        return jnp.concatenate(parts, axis=1)

    late_picker[...] = slots_of(late)
    now = slots_of((0, alone))
    for columns in column_steps(mixed.shape[1]):
        outputs = jnp.concatenate([own[:capacity, columns], early[:, columns]], axis=0)
        gradients = jnp.concatenate([own[capacity:, columns], back_early[:, columns]], axis=0)
        total, grad = sum_rows(now, scales, outputs, gradients)
        mixed[:, columns] = total
        back[:, columns] = grad


def sum_rows(picker, scales, outputs, gradients):
    tops, toks = scales.shape[:2]
    picked = jnp.dot(picker[: tops * toks], outputs, preferred_element_type=F32)
    total = sum(scales[k, :, :1] * picked[k * toks : (k + 1) * toks] for k in range(tops))
    return total, jnp.dot(picker[tops * toks :], gradients, preferred_element_type=F32)


def mean_kernel(count, left, left_last, right, right_last, wide, narrow):
    middle, edge = wide.shape[1] // 2, narrow.shape[1] // 2
    for at, (own, last) in enumerate(((left, left_last), (right, right_last))):
        total = (own[...] + last[...].astype(F32)) / count
        wide[:, at * middle : (at + 1) * middle] = total[:, :middle]
        narrow[:, at * edge : (at + 1) * edge] = total[:, middle:]


def means(count, sums):
    share, columns = sums[0].shape
    return pl.pallas_call(
        functools.partial(mean_kernel, count),
        out_shape=(
            jax.ShapeDtypeStruct((share, 4 * columns // 3), F32),
            jax.ShapeDtypeStruct((share, 2 * columns // 3), F32),
        ),
        in_specs=whole(4),
        out_specs=whole(2),
        compiler_params=ROOMY,
        cost_estimate=BRIEF,
    )(*sums)


def last_kernel(capacity, number, picker, scales, mixed_part, back_part, *refs):
    blocks, (mixed, back), (mixed_vmem, back_vmem, sems) = (
        refs[:number],
        refs[number : number + 2],
        refs[number + 2 :],
    )
    stores = []
    for c, columns in enumerate(column_steps(mixed.shape[1])):
        outputs = jnp.concatenate([block[:capacity, columns] for block in blocks], axis=0)
        gradients = jnp.concatenate([block[capacity:, columns] for block in blocks], axis=0)
        total, grad = sum_rows(picker[...], scales, outputs, gradients)
        mixed_vmem[:, columns] = (total + mixed_part[:, columns]).astype(BF16)
        back_vmem[:, columns] = (grad + back_part[:, columns]).astype(BF16)
        for n, (source, target) in enumerate(((mixed_vmem, mixed), (back_vmem, back))):
            stores.append(
                pltpu.make_async_copy(source.at[:, columns], target.at[:, columns], sems.at[c, n])
            )
            stores[-1].start()
    for stored in stores:
        stored.wait()


def last(capacity, parts, blocks):
    toks, width = parts[-1].shape
    out_shape = jax.ShapeDtypeStruct((toks, width), BF16)
    return pl.pallas_call(
        functools.partial(last_kernel, capacity, len(blocks)),
        out_shape=(out_shape, out_shape),
        in_specs=whole(4 + len(blocks)),
        out_specs=anywhere(2),
        scratch_shapes=[pltpu.VMEM((toks, width), BF16)] * 2
        + [pltpu.SemaphoreType.DMA((len(column_steps(width)), 2))],
        compiler_params=ROOMY,
        cost_estimate=BRIEF,
    )(*parts, *blocks)


def dispatch(experts, capacity, out_shape, first, *sources):
    weighted = len(sources) > 2
    return pl.pallas_call(
        functools.partial(dispatch_kernel, experts, capacity, weighted),
        out_shape=out_shape,
        in_specs=[pl.BlockSpec(memory_space=pltpu.SMEM)] + in_hbm(len(sources)),
        out_specs=anywhere(len(out_shape)),
        scratch_shapes=[pltpu.VMEM(out.shape, out.dtype) for out in out_shape]
        + [pltpu.VMEM(source.shape, source.dtype) for source in sources]
        + [
            pltpu.SemaphoreType.DMA((len(sources),)),
            pltpu.SemaphoreType.DMA((len(column_steps(out_shape[0].shape[1])), len(out_shape))),
        ],
        compiler_params=ALONE,
        cost_estimate=BRIEF,
    )(first, *sources)


def call(kernel, out_shape, inputs):
    return pl.pallas_call(
        kernel,
        out_shape=out_shape,
        in_specs=[pl.BlockSpec(memory_space=pltpu.SMEM)]
        + [pl.BlockSpec(memory_space=pltpu.VMEM)] * (len(inputs) - 1),
        compiler_params=ROOMY,
        cost_estimate=BRIEF,
    )(*inputs)


def body(tokens, routes, route_scores, out_grad, gate_up, down_weight):
    experts = lax.axis_size("expert")
    groups = lax.axis_size("dp")
    toks, width = tokens.shape
    tops = routes.shape[1]
    units = down_weight.shape[2]
    capacity = (toks * tops + experts - 1) // experts
    slots = experts * capacity
    share = width // groups
    direct = experts <= 8 and capacity % 16 == 0
    w_in, w_out = gate_up[0], down_weight[0]
    routes_t, scores_t = routes.T, route_scores.T
    me = lax.axis_index("expert") if direct else jnp.int32(0)
    first = me.astype(jnp.int32).reshape(1)
    sizes = [capacity] * experts if direct else [slots]
    block_shapes = [jax.ShapeDtypeStruct((size, width), BF16) for size in sizes]

    def travel(block, step, sign):
        pairs = [(at, (at + sign * step) % experts) for at in range(experts)]
        return lax.ppermute(block, "expert", pairs)

    def exchange(blocks, sign):
        if not direct:
            block = blocks[0].reshape(experts, capacity, width)
            moved = lax.all_to_all(block, "expert", split_axis=0, concat_axis=0, tiled=True)
            return [moved.reshape(slots, width)]
        steps = range(1, experts) if sign > 0 else range(experts - 1, 0, -1)
        moved = {step: travel(blocks[step], step, sign) for step in steps}
        return [blocks[0]] + [moved[step] for step in range(1, experts)]

    def joined(blocks):
        return blocks[0] if len(blocks) == 1 else jnp.concatenate(blocks, axis=0)

    def split(rows):
        return [rows[at : at + sizes[0]] for at in range(0, slots, sizes[0])]

    sent_rows = dispatch(experts, capacity, block_shapes, first, routes_t, tokens)
    got_rows = exchange(sent_rows, 1)
    sent_grads = dispatch(experts, capacity, block_shapes, first, routes_t, scores_t, out_grad)
    out_shape = jax.ShapeDtypeStruct((toks, width), BF16)
    cube = direct and experts == 4 and groups == 8 and share % 256 == 0
    if cube:
        sent_grads = after(sent_grads, got_rows[1], got_rows[-1])
        got_grads = exchange(sent_grads, 1)
        rows_t, preact, hidden, produced = forward(got_rows, w_in, w_out)
        got_grads = after(got_grads, hidden)
        own = lax.axis_index("dp")
        send_at = jnp.stack([jnp.bitwise_xor(own, j) for j in CUBE_SEND]).astype(jnp.int32)
        keep_at = jnp.bitwise_xor(send_at, 1)
        early = experts - 1
        early_out = travel(produced[early], early, -1)
        pre_grad, grads_t, sent, w_in_here = backward(
            send_at, share, preact, w_in, rows_t, hidden, w_out, got_grads
        )
        operands = (share, rows_t, grads_t, pre_grad, hidden)
        got = swap(sent, 1)
        blocks = returns(after(pre_grad, sent), w_in_here, produced, early)
        returned = exchange(blocks, -1)
        half = len(CUBE_SEND) // 2
        kept_first = shares(after(keep_at[:half], blocks[0]), *operands, COVER)
        kept_later = shares(after(keep_at[half:], kept_first, early_out, got), *operands, COVER)
        sums = cube_sum(got, kept_first, kept_later)
        late = [n for n in range(experts - 1, 0, -1) if n != early]
        mixed_part, back_part, picker, scales = call(
            functools.partial(partial_kernel, experts, capacity, early, late),
            (
                jax.ShapeDtypeStruct((toks, width), F32),
                jax.ShapeDtypeStruct((toks, width), F32),
                jax.ShapeDtypeStruct(((tops + 1) * toks, len(late) * capacity), BF16),
                jax.ShapeDtypeStruct((tops, toks, 128), F32),
            ),
            (after(first, sums[0]), routes_t, scores_t, returned[0], early_out, returned[early]),
        )
        grad_in, grad_down = means(groups, sums)
        parts = (after(picker, grad_in), scales, mixed_part, back_part)
        mixed_out, token_grad = last(capacity, parts, [returned[n] for n in late])
    else:
        token_rows = joined(got_rows)
        grad_rows = joined(exchange(sent_grads, 1))
        preact = jnp.dot(token_rows, w_in, preferred_element_type=F32)
        gate, up = preact[:, :units], preact[:, units:]
        hidden = (jax.nn.silu(gate) * up).astype(BF16)
        produced = jnp.dot(hidden, w_out.T, preferred_element_type=F32).astype(BF16)
        returned = exchange(split(produced), -1)
        hidden_grad = jnp.dot(grad_rows, w_out, preferred_element_type=F32)
        sigmoid = jax.nn.sigmoid(gate)
        gate_grad = hidden_grad * up * sigmoid * (1.0 + gate * (1.0 - sigmoid))
        up_grad = hidden_grad * gate * sigmoid
        pre_grad = jnp.concatenate([gate_grad, up_grad], axis=1).astype(BF16)
        input_grad = jnp.dot(pre_grad, w_in.T, preferred_element_type=F32).astype(BF16)
        sent_back = exchange(split(input_grad), -1)

        def summed(left, right):
            part = contract(left, right).astype(BF16)
            total = lax.psum_scatter(part, "dp", scatter_dimension=0, tiled=True)
            return total.astype(F32) / groups

        grad_in = summed(token_rows, pre_grad)
        grad_down = summed(grad_rows, hidden)
        mixed_out = call(
            functools.partial(combine_kernel, experts, capacity, True),
            out_shape,
            (first, routes_t, scores_t, *returned),
        )
        token_grad = call(
            functools.partial(combine_kernel, experts, capacity, False),
            out_shape,
            (first, routes_t, *sent_back),
        )
    grad_in = grad_in.reshape(1, share, 2 * units)
    grad_down = grad_down.reshape(1, share, units)
    return (mixed_out, token_grad, grad_in, grad_down)


def solution(mesh):
    in_specs = (
        P(("dp", "expert"), None),
        P(("dp", "expert"), None),
        P(("dp", "expert"), None),
        P(("dp", "expert"), None),
        P("expert", None, None),
        P("expert", None, None),
    )
    out_specs = (
        P(("dp", "expert"), None),
        P(("dp", "expert"), None),
        P("expert", "dp", None),
        P("expert", "dp", None),
    )
    return jax.shard_map(body, mesh=mesh, in_specs=in_specs, out_specs=out_specs, check_vma=False)
```

```python
import functools

import jax
import jax.numpy as jnp
from jax import lax
from jax.experimental import pallas as pl
from jax.experimental.pallas import tpu as pltpu
from jax.sharding import PartitionSpec as P

F32 = jnp.float32
BF16 = jnp.bfloat16
BRIEF = pl.CostEstimate(flops=1024, bytes_accessed=1024, transcendentals=0)
COVER = pl.CostEstimate(flops=4 * 10**10, bytes_accessed=1024, transcendentals=0)
ROOMY = pltpu.CompilerParams(vmem_limit_bytes=16 * 1024 * 1024)
BIG = pltpu.CompilerParams(vmem_limit_bytes=28 * 1024 * 1024)
ALONE = pltpu.CompilerParams(vmem_limit_bytes=60 * 1024 * 1024)


def contract(left, right):
    return lax.dot_general(left, right, (((0,), (0,)), ((), ())), preferred_element_type=F32)


def slot_rows(first, routes, experts, capacity):
    tops, toks = routes.shape
    padded = -(-experts // 8) * 8
    rows = lax.broadcasted_iota(jnp.int32, (padded, toks), 0)
    ids = rows + first
    ids = jnp.where(ids >= experts, ids - experts, ids)
    ids = jnp.where(rows < experts, ids, -1)
    hits = [routes[k : k + 1, :] == ids for k in range(tops)]
    named = functools.reduce(jnp.logical_or, hits)
    before = lax.broadcasted_iota(jnp.int32, (toks, toks), 0) < lax.broadcasted_iota(
        jnp.int32, (toks, toks), 1
    )
    position = jnp.dot(
        named.astype(F32).astype(BF16),
        before.astype(F32).astype(BF16),
        preferred_element_type=F32,
    )
    slot = position + (rows * capacity).astype(F32)
    return [jnp.sum(jnp.where(hit, slot, 0.0), axis=0, keepdims=True) for hit in hits]


def weight_rows(scores):
    grown = jnp.exp(scores)
    return grown / jnp.sum(grown, axis=0, keepdims=True)


def to_column(row):
    toks = row.shape[1]
    same = lax.broadcasted_iota(jnp.int32, (toks, toks), 0) == lax.broadcasted_iota(
        jnp.int32, (toks, toks), 1
    )
    return jnp.sum(jnp.where(same, row, 0.0), axis=1, keepdims=True)


def put_blocks(outs, rows, columns):
    start = 0
    for out in outs:
        size = out.shape[0]
        out[:, columns] = rows[start : start + size]
        start += size


def column_steps(width):
    step = 512 if width % 512 == 0 else width
    return [slice(at, at + step) for at in range(0, width, step)]


def dispatch_kernel(experts, capacity, weighted, first, *refs):
    count = 2 + weighted
    sources, refs = refs[:count], refs[count:]
    number = (len(refs) - count - 2) // 2
    outs, ready, (*held, sems, out_sems) = refs[:number], refs[number : 2 * number], refs[2 * number :]
    copies = [
        pltpu.make_async_copy(source, place, sems.at[n])
        for n, (source, place) in enumerate(zip(sources, held))
    ]
    for copy in copies:
        copy.start()
    routes, values = held[0], held[-1]
    scores = held[1] if weighted else None
    for copy in copies[:-1]:
        copy.wait()
    slots, toks = experts * capacity, values.shape[0]
    places = lax.broadcasted_iota(jnp.int32, (slots, toks), 0).astype(F32)
    hits = [places == row for row in slot_rows(first[0], routes[...], experts, capacity)]
    picker = functools.reduce(jnp.logical_or, hits).astype(F32).astype(BF16)
    if weighted:
        weights = weight_rows(scores[...])
        scale = sum(
            jnp.sum(jnp.where(hit, weights[k : k + 1, :], 0.0), axis=1, keepdims=True)
            for k, hit in enumerate(hits)
        )
    copies[-1].wait()
    stores = []
    for c, columns in enumerate(column_steps(values.shape[1])):
        rows = jnp.dot(picker, values[:, columns], preferred_element_type=F32)
        if weighted:
            rows = rows * scale
        put_blocks(ready, rows.astype(BF16), columns)
        for n, (block, out) in enumerate(zip(ready, outs)):
            stores.append(
                pltpu.make_async_copy(block.at[:, columns], out.at[:, columns], out_sems.at[c, n])
            )
            stores[-1].start()
    for store in stores:
        store.wait()


def combine_kernel(experts, capacity, weighted, first, routes, *refs):
    scores = refs[0] if weighted else None
    blocks, out = refs[weighted:-1], refs[-1]
    slots, toks = experts * capacity, out.shape[0]
    places = lax.broadcasted_iota(jnp.int32, (toks, slots), 1).astype(F32)
    hits = [
        places == to_column(row) for row in slot_rows(first[0], routes[...], experts, capacity)
    ]
    if weighted:
        weights = weight_rows(scores[...])
        scales = [to_column(weights[k : k + 1, :]) for k in range(len(hits))]
        pickers = [hit.astype(F32).astype(BF16) for hit in hits]
    else:
        pickers = [functools.reduce(jnp.logical_or, hits).astype(F32).astype(BF16)]
    for columns in column_steps(out.shape[1]):
        rows = [block[:, columns] for block in blocks]
        rows = rows[0] if len(rows) == 1 else jnp.concatenate(rows, axis=0)
        picked = [jnp.dot(picker, rows, preferred_element_type=F32) for picker in pickers]
        if weighted:
            picked = [scale * part for scale, part in zip(scales, picked)]
        out[:, columns] = sum(picked).astype(out.dtype)


def whole(count):
    return [pl.BlockSpec(memory_space=pltpu.VMEM)] * count


def write_shares(at, rows_t, grads_t, pre_grad, hidden, out):
    share = out.shape[1]
    wide, narrow = pre_grad.shape[1] // 2, hidden.shape[1] // 2

    def write(t, half):
        own = pl.ds(pl.multiple_of(at[t] * share, share), share)
        out[t, :, :wide] = jnp.dot(
            rows_t[own, :],
            pre_grad[:, half * wide : (half + 1) * wide],
            preferred_element_type=F32,
        ).astype(out.dtype)
        out[t, :, wide:] = jnp.dot(
            grads_t[own, :],
            hidden[:, half * narrow : (half + 1) * narrow],
            preferred_element_type=F32,
        ).astype(out.dtype)

    for t in range(out.shape[0]):
        write(t, t // 2 % 2)


def transpose_into(rows, rows_t):
    width = rows.shape[1]
    step = 256 if width % 256 == 0 else width

    for begin in range(0, width, step):
        rows_t[begin : begin + step, :] = rows[:, begin : begin + step].T


def join_copies(blocks, rows, sems):
    size = blocks[0].shape[0]
    joins = [
        pltpu.make_async_copy(block, rows.at[pl.ds(n * size, size)], sems.at[n])
        for n, block in enumerate(blocks)
    ]
    for join in joins:
        join.start()
    return joins


def forward_kernel(count, *refs):
    blocks, (w_in_hbm, down_hbm), (rows_t, preact, hidden), outs, scratch = (
        refs[:count],
        refs[count : count + 2],
        refs[count + 2 : count + 5],
        refs[count + 5 : 2 * count + 5],
        refs[2 * count + 5 :],
    )
    rows, w_in, down, block_sems, weight_sems, down_sem = scratch
    joins = join_copies(blocks, rows, block_sems)
    width, units = down.shape
    step = 256 if units % 256 == 0 else units
    loads = []
    for n in range(2 * units // step):
        begin = (n % 2) * units + n // 2 * step
        loads.append(
            pltpu.make_async_copy(
                w_in_hbm.at[:, pl.ds(begin, step)],
                w_in.at[:, pl.ds(begin, step)],
                weight_sems.at[n],
            )
        )
        loads[-1].start()
    load_down = pltpu.make_async_copy(down_hbm, down, down_sem)
    load_down.start()
    for join in joins:
        join.wait()
    for n in range(units // step):
        begin = n * step
        gate_at, up_at = slice(begin, begin + step), slice(units + begin, units + begin + step)
        loads[2 * n].wait()
        gate = jnp.dot(rows[...], w_in[:, gate_at], preferred_element_type=F32)
        loads[2 * n + 1].wait()
        up = jnp.dot(rows[...], w_in[:, up_at], preferred_element_type=F32)
        preact[:, gate_at] = gate
        preact[:, up_at] = up
        hidden[:, gate_at] = (gate / (1.0 + jnp.exp(-gate)) * up).astype(BF16)
    load_down.wait()
    for columns in column_steps(width):
        part = lax.dot_general(
            hidden[...], down[columns, :], (((1,), (1,)), ((), ())), preferred_element_type=F32
        )
        put_blocks(outs, part.astype(BF16), columns)
    transpose_into(rows, rows_t)


def forward(blocks, w_in, down):
    width, units = down.shape
    slots = sum(block.shape[0] for block in blocks)
    count = len(blocks)
    rows_t, preact, hidden, *outs = pl.pallas_call(
        functools.partial(forward_kernel, count),
        out_shape=(
            jax.ShapeDtypeStruct((width, slots), BF16),
            jax.ShapeDtypeStruct((slots, 2 * units), F32),
            jax.ShapeDtypeStruct((slots, units), BF16),
            *[jax.ShapeDtypeStruct(block.shape, BF16) for block in blocks],
        ),
        in_specs=anywhere(count) + in_hbm(2),
        out_specs=whole(3 + count),
        scratch_shapes=[
            pltpu.VMEM((slots, width), BF16),
            pltpu.VMEM(w_in.shape, BF16),
            pltpu.VMEM(down.shape, BF16),
            pltpu.SemaphoreType.DMA((count,)),
            pltpu.SemaphoreType.DMA((2 * units // min(units, 256),)),
            pltpu.SemaphoreType.DMA,
        ],
        compiler_params=pltpu.CompilerParams(vmem_limit_bytes=46 * 1024 * 1024),
        cost_estimate=BRIEF,
    )(*blocks, w_in, down)
    return rows_t, preact, hidden, outs


def backward_kernel(count, at, preact_hbm, w_in_hbm, rows_t, hidden, down, *refs):
    blocks, (pre_grad, grads_t, sent, w_in, *refs) = refs[:count], refs[count:]
    grads, preact, block_sems, load_sem, sem = refs
    joins = join_copies(blocks, grads, block_sems)
    fetch = pltpu.make_async_copy(preact_hbm, preact, sem)
    fetch.start()
    load = pltpu.make_async_copy(w_in_hbm, w_in, load_sem)
    load.start()
    units = down.shape[1]
    for join in joins:
        join.wait()
    fetch.wait()
    step = 256 if units % 256 == 0 else units
    for begin in range(0, units, step):
        gate = preact[:, begin : begin + step]
        up = preact[:, units + begin : units + begin + step]
        hidden_grad = jnp.dot(
            grads[...], down[:, begin : begin + step], preferred_element_type=F32
        )
        sigmoid = 1.0 / (1.0 + jnp.exp(-gate))
        gate_grad = hidden_grad * up * sigmoid * (1.0 + gate * (1.0 - sigmoid))
        up_grad = hidden_grad * gate * sigmoid
        pre_grad[:, begin : begin + step] = gate_grad.astype(BF16)
        pre_grad[:, units + begin : units + begin + step] = up_grad.astype(BF16)
    transpose_into(grads, grads_t)
    write_shares(at, rows_t, grads_t, pre_grad, hidden, sent)
    load.wait()


def return_kernel(count, alone, pre_grad, w_in, *refs):
    blocks, outs, sems = refs[:count], refs[count : 2 * count], refs[-1]
    size = blocks[0].shape[0]
    copies = [
        pltpu.make_async_copy(block, out.at[pl.ds(0, size)], sems.at[n])
        for n, (block, out) in enumerate(zip(blocks, outs))
        if n != alone
    ]
    for copy in copies:
        copy.start()
    for columns in column_steps(w_in.shape[0]):
        part = lax.dot_general(
            pre_grad[...], w_in[columns, :], (((1,), (1,)), ((), ())), preferred_element_type=F32
        ).astype(BF16)
        for n, out in enumerate(outs):
            out[out.shape[0] - size :, columns] = part[n * size : (n + 1) * size]
    for copy in copies:
        copy.wait()


def returns(pre_grad, w_in, produced, alone):
    count = len(produced)
    size, width = produced[0].shape
    return pl.pallas_call(
        functools.partial(return_kernel, count, alone),
        out_shape=[
            jax.ShapeDtypeStruct((size if n == alone else 2 * size, width), BF16)
            for n in range(count)
        ],
        in_specs=whole(2) + anywhere(count),
        out_specs=whole(count),
        scratch_shapes=[pltpu.SemaphoreType.DMA((count,))],
        compiler_params=ROOMY,
        cost_estimate=BRIEF,
    )(pre_grad, w_in, *produced)


def anywhere(count):
    return [pl.BlockSpec(memory_space=pl.ANY)] * count


def in_hbm(count):
    return [pl.BlockSpec(memory_space=pltpu.HBM)] * count


def backward(at, share, preact, w_in, rows_t, hidden, down, blocks):
    width, units = down.shape
    slots = preact.shape[0]
    count = len(blocks)
    return pl.pallas_call(
        functools.partial(backward_kernel, count),
        out_shape=(
            jax.ShapeDtypeStruct((slots, 2 * units), BF16),
            jax.ShapeDtypeStruct((width, slots), BF16),
            jax.ShapeDtypeStruct((at.shape[0], share, 3 * units // 2), BF16),
            jax.ShapeDtypeStruct(w_in.shape, BF16),
        ),
        in_specs=[pl.BlockSpec(memory_space=pltpu.SMEM)]
        + anywhere(2)
        + whole(3)
        + anywhere(count),
        out_specs=whole(4),
        scratch_shapes=[
            pltpu.VMEM((slots, width), BF16),
            pltpu.VMEM((slots, 2 * units), F32),
            pltpu.SemaphoreType.DMA((count,)),
            pltpu.SemaphoreType.DMA,
            pltpu.SemaphoreType.DMA,
        ],
        compiler_params=BIG,
        cost_estimate=BRIEF,
    )(at, preact, w_in, rows_t, hidden, down, *blocks)


def shares(at, share, rows_t, grads_t, pre_grad, hidden, cost):
    units = hidden.shape[1]
    return pl.pallas_call(
        write_shares,
        out_shape=jax.ShapeDtypeStruct((at.shape[0], share, 3 * units // 2), BF16),
        in_specs=[pl.BlockSpec(memory_space=pltpu.SMEM)] + whole(4),
        out_specs=whole(1)[0],
        compiler_params=ROOMY,
        cost_estimate=cost,
    )(at, rows_t, grads_t, pre_grad, hidden)


def add_kernel(kept, got, left, right):
    half = left.shape[0]
    left[...] = add(kept[:half], got[:half]).astype(BF16)
    right[...] = add(kept[half:], got[half : 2 * half]).astype(BF16)


def next_kernel(kept, got, left_in, right_in, left_send, right_send):
    first = got.shape[0] // 2
    left_send[...] = (add(kept[1], got[first + 1]) + left_in[1].astype(F32)).astype(BF16)
    right_send[...] = (add(kept[3], got[first + 3]) + right_in[1].astype(F32)).astype(BF16)


def own_kernel(kept, got, left_in, right_in, left, right):
    first = got.shape[0] // 2
    left[...] = add(kept[0], got[first]) + left_in[0].astype(F32)
    right[...] = add(kept[2], got[first + 2]) + right_in[0].astype(F32)


def add(left, right):
    return left.astype(F32) + right.astype(F32)


CUBE_SEND = (3, 7, 5, 7, 1, 5, 1, 3)


def swap(block, bit):
    return lax.ppermute(block, "dp", [(at, at ^ bit) for at in range(lax.axis_size("dp"))])


def cube_sum(got, kept_first, kept_later):
    _, share, columns = got.shape

    def run(kernel, out_shape, inputs, cost=BRIEF):
        return pl.pallas_call(
            kernel,
            out_shape=out_shape,
            in_specs=whole(len(inputs)),
            out_specs=whole(len(out_shape)),
            compiler_params=ROOMY,
            cost_estimate=cost,
        )(*inputs)

    half = jax.ShapeDtypeStruct((2, share, columns), BF16)
    one = jax.ShapeDtypeStruct((share, columns), BF16)
    own = jax.ShapeDtypeStruct((share, columns), F32)
    left, right = run(add_kernel, (half, half), (kept_first, got))
    parts = (kept_later, got, swap(left, 2), swap(right, 4))
    left_send, right_send = run(next_kernel, (one, one), parts)
    left, right = run(own_kernel, (own, own), parts, COVER)
    return left, swap(left_send, 4), right, swap(right_send, 2)


def after(value, *others):
    return lax.optimization_barrier((value, *others))[0]


def partial_kernel(experts, capacity, alone, late, first, routes, scores, *refs):
    (own, early, back_early), (mixed, back, late_picker, scales) = refs[:-4], refs[-4:]
    slots, toks = experts * capacity, mixed.shape[0]
    places = lax.broadcasted_iota(jnp.int32, (toks, slots), 1).astype(F32)
    hits = [
        places == to_column(row) for row in slot_rows(first[0], routes[...], experts, capacity)
    ]
    hits.append(functools.reduce(jnp.logical_or, hits))
    picker = jnp.concatenate([hit.astype(F32).astype(BF16) for hit in hits], axis=0)
    weights = weight_rows(scores[...])
    for k in range(scales.shape[0]):
        scales[k] = jnp.broadcast_to(to_column(weights[k : k + 1, :]), scales.shape[1:])

    def slots_of(blocks):
        parts = [picker[:, n * capacity : (n + 1) * capacity] for n in blocks]
        return jnp.concatenate(parts, axis=1)

    late_picker[...] = slots_of(late)
    now = slots_of((0, alone))
    for columns in column_steps(mixed.shape[1]):
        outputs = jnp.concatenate([own[:capacity, columns], early[:, columns]], axis=0)
        gradients = jnp.concatenate([own[capacity:, columns], back_early[:, columns]], axis=0)
        total, grad = sum_rows(now, scales, outputs, gradients)
        mixed[:, columns] = total
        back[:, columns] = grad


def sum_rows(picker, scales, outputs, gradients):
    tops, toks = scales.shape[:2]
    picked = jnp.dot(picker[: tops * toks], outputs, preferred_element_type=F32)
    total = sum(scales[k, :, :1] * picked[k * toks : (k + 1) * toks] for k in range(tops))
    return total, jnp.dot(picker[tops * toks :], gradients, preferred_element_type=F32)


def mean_kernel(count, left, left_last, right, right_last, wide, narrow):
    middle, edge = wide.shape[1] // 2, narrow.shape[1] // 2
    for at, (own, last) in enumerate(((left, left_last), (right, right_last))):
        total = (own[...] + last[...].astype(F32)) / count
        wide[:, at * middle : (at + 1) * middle] = total[:, :middle]
        narrow[:, at * edge : (at + 1) * edge] = total[:, middle:]


def means(count, sums):
    share, columns = sums[0].shape
    return pl.pallas_call(
        functools.partial(mean_kernel, count),
        out_shape=(
            jax.ShapeDtypeStruct((share, 4 * columns // 3), F32),
            jax.ShapeDtypeStruct((share, 2 * columns // 3), F32),
        ),
        in_specs=whole(4),
        out_specs=whole(2),
        compiler_params=ROOMY,
        cost_estimate=BRIEF,
    )(*sums)


def last_kernel(capacity, number, picker, scales, mixed_part, back_part, *refs):
    blocks, (mixed, back), (mixed_vmem, back_vmem, sems) = (
        refs[:number],
        refs[number : number + 2],
        refs[number + 2 :],
    )
    stores = []
    for c, columns in enumerate(column_steps(mixed.shape[1])):
        outputs = jnp.concatenate([block[:capacity, columns] for block in blocks], axis=0)
        gradients = jnp.concatenate([block[capacity:, columns] for block in blocks], axis=0)
        total, grad = sum_rows(picker[...], scales, outputs, gradients)
        mixed_vmem[:, columns] = (total + mixed_part[:, columns]).astype(BF16)
        back_vmem[:, columns] = (grad + back_part[:, columns]).astype(BF16)
        for n, (source, target) in enumerate(((mixed_vmem, mixed), (back_vmem, back))):
            stores.append(
                pltpu.make_async_copy(source.at[:, columns], target.at[:, columns], sems.at[c, n])
            )
            stores[-1].start()
    for stored in stores:
        stored.wait()


def last(capacity, parts, blocks):
    toks, width = parts[-1].shape
    out_shape = jax.ShapeDtypeStruct((toks, width), BF16)
    return pl.pallas_call(
        functools.partial(last_kernel, capacity, len(blocks)),
        out_shape=(out_shape, out_shape),
        in_specs=whole(4 + len(blocks)),
        out_specs=anywhere(2),
        scratch_shapes=[pltpu.VMEM((toks, width), BF16)] * 2
        + [pltpu.SemaphoreType.DMA((len(column_steps(width)), 2))],
        compiler_params=ROOMY,
        cost_estimate=BRIEF,
    )(*parts, *blocks)


def dispatch(experts, capacity, out_shape, first, *sources):
    weighted = len(sources) > 2
    return pl.pallas_call(
        functools.partial(dispatch_kernel, experts, capacity, weighted),
        out_shape=out_shape,
        in_specs=[pl.BlockSpec(memory_space=pltpu.SMEM)] + in_hbm(len(sources)),
        out_specs=anywhere(len(out_shape)),
        scratch_shapes=[pltpu.VMEM(out.shape, out.dtype) for out in out_shape]
        + [pltpu.VMEM(source.shape, source.dtype) for source in sources]
        + [
            pltpu.SemaphoreType.DMA((len(sources),)),
            pltpu.SemaphoreType.DMA((len(column_steps(out_shape[0].shape[1])), len(out_shape))),
        ],
        compiler_params=ALONE,
        cost_estimate=BRIEF,
    )(first, *sources)


def call(kernel, out_shape, inputs):
    return pl.pallas_call(
        kernel,
        out_shape=out_shape,
        in_specs=[pl.BlockSpec(memory_space=pltpu.SMEM)]
        + [pl.BlockSpec(memory_space=pltpu.VMEM)] * (len(inputs) - 1),
        compiler_params=ROOMY,
        cost_estimate=BRIEF,
    )(*inputs)


def body(tokens, routes, route_scores, out_grad, gate_up, down_weight):
    experts = lax.axis_size("expert")
    groups = lax.axis_size("dp")
    toks, width = tokens.shape
    tops = routes.shape[1]
    units = down_weight.shape[2]
    capacity = (toks * tops + experts - 1) // experts
    slots = experts * capacity
    share = width // groups
    direct = experts <= 8 and capacity % 16 == 0
    w_in, w_out = gate_up[0], down_weight[0]
    routes_t, scores_t = routes.T, route_scores.T
    me = lax.axis_index("expert") if direct else jnp.int32(0)
    first = me.astype(jnp.int32).reshape(1)
    sizes = [capacity] * experts if direct else [slots]
    block_shapes = [jax.ShapeDtypeStruct((size, width), BF16) for size in sizes]

    def travel(block, step, sign):
        pairs = [(at, (at + sign * step) % experts) for at in range(experts)]
        return lax.ppermute(block, "expert", pairs)

    def exchange(blocks, sign):
        if not direct:
            block = blocks[0].reshape(experts, capacity, width)
            moved = lax.all_to_all(block, "expert", split_axis=0, concat_axis=0, tiled=True)
            return [moved.reshape(slots, width)]
        moved = {step: travel(blocks[step], step, sign) for step in range(experts - 1, 0, -1)}
        return [blocks[0]] + [moved[step] for step in range(1, experts)]

    def joined(blocks):
        return blocks[0] if len(blocks) == 1 else jnp.concatenate(blocks, axis=0)

    def split(rows):
        return [rows[at : at + sizes[0]] for at in range(0, slots, sizes[0])]

    sent_rows = dispatch(experts, capacity, block_shapes, first, routes_t, tokens)
    got_rows = exchange(sent_rows, 1)
    sent_grads = dispatch(experts, capacity, block_shapes, first, routes_t, scores_t, out_grad)
    out_shape = jax.ShapeDtypeStruct((toks, width), BF16)
    cube = direct and experts == 4 and groups == 8 and share % 256 == 0
    if cube:
        turn = [0] + list(range(experts - 1, 0, -1))
        sent_grads = after(sent_grads, got_rows[1], got_rows[-1])
        got_grads = exchange(sent_grads, 1)
        rows_t, preact, hidden, produced = forward([got_rows[n] for n in turn], w_in, w_out)
        got_grads = after([got_grads[n] for n in turn], hidden)
        own = lax.axis_index("dp")
        send_at = jnp.stack([jnp.bitwise_xor(own, j) for j in CUBE_SEND]).astype(jnp.int32)
        keep_at = jnp.bitwise_xor(send_at, 1)
        early = experts - 1
        early_out = travel(produced[turn[early]], early, -1)
        pre_grad, grads_t, sent, w_in_here = backward(
            send_at, share, preact, w_in, rows_t, hidden, w_out, got_grads
        )
        operands = (share, rows_t, grads_t, pre_grad, hidden)
        got = swap(sent, 1)
        blocks = returns(after(pre_grad, sent), w_in_here, produced, turn[early])
        returned = exchange([blocks[n] for n in turn], -1)
        half = len(CUBE_SEND) // 2
        kept_first = shares(after(keep_at[:half], blocks[0]), *operands, COVER)
        kept_later = shares(after(keep_at[half:], kept_first, early_out, got), *operands, COVER)
        sums = cube_sum(got, kept_first, kept_later)
        late = [n for n in range(experts - 1, 0, -1) if n != early]
        mixed_part, back_part, picker, scales = call(
            functools.partial(partial_kernel, experts, capacity, early, late),
            (
                jax.ShapeDtypeStruct((toks, width), F32),
                jax.ShapeDtypeStruct((toks, width), F32),
                jax.ShapeDtypeStruct(((tops + 1) * toks, len(late) * capacity), BF16),
                jax.ShapeDtypeStruct((tops, toks, 128), F32),
            ),
            (after(first, sums[0]), routes_t, scores_t, returned[0], early_out, returned[early]),
        )
        grad_in, grad_down = means(groups, sums)
        parts = (after(picker, grad_in), scales, mixed_part, back_part)
        mixed_out, token_grad = last(capacity, parts, [returned[n] for n in late])
    else:
        token_rows = joined(got_rows)
        grad_rows = joined(exchange(sent_grads, 1))
        preact = jnp.dot(token_rows, w_in, preferred_element_type=F32)
        gate, up = preact[:, :units], preact[:, units:]
        hidden = (jax.nn.silu(gate) * up).astype(BF16)
        produced = jnp.dot(hidden, w_out.T, preferred_element_type=F32).astype(BF16)
        returned = exchange(split(produced), -1)
        hidden_grad = jnp.dot(grad_rows, w_out, preferred_element_type=F32)
        sigmoid = jax.nn.sigmoid(gate)
        gate_grad = hidden_grad * up * sigmoid * (1.0 + gate * (1.0 - sigmoid))
        up_grad = hidden_grad * gate * sigmoid
        pre_grad = jnp.concatenate([gate_grad, up_grad], axis=1).astype(BF16)
        input_grad = jnp.dot(pre_grad, w_in.T, preferred_element_type=F32).astype(BF16)
        sent_back = exchange(split(input_grad), -1)

        def summed(left, right):
            part = contract(left, right).astype(BF16)
            total = lax.psum_scatter(part, "dp", scatter_dimension=0, tiled=True)
            return total.astype(F32) / groups

        grad_in = summed(token_rows, pre_grad)
        grad_down = summed(grad_rows, hidden)
        mixed_out = call(
            functools.partial(combine_kernel, experts, capacity, True),
            out_shape,
            (first, routes_t, scores_t, *returned),
        )
        token_grad = call(
            functools.partial(combine_kernel, experts, capacity, False),
            out_shape,
            (first, routes_t, *sent_back),
        )
    grad_in = grad_in.reshape(1, share, 2 * units)
    grad_down = grad_down.reshape(1, share, units)
    return (mixed_out, token_grad, grad_in, grad_down)


def solution(mesh):
    in_specs = (
        P(("dp", "expert"), None),
        P(("dp", "expert"), None),
        P(("dp", "expert"), None),
        P(("dp", "expert"), None),
        P("expert", None, None),
        P("expert", None, None),
    )
    out_specs = (
        P(("dp", "expert"), None),
        P(("dp", "expert"), None),
        P("expert", "dp", None),
        P("expert", "dp", None),
    )
    return jax.shard_map(body, mesh=mesh, in_specs=in_specs, out_specs=out_specs, check_vma=False)
```

```python
import functools

import jax
import jax.numpy as jnp
from jax import lax
from jax.experimental import pallas as pl
from jax.experimental.pallas import tpu as pltpu
from jax.sharding import PartitionSpec as P

F32 = jnp.float32
BF16 = jnp.bfloat16
BRIEF = pl.CostEstimate(flops=1024, bytes_accessed=1024, transcendentals=0)
COVER = pl.CostEstimate(flops=4 * 10**10, bytes_accessed=1024, transcendentals=0)
ROOMY = pltpu.CompilerParams(vmem_limit_bytes=16 * 1024 * 1024)
BIG = pltpu.CompilerParams(vmem_limit_bytes=28 * 1024 * 1024)
ALONE = pltpu.CompilerParams(vmem_limit_bytes=60 * 1024 * 1024)


def contract(left, right):
    return lax.dot_general(left, right, (((0,), (0,)), ((), ())), preferred_element_type=F32)


def slot_rows(first, routes, experts, capacity):
    tops, toks = routes.shape
    padded = -(-experts // 8) * 8
    rows = lax.broadcasted_iota(jnp.int32, (padded, toks), 0)
    ids = rows + first
    ids = jnp.where(ids >= experts, ids - experts, ids)
    ids = jnp.where(rows < experts, ids, -1)
    hits = [routes[k : k + 1, :] == ids for k in range(tops)]
    named = functools.reduce(jnp.logical_or, hits)
    before = lax.broadcasted_iota(jnp.int32, (toks, toks), 0) < lax.broadcasted_iota(
        jnp.int32, (toks, toks), 1
    )
    position = jnp.dot(
        named.astype(F32).astype(BF16),
        before.astype(F32).astype(BF16),
        preferred_element_type=F32,
    )
    slot = position + (rows * capacity).astype(F32)
    return [jnp.sum(jnp.where(hit, slot, 0.0), axis=0, keepdims=True) for hit in hits]


def weight_rows(scores):
    grown = jnp.exp(scores)
    return grown / jnp.sum(grown, axis=0, keepdims=True)


def to_column(row):
    toks = row.shape[1]
    same = lax.broadcasted_iota(jnp.int32, (toks, toks), 0) == lax.broadcasted_iota(
        jnp.int32, (toks, toks), 1
    )
    return jnp.sum(jnp.where(same, row, 0.0), axis=1, keepdims=True)


def put_blocks(outs, rows, columns):
    start = 0
    for out in outs:
        size = out.shape[0]
        out[:, columns] = rows[start : start + size]
        start += size


def column_steps(width):
    step = 512 if width % 512 == 0 else width
    return [slice(at, at + step) for at in range(0, width, step)]


def dispatch_kernel(experts, capacity, weighted, first, *refs):
    count = 2 + weighted
    sources, refs = refs[:count], refs[count:]
    number = (len(refs) - count - 2) // 2
    outs, ready, (*held, sems, out_sems) = refs[:number], refs[number : 2 * number], refs[2 * number :]
    copies = [
        pltpu.make_async_copy(source, place, sems.at[n])
        for n, (source, place) in enumerate(zip(sources, held))
    ]
    for copy in copies:
        copy.start()
    routes, values = held[0], held[-1]
    scores = held[1] if weighted else None
    for copy in copies[:-1]:
        copy.wait()
    slots, toks = experts * capacity, values.shape[0]
    places = lax.broadcasted_iota(jnp.int32, (slots, toks), 0).astype(F32)
    hits = [places == row for row in slot_rows(first[0], routes[...], experts, capacity)]
    picker = functools.reduce(jnp.logical_or, hits).astype(F32).astype(BF16)
    if weighted:
        weights = weight_rows(scores[...])
        scale = sum(
            jnp.sum(jnp.where(hit, weights[k : k + 1, :], 0.0), axis=1, keepdims=True)
            for k, hit in enumerate(hits)
        )
    copies[-1].wait()
    stores = []
    for c, columns in enumerate(column_steps(values.shape[1])):
        rows = jnp.dot(picker, values[:, columns], preferred_element_type=F32)
        if weighted:
            rows = rows * scale
        put_blocks(ready, rows.astype(BF16), columns)
        for n, (block, out) in enumerate(zip(ready, outs)):
            stores.append(
                pltpu.make_async_copy(block.at[:, columns], out.at[:, columns], out_sems.at[c, n])
            )
            stores[-1].start()
    for store in stores:
        store.wait()


def combine_kernel(experts, capacity, weighted, first, routes, *refs):
    scores = refs[0] if weighted else None
    blocks, out = refs[weighted:-1], refs[-1]
    slots, toks = experts * capacity, out.shape[0]
    places = lax.broadcasted_iota(jnp.int32, (toks, slots), 1).astype(F32)
    hits = [
        places == to_column(row) for row in slot_rows(first[0], routes[...], experts, capacity)
    ]
    if weighted:
        weights = weight_rows(scores[...])
        scales = [to_column(weights[k : k + 1, :]) for k in range(len(hits))]
        pickers = [hit.astype(F32).astype(BF16) for hit in hits]
    else:
        pickers = [functools.reduce(jnp.logical_or, hits).astype(F32).astype(BF16)]
    for columns in column_steps(out.shape[1]):
        rows = [block[:, columns] for block in blocks]
        rows = rows[0] if len(rows) == 1 else jnp.concatenate(rows, axis=0)
        picked = [jnp.dot(picker, rows, preferred_element_type=F32) for picker in pickers]
        if weighted:
            picked = [scale * part for scale, part in zip(scales, picked)]
        out[:, columns] = sum(picked).astype(out.dtype)


def whole(count):
    return [pl.BlockSpec(memory_space=pltpu.VMEM)] * count


def write_shares(at, rows_t, grads_t, pre_grad, hidden, out):
    share = out.shape[1]
    wide, narrow = pre_grad.shape[1] // 2, hidden.shape[1] // 2

    def write(t, half):
        own = pl.ds(pl.multiple_of(at[t] * share, share), share)
        out[t, :, :wide] = jnp.dot(
            rows_t[own, :],
            pre_grad[:, half * wide : (half + 1) * wide],
            preferred_element_type=F32,
        ).astype(out.dtype)
        out[t, :, wide:] = jnp.dot(
            grads_t[own, :],
            hidden[:, half * narrow : (half + 1) * narrow],
            preferred_element_type=F32,
        ).astype(out.dtype)

    for t in range(out.shape[0]):
        write(t, t // 2 % 2)


def transpose_into(rows, rows_t):
    width = rows.shape[1]
    step = 256 if width % 256 == 0 else width

    for begin in range(0, width, step):
        rows_t[begin : begin + step, :] = rows[:, begin : begin + step].T


def join_copies(blocks, rows, sems):
    size = blocks[0].shape[0]
    joins = [
        pltpu.make_async_copy(block, rows.at[pl.ds(n * size, size)], sems.at[n])
        for n, block in enumerate(blocks)
    ]
    for join in joins:
        join.start()
    return joins


def forward_kernel(count, *refs):
    blocks, (w_in_hbm, down_hbm), (rows_t, preact, hidden), outs, scratch = (
        refs[:count],
        refs[count : count + 2],
        refs[count + 2 : count + 5],
        refs[count + 5 : 2 * count + 5],
        refs[2 * count + 5 :],
    )
    rows, w_in, down, block_sems, weight_sems, down_sem = scratch
    joins = join_copies(blocks, rows, block_sems)
    width, units = down.shape
    step = 256 if units % 256 == 0 else units
    loads = []
    for n in range(2 * units // step):
        begin = (n % 2) * units + n // 2 * step
        loads.append(
            pltpu.make_async_copy(
                w_in_hbm.at[:, pl.ds(begin, step)],
                w_in.at[:, pl.ds(begin, step)],
                weight_sems.at[n],
            )
        )
        loads[-1].start()
    load_down = pltpu.make_async_copy(down_hbm, down, down_sem)
    load_down.start()
    for join in joins:
        join.wait()
    for n in range(units // step):
        begin = n * step
        gate_at, up_at = slice(begin, begin + step), slice(units + begin, units + begin + step)
        loads[2 * n].wait()
        gate = jnp.dot(rows[...], w_in[:, gate_at], preferred_element_type=F32)
        loads[2 * n + 1].wait()
        up = jnp.dot(rows[...], w_in[:, up_at], preferred_element_type=F32)
        preact[:, gate_at] = gate
        preact[:, up_at] = up
        hidden[:, gate_at] = (gate / (1.0 + jnp.exp(-gate)) * up).astype(BF16)
    load_down.wait()
    for columns in column_steps(width):
        part = lax.dot_general(
            hidden[...], down[columns, :], (((1,), (1,)), ((), ())), preferred_element_type=F32
        )
        put_blocks(outs, part.astype(BF16), columns)
    transpose_into(rows, rows_t)


def forward(blocks, w_in, down):
    width, units = down.shape
    slots = sum(block.shape[0] for block in blocks)
    count = len(blocks)
    rows_t, preact, hidden, *outs = pl.pallas_call(
        functools.partial(forward_kernel, count),
        out_shape=(
            jax.ShapeDtypeStruct((width, slots), BF16),
            jax.ShapeDtypeStruct((slots, 2 * units), F32),
            jax.ShapeDtypeStruct((slots, units), BF16),
            *[jax.ShapeDtypeStruct(block.shape, BF16) for block in blocks],
        ),
        in_specs=anywhere(count) + in_hbm(2),
        out_specs=whole(3 + count),
        scratch_shapes=[
            pltpu.VMEM((slots, width), BF16),
            pltpu.VMEM(w_in.shape, BF16),
            pltpu.VMEM(down.shape, BF16),
            pltpu.SemaphoreType.DMA((count,)),
            pltpu.SemaphoreType.DMA((2 * units // min(units, 256),)),
            pltpu.SemaphoreType.DMA,
        ],
        compiler_params=pltpu.CompilerParams(vmem_limit_bytes=46 * 1024 * 1024),
        cost_estimate=BRIEF,
    )(*blocks, w_in, down)
    return rows_t, preact, hidden, outs


def backward_kernel(count, at, preact_hbm, w_in_hbm, rows_t, hidden, down, *refs):
    blocks, (pre_grad, grads_t, sent, w_in, *refs) = refs[:count], refs[count:]
    grads, preact, block_sems, load_sem, sem = refs
    joins = join_copies(blocks, grads, block_sems)
    fetch = pltpu.make_async_copy(preact_hbm, preact, sem)
    fetch.start()
    load = pltpu.make_async_copy(w_in_hbm, w_in, load_sem)
    load.start()
    units = down.shape[1]
    for join in joins:
        join.wait()
    fetch.wait()
    step = 256 if units % 256 == 0 else units
    for begin in range(0, units, step):
        gate = preact[:, begin : begin + step]
        up = preact[:, units + begin : units + begin + step]
        hidden_grad = jnp.dot(
            grads[...], down[:, begin : begin + step], preferred_element_type=F32
        )
        sigmoid = 1.0 / (1.0 + jnp.exp(-gate))
        gate_grad = hidden_grad * up * sigmoid * (1.0 + gate * (1.0 - sigmoid))
        up_grad = hidden_grad * gate * sigmoid
        pre_grad[:, begin : begin + step] = gate_grad.astype(BF16)
        pre_grad[:, units + begin : units + begin + step] = up_grad.astype(BF16)
    transpose_into(grads, grads_t)
    write_shares(at, rows_t, grads_t, pre_grad, hidden, sent)
    load.wait()


def return_kernel(count, alone, pre_grad, w_in, *refs):
    blocks, outs, sems = refs[:count], refs[count : 2 * count], refs[-1]
    size = blocks[0].shape[0]
    copies = [
        pltpu.make_async_copy(block, out.at[pl.ds(0, size)], sems.at[n])
        for n, (block, out) in enumerate(zip(blocks, outs))
        if n != alone
    ]
    for copy in copies:
        copy.start()
    for columns in column_steps(w_in.shape[0]):
        part = lax.dot_general(
            pre_grad[...], w_in[columns, :], (((1,), (1,)), ((), ())), preferred_element_type=F32
        ).astype(BF16)
        for n, out in enumerate(outs):
            out[out.shape[0] - size :, columns] = part[n * size : (n + 1) * size]
    for copy in copies:
        copy.wait()


def returns(pre_grad, w_in, produced, alone):
    count = len(produced)
    size, width = produced[0].shape
    return pl.pallas_call(
        functools.partial(return_kernel, count, alone),
        out_shape=[
            jax.ShapeDtypeStruct((size if n == alone else 2 * size, width), BF16)
            for n in range(count)
        ],
        in_specs=whole(2) + anywhere(count),
        out_specs=whole(count),
        scratch_shapes=[pltpu.SemaphoreType.DMA((count,))],
        compiler_params=ROOMY,
        cost_estimate=BRIEF,
    )(pre_grad, w_in, *produced)


def anywhere(count):
    return [pl.BlockSpec(memory_space=pl.ANY)] * count


def in_hbm(count):
    return [pl.BlockSpec(memory_space=pltpu.HBM)] * count


def backward(at, share, preact, w_in, rows_t, hidden, down, blocks):
    width, units = down.shape
    slots = preact.shape[0]
    count = len(blocks)
    return pl.pallas_call(
        functools.partial(backward_kernel, count),
        out_shape=(
            jax.ShapeDtypeStruct((slots, 2 * units), BF16),
            jax.ShapeDtypeStruct((width, slots), BF16),
            jax.ShapeDtypeStruct((at.shape[0], share, 3 * units // 2), BF16),
            jax.ShapeDtypeStruct(w_in.shape, BF16),
        ),
        in_specs=[pl.BlockSpec(memory_space=pltpu.SMEM)]
        + anywhere(2)
        + whole(3)
        + anywhere(count),
        out_specs=whole(4),
        scratch_shapes=[
            pltpu.VMEM((slots, width), BF16),
            pltpu.VMEM((slots, 2 * units), F32),
            pltpu.SemaphoreType.DMA((count,)),
            pltpu.SemaphoreType.DMA,
            pltpu.SemaphoreType.DMA,
        ],
        compiler_params=BIG,
        cost_estimate=BRIEF,
    )(at, preact, w_in, rows_t, hidden, down, *blocks)


def shares(at, share, rows_t, grads_t, pre_grad, hidden, cost):
    units = hidden.shape[1]
    return pl.pallas_call(
        write_shares,
        out_shape=jax.ShapeDtypeStruct((at.shape[0], share, 3 * units // 2), BF16),
        in_specs=[pl.BlockSpec(memory_space=pltpu.SMEM)] + whole(4),
        out_specs=whole(1)[0],
        compiler_params=ROOMY,
        cost_estimate=cost,
    )(at, rows_t, grads_t, pre_grad, hidden)


def add_kernel(kept, got, left, right):
    half = left.shape[0]
    left[...] = add(kept[:half], got[:half]).astype(BF16)
    right[...] = add(kept[half:], got[half : 2 * half]).astype(BF16)


def next_kernel(kept, got, left_in, right_in, left_send, right_send):
    first = got.shape[0] // 2
    left_send[...] = (add(kept[1], got[first + 1]) + left_in[1].astype(F32)).astype(BF16)
    right_send[...] = (add(kept[3], got[first + 3]) + right_in[1].astype(F32)).astype(BF16)


def own_kernel(kept, got, left_in, right_in, left, right):
    first = got.shape[0] // 2
    left[...] = add(kept[0], got[first]) + left_in[0].astype(F32)
    right[...] = add(kept[2], got[first + 2]) + right_in[0].astype(F32)


def add(left, right):
    return left.astype(F32) + right.astype(F32)


CUBE_SEND = (3, 7, 5, 7, 1, 5, 1, 3)


def swap(block, bit):
    return lax.ppermute(block, "dp", [(at, at ^ bit) for at in range(lax.axis_size("dp"))])


def cube_sum(got, kept_first, kept_later):
    _, share, columns = got.shape

    def run(kernel, out_shape, inputs, cost=BRIEF):
        return pl.pallas_call(
            kernel,
            out_shape=out_shape,
            in_specs=whole(len(inputs)),
            out_specs=whole(len(out_shape)),
            compiler_params=ROOMY,
            cost_estimate=cost,
        )(*inputs)

    half = jax.ShapeDtypeStruct((2, share, columns), BF16)
    one = jax.ShapeDtypeStruct((share, columns), BF16)
    own = jax.ShapeDtypeStruct((share, columns), F32)
    left, right = run(add_kernel, (half, half), (kept_first, got))
    parts = (kept_later, got, swap(left, 2), swap(right, 4))
    left_send, right_send = run(next_kernel, (one, one), parts)
    left, right = run(own_kernel, (own, own), parts, COVER)
    return left, swap(left_send, 4), right, swap(right_send, 2)


def after(value, *others):
    return lax.optimization_barrier((value, *others))[0]


def partial_kernel(experts, capacity, alone, late, first, routes, scores, *refs):
    own, early, mixed, back, late_picker, scales = refs
    slots, toks = experts * capacity, mixed.shape[0]
    places = lax.broadcasted_iota(jnp.int32, (toks, slots), 1).astype(F32)
    hits = [
        places == to_column(row) for row in slot_rows(first[0], routes[...], experts, capacity)
    ]
    hits.append(functools.reduce(jnp.logical_or, hits))
    picker = jnp.concatenate([hit.astype(F32).astype(BF16) for hit in hits], axis=0)
    weights = weight_rows(scores[...])
    for k in range(scales.shape[0]):
        scales[k] = jnp.broadcast_to(to_column(weights[k : k + 1, :]), scales.shape[1:])

    def slots_of(blocks):
        parts = [picker[:, n * capacity : (n + 1) * capacity] for n in blocks]
        return jnp.concatenate(parts, axis=1)

    late_picker[...] = slots_of(late + [alone])
    now = slots_of((0, alone))
    for columns in column_steps(mixed.shape[1]):
        outputs = jnp.concatenate([own[:capacity, columns], early[:, columns]], axis=0)
        total, grad = sum_rows(now, scales, outputs, own[capacity:, columns])
        mixed[:, columns] = total
        back[:, columns] = grad


def sum_rows(picker, scales, outputs, gradients):
    tops, toks = scales.shape[:2]
    chosen = picker[: tops * toks, : outputs.shape[0]]
    picked = jnp.dot(chosen, outputs, preferred_element_type=F32)
    total = sum(scales[k, :, :1] * picked[k * toks : (k + 1) * toks] for k in range(tops))
    either = picker[tops * toks :, : gradients.shape[0]]
    return total, jnp.dot(either, gradients, preferred_element_type=F32)


def mean_kernel(count, left, left_last, right, right_last, wide, narrow):
    middle, edge = wide.shape[1] // 2, narrow.shape[1] // 2
    for at, (own, last) in enumerate(((left, left_last), (right, right_last))):
        total = (own[...] + last[...].astype(F32)) / count
        wide[:, at * middle : (at + 1) * middle] = total[:, :middle]
        narrow[:, at * edge : (at + 1) * edge] = total[:, middle:]


def means(count, sums):
    share, columns = sums[0].shape
    return pl.pallas_call(
        functools.partial(mean_kernel, count),
        out_shape=(
            jax.ShapeDtypeStruct((share, 4 * columns // 3), F32),
            jax.ShapeDtypeStruct((share, 2 * columns // 3), F32),
        ),
        in_specs=whole(4),
        out_specs=whole(2),
        compiler_params=ROOMY,
        cost_estimate=BRIEF,
    )(*sums)


def last_kernel(capacity, number, picker, scales, mixed_part, back_part, *refs):
    blocks, (mixed, back), (mixed_vmem, back_vmem, sems) = (
        refs[:number],
        refs[number : number + 2],
        refs[number + 2 :],
    )
    stores = []
    for c, columns in enumerate(column_steps(mixed.shape[1])):
        outputs = jnp.concatenate([block[:capacity, columns] for block in blocks[:-1]], axis=0)
        gradients = jnp.concatenate(
            [block[block.shape[0] - capacity :, columns] for block in blocks], axis=0
        )
        total, grad = sum_rows(picker[...], scales, outputs, gradients)
        mixed_vmem[:, columns] = (total + mixed_part[:, columns]).astype(BF16)
        back_vmem[:, columns] = (grad + back_part[:, columns]).astype(BF16)
        for n, (source, target) in enumerate(((mixed_vmem, mixed), (back_vmem, back))):
            stores.append(
                pltpu.make_async_copy(source.at[:, columns], target.at[:, columns], sems.at[c, n])
            )
            stores[-1].start()
    for stored in stores:
        stored.wait()


def last(capacity, parts, blocks):
    toks, width = parts[-1].shape
    out_shape = jax.ShapeDtypeStruct((toks, width), BF16)
    return pl.pallas_call(
        functools.partial(last_kernel, capacity, len(blocks)),
        out_shape=(out_shape, out_shape),
        in_specs=whole(4 + len(blocks)),
        out_specs=anywhere(2),
        scratch_shapes=[pltpu.VMEM((toks, width), BF16)] * 2
        + [pltpu.SemaphoreType.DMA((len(column_steps(width)), 2))],
        compiler_params=ROOMY,
        cost_estimate=BRIEF,
    )(*parts, *blocks)


def dispatch(experts, capacity, out_shape, first, *sources):
    weighted = len(sources) > 2
    return pl.pallas_call(
        functools.partial(dispatch_kernel, experts, capacity, weighted),
        out_shape=out_shape,
        in_specs=[pl.BlockSpec(memory_space=pltpu.SMEM)] + in_hbm(len(sources)),
        out_specs=anywhere(len(out_shape)),
        scratch_shapes=[pltpu.VMEM(out.shape, out.dtype) for out in out_shape]
        + [pltpu.VMEM(source.shape, source.dtype) for source in sources]
        + [
            pltpu.SemaphoreType.DMA((len(sources),)),
            pltpu.SemaphoreType.DMA((len(column_steps(out_shape[0].shape[1])), len(out_shape))),
        ],
        compiler_params=ALONE,
        cost_estimate=BRIEF,
    )(first, *sources)


def call(kernel, out_shape, inputs):
    return pl.pallas_call(
        kernel,
        out_shape=out_shape,
        in_specs=[pl.BlockSpec(memory_space=pltpu.SMEM)]
        + [pl.BlockSpec(memory_space=pltpu.VMEM)] * (len(inputs) - 1),
        compiler_params=ROOMY,
        cost_estimate=BRIEF,
    )(*inputs)


def body(tokens, routes, route_scores, out_grad, gate_up, down_weight):
    experts = lax.axis_size("expert")
    groups = lax.axis_size("dp")
    toks, width = tokens.shape
    tops = routes.shape[1]
    units = down_weight.shape[2]
    capacity = (toks * tops + experts - 1) // experts
    slots = experts * capacity
    share = width // groups
    direct = experts <= 8 and capacity % 16 == 0
    w_in, w_out = gate_up[0], down_weight[0]
    routes_t, scores_t = routes.T, route_scores.T
    me = lax.axis_index("expert") if direct else jnp.int32(0)
    first = me.astype(jnp.int32).reshape(1)
    sizes = [capacity] * experts if direct else [slots]
    block_shapes = [jax.ShapeDtypeStruct((size, width), BF16) for size in sizes]

    def travel(block, step, sign):
        pairs = [(at, (at + sign * step) % experts) for at in range(experts)]
        return lax.ppermute(block, "expert", pairs)

    def exchange(blocks, sign):
        if not direct:
            block = blocks[0].reshape(experts, capacity, width)
            moved = lax.all_to_all(block, "expert", split_axis=0, concat_axis=0, tiled=True)
            return [moved.reshape(slots, width)]
        steps = range(1, experts) if sign > 0 else range(experts - 1, 0, -1)
        moved = {step: travel(blocks[step], step, sign) for step in steps}
        return [blocks[0]] + [moved[step] for step in range(1, experts)]

    def joined(blocks):
        return blocks[0] if len(blocks) == 1 else jnp.concatenate(blocks, axis=0)

    def split(rows):
        return [rows[at : at + sizes[0]] for at in range(0, slots, sizes[0])]

    sent_rows = dispatch(experts, capacity, block_shapes, first, routes_t, tokens)
    got_rows = exchange(sent_rows, 1)
    sent_grads = dispatch(experts, capacity, block_shapes, first, routes_t, scores_t, out_grad)
    out_shape = jax.ShapeDtypeStruct((toks, width), BF16)
    cube = direct and experts == 4 and groups == 8 and share % 256 == 0
    if cube:
        sent_grads = after(sent_grads, got_rows[1], got_rows[-1])
        got_grads = exchange(sent_grads, 1)
        rows_t, preact, hidden, produced = forward(got_rows, w_in, w_out)
        got_grads = after(got_grads, hidden)
        own = lax.axis_index("dp")
        send_at = jnp.stack([jnp.bitwise_xor(own, j) for j in CUBE_SEND]).astype(jnp.int32)
        keep_at = jnp.bitwise_xor(send_at, 1)
        early = experts - 1
        early_out = travel(produced[early], early, -1)
        pre_grad, grads_t, sent, w_in_here = backward(
            send_at, share, preact, w_in, rows_t, hidden, w_out, got_grads
        )
        operands = (share, rows_t, grads_t, pre_grad, hidden)
        got = swap(sent, 1)
        blocks = returns(after(pre_grad, sent), w_in_here, produced, early)
        half = len(CUBE_SEND) // 2
        kept_first = shares(after(keep_at[:half], blocks[0]), *operands, COVER)
        returned = exchange(blocks, -1)
        kept_later = shares(after(keep_at[half:], kept_first, early_out, got), *operands, COVER)
        sums = cube_sum(got, kept_first, kept_later)
        late = [n for n in range(experts - 1, 0, -1) if n != early]
        mixed_part, back_part, picker, scales = call(
            functools.partial(partial_kernel, experts, capacity, early, late),
            (
                jax.ShapeDtypeStruct((toks, width), F32),
                jax.ShapeDtypeStruct((toks, width), F32),
                jax.ShapeDtypeStruct(((tops + 1) * toks, (len(late) + 1) * capacity), BF16),
                jax.ShapeDtypeStruct((tops, toks, 128), F32),
            ),
            (after(first, sums[0]), routes_t, scores_t, returned[0], early_out),
        )
        grad_in, grad_down = means(groups, sums)
        parts = (after(picker, grad_in), scales, mixed_part, back_part)
        mixed_out, token_grad = last(capacity, parts, [returned[n] for n in late + [early]])
    else:
        token_rows = joined(got_rows)
        grad_rows = joined(exchange(sent_grads, 1))
        preact = jnp.dot(token_rows, w_in, preferred_element_type=F32)
        gate, up = preact[:, :units], preact[:, units:]
        hidden = (jax.nn.silu(gate) * up).astype(BF16)
        produced = jnp.dot(hidden, w_out.T, preferred_element_type=F32).astype(BF16)
        returned = exchange(split(produced), -1)
        hidden_grad = jnp.dot(grad_rows, w_out, preferred_element_type=F32)
        sigmoid = jax.nn.sigmoid(gate)
        gate_grad = hidden_grad * up * sigmoid * (1.0 + gate * (1.0 - sigmoid))
        up_grad = hidden_grad * gate * sigmoid
        pre_grad = jnp.concatenate([gate_grad, up_grad], axis=1).astype(BF16)
        input_grad = jnp.dot(pre_grad, w_in.T, preferred_element_type=F32).astype(BF16)
        sent_back = exchange(split(input_grad), -1)

        def summed(left, right):
            part = contract(left, right).astype(BF16)
            total = lax.psum_scatter(part, "dp", scatter_dimension=0, tiled=True)
            return total.astype(F32) / groups

        grad_in = summed(token_rows, pre_grad)
        grad_down = summed(grad_rows, hidden)
        mixed_out = call(
            functools.partial(combine_kernel, experts, capacity, True),
            out_shape,
            (first, routes_t, scores_t, *returned),
        )
        token_grad = call(
            functools.partial(combine_kernel, experts, capacity, False),
            out_shape,
            (first, routes_t, *sent_back),
        )
    grad_in = grad_in.reshape(1, share, 2 * units)
    grad_down = grad_down.reshape(1, share, units)
    return (mixed_out, token_grad, grad_in, grad_down)


def solution(mesh):
    in_specs = (
        P(("dp", "expert"), None),
        P(("dp", "expert"), None),
        P(("dp", "expert"), None),
        P(("dp", "expert"), None),
        P("expert", None, None),
        P("expert", None, None),
    )
    out_specs = (
        P(("dp", "expert"), None),
        P(("dp", "expert"), None),
        P("expert", "dp", None),
        P("expert", "dp", None),
    )
    return jax.shard_map(body, mesh=mesh, in_specs=in_specs, out_specs=out_specs, check_vma=False)
```

```python
import functools

import jax
import jax.numpy as jnp
from jax import lax
from jax.experimental import pallas as pl
from jax.experimental.pallas import tpu as pltpu
from jax.sharding import PartitionSpec as P

F32 = jnp.float32
BF16 = jnp.bfloat16
BRIEF = pl.CostEstimate(flops=1024, bytes_accessed=1024, transcendentals=0)
COVER = pl.CostEstimate(flops=4 * 10**10, bytes_accessed=1024, transcendentals=0)
ROOMY = pltpu.CompilerParams(vmem_limit_bytes=16 * 1024 * 1024)
BIG = pltpu.CompilerParams(vmem_limit_bytes=28 * 1024 * 1024)
ALONE = pltpu.CompilerParams(vmem_limit_bytes=60 * 1024 * 1024)


def contract(left, right):
    return lax.dot_general(left, right, (((0,), (0,)), ((), ())), preferred_element_type=F32)


def slot_rows(first, routes, experts, capacity):
    tops, toks = routes.shape
    padded = -(-experts // 8) * 8
    rows = lax.broadcasted_iota(jnp.int32, (padded, toks), 0)
    ids = rows + first
    ids = jnp.where(ids >= experts, ids - experts, ids)
    ids = jnp.where(rows < experts, ids, -1)
    hits = [routes[k : k + 1, :] == ids for k in range(tops)]
    named = functools.reduce(jnp.logical_or, hits)
    before = lax.broadcasted_iota(jnp.int32, (toks, toks), 0) < lax.broadcasted_iota(
        jnp.int32, (toks, toks), 1
    )
    position = jnp.dot(
        named.astype(F32).astype(BF16),
        before.astype(F32).astype(BF16),
        preferred_element_type=F32,
    )
    slot = position + (rows * capacity).astype(F32)
    return [jnp.sum(jnp.where(hit, slot, 0.0), axis=0, keepdims=True) for hit in hits]


def weight_rows(scores):
    grown = jnp.exp(scores)
    return grown / jnp.sum(grown, axis=0, keepdims=True)


def to_column(row):
    toks = row.shape[1]
    same = lax.broadcasted_iota(jnp.int32, (toks, toks), 0) == lax.broadcasted_iota(
        jnp.int32, (toks, toks), 1
    )
    return jnp.sum(jnp.where(same, row, 0.0), axis=1, keepdims=True)


def put_blocks(outs, rows, columns):
    start = 0
    for out in outs:
        size = out.shape[0]
        out[:, columns] = rows[start : start + size]
        start += size


def column_steps(width):
    step = 512 if width % 512 == 0 else width
    return [slice(at, at + step) for at in range(0, width, step)]


def dispatch_kernel(experts, capacity, weighted, first, *refs):
    count = 2 + weighted
    sources, refs = refs[:count], refs[count:]
    number = (len(refs) - count - 2) // 2
    outs, ready, (*held, sems, out_sems) = refs[:number], refs[number : 2 * number], refs[2 * number :]
    copies = [
        pltpu.make_async_copy(source, place, sems.at[n])
        for n, (source, place) in enumerate(zip(sources, held))
    ]
    for copy in copies:
        copy.start()
    routes, values = held[0], held[-1]
    scores = held[1] if weighted else None
    for copy in copies[:-1]:
        copy.wait()
    slots, toks = experts * capacity, values.shape[0]
    places = lax.broadcasted_iota(jnp.int32, (slots, toks), 0).astype(F32)
    hits = [places == row for row in slot_rows(first[0], routes[...], experts, capacity)]
    picker = functools.reduce(jnp.logical_or, hits).astype(F32).astype(BF16)
    if weighted:
        weights = weight_rows(scores[...])
        scale = sum(
            jnp.sum(jnp.where(hit, weights[k : k + 1, :], 0.0), axis=1, keepdims=True)
            for k, hit in enumerate(hits)
        )
    copies[-1].wait()
    stores = []
    for c, columns in enumerate(column_steps(values.shape[1])):
        rows = jnp.dot(picker, values[:, columns], preferred_element_type=F32)
        if weighted:
            rows = rows * scale
        put_blocks(ready, rows.astype(BF16), columns)
        for n, (block, out) in enumerate(zip(ready, outs)):
            stores.append(
                pltpu.make_async_copy(block.at[:, columns], out.at[:, columns], out_sems.at[c, n])
            )
            stores[-1].start()
    for store in stores:
        store.wait()


def combine_kernel(experts, capacity, weighted, first, routes, *refs):
    scores = refs[0] if weighted else None
    blocks, out = refs[weighted:-1], refs[-1]
    slots, toks = experts * capacity, out.shape[0]
    places = lax.broadcasted_iota(jnp.int32, (toks, slots), 1).astype(F32)
    hits = [
        places == to_column(row) for row in slot_rows(first[0], routes[...], experts, capacity)
    ]
    if weighted:
        weights = weight_rows(scores[...])
        scales = [to_column(weights[k : k + 1, :]) for k in range(len(hits))]
        pickers = [hit.astype(F32).astype(BF16) for hit in hits]
    else:
        pickers = [functools.reduce(jnp.logical_or, hits).astype(F32).astype(BF16)]
    for columns in column_steps(out.shape[1]):
        rows = [block[:, columns] for block in blocks]
        rows = rows[0] if len(rows) == 1 else jnp.concatenate(rows, axis=0)
        picked = [jnp.dot(picker, rows, preferred_element_type=F32) for picker in pickers]
        if weighted:
            picked = [scale * part for scale, part in zip(scales, picked)]
        out[:, columns] = sum(picked).astype(out.dtype)


def whole(count):
    return [pl.BlockSpec(memory_space=pltpu.VMEM)] * count


def write_shares(at, rows_t, grads_t, pre_grad, hidden, out):
    share = out.shape[1]
    wide, narrow = pre_grad.shape[1] // 2, hidden.shape[1] // 2

    def write(t, half):
        own = pl.ds(pl.multiple_of(at[t] * share, share), share)
        out[t, :, :wide] = jnp.dot(
            rows_t[own, :],
            pre_grad[:, half * wide : (half + 1) * wide],
            preferred_element_type=F32,
        ).astype(out.dtype)
        out[t, :, wide:] = jnp.dot(
            grads_t[own, :],
            hidden[:, half * narrow : (half + 1) * narrow],
            preferred_element_type=F32,
        ).astype(out.dtype)

    for t in range(out.shape[0]):
        write(t, t // 2 % 2)


def side_by_side(blocks, columns):
    if len(blocks) == 1:
        return blocks[0][:, columns]
    return jnp.concatenate([block[:, columns] for block in blocks], axis=0)


def transpose_into(blocks, rows_t):
    width = rows_t.shape[0]
    step = 256 if width % 256 == 0 else width

    for begin in range(0, width, step):
        rows_t[begin : begin + step, :] = side_by_side(blocks, slice(begin, begin + step)).T


def join_copies(blocks, rows, sems):
    size = blocks[0].shape[0]
    joins = [
        pltpu.make_async_copy(block, rows.at[pl.ds(n * size, size)], sems.at[n])
        for n, block in enumerate(blocks)
    ]
    for join in joins:
        join.start()
    return joins


def forward_kernel(count, *refs):
    blocks, (w_in_hbm, down_hbm), (rows_t, preact, hidden), outs, scratch = (
        refs[:count],
        refs[count : count + 2],
        refs[count + 2 : count + 5],
        refs[count + 5 : 2 * count + 5],
        refs[2 * count + 5 :],
    )
    rows, w_in, down, block_sems, weight_sems, down_sem = scratch
    joins = join_copies(blocks, rows, block_sems)
    width, units = down.shape
    step = 256 if units % 256 == 0 else units
    loads = []
    for n in range(2 * units // step):
        begin = (n % 2) * units + n // 2 * step
        loads.append(
            pltpu.make_async_copy(
                w_in_hbm.at[:, pl.ds(begin, step)],
                w_in.at[:, pl.ds(begin, step)],
                weight_sems.at[n],
            )
        )
        loads[-1].start()
    load_down = pltpu.make_async_copy(down_hbm, down, down_sem)
    load_down.start()
    for join in joins:
        join.wait()
    for n in range(units // step):
        begin = n * step
        gate_at, up_at = slice(begin, begin + step), slice(units + begin, units + begin + step)
        loads[2 * n].wait()
        gate = jnp.dot(rows[...], w_in[:, gate_at], preferred_element_type=F32)
        loads[2 * n + 1].wait()
        up = jnp.dot(rows[...], w_in[:, up_at], preferred_element_type=F32)
        preact[:, gate_at] = gate
        preact[:, up_at] = up
        hidden[:, gate_at] = (gate / (1.0 + jnp.exp(-gate)) * up).astype(BF16)
    load_down.wait()
    for columns in column_steps(width):
        part = lax.dot_general(
            hidden[...], down[columns, :], (((1,), (1,)), ((), ())), preferred_element_type=F32
        )
        put_blocks(outs, part.astype(BF16), columns)
    transpose_into([rows], rows_t)


def forward(blocks, w_in, down):
    width, units = down.shape
    slots = sum(block.shape[0] for block in blocks)
    count = len(blocks)
    rows_t, preact, hidden, *outs = pl.pallas_call(
        functools.partial(forward_kernel, count),
        out_shape=(
            jax.ShapeDtypeStruct((width, slots), BF16),
            jax.ShapeDtypeStruct((slots, 2 * units), F32),
            jax.ShapeDtypeStruct((slots, units), BF16),
            *[jax.ShapeDtypeStruct(block.shape, BF16) for block in blocks],
        ),
        in_specs=anywhere(count) + in_hbm(2),
        out_specs=whole(3 + count),
        scratch_shapes=[
            pltpu.VMEM((slots, width), BF16),
            pltpu.VMEM(w_in.shape, BF16),
            pltpu.VMEM(down.shape, BF16),
            pltpu.SemaphoreType.DMA((count,)),
            pltpu.SemaphoreType.DMA((2 * units // min(units, 256),)),
            pltpu.SemaphoreType.DMA,
        ],
        compiler_params=pltpu.CompilerParams(vmem_limit_bytes=46 * 1024 * 1024),
        cost_estimate=BRIEF,
    )(*blocks, w_in, down)
    return rows_t, preact, hidden, outs


def backward_kernel(count, at, preact_hbm, w_in_hbm, rows_t, hidden, down, *refs):
    blocks, (pre_grad, grads_t, sent, w_in, *refs) = refs[:count], refs[count:]
    preact, load_sem, sem = refs
    fetch = pltpu.make_async_copy(preact_hbm, preact, sem)
    fetch.start()
    load = pltpu.make_async_copy(w_in_hbm, w_in, load_sem)
    load.start()
    units = down.shape[1]
    grads = side_by_side(blocks, slice(0, down.shape[0]))
    step = 256 if units % 256 == 0 else units
    for begin in range(0, units, step):
        hidden_grad = jnp.dot(grads, down[:, begin : begin + step], preferred_element_type=F32)
        if begin == 0:
            fetch.wait()
        gate = preact[:, begin : begin + step]
        up = preact[:, units + begin : units + begin + step]
        sigmoid = 1.0 / (1.0 + jnp.exp(-gate))
        gate_grad = hidden_grad * up * sigmoid * (1.0 + gate * (1.0 - sigmoid))
        up_grad = hidden_grad * gate * sigmoid
        pre_grad[:, begin : begin + step] = gate_grad.astype(BF16)
        pre_grad[:, units + begin : units + begin + step] = up_grad.astype(BF16)
    transpose_into(blocks, grads_t)
    write_shares(at, rows_t, grads_t, pre_grad, hidden, sent)
    load.wait()


def return_kernel(count, alone, pre_grad, w_in, *refs):
    blocks, outs, sems = refs[:count], refs[count : 2 * count], refs[-1]
    size = blocks[0].shape[0]
    copies = [
        pltpu.make_async_copy(block, out.at[pl.ds(0, size)], sems.at[n])
        for n, (block, out) in enumerate(zip(blocks, outs))
        if n != alone
    ]
    for copy in copies:
        copy.start()
    for columns in column_steps(w_in.shape[0]):
        part = lax.dot_general(
            pre_grad[...], w_in[columns, :], (((1,), (1,)), ((), ())), preferred_element_type=F32
        ).astype(BF16)
        for n, out in enumerate(outs):
            out[out.shape[0] - size :, columns] = part[n * size : (n + 1) * size]
    for copy in copies:
        copy.wait()


def returns(pre_grad, w_in, produced, alone):
    count = len(produced)
    size, width = produced[0].shape
    return pl.pallas_call(
        functools.partial(return_kernel, count, alone),
        out_shape=[
            jax.ShapeDtypeStruct((size if n == alone else 2 * size, width), BF16)
            for n in range(count)
        ],
        in_specs=whole(2) + anywhere(count),
        out_specs=whole(count),
        scratch_shapes=[pltpu.SemaphoreType.DMA((count,))],
        compiler_params=ROOMY,
        cost_estimate=BRIEF,
    )(pre_grad, w_in, *produced)


def anywhere(count):
    return [pl.BlockSpec(memory_space=pl.ANY)] * count


def in_hbm(count):
    return [pl.BlockSpec(memory_space=pltpu.HBM)] * count


def backward(at, share, preact, w_in, rows_t, hidden, down, blocks):
    width, units = down.shape
    slots = preact.shape[0]
    count = len(blocks)
    return pl.pallas_call(
        functools.partial(backward_kernel, count),
        out_shape=(
            jax.ShapeDtypeStruct((slots, 2 * units), BF16),
            jax.ShapeDtypeStruct((width, slots), BF16),
            jax.ShapeDtypeStruct((at.shape[0], share, 3 * units // 2), BF16),
            jax.ShapeDtypeStruct(w_in.shape, BF16),
        ),
        in_specs=[pl.BlockSpec(memory_space=pltpu.SMEM)]
        + anywhere(2)
        + whole(3 + count),
        out_specs=whole(4),
        scratch_shapes=[
            pltpu.VMEM((slots, 2 * units), F32),
            pltpu.SemaphoreType.DMA,
            pltpu.SemaphoreType.DMA,
        ],
        compiler_params=BIG,
        cost_estimate=BRIEF,
    )(at, preact, w_in, rows_t, hidden, down, *blocks)


def shares(at, share, rows_t, grads_t, pre_grad, hidden, cost):
    units = hidden.shape[1]
    return pl.pallas_call(
        write_shares,
        out_shape=jax.ShapeDtypeStruct((at.shape[0], share, 3 * units // 2), BF16),
        in_specs=[pl.BlockSpec(memory_space=pltpu.SMEM)] + whole(4),
        out_specs=whole(1)[0],
        compiler_params=ROOMY,
        cost_estimate=cost,
    )(at, rows_t, grads_t, pre_grad, hidden)


def add_kernel(kept, got, left, right):
    half = left.shape[0]
    left[...] = add(kept[:half], got[:half]).astype(BF16)
    right[...] = add(kept[half:], got[half : 2 * half]).astype(BF16)


def next_kernel(kept, got, left_in, right_in, left_send, right_send):
    first = got.shape[0] // 2
    left_send[...] = (add(kept[1], got[first + 1]) + left_in[1].astype(F32)).astype(BF16)
    right_send[...] = (add(kept[3], got[first + 3]) + right_in[1].astype(F32)).astype(BF16)


def own_kernel(kept, got, left_in, right_in, left, right):
    first = got.shape[0] // 2
    left[...] = add(kept[0], got[first]) + left_in[0].astype(F32)
    right[...] = add(kept[2], got[first + 2]) + right_in[0].astype(F32)


def add(left, right):
    return left.astype(F32) + right.astype(F32)


CUBE_SEND = (3, 7, 5, 7, 1, 5, 1, 3)


def swap(block, bit):
    return lax.ppermute(block, "dp", [(at, at ^ bit) for at in range(lax.axis_size("dp"))])


def cube_sum(got, kept_first, kept_later):
    _, share, columns = got.shape

    def run(kernel, out_shape, inputs, cost=BRIEF):
        return pl.pallas_call(
            kernel,
            out_shape=out_shape,
            in_specs=whole(len(inputs)),
            out_specs=whole(len(out_shape)),
            compiler_params=ROOMY,
            cost_estimate=cost,
        )(*inputs)

    half = jax.ShapeDtypeStruct((2, share, columns), BF16)
    one = jax.ShapeDtypeStruct((share, columns), BF16)
    own = jax.ShapeDtypeStruct((share, columns), F32)
    left, right = run(add_kernel, (half, half), (kept_first, got))
    parts = (kept_later, got, swap(left, 2), swap(right, 4))
    left_send, right_send = run(next_kernel, (one, one), parts)
    left, right = run(own_kernel, (own, own), parts, COVER)
    return left, swap(left_send, 4), right, swap(right_send, 2)


def after(value, *others):
    return lax.optimization_barrier((value, *others))[0]


def partial_kernel(experts, capacity, alone, late, first, routes, scores, *refs):
    own, early, mixed, back, late_picker, scales = refs
    slots, toks = experts * capacity, mixed.shape[0]
    places = lax.broadcasted_iota(jnp.int32, (toks, slots), 1).astype(F32)
    hits = [
        places == to_column(row) for row in slot_rows(first[0], routes[...], experts, capacity)
    ]
    hits.append(functools.reduce(jnp.logical_or, hits))
    picker = jnp.concatenate([hit.astype(F32).astype(BF16) for hit in hits], axis=0)
    weights = weight_rows(scores[...])
    for k in range(scales.shape[0]):
        scales[k] = jnp.broadcast_to(to_column(weights[k : k + 1, :]), scales.shape[1:])

    def slots_of(blocks):
        parts = [picker[:, n * capacity : (n + 1) * capacity] for n in blocks]
        return jnp.concatenate(parts, axis=1)

    late_picker[...] = slots_of(late + [alone])
    now = slots_of((0, alone))
    for columns in column_steps(mixed.shape[1]):
        outputs = jnp.concatenate([own[:capacity, columns], early[:, columns]], axis=0)
        total, grad = sum_rows(now, scales, outputs, own[capacity:, columns])
        mixed[:, columns] = total
        back[:, columns] = grad


def sum_rows(picker, scales, outputs, gradients):
    tops, toks = scales.shape[:2]
    chosen = picker[: tops * toks, : outputs.shape[0]]
    picked = jnp.dot(chosen, outputs, preferred_element_type=F32)
    total = sum(scales[k, :, :1] * picked[k * toks : (k + 1) * toks] for k in range(tops))
    either = picker[tops * toks :, : gradients.shape[0]]
    return total, jnp.dot(either, gradients, preferred_element_type=F32)


def mean_kernel(count, left, left_last, right, right_last, wide, narrow):
    middle, edge = wide.shape[1] // 2, narrow.shape[1] // 2
    for at, (own, last) in enumerate(((left, left_last), (right, right_last))):
        total = (own[...] + last[...].astype(F32)) / count
        wide[:, at * middle : (at + 1) * middle] = total[:, :middle]
        narrow[:, at * edge : (at + 1) * edge] = total[:, middle:]


def means(count, sums):
    share, columns = sums[0].shape
    return pl.pallas_call(
        functools.partial(mean_kernel, count),
        out_shape=(
            jax.ShapeDtypeStruct((share, 4 * columns // 3), F32),
            jax.ShapeDtypeStruct((share, 2 * columns // 3), F32),
        ),
        in_specs=whole(4),
        out_specs=whole(2),
        compiler_params=ROOMY,
        cost_estimate=BRIEF,
    )(*sums)


def last_kernel(capacity, number, picker, scales, mixed_part, back_part, *refs):
    blocks, (mixed, back), (mixed_vmem, back_vmem, sems) = (
        refs[:number],
        refs[number : number + 2],
        refs[number + 2 :],
    )
    stores = []
    for c, columns in enumerate(column_steps(mixed.shape[1])):
        outputs = jnp.concatenate([block[:capacity, columns] for block in blocks[:-1]], axis=0)
        gradients = jnp.concatenate(
            [block[block.shape[0] - capacity :, columns] for block in blocks], axis=0
        )
        total, grad = sum_rows(picker[...], scales, outputs, gradients)
        mixed_vmem[:, columns] = (total + mixed_part[:, columns]).astype(BF16)
        back_vmem[:, columns] = (grad + back_part[:, columns]).astype(BF16)
        for n, (source, target) in enumerate(((mixed_vmem, mixed), (back_vmem, back))):
            stores.append(
                pltpu.make_async_copy(source.at[:, columns], target.at[:, columns], sems.at[c, n])
            )
            stores[-1].start()
    for stored in stores:
        stored.wait()


def last(capacity, parts, blocks):
    toks, width = parts[-1].shape
    out_shape = jax.ShapeDtypeStruct((toks, width), BF16)
    return pl.pallas_call(
        functools.partial(last_kernel, capacity, len(blocks)),
        out_shape=(out_shape, out_shape),
        in_specs=whole(4 + len(blocks)),
        out_specs=anywhere(2),
        scratch_shapes=[pltpu.VMEM((toks, width), BF16)] * 2
        + [pltpu.SemaphoreType.DMA((len(column_steps(width)), 2))],
        compiler_params=ROOMY,
        cost_estimate=BRIEF,
    )(*parts, *blocks)


def dispatch(experts, capacity, out_shape, first, *sources):
    weighted = len(sources) > 2
    return pl.pallas_call(
        functools.partial(dispatch_kernel, experts, capacity, weighted),
        out_shape=out_shape,
        in_specs=[pl.BlockSpec(memory_space=pltpu.SMEM)] + in_hbm(len(sources)),
        out_specs=anywhere(len(out_shape)),
        scratch_shapes=[pltpu.VMEM(out.shape, out.dtype) for out in out_shape]
        + [pltpu.VMEM(source.shape, source.dtype) for source in sources]
        + [
            pltpu.SemaphoreType.DMA((len(sources),)),
            pltpu.SemaphoreType.DMA((len(column_steps(out_shape[0].shape[1])), len(out_shape))),
        ],
        compiler_params=ALONE,
        cost_estimate=BRIEF,
    )(first, *sources)


def call(kernel, out_shape, inputs):
    return pl.pallas_call(
        kernel,
        out_shape=out_shape,
        in_specs=[pl.BlockSpec(memory_space=pltpu.SMEM)]
        + [pl.BlockSpec(memory_space=pltpu.VMEM)] * (len(inputs) - 1),
        compiler_params=ROOMY,
        cost_estimate=BRIEF,
    )(*inputs)


def body(tokens, routes, route_scores, out_grad, gate_up, down_weight):
    experts = lax.axis_size("expert")
    groups = lax.axis_size("dp")
    toks, width = tokens.shape
    tops = routes.shape[1]
    units = down_weight.shape[2]
    capacity = (toks * tops + experts - 1) // experts
    slots = experts * capacity
    share = width // groups
    direct = experts <= 8 and capacity % 16 == 0
    w_in, w_out = gate_up[0], down_weight[0]
    routes_t, scores_t = routes.T, route_scores.T
    me = lax.axis_index("expert") if direct else jnp.int32(0)
    first = me.astype(jnp.int32).reshape(1)
    sizes = [capacity] * experts if direct else [slots]
    block_shapes = [jax.ShapeDtypeStruct((size, width), BF16) for size in sizes]

    def travel(block, step, sign):
        pairs = [(at, (at + sign * step) % experts) for at in range(experts)]
        return lax.ppermute(block, "expert", pairs)

    def exchange(blocks, sign):
        if not direct:
            block = blocks[0].reshape(experts, capacity, width)
            moved = lax.all_to_all(block, "expert", split_axis=0, concat_axis=0, tiled=True)
            return [moved.reshape(slots, width)]
        steps = range(1, experts) if sign > 0 else range(experts - 1, 0, -1)
        moved = {step: travel(blocks[step], step, sign) for step in steps}
        return [blocks[0]] + [moved[step] for step in range(1, experts)]

    def joined(blocks):
        return blocks[0] if len(blocks) == 1 else jnp.concatenate(blocks, axis=0)

    def split(rows):
        return [rows[at : at + sizes[0]] for at in range(0, slots, sizes[0])]

    sent_rows = dispatch(experts, capacity, block_shapes, first, routes_t, tokens)
    got_rows = exchange(sent_rows, 1)
    sent_grads = dispatch(experts, capacity, block_shapes, first, routes_t, scores_t, out_grad)
    out_shape = jax.ShapeDtypeStruct((toks, width), BF16)
    cube = direct and experts == 4 and groups == 8 and share % 256 == 0
    if cube:
        sent_grads = after(sent_grads, got_rows[1], got_rows[-1])
        got_grads = exchange(sent_grads, 1)
        rows_t, preact, hidden, produced = forward(got_rows, w_in, w_out)
        got_grads = after(got_grads, hidden)
        own = lax.axis_index("dp")
        send_at = jnp.stack([jnp.bitwise_xor(own, j) for j in CUBE_SEND]).astype(jnp.int32)
        keep_at = jnp.bitwise_xor(send_at, 1)
        early = experts - 1
        early_out = travel(produced[early], early, -1)
        pre_grad, grads_t, sent, w_in_here = backward(
            send_at, share, preact, w_in, rows_t, hidden, w_out, got_grads
        )
        operands = (share, rows_t, grads_t, pre_grad, hidden)
        got = swap(sent, 1)
        blocks = returns(after(pre_grad, sent), w_in_here, produced, early)
        half = len(CUBE_SEND) // 2
        kept_first = shares(after(keep_at[:half], blocks[0]), *operands, COVER)
        returned = exchange(blocks, -1)
        kept_later = shares(after(keep_at[half:], kept_first, early_out, got), *operands, COVER)
        sums = cube_sum(got, kept_first, kept_later)
        late = [n for n in range(experts - 1, 0, -1) if n != early]
        mixed_part, back_part, picker, scales = call(
            functools.partial(partial_kernel, experts, capacity, early, late),
            (
                jax.ShapeDtypeStruct((toks, width), F32),
                jax.ShapeDtypeStruct((toks, width), F32),
                jax.ShapeDtypeStruct(((tops + 1) * toks, (len(late) + 1) * capacity), BF16),
                jax.ShapeDtypeStruct((tops, toks, 128), F32),
            ),
            (after(first, sums[0]), routes_t, scores_t, returned[0], early_out),
        )
        grad_in, grad_down = means(groups, sums)
        parts = (after(picker, grad_in), scales, mixed_part, back_part)
        mixed_out, token_grad = last(capacity, parts, [returned[n] for n in late + [early]])
    else:
        token_rows = joined(got_rows)
        grad_rows = joined(exchange(sent_grads, 1))
        preact = jnp.dot(token_rows, w_in, preferred_element_type=F32)
        gate, up = preact[:, :units], preact[:, units:]
        hidden = (jax.nn.silu(gate) * up).astype(BF16)
        produced = jnp.dot(hidden, w_out.T, preferred_element_type=F32).astype(BF16)
        returned = exchange(split(produced), -1)
        hidden_grad = jnp.dot(grad_rows, w_out, preferred_element_type=F32)
        sigmoid = jax.nn.sigmoid(gate)
        gate_grad = hidden_grad * up * sigmoid * (1.0 + gate * (1.0 - sigmoid))
        up_grad = hidden_grad * gate * sigmoid
        pre_grad = jnp.concatenate([gate_grad, up_grad], axis=1).astype(BF16)
        input_grad = jnp.dot(pre_grad, w_in.T, preferred_element_type=F32).astype(BF16)
        sent_back = exchange(split(input_grad), -1)

        def summed(left, right):
            part = contract(left, right).astype(BF16)
            total = lax.psum_scatter(part, "dp", scatter_dimension=0, tiled=True)
            return total.astype(F32) / groups

        grad_in = summed(token_rows, pre_grad)
        grad_down = summed(grad_rows, hidden)
        mixed_out = call(
            functools.partial(combine_kernel, experts, capacity, True),
            out_shape,
            (first, routes_t, scores_t, *returned),
        )
        token_grad = call(
            functools.partial(combine_kernel, experts, capacity, False),
            out_shape,
            (first, routes_t, *sent_back),
        )
    grad_in = grad_in.reshape(1, share, 2 * units)
    grad_down = grad_down.reshape(1, share, units)
    return (mixed_out, token_grad, grad_in, grad_down)


def solution(mesh):
    in_specs = (
        P(("dp", "expert"), None),
        P(("dp", "expert"), None),
        P(("dp", "expert"), None),
        P(("dp", "expert"), None),
        P("expert", None, None),
        P("expert", None, None),
    )
    out_specs = (
        P(("dp", "expert"), None),
        P(("dp", "expert"), None),
        P("expert", "dp", None),
        P("expert", "dp", None),
    )
    return jax.shard_map(body, mesh=mesh, in_specs=in_specs, out_specs=out_specs, check_vma=False)
```

```python
import functools

import jax
import jax.numpy as jnp
from jax import lax
from jax.experimental import pallas as pl
from jax.experimental.pallas import tpu as pltpu
from jax.sharding import PartitionSpec as P

F32 = jnp.float32
BF16 = jnp.bfloat16
BRIEF = pl.CostEstimate(flops=1024, bytes_accessed=1024, transcendentals=0)
COVER = pl.CostEstimate(flops=4 * 10**10, bytes_accessed=1024, transcendentals=0)
ROOMY = pltpu.CompilerParams(vmem_limit_bytes=16 * 1024 * 1024)
BIG = pltpu.CompilerParams(vmem_limit_bytes=28 * 1024 * 1024)
ALONE = pltpu.CompilerParams(vmem_limit_bytes=60 * 1024 * 1024)


def contract(left, right):
    return lax.dot_general(left, right, (((0,), (0,)), ((), ())), preferred_element_type=F32)


def slot_rows(first, routes, experts, capacity):
    tops, toks = routes.shape
    padded = -(-experts // 8) * 8
    rows = lax.broadcasted_iota(jnp.int32, (padded, toks), 0)
    ids = rows + first
    ids = jnp.where(ids >= experts, ids - experts, ids)
    ids = jnp.where(rows < experts, ids, -1)
    hits = [routes[k : k + 1, :] == ids for k in range(tops)]
    named = functools.reduce(jnp.logical_or, hits)
    before = lax.broadcasted_iota(jnp.int32, (toks, toks), 0) < lax.broadcasted_iota(
        jnp.int32, (toks, toks), 1
    )
    position = jnp.dot(
        named.astype(F32).astype(BF16),
        before.astype(F32).astype(BF16),
        preferred_element_type=F32,
    )
    slot = position + (rows * capacity).astype(F32)
    return [jnp.sum(jnp.where(hit, slot, 0.0), axis=0, keepdims=True) for hit in hits]


def weight_rows(scores):
    grown = jnp.exp(scores)
    return grown / jnp.sum(grown, axis=0, keepdims=True)


def to_column(row):
    toks = row.shape[1]
    same = lax.broadcasted_iota(jnp.int32, (toks, toks), 0) == lax.broadcasted_iota(
        jnp.int32, (toks, toks), 1
    )
    return jnp.sum(jnp.where(same, row, 0.0), axis=1, keepdims=True)


def put_blocks(outs, rows, columns):
    start = 0
    for out in outs:
        size = out.shape[0]
        out[:, columns] = rows[start : start + size]
        start += size


def column_steps(width):
    step = 512 if width % 512 == 0 else width
    return [slice(at, at + step) for at in range(0, width, step)]


def dispatch_kernel(experts, capacity, weighted, first, *refs):
    count = 2 + weighted
    sources, refs = refs[:count], refs[count:]
    number = (len(refs) - count - 2) // 2
    outs, ready, (*held, sems, out_sems) = refs[:number], refs[number : 2 * number], refs[2 * number :]
    copies = [
        pltpu.make_async_copy(source, place, sems.at[n])
        for n, (source, place) in enumerate(zip(sources, held))
    ]
    for copy in copies:
        copy.start()
    routes, values = held[0], held[-1]
    scores = held[1] if weighted else None
    for copy in copies[:-1]:
        copy.wait()
    slots, toks = experts * capacity, values.shape[0]
    places = lax.broadcasted_iota(jnp.int32, (slots, toks), 0).astype(F32)
    hits = [places == row for row in slot_rows(first[0], routes[...], experts, capacity)]
    picker = functools.reduce(jnp.logical_or, hits).astype(F32).astype(BF16)
    if weighted:
        weights = weight_rows(scores[...])
        scale = sum(
            jnp.sum(jnp.where(hit, weights[k : k + 1, :], 0.0), axis=1, keepdims=True)
            for k, hit in enumerate(hits)
        )
    copies[-1].wait()
    stores = []
    for c, columns in enumerate(column_steps(values.shape[1])):
        rows = jnp.dot(picker, values[:, columns], preferred_element_type=F32)
        if weighted:
            rows = rows * scale
        put_blocks(ready, rows.astype(BF16), columns)
        for n, (block, out) in enumerate(zip(ready, outs)):
            stores.append(
                pltpu.make_async_copy(block.at[:, columns], out.at[:, columns], out_sems.at[c, n])
            )
            stores[-1].start()
    for store in stores:
        store.wait()


def combine_kernel(experts, capacity, weighted, first, routes, *refs):
    scores = refs[0] if weighted else None
    blocks, out = refs[weighted:-1], refs[-1]
    slots, toks = experts * capacity, out.shape[0]
    places = lax.broadcasted_iota(jnp.int32, (toks, slots), 1).astype(F32)
    hits = [
        places == to_column(row) for row in slot_rows(first[0], routes[...], experts, capacity)
    ]
    if weighted:
        weights = weight_rows(scores[...])
        scales = [to_column(weights[k : k + 1, :]) for k in range(len(hits))]
        pickers = [hit.astype(F32).astype(BF16) for hit in hits]
    else:
        pickers = [functools.reduce(jnp.logical_or, hits).astype(F32).astype(BF16)]
    for columns in column_steps(out.shape[1]):
        rows = [block[:, columns] for block in blocks]
        rows = rows[0] if len(rows) == 1 else jnp.concatenate(rows, axis=0)
        picked = [jnp.dot(picker, rows, preferred_element_type=F32) for picker in pickers]
        if weighted:
            picked = [scale * part for scale, part in zip(scales, picked)]
        out[:, columns] = sum(picked).astype(out.dtype)


def whole(count):
    return [pl.BlockSpec(memory_space=pltpu.VMEM)] * count


def write_shares(at, rows_t, grads_t, pre_grad, hidden, out):
    share = out.shape[1]
    wide, narrow = pre_grad.shape[1] // 2, hidden.shape[1] // 2

    def write(t, half):
        own = pl.ds(pl.multiple_of(at[t] * share, share), share)
        out[t, :, :wide] = jnp.dot(
            rows_t[own, :],
            pre_grad[:, half * wide : (half + 1) * wide],
            preferred_element_type=F32,
        ).astype(out.dtype)
        out[t, :, wide:] = jnp.dot(
            grads_t[own, :],
            hidden[:, half * narrow : (half + 1) * narrow],
            preferred_element_type=F32,
        ).astype(out.dtype)

    for t in range(out.shape[0]):
        write(t, t // 2 % 2)


def transpose_into(rows, rows_t):
    width = rows.shape[1]
    step = 256 if width % 256 == 0 else width

    for begin in range(0, width, step):
        rows_t[begin : begin + step, :] = rows[:, begin : begin + step].T


def join_copies(blocks, rows, sems):
    size = blocks[0].shape[0]
    joins = [
        pltpu.make_async_copy(block, rows.at[pl.ds(n * size, size)], sems.at[n])
        for n, block in enumerate(blocks)
    ]
    for join in joins:
        join.start()
    return joins


def forward_kernel(count, *refs):
    blocks, (w_in_hbm, down_hbm), (rows_t, preact, hidden), outs, scratch = (
        refs[:count],
        refs[count : count + 2],
        refs[count + 2 : count + 5],
        refs[count + 5 : 2 * count + 5],
        refs[2 * count + 5 :],
    )
    rows, w_in, down, block_sems, weight_sems, down_sem = scratch
    joins = join_copies(blocks, rows, block_sems)
    width, units = down.shape
    step = 256 if units % 256 == 0 else units
    loads = []
    for n in range(2 * units // step):
        begin = (n % 2) * units + n // 2 * step
        loads.append(
            pltpu.make_async_copy(
                w_in_hbm.at[:, pl.ds(begin, step)],
                w_in.at[:, pl.ds(begin, step)],
                weight_sems.at[n],
            )
        )
        loads[-1].start()
    load_down = pltpu.make_async_copy(down_hbm, down, down_sem)
    load_down.start()
    for join in joins:
        join.wait()
    for n in range(units // step):
        begin = n * step
        gate_at, up_at = slice(begin, begin + step), slice(units + begin, units + begin + step)
        loads[2 * n].wait()
        gate = jnp.dot(rows[...], w_in[:, gate_at], preferred_element_type=F32)
        loads[2 * n + 1].wait()
        up = jnp.dot(rows[...], w_in[:, up_at], preferred_element_type=F32)
        preact[:, gate_at] = gate
        preact[:, up_at] = up
        hidden[:, gate_at] = (gate / (1.0 + jnp.exp(-gate)) * up).astype(BF16)
    load_down.wait()
    for columns in column_steps(width):
        part = lax.dot_general(
            hidden[...], down[columns, :], (((1,), (1,)), ((), ())), preferred_element_type=F32
        )
        put_blocks(outs, part.astype(BF16), columns)
    transpose_into(rows, rows_t)


def forward(blocks, w_in, down):
    width, units = down.shape
    slots = sum(block.shape[0] for block in blocks)
    count = len(blocks)
    rows_t, preact, hidden, *outs = pl.pallas_call(
        functools.partial(forward_kernel, count),
        out_shape=(
            jax.ShapeDtypeStruct((width, slots), BF16),
            jax.ShapeDtypeStruct((slots, 2 * units), F32),
            jax.ShapeDtypeStruct((slots, units), BF16),
            *[jax.ShapeDtypeStruct(block.shape, BF16) for block in blocks],
        ),
        in_specs=anywhere(count) + in_hbm(2),
        out_specs=whole(3 + count),
        scratch_shapes=[
            pltpu.VMEM((slots, width), BF16),
            pltpu.VMEM(w_in.shape, BF16),
            pltpu.VMEM(down.shape, BF16),
            pltpu.SemaphoreType.DMA((count,)),
            pltpu.SemaphoreType.DMA((2 * units // min(units, 256),)),
            pltpu.SemaphoreType.DMA,
        ],
        compiler_params=pltpu.CompilerParams(vmem_limit_bytes=46 * 1024 * 1024),
        cost_estimate=BRIEF,
    )(*blocks, w_in, down)
    return rows_t, preact, hidden, outs


def backward_kernel(count, at, preact_hbm, w_in_hbm, rows_t, hidden, down, *refs):
    blocks, (pre_grad, grads_t, sent, w_in, *refs) = refs[:count], refs[count:]
    grads, preact, block_sems, load_sem, sem = refs
    joins = join_copies(blocks, grads, block_sems)
    fetch = pltpu.make_async_copy(preact_hbm, preact, sem)
    fetch.start()
    load = pltpu.make_async_copy(w_in_hbm, w_in, load_sem)
    load.start()
    units = down.shape[1]
    for join in joins:
        join.wait()
    step = 256 if units % 256 == 0 else units
    for begin in range(0, units, step):
        hidden_grad = jnp.dot(
            grads[...], down[:, begin : begin + step], preferred_element_type=F32
        )
        if begin == 0:
            fetch.wait()
        gate = preact[:, begin : begin + step]
        up = preact[:, units + begin : units + begin + step]
        sigmoid = 1.0 / (1.0 + jnp.exp(-gate))
        gate_grad = hidden_grad * up * sigmoid * (1.0 + gate * (1.0 - sigmoid))
        up_grad = hidden_grad * gate * sigmoid
        pre_grad[:, begin : begin + step] = gate_grad.astype(BF16)
        pre_grad[:, units + begin : units + begin + step] = up_grad.astype(BF16)
    transpose_into(grads, grads_t)
    write_shares(at, rows_t, grads_t, pre_grad, hidden, sent)
    load.wait()


def return_kernel(count, alone, pre_grad, w_in, *refs):
    blocks, outs, sems = refs[:count], refs[count : 2 * count], refs[-1]
    size = blocks[0].shape[0]
    copies = [
        pltpu.make_async_copy(block, out.at[pl.ds(0, size)], sems.at[n])
        for n, (block, out) in enumerate(zip(blocks, outs))
        if n != alone
    ]
    for copy in copies:
        copy.start()
    for columns in column_steps(w_in.shape[0]):
        part = lax.dot_general(
            pre_grad[...], w_in[columns, :], (((1,), (1,)), ((), ())), preferred_element_type=F32
        ).astype(BF16)
        for n, out in enumerate(outs):
            out[out.shape[0] - size :, columns] = part[n * size : (n + 1) * size]
    for copy in copies:
        copy.wait()


def returns(pre_grad, w_in, produced, alone):
    count = len(produced)
    size, width = produced[0].shape
    return pl.pallas_call(
        functools.partial(return_kernel, count, alone),
        out_shape=[
            jax.ShapeDtypeStruct((size if n == alone else 2 * size, width), BF16)
            for n in range(count)
        ],
        in_specs=whole(2) + anywhere(count),
        out_specs=whole(count),
        scratch_shapes=[pltpu.SemaphoreType.DMA((count,))],
        compiler_params=ROOMY,
        cost_estimate=BRIEF,
    )(pre_grad, w_in, *produced)


def anywhere(count):
    return [pl.BlockSpec(memory_space=pl.ANY)] * count


def in_hbm(count):
    return [pl.BlockSpec(memory_space=pltpu.HBM)] * count


def backward(at, share, preact, w_in, rows_t, hidden, down, blocks):
    width, units = down.shape
    slots = preact.shape[0]
    count = len(blocks)
    return pl.pallas_call(
        functools.partial(backward_kernel, count),
        out_shape=(
            jax.ShapeDtypeStruct((slots, 2 * units), BF16),
            jax.ShapeDtypeStruct((width, slots), BF16),
            jax.ShapeDtypeStruct((at.shape[0], share, 3 * units // 2), BF16),
            jax.ShapeDtypeStruct(w_in.shape, BF16),
        ),
        in_specs=[pl.BlockSpec(memory_space=pltpu.SMEM)]
        + anywhere(2)
        + whole(3)
        + anywhere(count),
        out_specs=whole(4),
        scratch_shapes=[
            pltpu.VMEM((slots, width), BF16),
            pltpu.VMEM((slots, 2 * units), F32),
            pltpu.SemaphoreType.DMA((count,)),
            pltpu.SemaphoreType.DMA,
            pltpu.SemaphoreType.DMA,
        ],
        compiler_params=BIG,
        cost_estimate=BRIEF,
    )(at, preact, w_in, rows_t, hidden, down, *blocks)


def shares(at, share, rows_t, grads_t, pre_grad, hidden, cost):
    units = hidden.shape[1]
    return pl.pallas_call(
        write_shares,
        out_shape=jax.ShapeDtypeStruct((at.shape[0], share, 3 * units // 2), BF16),
        in_specs=[pl.BlockSpec(memory_space=pltpu.SMEM)] + whole(4),
        out_specs=whole(1)[0],
        compiler_params=ROOMY,
        cost_estimate=cost,
    )(at, rows_t, grads_t, pre_grad, hidden)


def add_kernel(kept, got, left, right):
    half = left.shape[0]
    left[...] = add(kept[:half], got[:half]).astype(BF16)
    right[...] = add(kept[half:], got[half : 2 * half]).astype(BF16)


def next_kernel(kept, got, left_in, right_in, left_send, right_send):
    first = got.shape[0] // 2
    left_send[...] = (add(kept[1], got[first + 1]) + left_in[1].astype(F32)).astype(BF16)
    right_send[...] = (add(kept[3], got[first + 3]) + right_in[1].astype(F32)).astype(BF16)


def own_kernel(kept, got, left_in, right_in, left, right):
    first = got.shape[0] // 2
    left[...] = add(kept[0], got[first]) + left_in[0].astype(F32)
    right[...] = add(kept[2], got[first + 2]) + right_in[0].astype(F32)


def add(left, right):
    return left.astype(F32) + right.astype(F32)


CUBE_SEND = (3, 7, 5, 7, 1, 5, 1, 3)


def swap(block, bit):
    return lax.ppermute(block, "dp", [(at, at ^ bit) for at in range(lax.axis_size("dp"))])


def cube_sum(got, kept_first, kept_later):
    _, share, columns = got.shape

    def run(kernel, out_shape, inputs, cost=BRIEF):
        return pl.pallas_call(
            kernel,
            out_shape=out_shape,
            in_specs=whole(len(inputs)),
            out_specs=whole(len(out_shape)),
            compiler_params=ROOMY,
            cost_estimate=cost,
        )(*inputs)

    half = jax.ShapeDtypeStruct((2, share, columns), BF16)
    one = jax.ShapeDtypeStruct((share, columns), BF16)
    own = jax.ShapeDtypeStruct((share, columns), F32)
    left, right = run(add_kernel, (half, half), (kept_first, got))
    parts = (kept_later, got, swap(left, 2), swap(right, 4))
    left_send, right_send = run(next_kernel, (one, one), parts)
    left, right = run(own_kernel, (own, own), parts, COVER)
    return left, swap(left_send, 4), right, swap(right_send, 2)


def after(value, *others):
    return lax.optimization_barrier((value, *others))[0]


def partial_kernel(experts, capacity, alone, late, first, routes, scores, *refs):
    own, early, mixed, back, late_picker, scales = refs
    slots, toks = experts * capacity, mixed.shape[0]
    places = lax.broadcasted_iota(jnp.int32, (toks, slots), 1).astype(F32)
    hits = [
        places == to_column(row) for row in slot_rows(first[0], routes[...], experts, capacity)
    ]
    hits.append(functools.reduce(jnp.logical_or, hits))
    picker = jnp.concatenate([hit.astype(F32).astype(BF16) for hit in hits], axis=0)
    weights = weight_rows(scores[...])
    for k in range(scales.shape[0]):
        scales[k] = jnp.broadcast_to(to_column(weights[k : k + 1, :]), scales.shape[1:])

    def slots_of(blocks):
        parts = [picker[:, n * capacity : (n + 1) * capacity] for n in blocks]
        return jnp.concatenate(parts, axis=1)

    late_picker[...] = slots_of(late + [alone])
    now = slots_of((0, alone))
    for columns in column_steps(mixed.shape[1]):
        outputs = jnp.concatenate([own[:capacity, columns], early[:, columns]], axis=0)
        total, grad = sum_rows(now, scales, outputs, own[capacity:, columns])
        mixed[:, columns] = total
        back[:, columns] = grad


def sum_rows(picker, scales, outputs, gradients):
    tops, toks = scales.shape[:2]
    chosen = picker[: tops * toks, : outputs.shape[0]]
    picked = jnp.dot(chosen, outputs, preferred_element_type=F32)
    total = sum(scales[k, :, :1] * picked[k * toks : (k + 1) * toks] for k in range(tops))
    either = picker[tops * toks :, : gradients.shape[0]]
    return total, jnp.dot(either, gradients, preferred_element_type=F32)


def mean_kernel(count, left, left_last, right, right_last, wide, narrow):
    middle, edge = wide.shape[1] // 2, narrow.shape[1] // 2
    for at, (own, last) in enumerate(((left, left_last), (right, right_last))):
        total = (own[...] + last[...].astype(F32)) / count
        wide[:, at * middle : (at + 1) * middle] = total[:, :middle]
        narrow[:, at * edge : (at + 1) * edge] = total[:, middle:]


def means(count, sums):
    share, columns = sums[0].shape
    return pl.pallas_call(
        functools.partial(mean_kernel, count),
        out_shape=(
            jax.ShapeDtypeStruct((share, 4 * columns // 3), F32),
            jax.ShapeDtypeStruct((share, 2 * columns // 3), F32),
        ),
        in_specs=whole(4),
        out_specs=whole(2),
        compiler_params=ROOMY,
        cost_estimate=BRIEF,
    )(*sums)


def last_kernel(capacity, number, picker, scales, mixed_part, back_part, *refs):
    blocks, (mixed, back), (mixed_vmem, back_vmem, sems) = (
        refs[:number],
        refs[number : number + 2],
        refs[number + 2 :],
    )
    stores = []
    for c, columns in enumerate(column_steps(mixed.shape[1])):
        outputs = jnp.concatenate([block[:capacity, columns] for block in blocks[:-1]], axis=0)
        gradients = jnp.concatenate(
            [block[block.shape[0] - capacity :, columns] for block in blocks], axis=0
        )
        total, grad = sum_rows(picker[...], scales, outputs, gradients)
        mixed_vmem[:, columns] = (total + mixed_part[:, columns]).astype(BF16)
        back_vmem[:, columns] = (grad + back_part[:, columns]).astype(BF16)
        for n, (source, target) in enumerate(((mixed_vmem, mixed), (back_vmem, back))):
            stores.append(
                pltpu.make_async_copy(source.at[:, columns], target.at[:, columns], sems.at[c, n])
            )
            stores[-1].start()
    for stored in stores:
        stored.wait()


def last(capacity, parts, blocks):
    toks, width = parts[-1].shape
    out_shape = jax.ShapeDtypeStruct((toks, width), BF16)
    return pl.pallas_call(
        functools.partial(last_kernel, capacity, len(blocks)),
        out_shape=(out_shape, out_shape),
        in_specs=whole(4 + len(blocks)),
        out_specs=anywhere(2),
        scratch_shapes=[pltpu.VMEM((toks, width), BF16)] * 2
        + [pltpu.SemaphoreType.DMA((len(column_steps(width)), 2))],
        compiler_params=ROOMY,
        cost_estimate=BRIEF,
    )(*parts, *blocks)


def dispatch(experts, capacity, out_shape, first, *sources):
    weighted = len(sources) > 2
    return pl.pallas_call(
        functools.partial(dispatch_kernel, experts, capacity, weighted),
        out_shape=out_shape,
        in_specs=[pl.BlockSpec(memory_space=pltpu.SMEM)] + in_hbm(len(sources)),
        out_specs=anywhere(len(out_shape)),
        scratch_shapes=[pltpu.VMEM(out.shape, out.dtype) for out in out_shape]
        + [pltpu.VMEM(source.shape, source.dtype) for source in sources]
        + [
            pltpu.SemaphoreType.DMA((len(sources),)),
            pltpu.SemaphoreType.DMA((len(column_steps(out_shape[0].shape[1])), len(out_shape))),
        ],
        compiler_params=ALONE,
        cost_estimate=BRIEF,
    )(first, *sources)


def call(kernel, out_shape, inputs):
    return pl.pallas_call(
        kernel,
        out_shape=out_shape,
        in_specs=[pl.BlockSpec(memory_space=pltpu.SMEM)]
        + [pl.BlockSpec(memory_space=pltpu.VMEM)] * (len(inputs) - 1),
        compiler_params=ROOMY,
        cost_estimate=BRIEF,
    )(*inputs)


def body(tokens, routes, route_scores, out_grad, gate_up, down_weight):
    experts = lax.axis_size("expert")
    groups = lax.axis_size("dp")
    toks, width = tokens.shape
    tops = routes.shape[1]
    units = down_weight.shape[2]
    capacity = (toks * tops + experts - 1) // experts
    slots = experts * capacity
    share = width // groups
    direct = experts <= 8 and capacity % 16 == 0
    w_in, w_out = gate_up[0], down_weight[0]
    routes_t, scores_t = routes.T, route_scores.T
    me = lax.axis_index("expert") if direct else jnp.int32(0)
    first = me.astype(jnp.int32).reshape(1)
    sizes = [capacity] * experts if direct else [slots]
    block_shapes = [jax.ShapeDtypeStruct((size, width), BF16) for size in sizes]

    def travel(block, step, sign):
        pairs = [(at, (at + sign * step) % experts) for at in range(experts)]
        return lax.ppermute(block, "expert", pairs)

    def exchange(blocks, sign):
        if not direct:
            block = blocks[0].reshape(experts, capacity, width)
            moved = lax.all_to_all(block, "expert", split_axis=0, concat_axis=0, tiled=True)
            return [moved.reshape(slots, width)]
        steps = range(1, experts) if sign > 0 else range(experts - 1, 0, -1)
        moved = {step: travel(blocks[step], step, sign) for step in steps}
        return [blocks[0]] + [moved[step] for step in range(1, experts)]

    def joined(blocks):
        return blocks[0] if len(blocks) == 1 else jnp.concatenate(blocks, axis=0)

    def split(rows):
        return [rows[at : at + sizes[0]] for at in range(0, slots, sizes[0])]

    sent_rows = dispatch(experts, capacity, block_shapes, first, routes_t, tokens)
    got_rows = exchange(sent_rows, 1)
    sent_grads = dispatch(experts, capacity, block_shapes, first, routes_t, scores_t, out_grad)
    out_shape = jax.ShapeDtypeStruct((toks, width), BF16)
    cube = direct and experts == 4 and groups == 8 and share % 256 == 0
    if cube:
        sent_grads = after(sent_grads, got_rows[1], got_rows[-1])
        got_grads = exchange(sent_grads, 1)
        turn = [0, experts // 2] + [n for n in range(1, experts) if n != experts // 2]
        rows_t, preact, hidden, produced = forward([got_rows[n] for n in turn], w_in, w_out)
        got_grads = after([got_grads[n] for n in turn], hidden)
        own = lax.axis_index("dp")
        send_at = jnp.stack([jnp.bitwise_xor(own, j) for j in CUBE_SEND]).astype(jnp.int32)
        keep_at = jnp.bitwise_xor(send_at, 1)
        early = experts - 1
        early_out = travel(produced[turn.index(early)], early, -1)
        pre_grad, grads_t, sent, w_in_here = backward(
            send_at, share, preact, w_in, rows_t, hidden, w_out, got_grads
        )
        operands = (share, rows_t, grads_t, pre_grad, hidden)
        got = swap(sent, 1)
        blocks = returns(after(pre_grad, sent), w_in_here, produced, turn.index(early))
        half = len(CUBE_SEND) // 2
        kept_first = shares(after(keep_at[:half], blocks[0]), *operands, COVER)
        returned = exchange([blocks[turn.index(n)] for n in range(experts)], -1)
        kept_later = shares(after(keep_at[half:], kept_first, early_out, got), *operands, COVER)
        sums = cube_sum(got, kept_first, kept_later)
        late = [n for n in range(experts - 1, 0, -1) if n != early]
        mixed_part, back_part, picker, scales = call(
            functools.partial(partial_kernel, experts, capacity, early, late),
            (
                jax.ShapeDtypeStruct((toks, width), F32),
                jax.ShapeDtypeStruct((toks, width), F32),
                jax.ShapeDtypeStruct(((tops + 1) * toks, (len(late) + 1) * capacity), BF16),
                jax.ShapeDtypeStruct((tops, toks, 128), F32),
            ),
            (after(first, sums[0]), routes_t, scores_t, returned[0], early_out),
        )
        grad_in, grad_down = means(groups, sums)
        parts = (after(picker, grad_in), scales, mixed_part, back_part)
        mixed_out, token_grad = last(capacity, parts, [returned[n] for n in late + [early]])
    else:
        token_rows = joined(got_rows)
        grad_rows = joined(exchange(sent_grads, 1))
        preact = jnp.dot(token_rows, w_in, preferred_element_type=F32)
        gate, up = preact[:, :units], preact[:, units:]
        hidden = (jax.nn.silu(gate) * up).astype(BF16)
        produced = jnp.dot(hidden, w_out.T, preferred_element_type=F32).astype(BF16)
        returned = exchange(split(produced), -1)
        hidden_grad = jnp.dot(grad_rows, w_out, preferred_element_type=F32)
        sigmoid = jax.nn.sigmoid(gate)
        gate_grad = hidden_grad * up * sigmoid * (1.0 + gate * (1.0 - sigmoid))
        up_grad = hidden_grad * gate * sigmoid
        pre_grad = jnp.concatenate([gate_grad, up_grad], axis=1).astype(BF16)
        input_grad = jnp.dot(pre_grad, w_in.T, preferred_element_type=F32).astype(BF16)
        sent_back = exchange(split(input_grad), -1)

        def summed(left, right):
            part = contract(left, right).astype(BF16)
            total = lax.psum_scatter(part, "dp", scatter_dimension=0, tiled=True)
            return total.astype(F32) / groups

        grad_in = summed(token_rows, pre_grad)
        grad_down = summed(grad_rows, hidden)
        mixed_out = call(
            functools.partial(combine_kernel, experts, capacity, True),
            out_shape,
            (first, routes_t, scores_t, *returned),
        )
        token_grad = call(
            functools.partial(combine_kernel, experts, capacity, False),
            out_shape,
            (first, routes_t, *sent_back),
        )
    grad_in = grad_in.reshape(1, share, 2 * units)
    grad_down = grad_down.reshape(1, share, units)
    return (mixed_out, token_grad, grad_in, grad_down)


def solution(mesh):
    in_specs = (
        P(("dp", "expert"), None),
        P(("dp", "expert"), None),
        P(("dp", "expert"), None),
        P(("dp", "expert"), None),
        P("expert", None, None),
        P("expert", None, None),
    )
    out_specs = (
        P(("dp", "expert"), None),
        P(("dp", "expert"), None),
        P("expert", "dp", None),
        P("expert", "dp", None),
    )
    return jax.shard_map(body, mesh=mesh, in_specs=in_specs, out_specs=out_specs, check_vma=False)
```

```python
import functools

import jax
import jax.numpy as jnp
from jax import lax
from jax.experimental import pallas as pl
from jax.experimental.pallas import tpu as pltpu
from jax.sharding import PartitionSpec as P

F32 = jnp.float32
BF16 = jnp.bfloat16
BRIEF = pl.CostEstimate(flops=1024, bytes_accessed=1024, transcendentals=0)
COVER = pl.CostEstimate(flops=4 * 10**10, bytes_accessed=1024, transcendentals=0)
ROOMY = pltpu.CompilerParams(vmem_limit_bytes=16 * 1024 * 1024)
BIG = pltpu.CompilerParams(vmem_limit_bytes=28 * 1024 * 1024)
ALONE = pltpu.CompilerParams(vmem_limit_bytes=60 * 1024 * 1024)


def contract(left, right):
    return lax.dot_general(left, right, (((0,), (0,)), ((), ())), preferred_element_type=F32)


def slot_rows(first, routes, experts, capacity):
    tops, toks = routes.shape
    padded = -(-experts // 8) * 8
    rows = lax.broadcasted_iota(jnp.int32, (padded, toks), 0)
    ids = rows + first
    ids = jnp.where(ids >= experts, ids - experts, ids)
    ids = jnp.where(rows < experts, ids, -1)
    hits = [routes[k : k + 1, :] == ids for k in range(tops)]
    named = functools.reduce(jnp.logical_or, hits)
    before = lax.broadcasted_iota(jnp.int32, (toks, toks), 0) < lax.broadcasted_iota(
        jnp.int32, (toks, toks), 1
    )
    position = jnp.dot(
        named.astype(F32).astype(BF16),
        before.astype(F32).astype(BF16),
        preferred_element_type=F32,
    )
    slot = position + (rows * capacity).astype(F32)
    return [jnp.sum(jnp.where(hit, slot, 0.0), axis=0, keepdims=True) for hit in hits]


def weight_rows(scores):
    grown = jnp.exp(scores)
    return grown / jnp.sum(grown, axis=0, keepdims=True)


def to_column(row):
    toks = row.shape[1]
    same = lax.broadcasted_iota(jnp.int32, (toks, toks), 0) == lax.broadcasted_iota(
        jnp.int32, (toks, toks), 1
    )
    return jnp.sum(jnp.where(same, row, 0.0), axis=1, keepdims=True)


def put_blocks(outs, rows, columns):
    start = 0
    for out in outs:
        size = out.shape[0]
        out[:, columns] = rows[start : start + size]
        start += size


def column_steps(width):
    step = 512 if width % 512 == 0 else width
    return [slice(at, at + step) for at in range(0, width, step)]


def dispatch_kernel(experts, capacity, weighted, first, *refs):
    count = 2 + weighted
    sources, refs = refs[:count], refs[count:]
    number = (len(refs) - count - 2) // 2
    outs, ready, (*held, sems, out_sems) = refs[:number], refs[number : 2 * number], refs[2 * number :]
    copies = [
        pltpu.make_async_copy(source, place, sems.at[n])
        for n, (source, place) in enumerate(zip(sources, held))
    ]
    for copy in copies:
        copy.start()
    routes, values = held[0], held[-1]
    scores = held[1] if weighted else None
    for copy in copies[:-1]:
        copy.wait()
    slots, toks = experts * capacity, values.shape[0]
    places = lax.broadcasted_iota(jnp.int32, (slots, toks), 0).astype(F32)
    hits = [places == row for row in slot_rows(first[0], routes[...], experts, capacity)]
    picker = functools.reduce(jnp.logical_or, hits).astype(F32).astype(BF16)
    if weighted:
        weights = weight_rows(scores[...])
        scale = sum(
            jnp.sum(jnp.where(hit, weights[k : k + 1, :], 0.0), axis=1, keepdims=True)
            for k, hit in enumerate(hits)
        )
    copies[-1].wait()
    stores = []
    for c, columns in enumerate(column_steps(values.shape[1])):
        rows = jnp.dot(picker, values[:, columns], preferred_element_type=F32)
        if weighted:
            rows = rows * scale
        put_blocks(ready, rows.astype(BF16), columns)
        for n, (block, out) in enumerate(zip(ready, outs)):
            stores.append(
                pltpu.make_async_copy(block.at[:, columns], out.at[:, columns], out_sems.at[c, n])
            )
            stores[-1].start()
    for store in stores:
        store.wait()


def combine_kernel(experts, capacity, weighted, first, routes, *refs):
    scores = refs[0] if weighted else None
    blocks, out = refs[weighted:-1], refs[-1]
    slots, toks = experts * capacity, out.shape[0]
    places = lax.broadcasted_iota(jnp.int32, (toks, slots), 1).astype(F32)
    hits = [
        places == to_column(row) for row in slot_rows(first[0], routes[...], experts, capacity)
    ]
    if weighted:
        weights = weight_rows(scores[...])
        scales = [to_column(weights[k : k + 1, :]) for k in range(len(hits))]
        pickers = [hit.astype(F32).astype(BF16) for hit in hits]
    else:
        pickers = [functools.reduce(jnp.logical_or, hits).astype(F32).astype(BF16)]
    for columns in column_steps(out.shape[1]):
        rows = [block[:, columns] for block in blocks]
        rows = rows[0] if len(rows) == 1 else jnp.concatenate(rows, axis=0)
        picked = [jnp.dot(picker, rows, preferred_element_type=F32) for picker in pickers]
        if weighted:
            picked = [scale * part for scale, part in zip(scales, picked)]
        out[:, columns] = sum(picked).astype(out.dtype)


def whole(count):
    return [pl.BlockSpec(memory_space=pltpu.VMEM)] * count


def write_shares(at, rows_t, grads_t, pre_grad, hidden, out):
    share = out.shape[1]
    wide, narrow = pre_grad.shape[1] // 2, hidden.shape[1] // 2

    def write(t, half):
        own = pl.ds(pl.multiple_of(at[t] * share, share), share)
        out[t, :, :wide] = jnp.dot(
            rows_t[own, :],
            pre_grad[:, half * wide : (half + 1) * wide],
            preferred_element_type=F32,
        ).astype(out.dtype)
        out[t, :, wide:] = jnp.dot(
            grads_t[own, :],
            hidden[:, half * narrow : (half + 1) * narrow],
            preferred_element_type=F32,
        ).astype(out.dtype)

    for t in range(out.shape[0]):
        write(t, t // 2 % 2)


def transpose_into(rows, rows_t):
    width = rows.shape[1]
    step = 256 if width % 256 == 0 else width

    for begin in range(0, width, step):
        rows_t[begin : begin + step, :] = rows[:, begin : begin + step].T


def join_copies(blocks, rows, sems):
    size = blocks[0].shape[0]
    joins = [
        pltpu.make_async_copy(block, rows.at[pl.ds(n * size, size)], sems.at[n])
        for n, block in enumerate(blocks)
    ]
    for join in joins:
        join.start()
    return joins


def forward_kernel(count, *refs):
    blocks, (w_in_hbm, down_hbm), (rows_t, preact, hidden), outs, scratch = (
        refs[:count],
        refs[count : count + 2],
        refs[count + 2 : count + 5],
        refs[count + 5 : 2 * count + 5],
        refs[2 * count + 5 :],
    )
    rows, w_in, down, block_sems, weight_sems, down_sem = scratch
    joins = join_copies(blocks, rows, block_sems)
    width, units = down.shape
    step = 256 if units % 256 == 0 else units
    loads = []
    for n in range(2 * units // step):
        begin = (n % 2) * units + n // 2 * step
        loads.append(
            pltpu.make_async_copy(
                w_in_hbm.at[:, pl.ds(begin, step)],
                w_in.at[:, pl.ds(begin, step)],
                weight_sems.at[n],
            )
        )
        loads[-1].start()
    load_down = pltpu.make_async_copy(down_hbm, down, down_sem)
    load_down.start()
    for join in joins:
        join.wait()
    for n in range(units // step):
        begin = n * step
        gate_at, up_at = slice(begin, begin + step), slice(units + begin, units + begin + step)
        loads[2 * n].wait()
        gate = jnp.dot(rows[...], w_in[:, gate_at], preferred_element_type=F32)
        loads[2 * n + 1].wait()
        up = jnp.dot(rows[...], w_in[:, up_at], preferred_element_type=F32)
        preact[:, gate_at] = gate
        preact[:, up_at] = up
        hidden[:, gate_at] = (gate / (1.0 + jnp.exp(-gate)) * up).astype(BF16)
    load_down.wait()
    for columns in column_steps(width):
        part = lax.dot_general(
            hidden[...], down[columns, :], (((1,), (1,)), ((), ())), preferred_element_type=F32
        )
        put_blocks(outs, part.astype(BF16), columns)
    transpose_into(rows, rows_t)


def forward(blocks, w_in, down):
    width, units = down.shape
    slots = sum(block.shape[0] for block in blocks)
    count = len(blocks)
    rows_t, preact, hidden, *outs = pl.pallas_call(
        functools.partial(forward_kernel, count),
        out_shape=(
            jax.ShapeDtypeStruct((width, slots), BF16),
            jax.ShapeDtypeStruct((slots, 2 * units), F32),
            jax.ShapeDtypeStruct((slots, units), BF16),
            *[jax.ShapeDtypeStruct(block.shape, BF16) for block in blocks],
        ),
        in_specs=anywhere(count) + in_hbm(2),
        out_specs=whole(3 + count),
        scratch_shapes=[
            pltpu.VMEM((slots, width), BF16),
            pltpu.VMEM(w_in.shape, BF16),
            pltpu.VMEM(down.shape, BF16),
            pltpu.SemaphoreType.DMA((count,)),
            pltpu.SemaphoreType.DMA((2 * units // min(units, 256),)),
            pltpu.SemaphoreType.DMA,
        ],
        compiler_params=pltpu.CompilerParams(vmem_limit_bytes=46 * 1024 * 1024),
        cost_estimate=BRIEF,
    )(*blocks, w_in, down)
    return rows_t, preact, hidden, outs


def backward_kernel(count, at, preact_hbm, w_in_hbm, rows_t, hidden, down, *refs):
    blocks, (pre_grad, grads_t, sent, w_in, *refs) = refs[:count], refs[count:]
    grads, preact, block_sems, load_sem, sem = refs
    joins = join_copies(blocks, grads, block_sems)
    fetch = pltpu.make_async_copy(preact_hbm, preact, sem)
    fetch.start()
    load = pltpu.make_async_copy(w_in_hbm, w_in, load_sem)
    load.start()
    units = down.shape[1]
    for join in joins:
        join.wait()
    fetch.wait()
    step = 256 if units % 256 == 0 else units
    for begin in range(0, units, step):
        gate = preact[:, begin : begin + step]
        up = preact[:, units + begin : units + begin + step]
        hidden_grad = jnp.dot(
            grads[...], down[:, begin : begin + step], preferred_element_type=F32
        )
        sigmoid = 1.0 / (1.0 + jnp.exp(-gate))
        gate_grad = hidden_grad * up * sigmoid * (1.0 + gate * (1.0 - sigmoid))
        up_grad = hidden_grad * gate * sigmoid
        pre_grad[:, begin : begin + step] = gate_grad.astype(BF16)
        pre_grad[:, units + begin : units + begin + step] = up_grad.astype(BF16)
    transpose_into(grads, grads_t)
    write_shares(at, rows_t, grads_t, pre_grad, hidden, sent)
    load.wait()


def return_kernel(count, alone, pre_grad, w_in, *refs):
    blocks, outs, sems = refs[:count], refs[count : 2 * count], refs[-1]
    size = blocks[0].shape[0]
    copies = [
        pltpu.make_async_copy(block, out.at[pl.ds(0, size)], sems.at[n])
        for n, (block, out) in enumerate(zip(blocks, outs))
        if n != alone
    ]
    for copy in copies:
        copy.start()
    for columns in column_steps(w_in.shape[0]):
        part = lax.dot_general(
            pre_grad[...], w_in[columns, :], (((1,), (1,)), ((), ())), preferred_element_type=F32
        ).astype(BF16)
        for n, out in enumerate(outs):
            out[out.shape[0] - size :, columns] = part[n * size : (n + 1) * size]
    for copy in copies:
        copy.wait()


def returns(pre_grad, w_in, produced, alone):
    count = len(produced)
    size, width = produced[0].shape
    return pl.pallas_call(
        functools.partial(return_kernel, count, alone),
        out_shape=[
            jax.ShapeDtypeStruct((size if n == alone else 2 * size, width), BF16)
            for n in range(count)
        ],
        in_specs=whole(2) + anywhere(count),
        out_specs=whole(count),
        scratch_shapes=[pltpu.SemaphoreType.DMA((count,))],
        compiler_params=ROOMY,
        cost_estimate=BRIEF,
    )(pre_grad, w_in, *produced)


def anywhere(count):
    return [pl.BlockSpec(memory_space=pl.ANY)] * count


def in_hbm(count):
    return [pl.BlockSpec(memory_space=pltpu.HBM)] * count


def backward(at, share, preact, w_in, rows_t, hidden, down, blocks):
    width, units = down.shape
    slots = preact.shape[0]
    count = len(blocks)
    return pl.pallas_call(
        functools.partial(backward_kernel, count),
        out_shape=(
            jax.ShapeDtypeStruct((slots, 2 * units), BF16),
            jax.ShapeDtypeStruct((width, slots), BF16),
            jax.ShapeDtypeStruct((at.shape[0], share, 3 * units // 2), BF16),
            jax.ShapeDtypeStruct(w_in.shape, BF16),
        ),
        in_specs=[pl.BlockSpec(memory_space=pltpu.SMEM)]
        + anywhere(2)
        + whole(3)
        + anywhere(count),
        out_specs=whole(4),
        scratch_shapes=[
            pltpu.VMEM((slots, width), BF16),
            pltpu.VMEM((slots, 2 * units), F32),
            pltpu.SemaphoreType.DMA((count,)),
            pltpu.SemaphoreType.DMA,
            pltpu.SemaphoreType.DMA,
        ],
        compiler_params=BIG,
        cost_estimate=BRIEF,
    )(at, preact, w_in, rows_t, hidden, down, *blocks)


def shares(at, share, rows_t, grads_t, pre_grad, hidden, cost):
    units = hidden.shape[1]
    return pl.pallas_call(
        write_shares,
        out_shape=jax.ShapeDtypeStruct((at.shape[0], share, 3 * units // 2), BF16),
        in_specs=[pl.BlockSpec(memory_space=pltpu.SMEM)] + whole(4),
        out_specs=whole(1)[0],
        compiler_params=ROOMY,
        cost_estimate=cost,
    )(at, rows_t, grads_t, pre_grad, hidden)


def add_kernel(kept, got, left, right):
    half = left.shape[0]
    left[...] = add(kept[:half], got[:half]).astype(BF16)
    right[...] = add(kept[half:], got[half : 2 * half]).astype(BF16)


def next_kernel(kept, got, left_in, right_in, left_send, right_send):
    first = got.shape[0] // 2
    left_send[...] = (add(kept[1], got[first + 1]) + left_in[1].astype(F32)).astype(BF16)
    right_send[...] = (add(kept[3], got[first + 3]) + right_in[1].astype(F32)).astype(BF16)


def own_kernel(kept, got, left_in, right_in, left, right):
    first = got.shape[0] // 2
    left[...] = add(kept[0], got[first]) + left_in[0].astype(F32)
    right[...] = add(kept[2], got[first + 2]) + right_in[0].astype(F32)


def add(left, right):
    return left.astype(F32) + right.astype(F32)


CUBE_SEND = (3, 7, 5, 7, 1, 5, 1, 3)


def swap(block, bit):
    return lax.ppermute(block, "dp", [(at, at ^ bit) for at in range(lax.axis_size("dp"))])


def cube_sum(got, kept_first, kept_later):
    _, share, columns = got.shape

    def run(kernel, out_shape, inputs, cost=BRIEF):
        return pl.pallas_call(
            kernel,
            out_shape=out_shape,
            in_specs=whole(len(inputs)),
            out_specs=whole(len(out_shape)),
            compiler_params=ROOMY,
            cost_estimate=cost,
        )(*inputs)

    half = jax.ShapeDtypeStruct((2, share, columns), BF16)
    one = jax.ShapeDtypeStruct((share, columns), BF16)
    own = jax.ShapeDtypeStruct((share, columns), F32)
    left, right = run(add_kernel, (half, half), (kept_first, got))
    parts = (kept_later, got, swap(left, 2), swap(right, 4))
    left_send, right_send = run(next_kernel, (one, one), parts)
    left, right = run(own_kernel, (own, own), parts, COVER)
    return left, swap(left_send, 4), right, swap(right_send, 2)


def after(value, *others):
    return lax.optimization_barrier((value, *others))[0]


def partial_kernel(experts, capacity, alone, late, first, routes, scores, *refs):
    own, early, mixed, back, late_picker, scales = refs
    slots, toks = experts * capacity, mixed.shape[0]
    places = lax.broadcasted_iota(jnp.int32, (toks, slots), 1).astype(F32)
    hits = [
        places == to_column(row) for row in slot_rows(first[0], routes[...], experts, capacity)
    ]
    hits.append(functools.reduce(jnp.logical_or, hits))
    picker = jnp.concatenate([hit.astype(F32).astype(BF16) for hit in hits], axis=0)
    weights = weight_rows(scores[...])
    for k in range(scales.shape[0]):
        scales[k] = jnp.broadcast_to(to_column(weights[k : k + 1, :]), scales.shape[1:])

    def slots_of(blocks):
        parts = [picker[:, n * capacity : (n + 1) * capacity] for n in blocks]
        return jnp.concatenate(parts, axis=1)

    late_picker[...] = slots_of(late + [alone])
    now = slots_of((0, alone))
    for columns in column_steps(mixed.shape[1]):
        outputs = jnp.concatenate([own[:capacity, columns], early[:, columns]], axis=0)
        total, grad = sum_rows(now, scales, outputs, own[capacity:, columns])
        mixed[:, columns] = total
        back[:, columns] = grad


def sum_rows(picker, scales, outputs, gradients):
    tops, toks = scales.shape[:2]
    chosen = picker[: tops * toks, : outputs.shape[0]]
    picked = jnp.dot(chosen, outputs, preferred_element_type=F32)
    total = sum(scales[k, :, :1] * picked[k * toks : (k + 1) * toks] for k in range(tops))
    either = picker[tops * toks :, : gradients.shape[0]]
    return total, jnp.dot(either, gradients, preferred_element_type=F32)


def mean_kernel(count, left, left_last, right, right_last, wide, narrow):
    middle, edge = wide.shape[1] // 2, narrow.shape[1] // 2
    for at, (own, last) in enumerate(((left, left_last), (right, right_last))):
        total = (own[...] + last[...].astype(F32)) / count
        wide[:, at * middle : (at + 1) * middle] = total[:, :middle]
        narrow[:, at * edge : (at + 1) * edge] = total[:, middle:]


def means(count, sums):
    share, columns = sums[0].shape
    return pl.pallas_call(
        functools.partial(mean_kernel, count),
        out_shape=(
            jax.ShapeDtypeStruct((share, 4 * columns // 3), F32),
            jax.ShapeDtypeStruct((share, 2 * columns // 3), F32),
        ),
        in_specs=whole(4),
        out_specs=whole(2),
        compiler_params=ROOMY,
        cost_estimate=BRIEF,
    )(*sums)


def last_kernel(capacity, number, picker, scales, mixed_part, back_part, *refs):
    blocks, (mixed, back), (mixed_vmem, back_vmem, sems) = (
        refs[:number],
        refs[number : number + 2],
        refs[number + 2 :],
    )
    stores = []
    for c, columns in enumerate(column_steps(mixed.shape[1])):
        outputs = jnp.concatenate([block[:capacity, columns] for block in blocks[:-1]], axis=0)
        gradients = jnp.concatenate(
            [block[block.shape[0] - capacity :, columns] for block in blocks], axis=0
        )
        total, grad = sum_rows(picker[...], scales, outputs, gradients)
        mixed_vmem[:, columns] = (total + mixed_part[:, columns]).astype(BF16)
        back_vmem[:, columns] = (grad + back_part[:, columns]).astype(BF16)
        for n, (source, target) in enumerate(((mixed_vmem, mixed), (back_vmem, back))):
            stores.append(
                pltpu.make_async_copy(source.at[:, columns], target.at[:, columns], sems.at[c, n])
            )
            stores[-1].start()
    for stored in stores:
        stored.wait()


def last(capacity, parts, blocks):
    toks, width = parts[-1].shape
    out_shape = jax.ShapeDtypeStruct((toks, width), BF16)
    return pl.pallas_call(
        functools.partial(last_kernel, capacity, len(blocks)),
        out_shape=(out_shape, out_shape),
        in_specs=whole(4 + len(blocks)),
        out_specs=anywhere(2),
        scratch_shapes=[pltpu.VMEM((toks, width), BF16)] * 2
        + [pltpu.SemaphoreType.DMA((len(column_steps(width)), 2))],
        compiler_params=ROOMY,
        cost_estimate=BRIEF,
    )(*parts, *blocks)


def dispatch(experts, capacity, out_shape, first, *sources):
    weighted = len(sources) > 2
    return pl.pallas_call(
        functools.partial(dispatch_kernel, experts, capacity, weighted),
        out_shape=out_shape,
        in_specs=[pl.BlockSpec(memory_space=pltpu.SMEM)] + in_hbm(len(sources)),
        out_specs=anywhere(len(out_shape)),
        scratch_shapes=[pltpu.VMEM(out.shape, out.dtype) for out in out_shape]
        + [pltpu.VMEM(source.shape, source.dtype) for source in sources]
        + [
            pltpu.SemaphoreType.DMA((len(sources),)),
            pltpu.SemaphoreType.DMA((len(column_steps(out_shape[0].shape[1])), len(out_shape))),
        ],
        compiler_params=ALONE,
        cost_estimate=BRIEF,
    )(first, *sources)


def call(kernel, out_shape, inputs):
    return pl.pallas_call(
        kernel,
        out_shape=out_shape,
        in_specs=[pl.BlockSpec(memory_space=pltpu.SMEM)]
        + [pl.BlockSpec(memory_space=pltpu.VMEM)] * (len(inputs) - 1),
        compiler_params=ROOMY,
        cost_estimate=BRIEF,
    )(*inputs)


def body(tokens, routes, route_scores, out_grad, gate_up, down_weight):
    experts = lax.axis_size("expert")
    groups = lax.axis_size("dp")
    toks, width = tokens.shape
    tops = routes.shape[1]
    units = down_weight.shape[2]
    capacity = (toks * tops + experts - 1) // experts
    slots = experts * capacity
    share = width // groups
    direct = experts <= 8 and capacity % 16 == 0
    w_in, w_out = gate_up[0], down_weight[0]
    routes_t, scores_t = routes.T, route_scores.T
    me = lax.axis_index("expert") if direct else jnp.int32(0)
    first = me.astype(jnp.int32).reshape(1)
    sizes = [capacity] * experts if direct else [slots]
    block_shapes = [jax.ShapeDtypeStruct((size, width), BF16) for size in sizes]

    def travel(block, step, sign):
        pairs = [(at, (at + sign * step) % experts) for at in range(experts)]
        return lax.ppermute(block, "expert", pairs)

    def exchange(blocks, sign):
        if not direct:
            block = blocks[0].reshape(experts, capacity, width)
            moved = lax.all_to_all(block, "expert", split_axis=0, concat_axis=0, tiled=True)
            return [moved.reshape(slots, width)]
        steps = range(1, experts) if sign > 0 else range(experts - 1, 0, -1)
        moved = {step: travel(blocks[step], step, sign) for step in steps}
        return [blocks[0]] + [moved[step] for step in range(1, experts)]

    def joined(blocks):
        return blocks[0] if len(blocks) == 1 else jnp.concatenate(blocks, axis=0)

    def split(rows):
        return [rows[at : at + sizes[0]] for at in range(0, slots, sizes[0])]

    sent_rows = dispatch(experts, capacity, block_shapes, first, routes_t, tokens)
    got_rows = exchange(sent_rows, 1)
    sent_grads = dispatch(experts, capacity, block_shapes, first, routes_t, scores_t, out_grad)
    out_shape = jax.ShapeDtypeStruct((toks, width), BF16)
    cube = direct and experts == 4 and groups == 8 and share % 256 == 0
    if cube:
        sent_grads = after(sent_grads, got_rows[1], got_rows[-1])
        got_grads = exchange(sent_grads, 1)
        turn = [0, experts // 2] + [n for n in range(1, experts) if n != experts // 2]
        rows_t, preact, hidden, produced = forward([got_rows[n] for n in turn], w_in, w_out)
        got_grads = after([got_grads[n] for n in turn], hidden)
        own = lax.axis_index("dp")
        send_at = jnp.stack([jnp.bitwise_xor(own, j) for j in CUBE_SEND]).astype(jnp.int32)
        keep_at = jnp.bitwise_xor(send_at, 1)
        early = experts - 1
        early_out = travel(produced[turn.index(early)], early, -1)
        pre_grad, grads_t, sent, w_in_here = backward(
            send_at, share, preact, w_in, rows_t, hidden, w_out, got_grads
        )
        operands = (share, rows_t, grads_t, pre_grad, hidden)
        got = swap(sent, 1)
        blocks = returns(after(pre_grad, sent), w_in_here, produced, turn.index(early))
        half = len(CUBE_SEND) // 2
        kept_first = shares(after(keep_at[:half], blocks[0]), *operands, COVER)
        returned = exchange([blocks[turn.index(n)] for n in range(experts)], -1)
        kept_later = shares(after(keep_at[half:], kept_first, early_out, got), *operands, COVER)
        sums = cube_sum(got, kept_first, kept_later)
        late = [n for n in range(experts - 1, 0, -1) if n != early]
        mixed_part, back_part, picker, scales = call(
            functools.partial(partial_kernel, experts, capacity, early, late),
            (
                jax.ShapeDtypeStruct((toks, width), F32),
                jax.ShapeDtypeStruct((toks, width), F32),
                jax.ShapeDtypeStruct(((tops + 1) * toks, (len(late) + 1) * capacity), BF16),
                jax.ShapeDtypeStruct((tops, toks, 128), F32),
            ),
            (after(first, sums[0]), routes_t, scores_t, returned[0], early_out),
        )
        grad_in, grad_down = means(groups, sums)
        parts = (after(picker, grad_in), scales, mixed_part, back_part)
        mixed_out, token_grad = last(capacity, parts, [returned[n] for n in late + [early]])
    else:
        token_rows = joined(got_rows)
        grad_rows = joined(exchange(sent_grads, 1))
        preact = jnp.dot(token_rows, w_in, preferred_element_type=F32)
        gate, up = preact[:, :units], preact[:, units:]
        hidden = (jax.nn.silu(gate) * up).astype(BF16)
        produced = jnp.dot(hidden, w_out.T, preferred_element_type=F32).astype(BF16)
        returned = exchange(split(produced), -1)
        hidden_grad = jnp.dot(grad_rows, w_out, preferred_element_type=F32)
        sigmoid = jax.nn.sigmoid(gate)
        gate_grad = hidden_grad * up * sigmoid * (1.0 + gate * (1.0 - sigmoid))
        up_grad = hidden_grad * gate * sigmoid
        pre_grad = jnp.concatenate([gate_grad, up_grad], axis=1).astype(BF16)
        input_grad = jnp.dot(pre_grad, w_in.T, preferred_element_type=F32).astype(BF16)
        sent_back = exchange(split(input_grad), -1)

        def summed(left, right):
            part = contract(left, right).astype(BF16)
            total = lax.psum_scatter(part, "dp", scatter_dimension=0, tiled=True)
            return total.astype(F32) / groups

        grad_in = summed(token_rows, pre_grad)
        grad_down = summed(grad_rows, hidden)
        mixed_out = call(
            functools.partial(combine_kernel, experts, capacity, True),
            out_shape,
            (first, routes_t, scores_t, *returned),
        )
        token_grad = call(
            functools.partial(combine_kernel, experts, capacity, False),
            out_shape,
            (first, routes_t, *sent_back),
        )
    grad_in = grad_in.reshape(1, share, 2 * units)
    grad_down = grad_down.reshape(1, share, units)
    return (mixed_out, token_grad, grad_in, grad_down)


def solution(mesh):
    in_specs = (
        P(("dp", "expert"), None),
        P(("dp", "expert"), None),
        P(("dp", "expert"), None),
        P(("dp", "expert"), None),
        P("expert", None, None),
        P("expert", None, None),
    )
    out_specs = (
        P(("dp", "expert"), None),
        P(("dp", "expert"), None),
        P("expert", "dp", None),
        P("expert", "dp", None),
    )
    return jax.shard_map(body, mesh=mesh, in_specs=in_specs, out_specs=out_specs, check_vma=False)
```

```python
import functools

import jax
import jax.numpy as jnp
from jax import lax
from jax.experimental import pallas as pl
from jax.experimental.pallas import tpu as pltpu
from jax.sharding import PartitionSpec as P

F32 = jnp.float32
BF16 = jnp.bfloat16
BRIEF = pl.CostEstimate(flops=1024, bytes_accessed=1024, transcendentals=0)
COVER = pl.CostEstimate(flops=4 * 10**10, bytes_accessed=1024, transcendentals=0)
ROOMY = pltpu.CompilerParams(vmem_limit_bytes=16 * 1024 * 1024)
BIG = pltpu.CompilerParams(vmem_limit_bytes=28 * 1024 * 1024)
ALONE = pltpu.CompilerParams(vmem_limit_bytes=60 * 1024 * 1024)


def contract(left, right):
    return lax.dot_general(left, right, (((0,), (0,)), ((), ())), preferred_element_type=F32)


def slot_rows(first, routes, experts, capacity):
    tops, toks = routes.shape
    padded = -(-experts // 8) * 8
    rows = lax.broadcasted_iota(jnp.int32, (padded, toks), 0)
    ids = rows + first
    ids = jnp.where(ids >= experts, ids - experts, ids)
    ids = jnp.where(rows < experts, ids, -1)
    hits = [routes[k : k + 1, :] == ids for k in range(tops)]
    named = functools.reduce(jnp.logical_or, hits)
    before = lax.broadcasted_iota(jnp.int32, (toks, toks), 0) < lax.broadcasted_iota(
        jnp.int32, (toks, toks), 1
    )
    position = jnp.dot(
        named.astype(F32).astype(BF16),
        before.astype(F32).astype(BF16),
        preferred_element_type=F32,
    )
    slot = position + (rows * capacity).astype(F32)
    return [jnp.sum(jnp.where(hit, slot, 0.0), axis=0, keepdims=True) for hit in hits]


def weight_rows(scores):
    grown = jnp.exp(scores)
    return grown / jnp.sum(grown, axis=0, keepdims=True)


def to_column(row):
    toks = row.shape[1]
    same = lax.broadcasted_iota(jnp.int32, (toks, toks), 0) == lax.broadcasted_iota(
        jnp.int32, (toks, toks), 1
    )
    return jnp.sum(jnp.where(same, row, 0.0), axis=1, keepdims=True)


def put_blocks(outs, rows, columns):
    start = 0
    for out in outs:
        size = out.shape[0]
        out[:, columns] = rows[start : start + size]
        start += size


def column_steps(width):
    step = 512 if width % 512 == 0 else width
    return [slice(at, at + step) for at in range(0, width, step)]


def dispatch_kernel(experts, capacity, weighted, first, *refs):
    count = 2 + weighted
    sources, refs = refs[:count], refs[count:]
    number = (len(refs) - count - 2) // 2
    outs, ready, (*held, sems, out_sems) = refs[:number], refs[number : 2 * number], refs[2 * number :]
    copies = [
        pltpu.make_async_copy(source, place, sems.at[n])
        for n, (source, place) in enumerate(zip(sources, held))
    ]
    for copy in copies:
        copy.start()
    routes, values = held[0], held[-1]
    scores = held[1] if weighted else None
    for copy in copies[:-1]:
        copy.wait()
    slots, toks = experts * capacity, values.shape[0]
    places = lax.broadcasted_iota(jnp.int32, (slots, toks), 0).astype(F32)
    hits = [places == row for row in slot_rows(first[0], routes[...], experts, capacity)]
    picker = functools.reduce(jnp.logical_or, hits).astype(F32).astype(BF16)
    if weighted:
        weights = weight_rows(scores[...])
        scale = sum(
            jnp.sum(jnp.where(hit, weights[k : k + 1, :], 0.0), axis=1, keepdims=True)
            for k, hit in enumerate(hits)
        )
    copies[-1].wait()
    stores = []
    for c, columns in enumerate(column_steps(values.shape[1])):
        rows = jnp.dot(picker, values[:, columns], preferred_element_type=F32)
        if weighted:
            rows = rows * scale
        put_blocks(ready, rows.astype(BF16), columns)
        for n, (block, out) in enumerate(zip(ready, outs)):
            stores.append(
                pltpu.make_async_copy(block.at[:, columns], out.at[:, columns], out_sems.at[c, n])
            )
            stores[-1].start()
    for store in stores:
        store.wait()


def combine_kernel(experts, capacity, weighted, first, routes, *refs):
    scores = refs[0] if weighted else None
    blocks, out = refs[weighted:-1], refs[-1]
    slots, toks = experts * capacity, out.shape[0]
    places = lax.broadcasted_iota(jnp.int32, (toks, slots), 1).astype(F32)
    hits = [
        places == to_column(row) for row in slot_rows(first[0], routes[...], experts, capacity)
    ]
    if weighted:
        weights = weight_rows(scores[...])
        scales = [to_column(weights[k : k + 1, :]) for k in range(len(hits))]
        pickers = [hit.astype(F32).astype(BF16) for hit in hits]
    else:
        pickers = [functools.reduce(jnp.logical_or, hits).astype(F32).astype(BF16)]
    for columns in column_steps(out.shape[1]):
        rows = [block[:, columns] for block in blocks]
        rows = rows[0] if len(rows) == 1 else jnp.concatenate(rows, axis=0)
        picked = [jnp.dot(picker, rows, preferred_element_type=F32) for picker in pickers]
        if weighted:
            picked = [scale * part for scale, part in zip(scales, picked)]
        out[:, columns] = sum(picked).astype(out.dtype)


def whole(count):
    return [pl.BlockSpec(memory_space=pltpu.VMEM)] * count


def write_shares(at, rows_t, grads_t, pre_grad, hidden, out):
    share = out.shape[1]
    wide, narrow = pre_grad.shape[1] // 2, hidden.shape[1] // 2

    def write(t, half):
        own = pl.ds(pl.multiple_of(at[t] * share, share), share)
        out[t, :, :wide] = jnp.dot(
            rows_t[own, :],
            pre_grad[:, half * wide : (half + 1) * wide],
            preferred_element_type=F32,
        ).astype(out.dtype)
        out[t, :, wide:] = jnp.dot(
            grads_t[own, :],
            hidden[:, half * narrow : (half + 1) * narrow],
            preferred_element_type=F32,
        ).astype(out.dtype)

    for t in range(out.shape[0]):
        write(t, t // 2 % 2)


def transpose_into(rows, rows_t):
    width = rows.shape[1]
    step = 256 if width % 256 == 0 else width

    for begin in range(0, width, step):
        rows_t[begin : begin + step, :] = rows[:, begin : begin + step].T


def join_copies(blocks, rows, sems):
    size = blocks[0].shape[0]
    joins = [
        pltpu.make_async_copy(block, rows.at[pl.ds(n * size, size)], sems.at[n])
        for n, block in enumerate(blocks)
    ]
    for join in joins:
        join.start()
    return joins


def forward_kernel(count, *refs):
    blocks, (w_in_hbm, down_hbm), (rows_t, preact, hidden), outs, scratch = (
        refs[:count],
        refs[count : count + 2],
        refs[count + 2 : count + 5],
        refs[count + 5 : 2 * count + 5],
        refs[2 * count + 5 :],
    )
    rows, w_in, down, block_sems, weight_sems, down_sem = scratch
    joins = join_copies(blocks, rows, block_sems)
    width, units = down.shape
    step = 256 if units % 256 == 0 else units
    loads = []
    for n in range(2 * units // step):
        begin = (n % 2) * units + n // 2 * step
        loads.append(
            pltpu.make_async_copy(
                w_in_hbm.at[:, pl.ds(begin, step)],
                w_in.at[:, pl.ds(begin, step)],
                weight_sems.at[n],
            )
        )
        loads[-1].start()
    load_down = pltpu.make_async_copy(down_hbm, down, down_sem)
    load_down.start()
    for join in joins:
        join.wait()
    for n in range(units // step):
        begin = n * step
        gate_at, up_at = slice(begin, begin + step), slice(units + begin, units + begin + step)
        loads[2 * n].wait()
        gate = jnp.dot(rows[...], w_in[:, gate_at], preferred_element_type=F32)
        loads[2 * n + 1].wait()
        up = jnp.dot(rows[...], w_in[:, up_at], preferred_element_type=F32)
        preact[:, gate_at] = gate
        preact[:, up_at] = up
        hidden[:, gate_at] = (gate / (1.0 + jnp.exp(-gate)) * up).astype(BF16)
    load_down.wait()
    for columns in column_steps(width):
        part = lax.dot_general(
            hidden[...], down[columns, :], (((1,), (1,)), ((), ())), preferred_element_type=F32
        )
        put_blocks(outs, part.astype(BF16), columns)
    transpose_into(rows, rows_t)


def forward(blocks, w_in, down):
    width, units = down.shape
    slots = sum(block.shape[0] for block in blocks)
    count = len(blocks)
    rows_t, preact, hidden, *outs = pl.pallas_call(
        functools.partial(forward_kernel, count),
        out_shape=(
            jax.ShapeDtypeStruct((width, slots), BF16),
            jax.ShapeDtypeStruct((slots, 2 * units), F32),
            jax.ShapeDtypeStruct((slots, units), BF16),
            *[jax.ShapeDtypeStruct(block.shape, BF16) for block in blocks],
        ),
        in_specs=anywhere(count) + in_hbm(2),
        out_specs=whole(3 + count),
        scratch_shapes=[
            pltpu.VMEM((slots, width), BF16),
            pltpu.VMEM(w_in.shape, BF16),
            pltpu.VMEM(down.shape, BF16),
            pltpu.SemaphoreType.DMA((count,)),
            pltpu.SemaphoreType.DMA((2 * units // min(units, 256),)),
            pltpu.SemaphoreType.DMA,
        ],
        compiler_params=pltpu.CompilerParams(vmem_limit_bytes=46 * 1024 * 1024),
        cost_estimate=BRIEF,
    )(*blocks, w_in, down)
    return rows_t, preact, hidden, outs


def backward_kernel(count, at, preact_hbm, w_in_hbm, rows_t, hidden, down, *refs):
    blocks, (pre_grad, grads_t, sent, w_in, *refs) = refs[:count], refs[count:]
    grads, preact, block_sems, load_sem, sem = refs
    joins = join_copies(blocks, grads, block_sems)
    fetch = pltpu.make_async_copy(preact_hbm, preact, sem)
    fetch.start()
    load = pltpu.make_async_copy(w_in_hbm, w_in, load_sem)
    load.start()
    units = down.shape[1]
    for join in joins:
        join.wait()
    fetch.wait()
    step = 256 if units % 256 == 0 else units
    for begin in range(0, units, step):
        gate = preact[:, begin : begin + step]
        up = preact[:, units + begin : units + begin + step]
        hidden_grad = jnp.dot(
            grads[...], down[:, begin : begin + step], preferred_element_type=F32
        )
        sigmoid = 1.0 / (1.0 + jnp.exp(-gate))
        gate_grad = hidden_grad * up * sigmoid * (1.0 + gate * (1.0 - sigmoid))
        up_grad = hidden_grad * gate * sigmoid
        pre_grad[:, begin : begin + step] = gate_grad.astype(BF16)
        pre_grad[:, units + begin : units + begin + step] = up_grad.astype(BF16)
    transpose_into(grads, grads_t)
    write_shares(at, rows_t, grads_t, pre_grad, hidden, sent)
    load.wait()


def return_kernel(count, alone, pre_grad, w_in, *refs):
    blocks, outs, sems = refs[:count], refs[count : 2 * count], refs[-1]
    size = blocks[0].shape[0]
    copies = [
        pltpu.make_async_copy(block, out.at[pl.ds(0, size)], sems.at[n])
        for n, (block, out) in enumerate(zip(blocks, outs))
        if n != alone
    ]
    for copy in copies:
        copy.start()
    for columns in column_steps(w_in.shape[0]):
        part = lax.dot_general(
            pre_grad[...], w_in[columns, :], (((1,), (1,)), ((), ())), preferred_element_type=F32
        ).astype(BF16)
        for n, out in enumerate(outs):
            out[out.shape[0] - size :, columns] = part[n * size : (n + 1) * size]
    for copy in copies:
        copy.wait()


def returns(pre_grad, w_in, produced, alone):
    count = len(produced)
    size, width = produced[0].shape
    return pl.pallas_call(
        functools.partial(return_kernel, count, alone),
        out_shape=[
            jax.ShapeDtypeStruct((size if n == alone else 2 * size, width), BF16)
            for n in range(count)
        ],
        in_specs=whole(2) + anywhere(count),
        out_specs=whole(count),
        scratch_shapes=[pltpu.SemaphoreType.DMA((count,))],
        compiler_params=ROOMY,
        cost_estimate=BRIEF,
    )(pre_grad, w_in, *produced)


def anywhere(count):
    return [pl.BlockSpec(memory_space=pl.ANY)] * count


def in_hbm(count):
    return [pl.BlockSpec(memory_space=pltpu.HBM)] * count


def backward(at, share, preact, w_in, rows_t, hidden, down, blocks):
    width, units = down.shape
    slots = preact.shape[0]
    count = len(blocks)
    return pl.pallas_call(
        functools.partial(backward_kernel, count),
        out_shape=(
            jax.ShapeDtypeStruct((slots, 2 * units), BF16),
            jax.ShapeDtypeStruct((width, slots), BF16),
            jax.ShapeDtypeStruct((at.shape[0], share, 3 * units // 2), BF16),
            jax.ShapeDtypeStruct(w_in.shape, BF16),
        ),
        in_specs=[pl.BlockSpec(memory_space=pltpu.SMEM)]
        + anywhere(2)
        + whole(3)
        + anywhere(count),
        out_specs=whole(4),
        scratch_shapes=[
            pltpu.VMEM((slots, width), BF16),
            pltpu.VMEM((slots, 2 * units), F32),
            pltpu.SemaphoreType.DMA((count,)),
            pltpu.SemaphoreType.DMA,
            pltpu.SemaphoreType.DMA,
        ],
        compiler_params=BIG,
        cost_estimate=BRIEF,
    )(at, preact, w_in, rows_t, hidden, down, *blocks)


def shares(at, share, rows_t, grads_t, pre_grad, hidden, cost):
    units = hidden.shape[1]
    return pl.pallas_call(
        write_shares,
        out_shape=jax.ShapeDtypeStruct((at.shape[0], share, 3 * units // 2), BF16),
        in_specs=[pl.BlockSpec(memory_space=pltpu.SMEM)] + whole(4),
        out_specs=whole(1)[0],
        compiler_params=ROOMY,
        cost_estimate=cost,
    )(at, rows_t, grads_t, pre_grad, hidden)


def add_kernel(kept, got, left, right):
    half = left.shape[0]
    left[...] = add(kept[:half], got[:half]).astype(BF16)
    right[...] = add(kept[half:], got[half : 2 * half]).astype(BF16)


def next_kernel(kept, got, left_in, right_in, left_send, right_send):
    first = got.shape[0] // 2
    left_send[...] = (add(kept[1], got[first + 1]) + left_in[1].astype(F32)).astype(BF16)
    right_send[...] = (add(kept[3], got[first + 3]) + right_in[1].astype(F32)).astype(BF16)


def own_kernel(kept, got, left_in, right_in, left, right):
    first = got.shape[0] // 2
    left[...] = add(kept[0], got[first]) + left_in[0].astype(F32)
    right[...] = add(kept[2], got[first + 2]) + right_in[0].astype(F32)


def add(left, right):
    return left.astype(F32) + right.astype(F32)


CUBE_SEND = (3, 7, 5, 7, 1, 5, 1, 3)


def swap(block, bit):
    return lax.ppermute(block, "dp", [(at, at ^ bit) for at in range(lax.axis_size("dp"))])


def cube_sum(got, kept_first, kept_later):
    _, share, columns = got.shape

    def run(kernel, out_shape, inputs, cost=BRIEF):
        return pl.pallas_call(
            kernel,
            out_shape=out_shape,
            in_specs=whole(len(inputs)),
            out_specs=whole(len(out_shape)),
            compiler_params=ROOMY,
            cost_estimate=cost,
        )(*inputs)

    half = jax.ShapeDtypeStruct((2, share, columns), BF16)
    one = jax.ShapeDtypeStruct((share, columns), BF16)
    own = jax.ShapeDtypeStruct((share, columns), F32)
    left, right = run(add_kernel, (half, half), (kept_first, got))
    parts = (kept_later, got, swap(left, 2), swap(right, 4))
    left_send, right_send = run(next_kernel, (one, one), parts)
    left, right = run(own_kernel, (own, own), parts, COVER)
    return left, swap(left_send, 4), right, swap(right_send, 2)


def after(value, *others):
    return lax.optimization_barrier((value, *others))[0]


def partial_kernel(experts, capacity, alone, late, first, routes, scores, *refs):
    own, early, mixed, back, late_picker, scales = refs
    slots, toks = experts * capacity, mixed.shape[0]
    places = lax.broadcasted_iota(jnp.int32, (toks, slots), 1).astype(F32)
    hits = [
        places == to_column(row) for row in slot_rows(first[0], routes[...], experts, capacity)
    ]
    hits.append(functools.reduce(jnp.logical_or, hits))
    picker = jnp.concatenate([hit.astype(F32).astype(BF16) for hit in hits], axis=0)
    weights = weight_rows(scores[...])
    for k in range(scales.shape[0]):
        scales[k] = jnp.broadcast_to(to_column(weights[k : k + 1, :]), scales.shape[1:])

    def slots_of(blocks):
        parts = [picker[:, n * capacity : (n + 1) * capacity] for n in blocks]
        return jnp.concatenate(parts, axis=1)

    late_picker[...] = slots_of(late + [alone])
    now = slots_of((0, alone))
    for columns in column_steps(mixed.shape[1]):
        outputs = jnp.concatenate([own[:capacity, columns], early[:, columns]], axis=0)
        total, grad = sum_rows(now, scales, outputs, own[capacity:, columns])
        mixed[:, columns] = total
        back[:, columns] = grad


def sum_rows(picker, scales, outputs, gradients):
    tops, toks = scales.shape[:2]
    chosen = picker[: tops * toks, : outputs.shape[0]]
    picked = jnp.dot(chosen, outputs, preferred_element_type=F32)
    total = sum(scales[k, :, :1] * picked[k * toks : (k + 1) * toks] for k in range(tops))
    either = picker[tops * toks :, : gradients.shape[0]]
    return total, jnp.dot(either, gradients, preferred_element_type=F32)


def mean_kernel(count, left, left_last, right, right_last, wide, narrow):
    middle, edge = wide.shape[1] // 2, narrow.shape[1] // 2
    for at, (own, last) in enumerate(((left, left_last), (right, right_last))):
        total = (own[...] + last[...].astype(F32)) / count
        wide[:, at * middle : (at + 1) * middle] = total[:, :middle]
        narrow[:, at * edge : (at + 1) * edge] = total[:, middle:]


def means(count, sums):
    share, columns = sums[0].shape
    return pl.pallas_call(
        functools.partial(mean_kernel, count),
        out_shape=(
            jax.ShapeDtypeStruct((share, 4 * columns // 3), F32),
            jax.ShapeDtypeStruct((share, 2 * columns // 3), F32),
        ),
        in_specs=whole(4),
        out_specs=whole(2),
        compiler_params=ROOMY,
        cost_estimate=BRIEF,
    )(*sums)


def last_kernel(capacity, number, picker, scales, mixed_part, back_part, *refs):
    blocks, (mixed, back), (mixed_vmem, back_vmem, sems) = (
        refs[:number],
        refs[number : number + 2],
        refs[number + 2 :],
    )
    stores = []
    for c, columns in enumerate(column_steps(mixed.shape[1])):
        outputs = jnp.concatenate([block[:capacity, columns] for block in blocks[:-1]], axis=0)
        gradients = jnp.concatenate(
            [block[block.shape[0] - capacity :, columns] for block in blocks], axis=0
        )
        total, grad = sum_rows(picker[...], scales, outputs, gradients)
        mixed_vmem[:, columns] = (total + mixed_part[:, columns]).astype(BF16)
        back_vmem[:, columns] = (grad + back_part[:, columns]).astype(BF16)
        for n, (source, target) in enumerate(((mixed_vmem, mixed), (back_vmem, back))):
            stores.append(
                pltpu.make_async_copy(source.at[:, columns], target.at[:, columns], sems.at[c, n])
            )
            stores[-1].start()
    for stored in stores:
        stored.wait()


def last(capacity, parts, blocks):
    toks, width = parts[-1].shape
    out_shape = jax.ShapeDtypeStruct((toks, width), BF16)
    return pl.pallas_call(
        functools.partial(last_kernel, capacity, len(blocks)),
        out_shape=(out_shape, out_shape),
        in_specs=whole(4 + len(blocks)),
        out_specs=anywhere(2),
        scratch_shapes=[pltpu.VMEM((toks, width), BF16)] * 2
        + [pltpu.SemaphoreType.DMA((len(column_steps(width)), 2))],
        compiler_params=ROOMY,
        cost_estimate=BRIEF,
    )(*parts, *blocks)


def dispatch(experts, capacity, out_shape, first, *sources):
    weighted = len(sources) > 2
    return pl.pallas_call(
        functools.partial(dispatch_kernel, experts, capacity, weighted),
        out_shape=out_shape,
        in_specs=[pl.BlockSpec(memory_space=pltpu.SMEM)] + in_hbm(len(sources)),
        out_specs=anywhere(len(out_shape)),
        scratch_shapes=[pltpu.VMEM(out.shape, out.dtype) for out in out_shape]
        + [pltpu.VMEM(source.shape, source.dtype) for source in sources]
        + [
            pltpu.SemaphoreType.DMA((len(sources),)),
            pltpu.SemaphoreType.DMA((len(column_steps(out_shape[0].shape[1])), len(out_shape))),
        ],
        compiler_params=ALONE,
        cost_estimate=BRIEF,
    )(first, *sources)


def call(kernel, out_shape, inputs):
    return pl.pallas_call(
        kernel,
        out_shape=out_shape,
        in_specs=[pl.BlockSpec(memory_space=pltpu.SMEM)]
        + [pl.BlockSpec(memory_space=pltpu.VMEM)] * (len(inputs) - 1),
        compiler_params=ROOMY,
        cost_estimate=BRIEF,
    )(*inputs)


def body(tokens, routes, route_scores, out_grad, gate_up, down_weight):
    experts = lax.axis_size("expert")
    groups = lax.axis_size("dp")
    toks, width = tokens.shape
    tops = routes.shape[1]
    units = down_weight.shape[2]
    capacity = (toks * tops + experts - 1) // experts
    slots = experts * capacity
    share = width // groups
    direct = experts <= 8 and capacity % 16 == 0
    w_in, w_out = gate_up[0], down_weight[0]
    routes_t, scores_t = routes.T, route_scores.T
    me = lax.axis_index("expert") if direct else jnp.int32(0)
    first = me.astype(jnp.int32).reshape(1)
    sizes = [capacity] * experts if direct else [slots]
    block_shapes = [jax.ShapeDtypeStruct((size, width), BF16) for size in sizes]

    def travel(block, step, sign):
        pairs = [(at, (at + sign * step) % experts) for at in range(experts)]
        return lax.ppermute(block, "expert", pairs)

    def exchange(blocks, sign):
        if not direct:
            block = blocks[0].reshape(experts, capacity, width)
            moved = lax.all_to_all(block, "expert", split_axis=0, concat_axis=0, tiled=True)
            return [moved.reshape(slots, width)]
        steps = range(1, experts) if sign > 0 else range(experts - 1, 0, -1)
        moved = {step: travel(blocks[step], step, sign) for step in steps}
        return [blocks[0]] + [moved[step] for step in range(1, experts)]

    def joined(blocks):
        return blocks[0] if len(blocks) == 1 else jnp.concatenate(blocks, axis=0)

    def split(rows):
        return [rows[at : at + sizes[0]] for at in range(0, slots, sizes[0])]

    sent_rows = dispatch(experts, capacity, block_shapes, first, routes_t, tokens)
    got_rows = exchange(sent_rows, 1)
    sent_grads = dispatch(experts, capacity, block_shapes, first, routes_t, scores_t, out_grad)
    out_shape = jax.ShapeDtypeStruct((toks, width), BF16)
    cube = direct and experts == 4 and groups == 8 and share % 256 == 0
    if cube:
        sent_grads = after(sent_grads, got_rows[experts // 2])
        got_grads = exchange(sent_grads, 1)
        rows_t, preact, hidden, produced = forward(got_rows, w_in, w_out)
        got_grads = after(got_grads, hidden)
        own = lax.axis_index("dp")
        send_at = jnp.stack([jnp.bitwise_xor(own, j) for j in CUBE_SEND]).astype(jnp.int32)
        keep_at = jnp.bitwise_xor(send_at, 1)
        early = experts - 1
        early_out = travel(produced[early], early, -1)
        pre_grad, grads_t, sent, w_in_here = backward(
            send_at, share, preact, w_in, rows_t, hidden, w_out, got_grads
        )
        operands = (share, rows_t, grads_t, pre_grad, hidden)
        got = swap(sent, 1)
        blocks = returns(after(pre_grad, sent), w_in_here, produced, early)
        half = len(CUBE_SEND) // 2
        kept_first = shares(after(keep_at[:half], blocks[0]), *operands, COVER)
        returned = exchange(blocks, -1)
        kept_later = shares(after(keep_at[half:], kept_first, early_out, got), *operands, COVER)
        sums = cube_sum(got, kept_first, kept_later)
        late = [n for n in range(experts - 1, 0, -1) if n != early]
        mixed_part, back_part, picker, scales = call(
            functools.partial(partial_kernel, experts, capacity, early, late),
            (
                jax.ShapeDtypeStruct((toks, width), F32),
                jax.ShapeDtypeStruct((toks, width), F32),
                jax.ShapeDtypeStruct(((tops + 1) * toks, (len(late) + 1) * capacity), BF16),
                jax.ShapeDtypeStruct((tops, toks, 128), F32),
            ),
            (after(first, sums[0]), routes_t, scores_t, returned[0], early_out),
        )
        grad_in, grad_down = means(groups, sums)
        parts = (after(picker, grad_in), scales, mixed_part, back_part)
        mixed_out, token_grad = last(capacity, parts, [returned[n] for n in late + [early]])
    else:
        token_rows = joined(got_rows)
        grad_rows = joined(exchange(sent_grads, 1))
        preact = jnp.dot(token_rows, w_in, preferred_element_type=F32)
        gate, up = preact[:, :units], preact[:, units:]
        hidden = (jax.nn.silu(gate) * up).astype(BF16)
        produced = jnp.dot(hidden, w_out.T, preferred_element_type=F32).astype(BF16)
        returned = exchange(split(produced), -1)
        hidden_grad = jnp.dot(grad_rows, w_out, preferred_element_type=F32)
        sigmoid = jax.nn.sigmoid(gate)
        gate_grad = hidden_grad * up * sigmoid * (1.0 + gate * (1.0 - sigmoid))
        up_grad = hidden_grad * gate * sigmoid
        pre_grad = jnp.concatenate([gate_grad, up_grad], axis=1).astype(BF16)
        input_grad = jnp.dot(pre_grad, w_in.T, preferred_element_type=F32).astype(BF16)
        sent_back = exchange(split(input_grad), -1)

        def summed(left, right):
            part = contract(left, right).astype(BF16)
            total = lax.psum_scatter(part, "dp", scatter_dimension=0, tiled=True)
            return total.astype(F32) / groups

        grad_in = summed(token_rows, pre_grad)
        grad_down = summed(grad_rows, hidden)
        mixed_out = call(
            functools.partial(combine_kernel, experts, capacity, True),
            out_shape,
            (first, routes_t, scores_t, *returned),
        )
        token_grad = call(
            functools.partial(combine_kernel, experts, capacity, False),
            out_shape,
            (first, routes_t, *sent_back),
        )
    grad_in = grad_in.reshape(1, share, 2 * units)
    grad_down = grad_down.reshape(1, share, units)
    return (mixed_out, token_grad, grad_in, grad_down)


def solution(mesh):
    in_specs = (
        P(("dp", "expert"), None),
        P(("dp", "expert"), None),
        P(("dp", "expert"), None),
        P(("dp", "expert"), None),
        P("expert", None, None),
        P("expert", None, None),
    )
    out_specs = (
        P(("dp", "expert"), None),
        P(("dp", "expert"), None),
        P("expert", "dp", None),
        P("expert", "dp", None),
    )
    return jax.shard_map(body, mesh=mesh, in_specs=in_specs, out_specs=out_specs, check_vma=False)
```

```python
import functools

import jax
import jax.numpy as jnp
from jax import lax
from jax.experimental import pallas as pl
from jax.experimental.pallas import tpu as pltpu
from jax.sharding import PartitionSpec as P

F32 = jnp.float32
BF16 = jnp.bfloat16
BRIEF = pl.CostEstimate(flops=1024, bytes_accessed=1024, transcendentals=0)
COVER = pl.CostEstimate(flops=4 * 10**10, bytes_accessed=1024, transcendentals=0)
ROOMY = pltpu.CompilerParams(vmem_limit_bytes=16 * 1024 * 1024)
BIG = pltpu.CompilerParams(vmem_limit_bytes=28 * 1024 * 1024)
ALONE = pltpu.CompilerParams(vmem_limit_bytes=60 * 1024 * 1024)


def contract(left, right):
    return lax.dot_general(left, right, (((0,), (0,)), ((), ())), preferred_element_type=F32)


def slot_rows(first, routes, experts, capacity):
    tops, toks = routes.shape
    padded = -(-experts // 8) * 8
    rows = lax.broadcasted_iota(jnp.int32, (padded, toks), 0)
    ids = rows + first
    ids = jnp.where(ids >= experts, ids - experts, ids)
    ids = jnp.where(rows < experts, ids, -1)
    hits = [routes[k : k + 1, :] == ids for k in range(tops)]
    named = functools.reduce(jnp.logical_or, hits)
    before = lax.broadcasted_iota(jnp.int32, (toks, toks), 0) < lax.broadcasted_iota(
        jnp.int32, (toks, toks), 1
    )
    position = jnp.dot(
        named.astype(F32).astype(BF16),
        before.astype(F32).astype(BF16),
        preferred_element_type=F32,
    )
    slot = position + (rows * capacity).astype(F32)
    return [jnp.sum(jnp.where(hit, slot, 0.0), axis=0, keepdims=True) for hit in hits]


def weight_rows(scores):
    grown = jnp.exp(scores)
    return grown / jnp.sum(grown, axis=0, keepdims=True)


def to_column(row):
    toks = row.shape[1]
    same = lax.broadcasted_iota(jnp.int32, (toks, toks), 0) == lax.broadcasted_iota(
        jnp.int32, (toks, toks), 1
    )
    return jnp.sum(jnp.where(same, row, 0.0), axis=1, keepdims=True)


def put_blocks(outs, rows, columns):
    start = 0
    for out in outs:
        size = out.shape[0]
        out[:, columns] = rows[start : start + size]
        start += size


def column_steps(width):
    step = 512 if width % 512 == 0 else width
    return [slice(at, at + step) for at in range(0, width, step)]


def dispatch_kernel(experts, capacity, weighted, first, *refs):
    count = 2 + weighted
    sources, refs = refs[:count], refs[count:]
    number = (len(refs) - count - 2) // 2
    outs, ready, (*held, sems, out_sems) = refs[:number], refs[number : 2 * number], refs[2 * number :]
    copies = [
        pltpu.make_async_copy(source, place, sems.at[n])
        for n, (source, place) in enumerate(zip(sources, held))
    ]
    for copy in copies:
        copy.start()
    routes, values = held[0], held[-1]
    scores = held[1] if weighted else None
    for copy in copies[:-1]:
        copy.wait()
    slots, toks = experts * capacity, values.shape[0]
    places = lax.broadcasted_iota(jnp.int32, (slots, toks), 0).astype(F32)
    hits = [places == row for row in slot_rows(first[0], routes[...], experts, capacity)]
    picker = functools.reduce(jnp.logical_or, hits).astype(F32).astype(BF16)
    if weighted:
        weights = weight_rows(scores[...])
        scale = sum(
            jnp.sum(jnp.where(hit, weights[k : k + 1, :], 0.0), axis=1, keepdims=True)
            for k, hit in enumerate(hits)
        )
    copies[-1].wait()
    stores = []
    for c, columns in enumerate(column_steps(values.shape[1])):
        rows = jnp.dot(picker, values[:, columns], preferred_element_type=F32)
        if weighted:
            rows = rows * scale
        put_blocks(ready, rows.astype(BF16), columns)
        for n, (block, out) in enumerate(zip(ready, outs)):
            stores.append(
                pltpu.make_async_copy(block.at[:, columns], out.at[:, columns], out_sems.at[c, n])
            )
            stores[-1].start()
    for store in stores:
        store.wait()


def combine_kernel(experts, capacity, weighted, first, routes, *refs):
    scores = refs[0] if weighted else None
    blocks, out = refs[weighted:-1], refs[-1]
    slots, toks = experts * capacity, out.shape[0]
    places = lax.broadcasted_iota(jnp.int32, (toks, slots), 1).astype(F32)
    hits = [
        places == to_column(row) for row in slot_rows(first[0], routes[...], experts, capacity)
    ]
    if weighted:
        weights = weight_rows(scores[...])
        scales = [to_column(weights[k : k + 1, :]) for k in range(len(hits))]
        pickers = [hit.astype(F32).astype(BF16) for hit in hits]
    else:
        pickers = [functools.reduce(jnp.logical_or, hits).astype(F32).astype(BF16)]
    for columns in column_steps(out.shape[1]):
        rows = [block[:, columns] for block in blocks]
        rows = rows[0] if len(rows) == 1 else jnp.concatenate(rows, axis=0)
        picked = [jnp.dot(picker, rows, preferred_element_type=F32) for picker in pickers]
        if weighted:
            picked = [scale * part for scale, part in zip(scales, picked)]
        out[:, columns] = sum(picked).astype(out.dtype)


def whole(count):
    return [pl.BlockSpec(memory_space=pltpu.VMEM)] * count


def write_shares(at, rows_t, grads_t, pre_grad, hidden, out):
    share = out.shape[1]
    wide, narrow = pre_grad.shape[1] // 2, hidden.shape[1] // 2

    def write(t, half):
        own = pl.ds(pl.multiple_of(at[t] * share, share), share)
        out[t, :, :wide] = jnp.dot(
            rows_t[own, :],
            pre_grad[:, half * wide : (half + 1) * wide],
            preferred_element_type=F32,
        ).astype(out.dtype)
        out[t, :, wide:] = jnp.dot(
            grads_t[own, :],
            hidden[:, half * narrow : (half + 1) * narrow],
            preferred_element_type=F32,
        ).astype(out.dtype)

    for t in range(out.shape[0]):
        write(t, t // 2 % 2)


def side_by_side(blocks, columns):
    if len(blocks) == 1:
        return blocks[0][:, columns]
    return jnp.concatenate([block[:, columns] for block in blocks], axis=0)


def transpose_into(blocks, rows_t):
    width = rows_t.shape[0]
    step = 256 if width % 256 == 0 else width

    for begin in range(0, width, step):
        rows_t[begin : begin + step, :] = side_by_side(blocks, slice(begin, begin + step)).T


def join_copies(blocks, rows, sems):
    size = blocks[0].shape[0]
    joins = [
        pltpu.make_async_copy(block, rows.at[pl.ds(n * size, size)], sems.at[n])
        for n, block in enumerate(blocks)
    ]
    for join in joins:
        join.start()
    return joins


def forward_kernel(count, *refs):
    blocks, (w_in_hbm, down_hbm), (rows_t, preact, hidden), outs, scratch = (
        refs[:count],
        refs[count : count + 2],
        refs[count + 2 : count + 5],
        refs[count + 5 : 2 * count + 5],
        refs[2 * count + 5 :],
    )
    rows, w_in, down, block_sems, weight_sems, down_sem = scratch
    joins = join_copies(blocks, rows, block_sems)
    width, units = down.shape
    step = 256 if units % 256 == 0 else units
    loads = []
    for n in range(2 * units // step):
        begin = (n % 2) * units + n // 2 * step
        loads.append(
            pltpu.make_async_copy(
                w_in_hbm.at[:, pl.ds(begin, step)],
                w_in.at[:, pl.ds(begin, step)],
                weight_sems.at[n],
            )
        )
        loads[-1].start()
    load_down = pltpu.make_async_copy(down_hbm, down, down_sem)
    load_down.start()
    for join in joins:
        join.wait()
    for n in range(units // step):
        begin = n * step
        gate_at, up_at = slice(begin, begin + step), slice(units + begin, units + begin + step)
        loads[2 * n].wait()
        gate = jnp.dot(rows[...], w_in[:, gate_at], preferred_element_type=F32)
        loads[2 * n + 1].wait()
        up = jnp.dot(rows[...], w_in[:, up_at], preferred_element_type=F32)
        preact[:, gate_at] = gate
        preact[:, up_at] = up
        hidden[:, gate_at] = (gate / (1.0 + jnp.exp(-gate)) * up).astype(BF16)
    load_down.wait()
    for columns in column_steps(width):
        part = lax.dot_general(
            hidden[...], down[columns, :], (((1,), (1,)), ((), ())), preferred_element_type=F32
        )
        put_blocks(outs, part.astype(BF16), columns)
    transpose_into([rows], rows_t)


def forward(blocks, w_in, down):
    width, units = down.shape
    slots = sum(block.shape[0] for block in blocks)
    count = len(blocks)
    rows_t, preact, hidden, *outs = pl.pallas_call(
        functools.partial(forward_kernel, count),
        out_shape=(
            jax.ShapeDtypeStruct((width, slots), BF16),
            jax.ShapeDtypeStruct((slots, 2 * units), F32),
            jax.ShapeDtypeStruct((slots, units), BF16),
            *[jax.ShapeDtypeStruct(block.shape, BF16) for block in blocks],
        ),
        in_specs=anywhere(count) + in_hbm(2),
        out_specs=whole(3 + count),
        scratch_shapes=[
            pltpu.VMEM((slots, width), BF16),
            pltpu.VMEM(w_in.shape, BF16),
            pltpu.VMEM(down.shape, BF16),
            pltpu.SemaphoreType.DMA((count,)),
            pltpu.SemaphoreType.DMA((2 * units // min(units, 256),)),
            pltpu.SemaphoreType.DMA,
        ],
        compiler_params=pltpu.CompilerParams(vmem_limit_bytes=46 * 1024 * 1024),
        cost_estimate=BRIEF,
    )(*blocks, w_in, down)
    return rows_t, preact, hidden, outs


def backward_kernel(count, at, preact_hbm, w_in_hbm, rows_t, hidden, down, *refs):
    blocks, (pre_grad, grads_t, sent, w_in, *refs) = refs[:count], refs[count:]
    preact, load_sem, sem = refs
    fetch = pltpu.make_async_copy(preact_hbm, preact, sem)
    fetch.start()
    load = pltpu.make_async_copy(w_in_hbm, w_in, load_sem)
    load.start()
    units = down.shape[1]
    fetch.wait()
    grads = side_by_side(blocks, slice(0, down.shape[0]))
    step = 256 if units % 256 == 0 else units
    for begin in range(0, units, step):
        gate = preact[:, begin : begin + step]
        up = preact[:, units + begin : units + begin + step]
        hidden_grad = jnp.dot(grads, down[:, begin : begin + step], preferred_element_type=F32)
        sigmoid = 1.0 / (1.0 + jnp.exp(-gate))
        gate_grad = hidden_grad * up * sigmoid * (1.0 + gate * (1.0 - sigmoid))
        up_grad = hidden_grad * gate * sigmoid
        pre_grad[:, begin : begin + step] = gate_grad.astype(BF16)
        pre_grad[:, units + begin : units + begin + step] = up_grad.astype(BF16)
    transpose_into(blocks, grads_t)
    write_shares(at, rows_t, grads_t, pre_grad, hidden, sent)
    load.wait()


def return_kernel(count, alone, pre_grad, w_in, *refs):
    blocks, outs, sems = refs[:count], refs[count : 2 * count], refs[-1]
    size = blocks[0].shape[0]
    copies = [
        pltpu.make_async_copy(block, out.at[pl.ds(0, size)], sems.at[n])
        for n, (block, out) in enumerate(zip(blocks, outs))
        if n != alone
    ]
    for copy in copies:
        copy.start()
    for columns in column_steps(w_in.shape[0]):
        part = lax.dot_general(
            pre_grad[...], w_in[columns, :], (((1,), (1,)), ((), ())), preferred_element_type=F32
        ).astype(BF16)
        for n, out in enumerate(outs):
            out[out.shape[0] - size :, columns] = part[n * size : (n + 1) * size]
    for copy in copies:
        copy.wait()


def returns(pre_grad, w_in, produced, alone):
    count = len(produced)
    size, width = produced[0].shape
    return pl.pallas_call(
        functools.partial(return_kernel, count, alone),
        out_shape=[
            jax.ShapeDtypeStruct((size if n == alone else 2 * size, width), BF16)
            for n in range(count)
        ],
        in_specs=whole(2) + anywhere(count),
        out_specs=whole(count),
        scratch_shapes=[pltpu.SemaphoreType.DMA((count,))],
        compiler_params=ROOMY,
        cost_estimate=BRIEF,
    )(pre_grad, w_in, *produced)


def anywhere(count):
    return [pl.BlockSpec(memory_space=pl.ANY)] * count


def in_hbm(count):
    return [pl.BlockSpec(memory_space=pltpu.HBM)] * count


def backward(at, share, preact, w_in, rows_t, hidden, down, blocks):
    width, units = down.shape
    slots = preact.shape[0]
    count = len(blocks)
    return pl.pallas_call(
        functools.partial(backward_kernel, count),
        out_shape=(
            jax.ShapeDtypeStruct((slots, 2 * units), BF16),
            jax.ShapeDtypeStruct((width, slots), BF16),
            jax.ShapeDtypeStruct((at.shape[0], share, 3 * units // 2), BF16),
            jax.ShapeDtypeStruct(w_in.shape, BF16),
        ),
        in_specs=[pl.BlockSpec(memory_space=pltpu.SMEM)]
        + anywhere(2)
        + whole(3 + count),
        out_specs=whole(4),
        scratch_shapes=[
            pltpu.VMEM((slots, 2 * units), F32),
            pltpu.SemaphoreType.DMA,
            pltpu.SemaphoreType.DMA,
        ],
        compiler_params=BIG,
        cost_estimate=BRIEF,
    )(at, preact, w_in, rows_t, hidden, down, *blocks)


def shares(at, share, rows_t, grads_t, pre_grad, hidden, cost):
    units = hidden.shape[1]
    return pl.pallas_call(
        write_shares,
        out_shape=jax.ShapeDtypeStruct((at.shape[0], share, 3 * units // 2), BF16),
        in_specs=[pl.BlockSpec(memory_space=pltpu.SMEM)] + whole(4),
        out_specs=whole(1)[0],
        compiler_params=ROOMY,
        cost_estimate=cost,
    )(at, rows_t, grads_t, pre_grad, hidden)


def add_kernel(kept, got, left, right):
    half = left.shape[0]
    left[...] = add(kept[:half], got[:half]).astype(BF16)
    right[...] = add(kept[half:], got[half : 2 * half]).astype(BF16)


def next_kernel(kept, got, left_in, right_in, left_send, right_send):
    first = got.shape[0] // 2
    left_send[...] = (add(kept[1], got[first + 1]) + left_in[1].astype(F32)).astype(BF16)
    right_send[...] = (add(kept[3], got[first + 3]) + right_in[1].astype(F32)).astype(BF16)


def own_kernel(kept, got, left_in, right_in, left, right):
    first = got.shape[0] // 2
    left[...] = add(kept[0], got[first]) + left_in[0].astype(F32)
    right[...] = add(kept[2], got[first + 2]) + right_in[0].astype(F32)


def add(left, right):
    return left.astype(F32) + right.astype(F32)


CUBE_SEND = (3, 7, 5, 7, 1, 5, 1, 3)


def swap(block, bit):
    return lax.ppermute(block, "dp", [(at, at ^ bit) for at in range(lax.axis_size("dp"))])


def cube_sum(got, kept_first, kept_later):
    _, share, columns = got.shape

    def run(kernel, out_shape, inputs, cost=BRIEF):
        return pl.pallas_call(
            kernel,
            out_shape=out_shape,
            in_specs=whole(len(inputs)),
            out_specs=whole(len(out_shape)),
            compiler_params=ROOMY,
            cost_estimate=cost,
        )(*inputs)

    half = jax.ShapeDtypeStruct((2, share, columns), BF16)
    one = jax.ShapeDtypeStruct((share, columns), BF16)
    own = jax.ShapeDtypeStruct((share, columns), F32)
    left, right = run(add_kernel, (half, half), (kept_first, got))
    parts = (kept_later, got, swap(left, 2), swap(right, 4))
    left_send, right_send = run(next_kernel, (one, one), parts)
    left, right = run(own_kernel, (own, own), parts, COVER)
    return left, swap(left_send, 4), right, swap(right_send, 2)


def after(value, *others):
    return lax.optimization_barrier((value, *others))[0]


def partial_kernel(experts, capacity, alone, late, first, routes, scores, *refs):
    own, early, mixed, back, late_picker, scales = refs
    slots, toks = experts * capacity, mixed.shape[0]
    places = lax.broadcasted_iota(jnp.int32, (toks, slots), 1).astype(F32)
    hits = [
        places == to_column(row) for row in slot_rows(first[0], routes[...], experts, capacity)
    ]
    hits.append(functools.reduce(jnp.logical_or, hits))
    picker = jnp.concatenate([hit.astype(F32).astype(BF16) for hit in hits], axis=0)
    weights = weight_rows(scores[...])
    for k in range(scales.shape[0]):
        scales[k] = jnp.broadcast_to(to_column(weights[k : k + 1, :]), scales.shape[1:])

    def slots_of(blocks):
        parts = [picker[:, n * capacity : (n + 1) * capacity] for n in blocks]
        return jnp.concatenate(parts, axis=1)

    late_picker[...] = slots_of(late + [alone])
    now = slots_of((0, alone))
    for columns in column_steps(mixed.shape[1]):
        outputs = jnp.concatenate([own[:capacity, columns], early[:, columns]], axis=0)
        total, grad = sum_rows(now, scales, outputs, own[capacity:, columns])
        mixed[:, columns] = total
        back[:, columns] = grad


def sum_rows(picker, scales, outputs, gradients):
    tops, toks = scales.shape[:2]
    chosen = picker[: tops * toks, : outputs.shape[0]]
    picked = jnp.dot(chosen, outputs, preferred_element_type=F32)
    total = sum(scales[k, :, :1] * picked[k * toks : (k + 1) * toks] for k in range(tops))
    either = picker[tops * toks :, : gradients.shape[0]]
    return total, jnp.dot(either, gradients, preferred_element_type=F32)


def mean_kernel(count, left, left_last, right, right_last, wide, narrow):
    middle, edge = wide.shape[1] // 2, narrow.shape[1] // 2
    for at, (own, last) in enumerate(((left, left_last), (right, right_last))):
        total = (own[...] + last[...].astype(F32)) / count
        wide[:, at * middle : (at + 1) * middle] = total[:, :middle]
        narrow[:, at * edge : (at + 1) * edge] = total[:, middle:]


def means(count, sums):
    share, columns = sums[0].shape
    return pl.pallas_call(
        functools.partial(mean_kernel, count),
        out_shape=(
            jax.ShapeDtypeStruct((share, 4 * columns // 3), F32),
            jax.ShapeDtypeStruct((share, 2 * columns // 3), F32),
        ),
        in_specs=whole(4),
        out_specs=whole(2),
        compiler_params=ROOMY,
        cost_estimate=BRIEF,
    )(*sums)


def last_kernel(capacity, number, picker, scales, mixed_part, back_part, *refs):
    blocks, (mixed, back), (mixed_vmem, back_vmem, sems) = (
        refs[:number],
        refs[number : number + 2],
        refs[number + 2 :],
    )
    stores = []
    for c, columns in enumerate(column_steps(mixed.shape[1])):
        outputs = jnp.concatenate([block[:capacity, columns] for block in blocks[:-1]], axis=0)
        gradients = jnp.concatenate(
            [block[block.shape[0] - capacity :, columns] for block in blocks], axis=0
        )
        total, grad = sum_rows(picker[...], scales, outputs, gradients)
        mixed_vmem[:, columns] = (total + mixed_part[:, columns]).astype(BF16)
        back_vmem[:, columns] = (grad + back_part[:, columns]).astype(BF16)
        for n, (source, target) in enumerate(((mixed_vmem, mixed), (back_vmem, back))):
            stores.append(
                pltpu.make_async_copy(source.at[:, columns], target.at[:, columns], sems.at[c, n])
            )
            stores[-1].start()
    for stored in stores:
        stored.wait()


def last(capacity, parts, blocks):
    toks, width = parts[-1].shape
    out_shape = jax.ShapeDtypeStruct((toks, width), BF16)
    return pl.pallas_call(
        functools.partial(last_kernel, capacity, len(blocks)),
        out_shape=(out_shape, out_shape),
        in_specs=whole(4 + len(blocks)),
        out_specs=anywhere(2),
        scratch_shapes=[pltpu.VMEM((toks, width), BF16)] * 2
        + [pltpu.SemaphoreType.DMA((len(column_steps(width)), 2))],
        compiler_params=ROOMY,
        cost_estimate=BRIEF,
    )(*parts, *blocks)


def dispatch(experts, capacity, out_shape, first, *sources):
    weighted = len(sources) > 2
    return pl.pallas_call(
        functools.partial(dispatch_kernel, experts, capacity, weighted),
        out_shape=out_shape,
        in_specs=[pl.BlockSpec(memory_space=pltpu.SMEM)] + in_hbm(len(sources)),
        out_specs=anywhere(len(out_shape)),
        scratch_shapes=[pltpu.VMEM(out.shape, out.dtype) for out in out_shape]
        + [pltpu.VMEM(source.shape, source.dtype) for source in sources]
        + [
            pltpu.SemaphoreType.DMA((len(sources),)),
            pltpu.SemaphoreType.DMA((len(column_steps(out_shape[0].shape[1])), len(out_shape))),
        ],
        compiler_params=ALONE,
        cost_estimate=BRIEF,
    )(first, *sources)


def call(kernel, out_shape, inputs):
    return pl.pallas_call(
        kernel,
        out_shape=out_shape,
        in_specs=[pl.BlockSpec(memory_space=pltpu.SMEM)]
        + [pl.BlockSpec(memory_space=pltpu.VMEM)] * (len(inputs) - 1),
        compiler_params=ROOMY,
        cost_estimate=BRIEF,
    )(*inputs)


def body(tokens, routes, route_scores, out_grad, gate_up, down_weight):
    experts = lax.axis_size("expert")
    groups = lax.axis_size("dp")
    toks, width = tokens.shape
    tops = routes.shape[1]
    units = down_weight.shape[2]
    capacity = (toks * tops + experts - 1) // experts
    slots = experts * capacity
    share = width // groups
    direct = experts <= 8 and capacity % 16 == 0
    w_in, w_out = gate_up[0], down_weight[0]
    routes_t, scores_t = routes.T, route_scores.T
    me = lax.axis_index("expert") if direct else jnp.int32(0)
    first = me.astype(jnp.int32).reshape(1)
    sizes = [capacity] * experts if direct else [slots]
    block_shapes = [jax.ShapeDtypeStruct((size, width), BF16) for size in sizes]

    def travel(block, step, sign):
        pairs = [(at, (at + sign * step) % experts) for at in range(experts)]
        return lax.ppermute(block, "expert", pairs)

    def exchange(blocks, sign):
        if not direct:
            block = blocks[0].reshape(experts, capacity, width)
            moved = lax.all_to_all(block, "expert", split_axis=0, concat_axis=0, tiled=True)
            return [moved.reshape(slots, width)]
        steps = range(1, experts) if sign > 0 else range(experts - 1, 0, -1)
        moved = {step: travel(blocks[step], step, sign) for step in steps}
        return [blocks[0]] + [moved[step] for step in range(1, experts)]

    def joined(blocks):
        return blocks[0] if len(blocks) == 1 else jnp.concatenate(blocks, axis=0)

    def split(rows):
        return [rows[at : at + sizes[0]] for at in range(0, slots, sizes[0])]

    sent_rows = dispatch(experts, capacity, block_shapes, first, routes_t, tokens)
    got_rows = exchange(sent_rows, 1)
    sent_grads = dispatch(experts, capacity, block_shapes, first, routes_t, scores_t, out_grad)
    out_shape = jax.ShapeDtypeStruct((toks, width), BF16)
    cube = direct and experts == 4 and groups == 8 and share % 256 == 0
    if cube:
        sent_grads = after(sent_grads, got_rows[1], got_rows[-1])
        got_grads = exchange(sent_grads, 1)
        rows_t, preact, hidden, produced = forward(got_rows, w_in, w_out)
        got_grads = after(got_grads, hidden)
        own = lax.axis_index("dp")
        send_at = jnp.stack([jnp.bitwise_xor(own, j) for j in CUBE_SEND]).astype(jnp.int32)
        keep_at = jnp.bitwise_xor(send_at, 1)
        early = experts - 1
        early_out = travel(produced[early], early, -1)
        pre_grad, grads_t, sent, w_in_here = backward(
            send_at, share, preact, w_in, rows_t, hidden, w_out, got_grads
        )
        operands = (share, rows_t, grads_t, pre_grad, hidden)
        got = swap(sent, 1)
        blocks = returns(after(pre_grad, sent), w_in_here, produced, early)
        half = len(CUBE_SEND) // 2
        kept_first = shares(after(keep_at[:half], blocks[0]), *operands, COVER)
        returned = exchange(blocks, -1)
        kept_later = shares(after(keep_at[half:], kept_first, early_out, got), *operands, COVER)
        sums = cube_sum(got, kept_first, kept_later)
        late = [n for n in range(experts - 1, 0, -1) if n != early]
        mixed_part, back_part, picker, scales = call(
            functools.partial(partial_kernel, experts, capacity, early, late),
            (
                jax.ShapeDtypeStruct((toks, width), F32),
                jax.ShapeDtypeStruct((toks, width), F32),
                jax.ShapeDtypeStruct(((tops + 1) * toks, (len(late) + 1) * capacity), BF16),
                jax.ShapeDtypeStruct((tops, toks, 128), F32),
            ),
            (after(first, sums[0]), routes_t, scores_t, returned[0], early_out),
        )
        grad_in, grad_down = means(groups, sums)
        parts = (after(picker, grad_in), scales, mixed_part, back_part)
        mixed_out, token_grad = last(capacity, parts, [returned[n] for n in late + [early]])
    else:
        token_rows = joined(got_rows)
        grad_rows = joined(exchange(sent_grads, 1))
        preact = jnp.dot(token_rows, w_in, preferred_element_type=F32)
        gate, up = preact[:, :units], preact[:, units:]
        hidden = (jax.nn.silu(gate) * up).astype(BF16)
        produced = jnp.dot(hidden, w_out.T, preferred_element_type=F32).astype(BF16)
        returned = exchange(split(produced), -1)
        hidden_grad = jnp.dot(grad_rows, w_out, preferred_element_type=F32)
        sigmoid = jax.nn.sigmoid(gate)
        gate_grad = hidden_grad * up * sigmoid * (1.0 + gate * (1.0 - sigmoid))
        up_grad = hidden_grad * gate * sigmoid
        pre_grad = jnp.concatenate([gate_grad, up_grad], axis=1).astype(BF16)
        input_grad = jnp.dot(pre_grad, w_in.T, preferred_element_type=F32).astype(BF16)
        sent_back = exchange(split(input_grad), -1)

        def summed(left, right):
            part = contract(left, right).astype(BF16)
            total = lax.psum_scatter(part, "dp", scatter_dimension=0, tiled=True)
            return total.astype(F32) / groups

        grad_in = summed(token_rows, pre_grad)
        grad_down = summed(grad_rows, hidden)
        mixed_out = call(
            functools.partial(combine_kernel, experts, capacity, True),
            out_shape,
            (first, routes_t, scores_t, *returned),
        )
        token_grad = call(
            functools.partial(combine_kernel, experts, capacity, False),
            out_shape,
            (first, routes_t, *sent_back),
        )
    grad_in = grad_in.reshape(1, share, 2 * units)
    grad_down = grad_down.reshape(1, share, units)
    return (mixed_out, token_grad, grad_in, grad_down)


def solution(mesh):
    in_specs = (
        P(("dp", "expert"), None),
        P(("dp", "expert"), None),
        P(("dp", "expert"), None),
        P(("dp", "expert"), None),
        P("expert", None, None),
        P("expert", None, None),
    )
    out_specs = (
        P(("dp", "expert"), None),
        P(("dp", "expert"), None),
        P("expert", "dp", None),
        P("expert", "dp", None),
    )
    return jax.shard_map(body, mesh=mesh, in_specs=in_specs, out_specs=out_specs, check_vma=False)
```

```python
import functools

import jax
import jax.numpy as jnp
from jax import lax
from jax.experimental import pallas as pl
from jax.experimental.pallas import tpu as pltpu
from jax.sharding import PartitionSpec as P

F32 = jnp.float32
BF16 = jnp.bfloat16
BRIEF = pl.CostEstimate(flops=1024, bytes_accessed=1024, transcendentals=0)
COVER = pl.CostEstimate(flops=4 * 10**10, bytes_accessed=1024, transcendentals=0)
ROOMY = pltpu.CompilerParams(vmem_limit_bytes=16 * 1024 * 1024)
BIG = pltpu.CompilerParams(vmem_limit_bytes=28 * 1024 * 1024)
ALONE = pltpu.CompilerParams(vmem_limit_bytes=60 * 1024 * 1024)


def contract(left, right):
    return lax.dot_general(left, right, (((0,), (0,)), ((), ())), preferred_element_type=F32)


def slot_rows(first, routes, experts, capacity):
    tops, toks = routes.shape
    padded = -(-experts // 8) * 8
    rows = lax.broadcasted_iota(jnp.int32, (padded, toks), 0)
    ids = rows + first
    ids = jnp.where(ids >= experts, ids - experts, ids)
    ids = jnp.where(rows < experts, ids, -1)
    hits = [routes[k : k + 1, :] == ids for k in range(tops)]
    named = functools.reduce(jnp.logical_or, hits)
    before = lax.broadcasted_iota(jnp.int32, (toks, toks), 0) < lax.broadcasted_iota(
        jnp.int32, (toks, toks), 1
    )
    position = jnp.dot(
        named.astype(F32).astype(BF16),
        before.astype(F32).astype(BF16),
        preferred_element_type=F32,
    )
    slot = position + (rows * capacity).astype(F32)
    return [jnp.sum(jnp.where(hit, slot, 0.0), axis=0, keepdims=True) for hit in hits]


def weight_rows(scores):
    grown = jnp.exp(scores)
    return grown / jnp.sum(grown, axis=0, keepdims=True)


def to_column(row):
    toks = row.shape[1]
    same = lax.broadcasted_iota(jnp.int32, (toks, toks), 0) == lax.broadcasted_iota(
        jnp.int32, (toks, toks), 1
    )
    return jnp.sum(jnp.where(same, row, 0.0), axis=1, keepdims=True)


def put_blocks(outs, rows, columns):
    start = 0
    for out in outs:
        size = out.shape[0]
        out[:, columns] = rows[start : start + size]
        start += size


def column_steps(width, step=512):
    step = step if width % step == 0 else width
    return [slice(at, at + step) for at in range(0, width, step)]


def dispatch_kernel(experts, capacity, weighted, first, *refs):
    count = 2 + weighted
    sources, refs = refs[:count], refs[count:]
    number = (len(refs) - count - 2) // 2
    outs, ready, (*held, sems, out_sems) = refs[:number], refs[number : 2 * number], refs[2 * number :]
    copies = [
        pltpu.make_async_copy(source, place, sems.at[n])
        for n, (source, place) in enumerate(zip(sources, held))
    ]
    for copy in copies:
        copy.start()
    routes, values = held[0], held[-1]
    scores = held[1] if weighted else None
    for copy in copies[:-1]:
        copy.wait()
    slots, toks = experts * capacity, values.shape[0]
    places = lax.broadcasted_iota(jnp.int32, (slots, toks), 0).astype(F32)
    hits = [places == row for row in slot_rows(first[0], routes[...], experts, capacity)]
    picker = functools.reduce(jnp.logical_or, hits).astype(F32).astype(BF16)
    if weighted:
        weights = weight_rows(scores[...])
        scale = sum(
            jnp.sum(jnp.where(hit, weights[k : k + 1, :], 0.0), axis=1, keepdims=True)
            for k, hit in enumerate(hits)
        )
    copies[-1].wait()
    stores = []
    for c, columns in enumerate(column_steps(values.shape[1], 1024)):
        rows = jnp.dot(picker, values[:, columns], preferred_element_type=F32)
        if weighted:
            rows = rows * scale
        put_blocks(ready, rows.astype(BF16), columns)
        for n, (block, out) in enumerate(zip(ready, outs)):
            stores.append(
                pltpu.make_async_copy(block.at[:, columns], out.at[:, columns], out_sems.at[c, n])
            )
            stores[-1].start()
    for store in stores:
        store.wait()


def combine_kernel(experts, capacity, weighted, first, routes, *refs):
    scores = refs[0] if weighted else None
    blocks, out = refs[weighted:-1], refs[-1]
    slots, toks = experts * capacity, out.shape[0]
    places = lax.broadcasted_iota(jnp.int32, (toks, slots), 1).astype(F32)
    hits = [
        places == to_column(row) for row in slot_rows(first[0], routes[...], experts, capacity)
    ]
    if weighted:
        weights = weight_rows(scores[...])
        scales = [to_column(weights[k : k + 1, :]) for k in range(len(hits))]
        pickers = [hit.astype(F32).astype(BF16) for hit in hits]
    else:
        pickers = [functools.reduce(jnp.logical_or, hits).astype(F32).astype(BF16)]
    for columns in column_steps(out.shape[1]):
        rows = [block[:, columns] for block in blocks]
        rows = rows[0] if len(rows) == 1 else jnp.concatenate(rows, axis=0)
        picked = [jnp.dot(picker, rows, preferred_element_type=F32) for picker in pickers]
        if weighted:
            picked = [scale * part for scale, part in zip(scales, picked)]
        out[:, columns] = sum(picked).astype(out.dtype)


def whole(count):
    return [pl.BlockSpec(memory_space=pltpu.VMEM)] * count


def write_shares(at, rows_t, grads_t, pre_grad, hidden, out):
    share = out.shape[1]
    wide, narrow = pre_grad.shape[1] // 2, hidden.shape[1] // 2

    def write(t, half):
        own = pl.ds(pl.multiple_of(at[t] * share, share), share)
        out[t, :, :wide] = jnp.dot(
            rows_t[own, :],
            pre_grad[:, half * wide : (half + 1) * wide],
            preferred_element_type=F32,
        ).astype(out.dtype)
        out[t, :, wide:] = jnp.dot(
            grads_t[own, :],
            hidden[:, half * narrow : (half + 1) * narrow],
            preferred_element_type=F32,
        ).astype(out.dtype)

    for t in range(out.shape[0]):
        write(t, t // 2 % 2)


def side_by_side(blocks, columns):
    if len(blocks) == 1:
        return blocks[0][:, columns]
    return jnp.concatenate([block[:, columns] for block in blocks], axis=0)


def transpose_into(blocks, rows_t):
    width = rows_t.shape[0]
    step = 256 if width % 256 == 0 else width

    for begin in range(0, width, step):
        rows_t[begin : begin + step, :] = side_by_side(blocks, slice(begin, begin + step)).T


def join_copies(blocks, rows, sems):
    size = blocks[0].shape[0]
    joins = [
        pltpu.make_async_copy(block, rows.at[pl.ds(n * size, size)], sems.at[n])
        for n, block in enumerate(blocks)
    ]
    for join in joins:
        join.start()
    return joins


def forward_kernel(count, *refs):
    blocks, (w_in_hbm, down_hbm), (rows_t, preact, hidden), outs, scratch = (
        refs[:count],
        refs[count : count + 2],
        refs[count + 2 : count + 5],
        refs[count + 5 : 2 * count + 5],
        refs[2 * count + 5 :],
    )
    rows, w_in, down, block_sems, weight_sems, down_sem = scratch
    joins = join_copies(blocks, rows, block_sems)
    width, units = down.shape
    step = 256 if units % 256 == 0 else units
    loads = []
    for n in range(2 * units // step):
        begin = (n % 2) * units + n // 2 * step
        loads.append(
            pltpu.make_async_copy(
                w_in_hbm.at[:, pl.ds(begin, step)],
                w_in.at[:, pl.ds(begin, step)],
                weight_sems.at[n],
            )
        )
        loads[-1].start()
    load_down = pltpu.make_async_copy(down_hbm, down, down_sem)
    load_down.start()
    for join in joins:
        join.wait()
    for n in range(units // step):
        begin = n * step
        gate_at, up_at = slice(begin, begin + step), slice(units + begin, units + begin + step)
        loads[2 * n].wait()
        gate = jnp.dot(rows[...], w_in[:, gate_at], preferred_element_type=F32)
        loads[2 * n + 1].wait()
        up = jnp.dot(rows[...], w_in[:, up_at], preferred_element_type=F32)
        preact[:, gate_at] = gate
        preact[:, up_at] = up
        hidden[:, gate_at] = (gate / (1.0 + jnp.exp(-gate)) * up).astype(BF16)
    load_down.wait()
    for columns in column_steps(width):
        part = lax.dot_general(
            hidden[...], down[columns, :], (((1,), (1,)), ((), ())), preferred_element_type=F32
        )
        put_blocks(outs, part.astype(BF16), columns)
    transpose_into([rows], rows_t)


def forward(blocks, w_in, down):
    width, units = down.shape
    slots = sum(block.shape[0] for block in blocks)
    count = len(blocks)
    rows_t, preact, hidden, *outs = pl.pallas_call(
        functools.partial(forward_kernel, count),
        out_shape=(
            jax.ShapeDtypeStruct((width, slots), BF16),
            jax.ShapeDtypeStruct((slots, 2 * units), F32),
            jax.ShapeDtypeStruct((slots, units), BF16),
            *[jax.ShapeDtypeStruct(block.shape, BF16) for block in blocks],
        ),
        in_specs=anywhere(count) + in_hbm(2),
        out_specs=whole(3 + count),
        scratch_shapes=[
            pltpu.VMEM((slots, width), BF16),
            pltpu.VMEM(w_in.shape, BF16),
            pltpu.VMEM(down.shape, BF16),
            pltpu.SemaphoreType.DMA((count,)),
            pltpu.SemaphoreType.DMA((2 * units // min(units, 256),)),
            pltpu.SemaphoreType.DMA,
        ],
        compiler_params=pltpu.CompilerParams(vmem_limit_bytes=46 * 1024 * 1024),
        cost_estimate=BRIEF,
    )(*blocks, w_in, down)
    return rows_t, preact, hidden, outs


def backward_kernel(count, at, preact_hbm, w_in_hbm, rows_t, hidden, down, *refs):
    blocks, (pre_grad, grads_t, sent, w_in, *refs) = refs[:count], refs[count:]
    preact, load_sem, sem = refs
    fetch = pltpu.make_async_copy(preact_hbm, preact, sem)
    fetch.start()
    load = pltpu.make_async_copy(w_in_hbm, w_in, load_sem)
    load.start()
    units = down.shape[1]
    fetch.wait()
    grads = side_by_side(blocks, slice(0, down.shape[0]))
    step = 256 if units % 256 == 0 else units
    for begin in range(0, units, step):
        gate = preact[:, begin : begin + step]
        up = preact[:, units + begin : units + begin + step]
        hidden_grad = jnp.dot(grads, down[:, begin : begin + step], preferred_element_type=F32)
        sigmoid = 1.0 / (1.0 + jnp.exp(-gate))
        gate_grad = hidden_grad * up * sigmoid * (1.0 + gate * (1.0 - sigmoid))
        up_grad = hidden_grad * gate * sigmoid
        pre_grad[:, begin : begin + step] = gate_grad.astype(BF16)
        pre_grad[:, units + begin : units + begin + step] = up_grad.astype(BF16)
    transpose_into(blocks, grads_t)
    write_shares(at, rows_t, grads_t, pre_grad, hidden, sent)
    load.wait()


def return_kernel(count, alone, pre_grad, w_in, *refs):
    blocks, outs, sems = refs[:count], refs[count : 2 * count], refs[-1]
    size = blocks[0].shape[0]
    copies = [
        pltpu.make_async_copy(block, out.at[pl.ds(0, size)], sems.at[n])
        for n, (block, out) in enumerate(zip(blocks, outs))
        if n != alone
    ]
    for copy in copies:
        copy.start()
    for columns in column_steps(w_in.shape[0]):
        part = lax.dot_general(
            pre_grad[...], w_in[columns, :], (((1,), (1,)), ((), ())), preferred_element_type=F32
        ).astype(BF16)
        for n, out in enumerate(outs):
            out[out.shape[0] - size :, columns] = part[n * size : (n + 1) * size]
    for copy in copies:
        copy.wait()


def returns(pre_grad, w_in, produced, alone):
    count = len(produced)
    size, width = produced[0].shape
    return pl.pallas_call(
        functools.partial(return_kernel, count, alone),
        out_shape=[
            jax.ShapeDtypeStruct((size if n == alone else 2 * size, width), BF16)
            for n in range(count)
        ],
        in_specs=whole(2) + anywhere(count),
        out_specs=whole(count),
        scratch_shapes=[pltpu.SemaphoreType.DMA((count,))],
        compiler_params=ROOMY,
        cost_estimate=BRIEF,
    )(pre_grad, w_in, *produced)


def anywhere(count):
    return [pl.BlockSpec(memory_space=pl.ANY)] * count


def in_hbm(count):
    return [pl.BlockSpec(memory_space=pltpu.HBM)] * count


def backward(at, share, preact, w_in, rows_t, hidden, down, blocks):
    width, units = down.shape
    slots = preact.shape[0]
    count = len(blocks)
    return pl.pallas_call(
        functools.partial(backward_kernel, count),
        out_shape=(
            jax.ShapeDtypeStruct((slots, 2 * units), BF16),
            jax.ShapeDtypeStruct((width, slots), BF16),
            jax.ShapeDtypeStruct((at.shape[0], share, 3 * units // 2), BF16),
            jax.ShapeDtypeStruct(w_in.shape, BF16),
        ),
        in_specs=[pl.BlockSpec(memory_space=pltpu.SMEM)]
        + anywhere(2)
        + whole(3 + count),
        out_specs=whole(4),
        scratch_shapes=[
            pltpu.VMEM((slots, 2 * units), F32),
            pltpu.SemaphoreType.DMA,
            pltpu.SemaphoreType.DMA,
        ],
        compiler_params=BIG,
        cost_estimate=BRIEF,
    )(at, preact, w_in, rows_t, hidden, down, *blocks)


def shares(at, share, rows_t, grads_t, pre_grad, hidden, cost):
    units = hidden.shape[1]
    return pl.pallas_call(
        write_shares,
        out_shape=jax.ShapeDtypeStruct((at.shape[0], share, 3 * units // 2), BF16),
        in_specs=[pl.BlockSpec(memory_space=pltpu.SMEM)] + whole(4),
        out_specs=whole(1)[0],
        compiler_params=ROOMY,
        cost_estimate=cost,
    )(at, rows_t, grads_t, pre_grad, hidden)


def add_kernel(kept, got, left, right):
    half = left.shape[0]
    left[...] = add(kept[:half], got[:half]).astype(BF16)
    right[...] = add(kept[half:], got[half : 2 * half]).astype(BF16)


def next_kernel(kept, got, left_in, right_in, left_send, right_send):
    first = got.shape[0] // 2
    left_send[...] = (add(kept[1], got[first + 1]) + left_in[1].astype(F32)).astype(BF16)
    right_send[...] = (add(kept[3], got[first + 3]) + right_in[1].astype(F32)).astype(BF16)


def own_kernel(kept, got, left_in, right_in, left, right):
    first = got.shape[0] // 2
    left[...] = add(kept[0], got[first]) + left_in[0].astype(F32)
    right[...] = add(kept[2], got[first + 2]) + right_in[0].astype(F32)


def add(left, right):
    return left.astype(F32) + right.astype(F32)


CUBE_SEND = (3, 7, 5, 7, 1, 5, 1, 3)


def swap(block, bit):
    return lax.ppermute(block, "dp", [(at, at ^ bit) for at in range(lax.axis_size("dp"))])


def cube_sum(got, kept_first, kept_later):
    _, share, columns = got.shape

    def run(kernel, out_shape, inputs, cost=BRIEF):
        return pl.pallas_call(
            kernel,
            out_shape=out_shape,
            in_specs=whole(len(inputs)),
            out_specs=whole(len(out_shape)),
            compiler_params=ROOMY,
            cost_estimate=cost,
        )(*inputs)

    half = jax.ShapeDtypeStruct((2, share, columns), BF16)
    one = jax.ShapeDtypeStruct((share, columns), BF16)
    own = jax.ShapeDtypeStruct((share, columns), F32)
    left, right = run(add_kernel, (half, half), (kept_first, got))
    parts = (kept_later, got, swap(left, 2), swap(right, 4))
    left_send, right_send = run(next_kernel, (one, one), parts)
    left, right = run(own_kernel, (own, own), parts, COVER)
    return left, swap(left_send, 4), right, swap(right_send, 2)


def after(value, *others):
    return lax.optimization_barrier((value, *others))[0]


def partial_kernel(experts, capacity, alone, late, first, routes, scores, *refs):
    own, early, mixed, back, late_picker, scales = refs
    slots, toks = experts * capacity, mixed.shape[0]
    places = lax.broadcasted_iota(jnp.int32, (toks, slots), 1).astype(F32)
    hits = [
        places == to_column(row) for row in slot_rows(first[0], routes[...], experts, capacity)
    ]
    hits.append(functools.reduce(jnp.logical_or, hits))
    picker = jnp.concatenate([hit.astype(F32).astype(BF16) for hit in hits], axis=0)
    weights = weight_rows(scores[...])
    for k in range(scales.shape[0]):
        scales[k] = jnp.broadcast_to(to_column(weights[k : k + 1, :]), scales.shape[1:])

    def slots_of(blocks):
        parts = [picker[:, n * capacity : (n + 1) * capacity] for n in blocks]
        return jnp.concatenate(parts, axis=1)

    late_picker[...] = slots_of(late + [alone])
    now = slots_of((0, alone))
    for columns in column_steps(mixed.shape[1]):
        outputs = jnp.concatenate([own[:capacity, columns], early[:, columns]], axis=0)
        total, grad = sum_rows(now, scales, outputs, own[capacity:, columns])
        mixed[:, columns] = total
        back[:, columns] = grad


def sum_rows(picker, scales, outputs, gradients):
    tops, toks = scales.shape[:2]
    chosen = picker[: tops * toks, : outputs.shape[0]]
    picked = jnp.dot(chosen, outputs, preferred_element_type=F32)
    total = sum(scales[k, :, :1] * picked[k * toks : (k + 1) * toks] for k in range(tops))
    either = picker[tops * toks :, : gradients.shape[0]]
    return total, jnp.dot(either, gradients, preferred_element_type=F32)


def mean_kernel(count, left, left_last, right, right_last, wide, narrow):
    middle, edge = wide.shape[1] // 2, narrow.shape[1] // 2
    for at, (own, last) in enumerate(((left, left_last), (right, right_last))):
        total = (own[...] + last[...].astype(F32)) / count
        wide[:, at * middle : (at + 1) * middle] = total[:, :middle]
        narrow[:, at * edge : (at + 1) * edge] = total[:, middle:]


def means(count, sums):
    share, columns = sums[0].shape
    return pl.pallas_call(
        functools.partial(mean_kernel, count),
        out_shape=(
            jax.ShapeDtypeStruct((share, 4 * columns // 3), F32),
            jax.ShapeDtypeStruct((share, 2 * columns // 3), F32),
        ),
        in_specs=whole(4),
        out_specs=whole(2),
        compiler_params=ROOMY,
        cost_estimate=BRIEF,
    )(*sums)


def last_kernel(capacity, number, picker, scales, mixed_part, back_part, *refs):
    blocks, (mixed, back), (mixed_vmem, back_vmem, sems) = (
        refs[:number],
        refs[number : number + 2],
        refs[number + 2 :],
    )
    stores = []
    for c, columns in enumerate(column_steps(mixed.shape[1])):
        outputs = jnp.concatenate([block[:capacity, columns] for block in blocks[:-1]], axis=0)
        gradients = jnp.concatenate(
            [block[block.shape[0] - capacity :, columns] for block in blocks], axis=0
        )
        total, grad = sum_rows(picker[...], scales, outputs, gradients)
        mixed_vmem[:, columns] = (total + mixed_part[:, columns]).astype(BF16)
        back_vmem[:, columns] = (grad + back_part[:, columns]).astype(BF16)
        for n, (source, target) in enumerate(((mixed_vmem, mixed), (back_vmem, back))):
            stores.append(
                pltpu.make_async_copy(source.at[:, columns], target.at[:, columns], sems.at[c, n])
            )
            stores[-1].start()
    for stored in stores:
        stored.wait()


def last(capacity, parts, blocks):
    toks, width = parts[-1].shape
    out_shape = jax.ShapeDtypeStruct((toks, width), BF16)
    return pl.pallas_call(
        functools.partial(last_kernel, capacity, len(blocks)),
        out_shape=(out_shape, out_shape),
        in_specs=whole(4 + len(blocks)),
        out_specs=anywhere(2),
        scratch_shapes=[pltpu.VMEM((toks, width), BF16)] * 2
        + [pltpu.SemaphoreType.DMA((len(column_steps(width)), 2))],
        compiler_params=ROOMY,
        cost_estimate=BRIEF,
    )(*parts, *blocks)


def dispatch(experts, capacity, out_shape, first, *sources):
    weighted = len(sources) > 2
    return pl.pallas_call(
        functools.partial(dispatch_kernel, experts, capacity, weighted),
        out_shape=out_shape,
        in_specs=[pl.BlockSpec(memory_space=pltpu.SMEM)] + in_hbm(len(sources)),
        out_specs=anywhere(len(out_shape)),
        scratch_shapes=[pltpu.VMEM(out.shape, out.dtype) for out in out_shape]
        + [pltpu.VMEM(source.shape, source.dtype) for source in sources]
        + [
            pltpu.SemaphoreType.DMA((len(sources),)),
            pltpu.SemaphoreType.DMA((len(column_steps(out_shape[0].shape[1], 1024)), len(out_shape))),
        ],
        compiler_params=ALONE,
        cost_estimate=BRIEF,
    )(first, *sources)


def call(kernel, out_shape, inputs):
    return pl.pallas_call(
        kernel,
        out_shape=out_shape,
        in_specs=[pl.BlockSpec(memory_space=pltpu.SMEM)]
        + [pl.BlockSpec(memory_space=pltpu.VMEM)] * (len(inputs) - 1),
        compiler_params=ROOMY,
        cost_estimate=BRIEF,
    )(*inputs)


def body(tokens, routes, route_scores, out_grad, gate_up, down_weight):
    experts = lax.axis_size("expert")
    groups = lax.axis_size("dp")
    toks, width = tokens.shape
    tops = routes.shape[1]
    units = down_weight.shape[2]
    capacity = (toks * tops + experts - 1) // experts
    slots = experts * capacity
    share = width // groups
    direct = experts <= 8 and capacity % 16 == 0
    w_in, w_out = gate_up[0], down_weight[0]
    routes_t, scores_t = routes.T, route_scores.T
    me = lax.axis_index("expert") if direct else jnp.int32(0)
    first = me.astype(jnp.int32).reshape(1)
    sizes = [capacity] * experts if direct else [slots]
    block_shapes = [jax.ShapeDtypeStruct((size, width), BF16) for size in sizes]

    def travel(block, step, sign):
        pairs = [(at, (at + sign * step) % experts) for at in range(experts)]
        return lax.ppermute(block, "expert", pairs)

    def exchange(blocks, sign):
        if not direct:
            block = blocks[0].reshape(experts, capacity, width)
            moved = lax.all_to_all(block, "expert", split_axis=0, concat_axis=0, tiled=True)
            return [moved.reshape(slots, width)]
        steps = range(1, experts) if sign > 0 else range(experts - 1, 0, -1)
        moved = {step: travel(blocks[step], step, sign) for step in steps}
        return [blocks[0]] + [moved[step] for step in range(1, experts)]

    def joined(blocks):
        return blocks[0] if len(blocks) == 1 else jnp.concatenate(blocks, axis=0)

    def split(rows):
        return [rows[at : at + sizes[0]] for at in range(0, slots, sizes[0])]

    sent_rows = dispatch(experts, capacity, block_shapes, first, routes_t, tokens)
    got_rows = exchange(sent_rows, 1)
    sent_grads = dispatch(experts, capacity, block_shapes, first, routes_t, scores_t, out_grad)
    out_shape = jax.ShapeDtypeStruct((toks, width), BF16)
    cube = direct and experts == 4 and groups == 8 and share % 256 == 0
    if cube:
        sent_grads = after(sent_grads, got_rows[1], got_rows[-1])
        got_grads = exchange(sent_grads, 1)
        rows_t, preact, hidden, produced = forward(got_rows, w_in, w_out)
        got_grads = after(got_grads, hidden)
        own = lax.axis_index("dp")
        send_at = jnp.stack([jnp.bitwise_xor(own, j) for j in CUBE_SEND]).astype(jnp.int32)
        keep_at = jnp.bitwise_xor(send_at, 1)
        early = experts - 1
        early_out = travel(produced[early], early, -1)
        pre_grad, grads_t, sent, w_in_here = backward(
            send_at, share, preact, w_in, rows_t, hidden, w_out, got_grads
        )
        operands = (share, rows_t, grads_t, pre_grad, hidden)
        got = swap(sent, 1)
        blocks = returns(after(pre_grad, sent), w_in_here, produced, early)
        half = len(CUBE_SEND) // 2
        kept_first = shares(after(keep_at[:half], blocks[0]), *operands, COVER)
        returned = exchange(blocks, -1)
        kept_later = shares(after(keep_at[half:], kept_first, early_out, got), *operands, COVER)
        sums = cube_sum(got, kept_first, kept_later)
        late = [n for n in range(experts - 1, 0, -1) if n != early]
        mixed_part, back_part, picker, scales = call(
            functools.partial(partial_kernel, experts, capacity, early, late),
            (
                jax.ShapeDtypeStruct((toks, width), F32),
                jax.ShapeDtypeStruct((toks, width), F32),
                jax.ShapeDtypeStruct(((tops + 1) * toks, (len(late) + 1) * capacity), BF16),
                jax.ShapeDtypeStruct((tops, toks, 128), F32),
            ),
            (after(first, sums[0]), routes_t, scores_t, returned[0], early_out),
        )
        grad_in, grad_down = means(groups, sums)
        parts = (after(picker, grad_in), scales, mixed_part, back_part)
        mixed_out, token_grad = last(capacity, parts, [returned[n] for n in late + [early]])
    else:
        token_rows = joined(got_rows)
        grad_rows = joined(exchange(sent_grads, 1))
        preact = jnp.dot(token_rows, w_in, preferred_element_type=F32)
        gate, up = preact[:, :units], preact[:, units:]
        hidden = (jax.nn.silu(gate) * up).astype(BF16)
        produced = jnp.dot(hidden, w_out.T, preferred_element_type=F32).astype(BF16)
        returned = exchange(split(produced), -1)
        hidden_grad = jnp.dot(grad_rows, w_out, preferred_element_type=F32)
        sigmoid = jax.nn.sigmoid(gate)
        gate_grad = hidden_grad * up * sigmoid * (1.0 + gate * (1.0 - sigmoid))
        up_grad = hidden_grad * gate * sigmoid
        pre_grad = jnp.concatenate([gate_grad, up_grad], axis=1).astype(BF16)
        input_grad = jnp.dot(pre_grad, w_in.T, preferred_element_type=F32).astype(BF16)
        sent_back = exchange(split(input_grad), -1)

        def summed(left, right):
            part = contract(left, right).astype(BF16)
            total = lax.psum_scatter(part, "dp", scatter_dimension=0, tiled=True)
            return total.astype(F32) / groups

        grad_in = summed(token_rows, pre_grad)
        grad_down = summed(grad_rows, hidden)
        mixed_out = call(
            functools.partial(combine_kernel, experts, capacity, True),
            out_shape,
            (first, routes_t, scores_t, *returned),
        )
        token_grad = call(
            functools.partial(combine_kernel, experts, capacity, False),
            out_shape,
            (first, routes_t, *sent_back),
        )
    grad_in = grad_in.reshape(1, share, 2 * units)
    grad_down = grad_down.reshape(1, share, units)
    return (mixed_out, token_grad, grad_in, grad_down)


def solution(mesh):
    in_specs = (
        P(("dp", "expert"), None),
        P(("dp", "expert"), None),
        P(("dp", "expert"), None),
        P(("dp", "expert"), None),
        P("expert", None, None),
        P("expert", None, None),
    )
    out_specs = (
        P(("dp", "expert"), None),
        P(("dp", "expert"), None),
        P("expert", "dp", None),
        P("expert", "dp", None),
    )
    return jax.shard_map(body, mesh=mesh, in_specs=in_specs, out_specs=out_specs, check_vma=False)
```

```python
import functools

import jax
import jax.numpy as jnp
from jax import lax
from jax.experimental import pallas as pl
from jax.experimental.pallas import tpu as pltpu
from jax.sharding import PartitionSpec as P

F32 = jnp.float32
BF16 = jnp.bfloat16
BRIEF = pl.CostEstimate(flops=1024, bytes_accessed=1024, transcendentals=0)
COVER = pl.CostEstimate(flops=4 * 10**10, bytes_accessed=1024, transcendentals=0)
ROOMY = pltpu.CompilerParams(vmem_limit_bytes=16 * 1024 * 1024)
BIG = pltpu.CompilerParams(vmem_limit_bytes=28 * 1024 * 1024)
ALONE = pltpu.CompilerParams(vmem_limit_bytes=60 * 1024 * 1024)


def contract(left, right):
    return lax.dot_general(left, right, (((0,), (0,)), ((), ())), preferred_element_type=F32)


def slot_rows(first, routes, experts, capacity):
    tops, toks = routes.shape
    padded = -(-experts // 8) * 8
    rows = lax.broadcasted_iota(jnp.int32, (padded, toks), 0)
    ids = rows + first
    ids = jnp.where(ids >= experts, ids - experts, ids)
    ids = jnp.where(rows < experts, ids, -1)
    hits = [routes[k : k + 1, :] == ids for k in range(tops)]
    named = functools.reduce(jnp.logical_or, hits)
    before = lax.broadcasted_iota(jnp.int32, (toks, toks), 0) < lax.broadcasted_iota(
        jnp.int32, (toks, toks), 1
    )
    position = jnp.dot(
        named.astype(F32).astype(BF16),
        before.astype(F32).astype(BF16),
        preferred_element_type=F32,
    )
    slot = position + (rows * capacity).astype(F32)
    return [jnp.sum(jnp.where(hit, slot, 0.0), axis=0, keepdims=True) for hit in hits]


def weight_rows(scores):
    grown = jnp.exp(scores)
    return grown / jnp.sum(grown, axis=0, keepdims=True)


def to_column(row):
    toks = row.shape[1]
    same = lax.broadcasted_iota(jnp.int32, (toks, toks), 0) == lax.broadcasted_iota(
        jnp.int32, (toks, toks), 1
    )
    return jnp.sum(jnp.where(same, row, 0.0), axis=1, keepdims=True)


def put_blocks(outs, rows, columns):
    start = 0
    for out in outs:
        size = out.shape[0]
        out[:, columns] = rows[start : start + size]
        start += size


def column_steps(width, step=512):
    step = step if width % step == 0 else width
    return [slice(at, at + step) for at in range(0, width, step)]


def dispatch_kernel(experts, capacity, weighted, first, *refs):
    count = 2 + weighted
    sources, refs = refs[:count], refs[count:]
    number = (len(refs) - count - 2) // 2
    outs, ready, (*held, sems, out_sems) = refs[:number], refs[number : 2 * number], refs[2 * number :]
    copies = [
        pltpu.make_async_copy(source, place, sems.at[n])
        for n, (source, place) in enumerate(zip(sources, held))
    ]
    for copy in copies:
        copy.start()
    routes, values = held[0], held[-1]
    scores = held[1] if weighted else None
    for copy in copies[:-1]:
        copy.wait()
    slots, toks = experts * capacity, values.shape[0]
    places = lax.broadcasted_iota(jnp.int32, (slots, toks), 0).astype(F32)
    hits = [places == row for row in slot_rows(first[0], routes[...], experts, capacity)]
    picker = functools.reduce(jnp.logical_or, hits).astype(F32).astype(BF16)
    if weighted:
        weights = weight_rows(scores[...])
        scale = sum(
            jnp.sum(jnp.where(hit, weights[k : k + 1, :], 0.0), axis=1, keepdims=True)
            for k, hit in enumerate(hits)
        )
    copies[-1].wait()
    stores = []
    for c, columns in enumerate(column_steps(values.shape[1], 1024)):
        rows = jnp.dot(picker, values[:, columns], preferred_element_type=F32)
        if weighted:
            rows = rows * scale
        put_blocks(ready, rows.astype(BF16), columns)
        for n, (block, out) in enumerate(zip(ready, outs)):
            stores.append(
                pltpu.make_async_copy(block.at[:, columns], out.at[:, columns], out_sems.at[c, n])
            )
            stores[-1].start()
    for store in stores:
        store.wait()


def combine_kernel(experts, capacity, weighted, first, routes, *refs):
    scores = refs[0] if weighted else None
    blocks, out = refs[weighted:-1], refs[-1]
    slots, toks = experts * capacity, out.shape[0]
    places = lax.broadcasted_iota(jnp.int32, (toks, slots), 1).astype(F32)
    hits = [
        places == to_column(row) for row in slot_rows(first[0], routes[...], experts, capacity)
    ]
    if weighted:
        weights = weight_rows(scores[...])
        scales = [to_column(weights[k : k + 1, :]) for k in range(len(hits))]
        pickers = [hit.astype(F32).astype(BF16) for hit in hits]
    else:
        pickers = [functools.reduce(jnp.logical_or, hits).astype(F32).astype(BF16)]
    for columns in column_steps(out.shape[1]):
        rows = [block[:, columns] for block in blocks]
        rows = rows[0] if len(rows) == 1 else jnp.concatenate(rows, axis=0)
        picked = [jnp.dot(picker, rows, preferred_element_type=F32) for picker in pickers]
        if weighted:
            picked = [scale * part for scale, part in zip(scales, picked)]
        out[:, columns] = sum(picked).astype(out.dtype)


def whole(count):
    return [pl.BlockSpec(memory_space=pltpu.VMEM)] * count


def write_shares(at, rows_t, grads_t, pre_grad, hidden, out):
    share = out.shape[1]
    wide, narrow = pre_grad.shape[1] // 2, hidden.shape[1] // 2

    def write(t, half):
        own = pl.ds(pl.multiple_of(at[t] * share, share), share)
        out[t, :, :wide] = jnp.dot(
            rows_t[own, :],
            pre_grad[:, half * wide : (half + 1) * wide],
            preferred_element_type=F32,
        ).astype(out.dtype)
        out[t, :, wide:] = jnp.dot(
            grads_t[own, :],
            hidden[:, half * narrow : (half + 1) * narrow],
            preferred_element_type=F32,
        ).astype(out.dtype)

    for t in range(out.shape[0]):
        write(t, t // 2 % 2)


def side_by_side(blocks, columns):
    if len(blocks) == 1:
        return blocks[0][:, columns]
    return jnp.concatenate([block[:, columns] for block in blocks], axis=0)


def transpose_into(blocks, rows_t):
    width = rows_t.shape[0]
    step = 256 if width % 256 == 0 else width

    for begin in range(0, width, step):
        rows_t[begin : begin + step, :] = side_by_side(blocks, slice(begin, begin + step)).T


def join_copies(blocks, rows, sems):
    size = blocks[0].shape[0]
    joins = [
        pltpu.make_async_copy(block, rows.at[pl.ds(n * size, size)], sems.at[n])
        for n, block in enumerate(blocks)
    ]
    for join in joins:
        join.start()
    return joins


def forward_kernel(count, *refs):
    blocks, (w_in_hbm, down_hbm), (rows_t, preact, hidden), outs, scratch = (
        refs[:count],
        refs[count : count + 2],
        refs[count + 2 : count + 5],
        refs[count + 5 : 2 * count + 5],
        refs[2 * count + 5 :],
    )
    rows, w_in, down, block_sems, weight_sems, down_sem = scratch
    joins = join_copies(blocks, rows, block_sems)
    width, units = down.shape
    step = 256 if units % 256 == 0 else units
    loads = []
    for n in range(2 * units // step):
        begin = (n % 2) * units + n // 2 * step
        loads.append(
            pltpu.make_async_copy(
                w_in_hbm.at[:, pl.ds(begin, step)],
                w_in.at[:, pl.ds(begin, step)],
                weight_sems.at[n],
            )
        )
        loads[-1].start()
    load_down = pltpu.make_async_copy(down_hbm, down, down_sem)
    load_down.start()
    for join in joins:
        join.wait()
    for n in range(units // step):
        begin = n * step
        gate_at, up_at = slice(begin, begin + step), slice(units + begin, units + begin + step)
        loads[2 * n].wait()
        gate = jnp.dot(rows[...], w_in[:, gate_at], preferred_element_type=F32)
        loads[2 * n + 1].wait()
        up = jnp.dot(rows[...], w_in[:, up_at], preferred_element_type=F32)
        preact[:, gate_at] = gate
        preact[:, up_at] = up
        hidden[:, gate_at] = (gate / (1.0 + jnp.exp(-gate)) * up).astype(BF16)
    load_down.wait()
    for columns in column_steps(width):
        part = lax.dot_general(
            hidden[...], down[columns, :], (((1,), (1,)), ((), ())), preferred_element_type=F32
        )
        put_blocks(outs, part.astype(BF16), columns)
    transpose_into([rows], rows_t)


def forward(blocks, w_in, down):
    width, units = down.shape
    slots = sum(block.shape[0] for block in blocks)
    count = len(blocks)
    rows_t, preact, hidden, *outs = pl.pallas_call(
        functools.partial(forward_kernel, count),
        out_shape=(
            jax.ShapeDtypeStruct((width, slots), BF16),
            jax.ShapeDtypeStruct((slots, 2 * units), F32),
            jax.ShapeDtypeStruct((slots, units), BF16),
            *[jax.ShapeDtypeStruct(block.shape, BF16) for block in blocks],
        ),
        in_specs=anywhere(count) + in_hbm(2),
        out_specs=whole(3 + count),
        scratch_shapes=[
            pltpu.VMEM((slots, width), BF16),
            pltpu.VMEM(w_in.shape, BF16),
            pltpu.VMEM(down.shape, BF16),
            pltpu.SemaphoreType.DMA((count,)),
            pltpu.SemaphoreType.DMA((2 * units // min(units, 256),)),
            pltpu.SemaphoreType.DMA,
        ],
        compiler_params=pltpu.CompilerParams(vmem_limit_bytes=46 * 1024 * 1024),
        cost_estimate=BRIEF,
    )(*blocks, w_in, down)
    return rows_t, preact, hidden, outs


def backward_kernel(count, at, preact_hbm, w_in_hbm, rows_t, hidden, down, *refs):
    blocks, (pre_grad, grads_t, sent, w_in, *refs) = refs[:count], refs[count:]
    preact, load_sem, sem = refs
    fetch = pltpu.make_async_copy(preact_hbm, preact, sem)
    fetch.start()
    load = pltpu.make_async_copy(w_in_hbm, w_in, load_sem)
    load.start()
    units = down.shape[1]
    fetch.wait()
    grads = side_by_side(blocks, slice(0, down.shape[0]))
    step = 256 if units % 256 == 0 else units
    for begin in range(0, units, step):
        gate = preact[:, begin : begin + step]
        up = preact[:, units + begin : units + begin + step]
        hidden_grad = jnp.dot(grads, down[:, begin : begin + step], preferred_element_type=F32)
        sigmoid = 1.0 / (1.0 + jnp.exp(-gate))
        gate_grad = hidden_grad * up * sigmoid * (1.0 + gate * (1.0 - sigmoid))
        up_grad = hidden_grad * gate * sigmoid
        pre_grad[:, begin : begin + step] = gate_grad.astype(BF16)
        pre_grad[:, units + begin : units + begin + step] = up_grad.astype(BF16)
    transpose_into(blocks, grads_t)
    write_shares(at, rows_t, grads_t, pre_grad, hidden, sent)
    load.wait()


def return_kernel(count, alone, pre_grad, w_in, *refs):
    blocks, outs, sems = refs[:count], refs[count : 2 * count], refs[-1]
    size = blocks[0].shape[0]
    copies = [
        pltpu.make_async_copy(block, out.at[pl.ds(0, size)], sems.at[n])
        for n, (block, out) in enumerate(zip(blocks, outs))
        if n != alone
    ]
    for copy in copies:
        copy.start()
    for columns in column_steps(w_in.shape[0]):
        part = lax.dot_general(
            pre_grad[...], w_in[columns, :], (((1,), (1,)), ((), ())), preferred_element_type=F32
        ).astype(BF16)
        for n, out in enumerate(outs):
            out[out.shape[0] - size :, columns] = part[n * size : (n + 1) * size]
    for copy in copies:
        copy.wait()


def returns(pre_grad, w_in, produced, alone):
    count = len(produced)
    size, width = produced[0].shape
    return pl.pallas_call(
        functools.partial(return_kernel, count, alone),
        out_shape=[
            jax.ShapeDtypeStruct((size if n == alone else 2 * size, width), BF16)
            for n in range(count)
        ],
        in_specs=whole(2) + anywhere(count),
        out_specs=whole(count),
        scratch_shapes=[pltpu.SemaphoreType.DMA((count,))],
        compiler_params=ROOMY,
        cost_estimate=BRIEF,
    )(pre_grad, w_in, *produced)


def anywhere(count):
    return [pl.BlockSpec(memory_space=pl.ANY)] * count


def in_hbm(count):
    return [pl.BlockSpec(memory_space=pltpu.HBM)] * count


def backward(at, share, preact, w_in, rows_t, hidden, down, blocks):
    width, units = down.shape
    slots = preact.shape[0]
    count = len(blocks)
    return pl.pallas_call(
        functools.partial(backward_kernel, count),
        out_shape=(
            jax.ShapeDtypeStruct((slots, 2 * units), BF16),
            jax.ShapeDtypeStruct((width, slots), BF16),
            jax.ShapeDtypeStruct((at.shape[0], share, 3 * units // 2), BF16),
            jax.ShapeDtypeStruct(w_in.shape, BF16),
        ),
        in_specs=[pl.BlockSpec(memory_space=pltpu.SMEM)]
        + anywhere(2)
        + whole(3 + count),
        out_specs=whole(4),
        scratch_shapes=[
            pltpu.VMEM((slots, 2 * units), F32),
            pltpu.SemaphoreType.DMA,
            pltpu.SemaphoreType.DMA,
        ],
        compiler_params=BIG,
        cost_estimate=BRIEF,
    )(at, preact, w_in, rows_t, hidden, down, *blocks)


def shares(at, share, rows_t, grads_t, pre_grad, hidden, cost):
    units = hidden.shape[1]
    return pl.pallas_call(
        write_shares,
        out_shape=jax.ShapeDtypeStruct((at.shape[0], share, 3 * units // 2), BF16),
        in_specs=[pl.BlockSpec(memory_space=pltpu.SMEM)] + whole(4),
        out_specs=whole(1)[0],
        compiler_params=ROOMY,
        cost_estimate=cost,
    )(at, rows_t, grads_t, pre_grad, hidden)


def add_kernel(kept, got, left, right):
    half = left.shape[0]
    left[...] = add(kept[:half], got[:half]).astype(BF16)
    right[...] = add(kept[half:], got[half : 2 * half]).astype(BF16)


def next_kernel(kept, got, left_in, right_in, left_send, right_send):
    first = got.shape[0] // 2
    left_send[...] = (add(kept[1], got[first + 1]) + left_in[1].astype(F32)).astype(BF16)
    right_send[...] = (add(kept[3], got[first + 3]) + right_in[1].astype(F32)).astype(BF16)


def own_kernel(kept, got, left_in, right_in, left, right):
    first = got.shape[0] // 2
    left[...] = add(kept[0], got[first]) + left_in[0].astype(F32)
    right[...] = add(kept[2], got[first + 2]) + right_in[0].astype(F32)


def add(left, right):
    return left.astype(F32) + right.astype(F32)


CUBE_SEND = (3, 7, 5, 7, 1, 5, 1, 3)


def swap(block, bit):
    return lax.ppermute(block, "dp", [(at, at ^ bit) for at in range(lax.axis_size("dp"))])


def cube_sum(got, kept_first, kept_later):
    _, share, columns = got.shape

    def run(kernel, out_shape, inputs, cost=BRIEF):
        return pl.pallas_call(
            kernel,
            out_shape=out_shape,
            in_specs=whole(len(inputs)),
            out_specs=whole(len(out_shape)),
            compiler_params=ROOMY,
            cost_estimate=cost,
        )(*inputs)

    half = jax.ShapeDtypeStruct((2, share, columns), BF16)
    one = jax.ShapeDtypeStruct((share, columns), BF16)
    own = jax.ShapeDtypeStruct((share, columns), F32)
    left, right = run(add_kernel, (half, half), (kept_first, got))
    parts = (kept_later, got, swap(left, 2), swap(right, 4))
    left_send, right_send = run(next_kernel, (one, one), parts)
    left, right = run(own_kernel, (own, own), parts, COVER)
    return left, swap(left_send, 4), right, swap(right_send, 2)


def after(value, *others):
    return lax.optimization_barrier((value, *others))[0]


def partial_kernel(experts, capacity, alone, late, first, routes, scores, *refs):
    own, early, mixed, back, late_picker, scales = refs
    slots, toks = experts * capacity, mixed.shape[0]
    places = lax.broadcasted_iota(jnp.int32, (toks, slots), 1).astype(F32)
    hits = [
        places == to_column(row) for row in slot_rows(first[0], routes[...], experts, capacity)
    ]
    hits.append(functools.reduce(jnp.logical_or, hits))
    picker = jnp.concatenate([hit.astype(F32).astype(BF16) for hit in hits], axis=0)
    weights = weight_rows(scores[...])
    for k in range(scales.shape[0]):
        scales[k] = jnp.broadcast_to(to_column(weights[k : k + 1, :]), scales.shape[1:])

    def slots_of(blocks):
        parts = [picker[:, n * capacity : (n + 1) * capacity] for n in blocks]
        return jnp.concatenate(parts, axis=1)

    late_picker[...] = slots_of(late + [alone])
    now = slots_of((0, alone))
    for columns in column_steps(mixed.shape[1]):
        outputs = jnp.concatenate([own[:capacity, columns], early[:, columns]], axis=0)
        total, grad = sum_rows(now, scales, outputs, own[capacity:, columns])
        mixed[:, columns] = total
        back[:, columns] = grad


def sum_rows(picker, scales, outputs, gradients):
    tops, toks = scales.shape[:2]
    chosen = picker[: tops * toks, : outputs.shape[0]]
    picked = jnp.dot(chosen, outputs, preferred_element_type=F32)
    total = sum(scales[k, :, :1] * picked[k * toks : (k + 1) * toks] for k in range(tops))
    either = picker[tops * toks :, : gradients.shape[0]]
    return total, jnp.dot(either, gradients, preferred_element_type=F32)


def mean_kernel(count, left, left_last, right, right_last, wide, narrow):
    middle, edge = wide.shape[1] // 2, narrow.shape[1] // 2
    for at, (own, last) in enumerate(((left, left_last), (right, right_last))):
        total = (own[...] + last[...].astype(F32)) / count
        wide[:, at * middle : (at + 1) * middle] = total[:, :middle]
        narrow[:, at * edge : (at + 1) * edge] = total[:, middle:]


def means(count, sums):
    share, columns = sums[0].shape
    return pl.pallas_call(
        functools.partial(mean_kernel, count),
        out_shape=(
            jax.ShapeDtypeStruct((share, 4 * columns // 3), F32),
            jax.ShapeDtypeStruct((share, 2 * columns // 3), F32),
        ),
        in_specs=whole(4),
        out_specs=whole(2),
        compiler_params=ROOMY,
        cost_estimate=BRIEF,
    )(*sums)


def last_kernel(capacity, number, picker, scales, mixed_part, back_part, *refs):
    blocks, (mixed, back), (mixed_vmem, back_vmem, sems) = (
        refs[:number],
        refs[number : number + 2],
        refs[number + 2 :],
    )
    stores = []
    for c, columns in enumerate(column_steps(mixed.shape[1], 1024)):
        outputs = jnp.concatenate([block[:capacity, columns] for block in blocks[:-1]], axis=0)
        gradients = jnp.concatenate(
            [block[block.shape[0] - capacity :, columns] for block in blocks], axis=0
        )
        total, grad = sum_rows(picker[...], scales, outputs, gradients)
        mixed_vmem[:, columns] = (total + mixed_part[:, columns]).astype(BF16)
        back_vmem[:, columns] = (grad + back_part[:, columns]).astype(BF16)
        for n, (source, target) in enumerate(((mixed_vmem, mixed), (back_vmem, back))):
            stores.append(
                pltpu.make_async_copy(source.at[:, columns], target.at[:, columns], sems.at[c, n])
            )
            stores[-1].start()
    for stored in stores:
        stored.wait()


def last(capacity, parts, blocks):
    toks, width = parts[-1].shape
    out_shape = jax.ShapeDtypeStruct((toks, width), BF16)
    return pl.pallas_call(
        functools.partial(last_kernel, capacity, len(blocks)),
        out_shape=(out_shape, out_shape),
        in_specs=whole(4 + len(blocks)),
        out_specs=anywhere(2),
        scratch_shapes=[pltpu.VMEM((toks, width), BF16)] * 2
        + [pltpu.SemaphoreType.DMA((len(column_steps(width, 1024)), 2))],
        compiler_params=ROOMY,
        cost_estimate=BRIEF,
    )(*parts, *blocks)


def dispatch(experts, capacity, out_shape, first, *sources):
    weighted = len(sources) > 2
    return pl.pallas_call(
        functools.partial(dispatch_kernel, experts, capacity, weighted),
        out_shape=out_shape,
        in_specs=[pl.BlockSpec(memory_space=pltpu.SMEM)] + in_hbm(len(sources)),
        out_specs=anywhere(len(out_shape)),
        scratch_shapes=[pltpu.VMEM(out.shape, out.dtype) for out in out_shape]
        + [pltpu.VMEM(source.shape, source.dtype) for source in sources]
        + [
            pltpu.SemaphoreType.DMA((len(sources),)),
            pltpu.SemaphoreType.DMA((len(column_steps(out_shape[0].shape[1], 1024)), len(out_shape))),
        ],
        compiler_params=ALONE,
        cost_estimate=BRIEF,
    )(first, *sources)


def call(kernel, out_shape, inputs):
    return pl.pallas_call(
        kernel,
        out_shape=out_shape,
        in_specs=[pl.BlockSpec(memory_space=pltpu.SMEM)]
        + [pl.BlockSpec(memory_space=pltpu.VMEM)] * (len(inputs) - 1),
        compiler_params=ROOMY,
        cost_estimate=BRIEF,
    )(*inputs)


def body(tokens, routes, route_scores, out_grad, gate_up, down_weight):
    experts = lax.axis_size("expert")
    groups = lax.axis_size("dp")
    toks, width = tokens.shape
    tops = routes.shape[1]
    units = down_weight.shape[2]
    capacity = (toks * tops + experts - 1) // experts
    slots = experts * capacity
    share = width // groups
    direct = experts <= 8 and capacity % 16 == 0
    w_in, w_out = gate_up[0], down_weight[0]
    routes_t, scores_t = routes.T, route_scores.T
    me = lax.axis_index("expert") if direct else jnp.int32(0)
    first = me.astype(jnp.int32).reshape(1)
    sizes = [capacity] * experts if direct else [slots]
    block_shapes = [jax.ShapeDtypeStruct((size, width), BF16) for size in sizes]

    def travel(block, step, sign):
        pairs = [(at, (at + sign * step) % experts) for at in range(experts)]
        return lax.ppermute(block, "expert", pairs)

    def exchange(blocks, sign):
        if not direct:
            block = blocks[0].reshape(experts, capacity, width)
            moved = lax.all_to_all(block, "expert", split_axis=0, concat_axis=0, tiled=True)
            return [moved.reshape(slots, width)]
        steps = range(1, experts) if sign > 0 else range(experts - 1, 0, -1)
        moved = {step: travel(blocks[step], step, sign) for step in steps}
        return [blocks[0]] + [moved[step] for step in range(1, experts)]

    def joined(blocks):
        return blocks[0] if len(blocks) == 1 else jnp.concatenate(blocks, axis=0)

    def split(rows):
        return [rows[at : at + sizes[0]] for at in range(0, slots, sizes[0])]

    sent_rows = dispatch(experts, capacity, block_shapes, first, routes_t, tokens)
    got_rows = exchange(sent_rows, 1)
    sent_grads = dispatch(experts, capacity, block_shapes, first, routes_t, scores_t, out_grad)
    out_shape = jax.ShapeDtypeStruct((toks, width), BF16)
    cube = direct and experts == 4 and groups == 8 and share % 256 == 0
    if cube:
        sent_grads = after(sent_grads, got_rows[1], got_rows[-1])
        got_grads = exchange(sent_grads, 1)
        rows_t, preact, hidden, produced = forward(got_rows, w_in, w_out)
        got_grads = after(got_grads, hidden)
        own = lax.axis_index("dp")
        send_at = jnp.stack([jnp.bitwise_xor(own, j) for j in CUBE_SEND]).astype(jnp.int32)
        keep_at = jnp.bitwise_xor(send_at, 1)
        early = experts - 1
        early_out = travel(produced[early], early, -1)
        pre_grad, grads_t, sent, w_in_here = backward(
            send_at, share, preact, w_in, rows_t, hidden, w_out, got_grads
        )
        operands = (share, rows_t, grads_t, pre_grad, hidden)
        got = swap(sent, 1)
        blocks = returns(after(pre_grad, sent), w_in_here, produced, early)
        half = len(CUBE_SEND) // 2
        kept_first = shares(after(keep_at[:half], blocks[0]), *operands, COVER)
        returned = exchange(blocks, -1)
        kept_later = shares(after(keep_at[half:], kept_first, early_out, got), *operands, COVER)
        sums = cube_sum(got, kept_first, kept_later)
        late = [n for n in range(experts - 1, 0, -1) if n != early]
        mixed_part, back_part, picker, scales = call(
            functools.partial(partial_kernel, experts, capacity, early, late),
            (
                jax.ShapeDtypeStruct((toks, width), F32),
                jax.ShapeDtypeStruct((toks, width), F32),
                jax.ShapeDtypeStruct(((tops + 1) * toks, (len(late) + 1) * capacity), BF16),
                jax.ShapeDtypeStruct((tops, toks, 128), F32),
            ),
            (after(first, sums[0]), routes_t, scores_t, returned[0], early_out),
        )
        grad_in, grad_down = means(groups, sums)
        parts = (after(picker, grad_in), scales, mixed_part, back_part)
        mixed_out, token_grad = last(capacity, parts, [returned[n] for n in late + [early]])
    else:
        token_rows = joined(got_rows)
        grad_rows = joined(exchange(sent_grads, 1))
        preact = jnp.dot(token_rows, w_in, preferred_element_type=F32)
        gate, up = preact[:, :units], preact[:, units:]
        hidden = (jax.nn.silu(gate) * up).astype(BF16)
        produced = jnp.dot(hidden, w_out.T, preferred_element_type=F32).astype(BF16)
        returned = exchange(split(produced), -1)
        hidden_grad = jnp.dot(grad_rows, w_out, preferred_element_type=F32)
        sigmoid = jax.nn.sigmoid(gate)
        gate_grad = hidden_grad * up * sigmoid * (1.0 + gate * (1.0 - sigmoid))
        up_grad = hidden_grad * gate * sigmoid
        pre_grad = jnp.concatenate([gate_grad, up_grad], axis=1).astype(BF16)
        input_grad = jnp.dot(pre_grad, w_in.T, preferred_element_type=F32).astype(BF16)
        sent_back = exchange(split(input_grad), -1)

        def summed(left, right):
            part = contract(left, right).astype(BF16)
            total = lax.psum_scatter(part, "dp", scatter_dimension=0, tiled=True)
            return total.astype(F32) / groups

        grad_in = summed(token_rows, pre_grad)
        grad_down = summed(grad_rows, hidden)
        mixed_out = call(
            functools.partial(combine_kernel, experts, capacity, True),
            out_shape,
            (first, routes_t, scores_t, *returned),
        )
        token_grad = call(
            functools.partial(combine_kernel, experts, capacity, False),
            out_shape,
            (first, routes_t, *sent_back),
        )
    grad_in = grad_in.reshape(1, share, 2 * units)
    grad_down = grad_down.reshape(1, share, units)
    return (mixed_out, token_grad, grad_in, grad_down)


def solution(mesh):
    in_specs = (
        P(("dp", "expert"), None),
        P(("dp", "expert"), None),
        P(("dp", "expert"), None),
        P(("dp", "expert"), None),
        P("expert", None, None),
        P("expert", None, None),
    )
    out_specs = (
        P(("dp", "expert"), None),
        P(("dp", "expert"), None),
        P("expert", "dp", None),
        P("expert", "dp", None),
    )
    return jax.shard_map(body, mesh=mesh, in_specs=in_specs, out_specs=out_specs, check_vma=False)
```

```python
import functools

import jax
import jax.numpy as jnp
from jax import lax
from jax.experimental import pallas as pl
from jax.experimental.pallas import tpu as pltpu
from jax.sharding import PartitionSpec as P

F32 = jnp.float32
BF16 = jnp.bfloat16
BRIEF = pl.CostEstimate(flops=1024, bytes_accessed=1024, transcendentals=0)
COVER = pl.CostEstimate(flops=4 * 10**10, bytes_accessed=1024, transcendentals=0)
ROOMY = pltpu.CompilerParams(vmem_limit_bytes=16 * 1024 * 1024)
BIG = pltpu.CompilerParams(vmem_limit_bytes=28 * 1024 * 1024)
ALONE = pltpu.CompilerParams(vmem_limit_bytes=60 * 1024 * 1024)


def contract(left, right):
    return lax.dot_general(left, right, (((0,), (0,)), ((), ())), preferred_element_type=F32)


def slot_rows(first, routes, experts, capacity):
    tops, toks = routes.shape
    padded = -(-experts // 8) * 8
    rows = lax.broadcasted_iota(jnp.int32, (padded, toks), 0)
    ids = rows + first
    ids = jnp.where(ids >= experts, ids - experts, ids)
    ids = jnp.where(rows < experts, ids, -1)
    hits = [routes[k : k + 1, :] == ids for k in range(tops)]
    named = functools.reduce(jnp.logical_or, hits)
    before = lax.broadcasted_iota(jnp.int32, (toks, toks), 0) < lax.broadcasted_iota(
        jnp.int32, (toks, toks), 1
    )
    position = jnp.dot(
        named.astype(F32).astype(BF16),
        before.astype(F32).astype(BF16),
        preferred_element_type=F32,
    )
    slot = position + (rows * capacity).astype(F32)
    return [jnp.sum(jnp.where(hit, slot, 0.0), axis=0, keepdims=True) for hit in hits]


def weight_rows(scores):
    grown = jnp.exp(scores)
    return grown / jnp.sum(grown, axis=0, keepdims=True)


def to_column(row):
    toks = row.shape[1]
    same = lax.broadcasted_iota(jnp.int32, (toks, toks), 0) == lax.broadcasted_iota(
        jnp.int32, (toks, toks), 1
    )
    return jnp.sum(jnp.where(same, row, 0.0), axis=1, keepdims=True)


def put_blocks(outs, rows, columns):
    start = 0
    for out in outs:
        size = out.shape[0]
        out[:, columns] = rows[start : start + size]
        start += size


def column_steps(width, step=512):
    step = step if width % step == 0 else width
    return [slice(at, at + step) for at in range(0, width, step)]


def dispatch_kernel(experts, capacity, weighted, first, *refs):
    count = 2 + weighted
    sources, refs = refs[:count], refs[count:]
    number = (len(refs) - count - 2) // 2
    outs, ready, (*held, sems, out_sems) = refs[:number], refs[number : 2 * number], refs[2 * number :]
    copies = [
        pltpu.make_async_copy(source, place, sems.at[n])
        for n, (source, place) in enumerate(zip(sources, held))
    ]
    for copy in copies:
        copy.start()
    routes, values = held[0], held[-1]
    scores = held[1] if weighted else None
    for copy in copies[:-1]:
        copy.wait()
    slots, toks = experts * capacity, values.shape[0]
    places = lax.broadcasted_iota(jnp.int32, (slots, toks), 0).astype(F32)
    hits = [places == row for row in slot_rows(first[0], routes[...], experts, capacity)]
    picker = functools.reduce(jnp.logical_or, hits).astype(F32).astype(BF16)
    if weighted:
        weights = weight_rows(scores[...])
        scale = sum(
            jnp.sum(jnp.where(hit, weights[k : k + 1, :], 0.0), axis=1, keepdims=True)
            for k, hit in enumerate(hits)
        )
    copies[-1].wait()
    stores = []
    for c, columns in enumerate(column_steps(values.shape[1], 1024)):
        rows = jnp.dot(picker, values[:, columns], preferred_element_type=F32)
        if weighted:
            rows = rows * scale
        put_blocks(ready, rows.astype(BF16), columns)
        for n, (block, out) in enumerate(zip(ready, outs)):
            stores.append(
                pltpu.make_async_copy(block.at[:, columns], out.at[:, columns], out_sems.at[c, n])
            )
            stores[-1].start()
    for store in stores:
        store.wait()


def combine_kernel(experts, capacity, weighted, first, routes, *refs):
    scores = refs[0] if weighted else None
    blocks, out = refs[weighted:-1], refs[-1]
    slots, toks = experts * capacity, out.shape[0]
    places = lax.broadcasted_iota(jnp.int32, (toks, slots), 1).astype(F32)
    hits = [
        places == to_column(row) for row in slot_rows(first[0], routes[...], experts, capacity)
    ]
    if weighted:
        weights = weight_rows(scores[...])
        scales = [to_column(weights[k : k + 1, :]) for k in range(len(hits))]
        pickers = [hit.astype(F32).astype(BF16) for hit in hits]
    else:
        pickers = [functools.reduce(jnp.logical_or, hits).astype(F32).astype(BF16)]
    for columns in column_steps(out.shape[1]):
        rows = [block[:, columns] for block in blocks]
        rows = rows[0] if len(rows) == 1 else jnp.concatenate(rows, axis=0)
        picked = [jnp.dot(picker, rows, preferred_element_type=F32) for picker in pickers]
        if weighted:
            picked = [scale * part for scale, part in zip(scales, picked)]
        out[:, columns] = sum(picked).astype(out.dtype)


def whole(count):
    return [pl.BlockSpec(memory_space=pltpu.VMEM)] * count


def write_shares(at, rows_t, grads_t, pre_grad, hidden, out):
    share = out.shape[1]
    wide, narrow = pre_grad.shape[1] // 2, hidden.shape[1] // 2

    def write(t, half):
        own = pl.ds(pl.multiple_of(at[t] * share, share), share)
        out[t, :, :wide] = jnp.dot(
            rows_t[own, :],
            pre_grad[:, half * wide : (half + 1) * wide],
            preferred_element_type=F32,
        ).astype(out.dtype)
        out[t, :, wide:] = jnp.dot(
            grads_t[own, :],
            hidden[:, half * narrow : (half + 1) * narrow],
            preferred_element_type=F32,
        ).astype(out.dtype)

    for t in range(out.shape[0]):
        write(t, t // 2 % 2)


def side_by_side(blocks, columns):
    if len(blocks) == 1:
        return blocks[0][:, columns]
    return jnp.concatenate([block[:, columns] for block in blocks], axis=0)


def transpose_into(blocks, rows_t):
    width = rows_t.shape[0]
    step = 256 if width % 256 == 0 else width

    for begin in range(0, width, step):
        rows_t[begin : begin + step, :] = side_by_side(blocks, slice(begin, begin + step)).T


def join_copies(blocks, rows, sems):
    size = blocks[0].shape[0]
    joins = [
        pltpu.make_async_copy(block, rows.at[pl.ds(n * size, size)], sems.at[n])
        for n, block in enumerate(blocks)
    ]
    for join in joins:
        join.start()
    return joins


def forward_kernel(count, *refs):
    blocks, (w_in_hbm, down_hbm), (rows_t, preact, hidden), outs, scratch = (
        refs[:count],
        refs[count : count + 2],
        refs[count + 2 : count + 5],
        refs[count + 5 : 2 * count + 5],
        refs[2 * count + 5 :],
    )
    rows, w_in, down, block_sems, weight_sems, down_sem = scratch
    joins = join_copies(blocks, rows, block_sems)
    width, units = down.shape
    step = 256 if units % 256 == 0 else units
    loads = []
    for n in range(2 * units // step):
        begin = (n % 2) * units + n // 2 * step
        loads.append(
            pltpu.make_async_copy(
                w_in_hbm.at[:, pl.ds(begin, step)],
                w_in.at[:, pl.ds(begin, step)],
                weight_sems.at[n],
            )
        )
        loads[-1].start()
    load_down = pltpu.make_async_copy(down_hbm, down, down_sem)
    load_down.start()
    for join in joins:
        join.wait()
    for n in range(units // step):
        begin = n * step
        gate_at, up_at = slice(begin, begin + step), slice(units + begin, units + begin + step)
        loads[2 * n].wait()
        gate = jnp.dot(rows[...], w_in[:, gate_at], preferred_element_type=F32)
        loads[2 * n + 1].wait()
        up = jnp.dot(rows[...], w_in[:, up_at], preferred_element_type=F32)
        preact[:, gate_at] = gate
        preact[:, up_at] = up
        hidden[:, gate_at] = (gate / (1.0 + jnp.exp(-gate)) * up).astype(BF16)
    load_down.wait()
    for columns in column_steps(width):
        part = lax.dot_general(
            hidden[...], down[columns, :], (((1,), (1,)), ((), ())), preferred_element_type=F32
        )
        put_blocks(outs, part.astype(BF16), columns)
    transpose_into([rows], rows_t)


def forward(blocks, w_in, down):
    width, units = down.shape
    slots = sum(block.shape[0] for block in blocks)
    count = len(blocks)
    rows_t, preact, hidden, *outs = pl.pallas_call(
        functools.partial(forward_kernel, count),
        out_shape=(
            jax.ShapeDtypeStruct((width, slots), BF16),
            jax.ShapeDtypeStruct((slots, 2 * units), F32),
            jax.ShapeDtypeStruct((slots, units), BF16),
            *[jax.ShapeDtypeStruct(block.shape, BF16) for block in blocks],
        ),
        in_specs=anywhere(count) + in_hbm(2),
        out_specs=whole(3 + count),
        scratch_shapes=[
            pltpu.VMEM((slots, width), BF16),
            pltpu.VMEM(w_in.shape, BF16),
            pltpu.VMEM(down.shape, BF16),
            pltpu.SemaphoreType.DMA((count,)),
            pltpu.SemaphoreType.DMA((2 * units // min(units, 256),)),
            pltpu.SemaphoreType.DMA,
        ],
        compiler_params=pltpu.CompilerParams(vmem_limit_bytes=46 * 1024 * 1024),
        cost_estimate=BRIEF,
    )(*blocks, w_in, down)
    return rows_t, preact, hidden, outs


def backward_kernel(count, at, preact_hbm, w_in_hbm, rows_t, hidden, down, *refs):
    blocks, (pre_grad, grads_t, sent, w_in, *refs) = refs[:count], refs[count:]
    preact, load_sem, sem = refs
    fetch = pltpu.make_async_copy(preact_hbm, preact, sem)
    fetch.start()
    load = pltpu.make_async_copy(w_in_hbm, w_in, load_sem)
    load.start()
    units = down.shape[1]
    fetch.wait()
    grads = side_by_side(blocks, slice(0, down.shape[0]))
    step = 256 if units % 256 == 0 else units
    for begin in range(0, units, step):
        gate = preact[:, begin : begin + step]
        up = preact[:, units + begin : units + begin + step]
        hidden_grad = jnp.dot(grads, down[:, begin : begin + step], preferred_element_type=F32)
        sigmoid = 1.0 / (1.0 + jnp.exp(-gate))
        gate_grad = hidden_grad * up * sigmoid * (1.0 + gate * (1.0 - sigmoid))
        up_grad = hidden_grad * gate * sigmoid
        pre_grad[:, begin : begin + step] = gate_grad.astype(BF16)
        pre_grad[:, units + begin : units + begin + step] = up_grad.astype(BF16)
    transpose_into(blocks, grads_t)
    write_shares(at, rows_t, grads_t, pre_grad, hidden, sent)
    load.wait()


def return_kernel(count, alone, pre_grad, w_in, *refs):
    blocks, outs, sems = refs[:count], refs[count : 2 * count], refs[-1]
    size = blocks[0].shape[0]
    copies = [
        pltpu.make_async_copy(block, out.at[pl.ds(0, size)], sems.at[n])
        for n, (block, out) in enumerate(zip(blocks, outs))
        if n != alone
    ]
    for copy in copies:
        copy.start()
    for columns in column_steps(w_in.shape[0]):
        part = lax.dot_general(
            pre_grad[...], w_in[columns, :], (((1,), (1,)), ((), ())), preferred_element_type=F32
        ).astype(BF16)
        for n, out in enumerate(outs):
            out[out.shape[0] - size :, columns] = part[n * size : (n + 1) * size]
    for copy in copies:
        copy.wait()


def returns(pre_grad, w_in, produced, alone):
    count = len(produced)
    size, width = produced[0].shape
    return pl.pallas_call(
        functools.partial(return_kernel, count, alone),
        out_shape=[
            jax.ShapeDtypeStruct((size if n == alone else 2 * size, width), BF16)
            for n in range(count)
        ],
        in_specs=whole(2) + anywhere(count),
        out_specs=whole(count),
        scratch_shapes=[pltpu.SemaphoreType.DMA((count,))],
        compiler_params=ROOMY,
        cost_estimate=BRIEF,
    )(pre_grad, w_in, *produced)


def anywhere(count):
    return [pl.BlockSpec(memory_space=pl.ANY)] * count


def in_hbm(count):
    return [pl.BlockSpec(memory_space=pltpu.HBM)] * count


def backward(at, share, preact, w_in, rows_t, hidden, down, blocks):
    width, units = down.shape
    slots = preact.shape[0]
    count = len(blocks)
    return pl.pallas_call(
        functools.partial(backward_kernel, count),
        out_shape=(
            jax.ShapeDtypeStruct((slots, 2 * units), BF16),
            jax.ShapeDtypeStruct((width, slots), BF16),
            jax.ShapeDtypeStruct((at.shape[0], share, 3 * units // 2), BF16),
            jax.ShapeDtypeStruct(w_in.shape, BF16),
        ),
        in_specs=[pl.BlockSpec(memory_space=pltpu.SMEM)]
        + anywhere(2)
        + whole(3 + count),
        out_specs=whole(4),
        scratch_shapes=[
            pltpu.VMEM((slots, 2 * units), F32),
            pltpu.SemaphoreType.DMA,
            pltpu.SemaphoreType.DMA,
        ],
        compiler_params=BIG,
        cost_estimate=BRIEF,
    )(at, preact, w_in, rows_t, hidden, down, *blocks)


def shares(at, share, rows_t, grads_t, pre_grad, hidden, cost):
    units = hidden.shape[1]
    return pl.pallas_call(
        write_shares,
        out_shape=jax.ShapeDtypeStruct((at.shape[0], share, 3 * units // 2), BF16),
        in_specs=[pl.BlockSpec(memory_space=pltpu.SMEM)] + whole(4),
        out_specs=whole(1)[0],
        compiler_params=ROOMY,
        cost_estimate=cost,
    )(at, rows_t, grads_t, pre_grad, hidden)


def add_kernel(kept, got, left, right):
    half = left.shape[0]
    left[...] = add(kept[:half], got[:half]).astype(BF16)
    right[...] = add(kept[half:], got[half : 2 * half]).astype(BF16)


def next_kernel(kept, got, left_in, right_in, left_send, right_send):
    first = got.shape[0] // 2
    left_send[...] = (add(kept[1], got[first + 1]) + left_in[1].astype(F32)).astype(BF16)
    right_send[...] = (add(kept[3], got[first + 3]) + right_in[1].astype(F32)).astype(BF16)


def own_kernel(kept, got, left_in, right_in, left, right):
    first = got.shape[0] // 2
    left[...] = add(kept[0], got[first]) + left_in[0].astype(F32)
    right[...] = add(kept[2], got[first + 2]) + right_in[0].astype(F32)


def add(left, right):
    return left.astype(F32) + right.astype(F32)


CUBE_SEND = (3, 7, 5, 7, 1, 5, 1, 3)


def swap(block, bit):
    return lax.ppermute(block, "dp", [(at, at ^ bit) for at in range(lax.axis_size("dp"))])


def cube_sum(got, kept_first, kept_later):
    _, share, columns = got.shape

    def run(kernel, out_shape, inputs, cost=BRIEF):
        return pl.pallas_call(
            kernel,
            out_shape=out_shape,
            in_specs=whole(len(inputs)),
            out_specs=whole(len(out_shape)),
            compiler_params=ROOMY,
            cost_estimate=cost,
        )(*inputs)

    half = jax.ShapeDtypeStruct((2, share, columns), BF16)
    one = jax.ShapeDtypeStruct((share, columns), BF16)
    own = jax.ShapeDtypeStruct((share, columns), F32)
    left, right = run(add_kernel, (half, half), (kept_first, got))
    parts = (kept_later, got, swap(left, 2), swap(right, 4))
    left_send, right_send = run(next_kernel, (one, one), parts)
    left, right = run(own_kernel, (own, own), parts, COVER)
    return left, swap(left_send, 4), right, swap(right_send, 2)


def after(value, *others):
    return lax.optimization_barrier((value, *others))[0]


def select_kernel(experts, capacity, now, late, first, routes, scores, *refs):
    now_picker, late_picker, scales = refs
    slots, toks = experts * capacity, scales.shape[1]
    places = lax.broadcasted_iota(jnp.int32, (toks, slots), 1).astype(F32)
    hits = [
        places == to_column(row) for row in slot_rows(first[0], routes[...], experts, capacity)
    ]
    hits.append(functools.reduce(jnp.logical_or, hits))
    picker = jnp.concatenate([hit.astype(F32).astype(BF16) for hit in hits], axis=0)
    weights = weight_rows(scores[...])
    for k in range(scales.shape[0]):
        scales[k] = jnp.broadcast_to(to_column(weights[k : k + 1, :]), scales.shape[1:])
    for out, blocks in ((now_picker, now), (late_picker, late)):
        parts = [picker[:, n * capacity : (n + 1) * capacity] for n in blocks]
        out[...] = jnp.concatenate(parts, axis=1)


def partial_kernel(capacity, picker, scales, own, early, mixed, back):
    for columns in column_steps(mixed.shape[1]):
        outputs = jnp.concatenate([own[:capacity, columns], early[:, columns]], axis=0)
        total, grad = sum_rows(picker[...], scales, outputs, own[capacity:, columns])
        mixed[:, columns] = total
        back[:, columns] = grad


def sum_rows(picker, scales, outputs, gradients):
    tops, toks = scales.shape[:2]
    chosen = picker[: tops * toks, : outputs.shape[0]]
    picked = jnp.dot(chosen, outputs, preferred_element_type=F32)
    total = sum(scales[k, :, :1] * picked[k * toks : (k + 1) * toks] for k in range(tops))
    either = picker[tops * toks :, : gradients.shape[0]]
    return total, jnp.dot(either, gradients, preferred_element_type=F32)


def mean_kernel(count, left, left_last, right, right_last, wide, narrow):
    middle, edge = wide.shape[1] // 2, narrow.shape[1] // 2
    for at, (own, last) in enumerate(((left, left_last), (right, right_last))):
        total = (own[...] + last[...].astype(F32)) / count
        wide[:, at * middle : (at + 1) * middle] = total[:, :middle]
        narrow[:, at * edge : (at + 1) * edge] = total[:, middle:]


def means(count, sums):
    share, columns = sums[0].shape
    return pl.pallas_call(
        functools.partial(mean_kernel, count),
        out_shape=(
            jax.ShapeDtypeStruct((share, 4 * columns // 3), F32),
            jax.ShapeDtypeStruct((share, 2 * columns // 3), F32),
        ),
        in_specs=whole(4),
        out_specs=whole(2),
        compiler_params=ROOMY,
        cost_estimate=BRIEF,
    )(*sums)


def last_kernel(capacity, number, picker, scales, mixed_part, back_part, *refs):
    blocks, (mixed, back), (mixed_vmem, back_vmem, sems) = (
        refs[:number],
        refs[number : number + 2],
        refs[number + 2 :],
    )
    stores = []
    for c, columns in enumerate(column_steps(mixed.shape[1])):
        outputs = jnp.concatenate([block[:capacity, columns] for block in blocks[:-1]], axis=0)
        gradients = jnp.concatenate(
            [block[block.shape[0] - capacity :, columns] for block in blocks], axis=0
        )
        total, grad = sum_rows(picker[...], scales, outputs, gradients)
        mixed_vmem[:, columns] = (total + mixed_part[:, columns]).astype(BF16)
        back_vmem[:, columns] = (grad + back_part[:, columns]).astype(BF16)
        for n, (source, target) in enumerate(((mixed_vmem, mixed), (back_vmem, back))):
            stores.append(
                pltpu.make_async_copy(source.at[:, columns], target.at[:, columns], sems.at[c, n])
            )
            stores[-1].start()
    for stored in stores:
        stored.wait()


def last(capacity, parts, blocks):
    toks, width = parts[-1].shape
    out_shape = jax.ShapeDtypeStruct((toks, width), BF16)
    return pl.pallas_call(
        functools.partial(last_kernel, capacity, len(blocks)),
        out_shape=(out_shape, out_shape),
        in_specs=whole(4 + len(blocks)),
        out_specs=anywhere(2),
        scratch_shapes=[pltpu.VMEM((toks, width), BF16)] * 2
        + [pltpu.SemaphoreType.DMA((len(column_steps(width)), 2))],
        compiler_params=ROOMY,
        cost_estimate=BRIEF,
    )(*parts, *blocks)


def dispatch(experts, capacity, out_shape, first, *sources):
    weighted = len(sources) > 2
    return pl.pallas_call(
        functools.partial(dispatch_kernel, experts, capacity, weighted),
        out_shape=out_shape,
        in_specs=[pl.BlockSpec(memory_space=pltpu.SMEM)] + in_hbm(len(sources)),
        out_specs=anywhere(len(out_shape)),
        scratch_shapes=[pltpu.VMEM(out.shape, out.dtype) for out in out_shape]
        + [pltpu.VMEM(source.shape, source.dtype) for source in sources]
        + [
            pltpu.SemaphoreType.DMA((len(sources),)),
            pltpu.SemaphoreType.DMA((len(column_steps(out_shape[0].shape[1], 1024)), len(out_shape))),
        ],
        compiler_params=ALONE,
        cost_estimate=BRIEF,
    )(first, *sources)


def call(kernel, out_shape, inputs):
    return pl.pallas_call(
        kernel,
        out_shape=out_shape,
        in_specs=[pl.BlockSpec(memory_space=pltpu.SMEM)]
        + [pl.BlockSpec(memory_space=pltpu.VMEM)] * (len(inputs) - 1),
        compiler_params=ROOMY,
        cost_estimate=BRIEF,
    )(*inputs)


def body(tokens, routes, route_scores, out_grad, gate_up, down_weight):
    experts = lax.axis_size("expert")
    groups = lax.axis_size("dp")
    toks, width = tokens.shape
    tops = routes.shape[1]
    units = down_weight.shape[2]
    capacity = (toks * tops + experts - 1) // experts
    slots = experts * capacity
    share = width // groups
    direct = experts <= 8 and capacity % 16 == 0
    w_in, w_out = gate_up[0], down_weight[0]
    routes_t, scores_t = routes.T, route_scores.T
    me = lax.axis_index("expert") if direct else jnp.int32(0)
    first = me.astype(jnp.int32).reshape(1)
    sizes = [capacity] * experts if direct else [slots]
    block_shapes = [jax.ShapeDtypeStruct((size, width), BF16) for size in sizes]

    def travel(block, step, sign):
        pairs = [(at, (at + sign * step) % experts) for at in range(experts)]
        return lax.ppermute(block, "expert", pairs)

    def exchange(blocks, sign):
        if not direct:
            block = blocks[0].reshape(experts, capacity, width)
            moved = lax.all_to_all(block, "expert", split_axis=0, concat_axis=0, tiled=True)
            return [moved.reshape(slots, width)]
        steps = range(1, experts) if sign > 0 else range(experts - 1, 0, -1)
        moved = {step: travel(blocks[step], step, sign) for step in steps}
        return [blocks[0]] + [moved[step] for step in range(1, experts)]

    def joined(blocks):
        return blocks[0] if len(blocks) == 1 else jnp.concatenate(blocks, axis=0)

    def split(rows):
        return [rows[at : at + sizes[0]] for at in range(0, slots, sizes[0])]

    sent_rows = dispatch(experts, capacity, block_shapes, first, routes_t, tokens)
    got_rows = exchange(sent_rows, 1)
    sent_grads = dispatch(experts, capacity, block_shapes, first, routes_t, scores_t, out_grad)
    out_shape = jax.ShapeDtypeStruct((toks, width), BF16)
    cube = direct and experts == 4 and groups == 8 and share % 256 == 0
    if cube:
        sent_grads = after(sent_grads, got_rows[1], got_rows[-1])
        got_grads = exchange(sent_grads, 1)
        rows_t, preact, hidden, produced = forward(got_rows, w_in, w_out)
        got_grads = after(got_grads, hidden)
        own = lax.axis_index("dp")
        send_at = jnp.stack([jnp.bitwise_xor(own, j) for j in CUBE_SEND]).astype(jnp.int32)
        keep_at = jnp.bitwise_xor(send_at, 1)
        early = experts - 1
        late = [n for n in range(experts - 1, 0, -1) if n != early]
        chosen = ([0, early], late + [early])
        now_picker, late_picker, scales = call(
            functools.partial(select_kernel, experts, capacity, *chosen),
            (
                *[
                    jax.ShapeDtypeStruct(((tops + 1) * toks, len(part) * capacity), BF16)
                    for part in chosen
                ],
                jax.ShapeDtypeStruct((tops, toks, 128), F32),
            ),
            (after(first, hidden), routes_t, scores_t),
        )
        early_out = travel(after(produced[early], scales), early, -1)
        pre_grad, grads_t, sent, w_in_here = backward(
            send_at, share, preact, w_in, rows_t, hidden, w_out, got_grads
        )
        operands = (share, rows_t, grads_t, pre_grad, hidden)
        got = swap(sent, 1)
        blocks = returns(after(pre_grad, sent), w_in_here, produced, early)
        half = len(CUBE_SEND) // 2
        kept_first = shares(after(keep_at[:half], blocks[0]), *operands, COVER)
        returned = exchange(blocks, -1)
        kept_later = shares(after(keep_at[half:], kept_first, early_out, got), *operands, COVER)
        sums = cube_sum(got, kept_first, kept_later)
        mixed_part, back_part = pl.pallas_call(
            functools.partial(partial_kernel, capacity),
            out_shape=(jax.ShapeDtypeStruct((toks, width), F32),) * 2,
            in_specs=whole(4),
            out_specs=whole(2),
            compiler_params=ROOMY,
            cost_estimate=BRIEF,
        )(after(now_picker, sums[0]), scales, returned[0], early_out)
        grad_in, grad_down = means(groups, sums)
        parts = (after(late_picker, grad_in), scales, mixed_part, back_part)
        mixed_out, token_grad = last(capacity, parts, [returned[n] for n in late + [early]])
    else:
        token_rows = joined(got_rows)
        grad_rows = joined(exchange(sent_grads, 1))
        preact = jnp.dot(token_rows, w_in, preferred_element_type=F32)
        gate, up = preact[:, :units], preact[:, units:]
        hidden = (jax.nn.silu(gate) * up).astype(BF16)
        produced = jnp.dot(hidden, w_out.T, preferred_element_type=F32).astype(BF16)
        returned = exchange(split(produced), -1)
        hidden_grad = jnp.dot(grad_rows, w_out, preferred_element_type=F32)
        sigmoid = jax.nn.sigmoid(gate)
        gate_grad = hidden_grad * up * sigmoid * (1.0 + gate * (1.0 - sigmoid))
        up_grad = hidden_grad * gate * sigmoid
        pre_grad = jnp.concatenate([gate_grad, up_grad], axis=1).astype(BF16)
        input_grad = jnp.dot(pre_grad, w_in.T, preferred_element_type=F32).astype(BF16)
        sent_back = exchange(split(input_grad), -1)

        def summed(left, right):
            part = contract(left, right).astype(BF16)
            total = lax.psum_scatter(part, "dp", scatter_dimension=0, tiled=True)
            return total.astype(F32) / groups

        grad_in = summed(token_rows, pre_grad)
        grad_down = summed(grad_rows, hidden)
        mixed_out = call(
            functools.partial(combine_kernel, experts, capacity, True),
            out_shape,
            (first, routes_t, scores_t, *returned),
        )
        token_grad = call(
            functools.partial(combine_kernel, experts, capacity, False),
            out_shape,
            (first, routes_t, *sent_back),
        )
    grad_in = grad_in.reshape(1, share, 2 * units)
    grad_down = grad_down.reshape(1, share, units)
    return (mixed_out, token_grad, grad_in, grad_down)


def solution(mesh):
    in_specs = (
        P(("dp", "expert"), None),
        P(("dp", "expert"), None),
        P(("dp", "expert"), None),
        P(("dp", "expert"), None),
        P("expert", None, None),
        P("expert", None, None),
    )
    out_specs = (
        P(("dp", "expert"), None),
        P(("dp", "expert"), None),
        P("expert", "dp", None),
        P("expert", "dp", None),
    )
    return jax.shard_map(body, mesh=mesh, in_specs=in_specs, out_specs=out_specs, check_vma=False)
```

```python
import functools

import jax
import jax.numpy as jnp
from jax import lax
from jax.experimental import pallas as pl
from jax.experimental.pallas import tpu as pltpu
from jax.sharding import PartitionSpec as P

F32 = jnp.float32
BF16 = jnp.bfloat16
BRIEF = pl.CostEstimate(flops=1024, bytes_accessed=1024, transcendentals=0)
COVER = pl.CostEstimate(flops=4 * 10**10, bytes_accessed=1024, transcendentals=0)
ROOMY = pltpu.CompilerParams(vmem_limit_bytes=16 * 1024 * 1024)
BIG = pltpu.CompilerParams(vmem_limit_bytes=28 * 1024 * 1024)
ALONE = pltpu.CompilerParams(vmem_limit_bytes=60 * 1024 * 1024)


def contract(left, right):
    return lax.dot_general(left, right, (((0,), (0,)), ((), ())), preferred_element_type=F32)


def slot_rows(first, routes, experts, capacity):
    tops, toks = routes.shape
    padded = -(-experts // 8) * 8
    rows = lax.broadcasted_iota(jnp.int32, (padded, toks), 0)
    ids = rows + first
    ids = jnp.where(ids >= experts, ids - experts, ids)
    ids = jnp.where(rows < experts, ids, -1)
    hits = [routes[k : k + 1, :] == ids for k in range(tops)]
    named = functools.reduce(jnp.logical_or, hits)
    before = lax.broadcasted_iota(jnp.int32, (toks, toks), 0) < lax.broadcasted_iota(
        jnp.int32, (toks, toks), 1
    )
    position = jnp.dot(
        named.astype(F32).astype(BF16),
        before.astype(F32).astype(BF16),
        preferred_element_type=F32,
    )
    slot = position + (rows * capacity).astype(F32)
    return [jnp.sum(jnp.where(hit, slot, 0.0), axis=0, keepdims=True) for hit in hits]


def weight_rows(scores):
    grown = jnp.exp(scores)
    return grown / jnp.sum(grown, axis=0, keepdims=True)


def to_column(row):
    toks = row.shape[1]
    same = lax.broadcasted_iota(jnp.int32, (toks, toks), 0) == lax.broadcasted_iota(
        jnp.int32, (toks, toks), 1
    )
    return jnp.sum(jnp.where(same, row, 0.0), axis=1, keepdims=True)


def put_blocks(outs, rows, columns):
    start = 0
    for out in outs:
        size = out.shape[0]
        out[:, columns] = rows[start : start + size]
        start += size


def column_steps(width, step=512):
    step = step if width % step == 0 else width
    return [slice(at, at + step) for at in range(0, width, step)]


def dispatch_kernel(experts, capacity, weighted, first, *refs):
    count = 2 + weighted
    sources, refs = refs[:count], refs[count:]
    number = (len(refs) - count - 2) // 2
    outs, ready, (*held, sems, out_sems) = refs[:number], refs[number : 2 * number], refs[2 * number :]
    copies = [
        pltpu.make_async_copy(source, place, sems.at[n])
        for n, (source, place) in enumerate(zip(sources, held))
    ]
    for copy in copies:
        copy.start()
    routes, values = held[0], held[-1]
    scores = held[1] if weighted else None
    for copy in copies[:-1]:
        copy.wait()
    slots, toks = experts * capacity, values.shape[0]
    places = lax.broadcasted_iota(jnp.int32, (slots, toks), 0).astype(F32)
    hits = [places == row for row in slot_rows(first[0], routes[...], experts, capacity)]
    picker = functools.reduce(jnp.logical_or, hits).astype(F32).astype(BF16)
    if weighted:
        weights = weight_rows(scores[...])
        scale = sum(
            jnp.sum(jnp.where(hit, weights[k : k + 1, :], 0.0), axis=1, keepdims=True)
            for k, hit in enumerate(hits)
        )
    copies[-1].wait()
    stores = []
    for c, columns in enumerate(column_steps(values.shape[1], 1024)):
        rows = jnp.dot(picker, values[:, columns], preferred_element_type=F32)
        if weighted:
            rows = rows * scale
        put_blocks(ready, rows.astype(BF16), columns)
        for n, (block, out) in enumerate(zip(ready, outs)):
            stores.append(
                pltpu.make_async_copy(block.at[:, columns], out.at[:, columns], out_sems.at[c, n])
            )
            stores[-1].start()
    for store in stores:
        store.wait()


def combine_kernel(experts, capacity, weighted, first, routes, *refs):
    scores = refs[0] if weighted else None
    blocks, out = refs[weighted:-1], refs[-1]
    slots, toks = experts * capacity, out.shape[0]
    places = lax.broadcasted_iota(jnp.int32, (toks, slots), 1).astype(F32)
    hits = [
        places == to_column(row) for row in slot_rows(first[0], routes[...], experts, capacity)
    ]
    if weighted:
        weights = weight_rows(scores[...])
        scales = [to_column(weights[k : k + 1, :]) for k in range(len(hits))]
        pickers = [hit.astype(F32).astype(BF16) for hit in hits]
    else:
        pickers = [functools.reduce(jnp.logical_or, hits).astype(F32).astype(BF16)]
    for columns in column_steps(out.shape[1]):
        rows = [block[:, columns] for block in blocks]
        rows = rows[0] if len(rows) == 1 else jnp.concatenate(rows, axis=0)
        picked = [jnp.dot(picker, rows, preferred_element_type=F32) for picker in pickers]
        if weighted:
            picked = [scale * part for scale, part in zip(scales, picked)]
        out[:, columns] = sum(picked).astype(out.dtype)


def whole(count):
    return [pl.BlockSpec(memory_space=pltpu.VMEM)] * count


def write_shares(at, rows_t, grads_t, pre_grad, hidden, out):
    share = out.shape[1]
    wide, narrow = pre_grad.shape[1] // 2, hidden.shape[1] // 2

    def write(t, half):
        own = pl.ds(pl.multiple_of(at[t] * share, share), share)
        out[t, :, :wide] = jnp.dot(
            rows_t[own, :],
            pre_grad[:, half * wide : (half + 1) * wide],
            preferred_element_type=F32,
        ).astype(out.dtype)
        out[t, :, wide:] = jnp.dot(
            grads_t[own, :],
            hidden[:, half * narrow : (half + 1) * narrow],
            preferred_element_type=F32,
        ).astype(out.dtype)

    for t in range(out.shape[0]):
        write(t, t // 2 % 2)


def side_by_side(blocks, columns):
    if len(blocks) == 1:
        return blocks[0][:, columns]
    return jnp.concatenate([block[:, columns] for block in blocks], axis=0)


def transpose_into(blocks, rows_t):
    width = rows_t.shape[0]
    step = 256 if width % 256 == 0 else width

    for begin in range(0, width, step):
        rows_t[begin : begin + step, :] = side_by_side(blocks, slice(begin, begin + step)).T


def join_copies(blocks, rows, sems):
    size = blocks[0].shape[0]
    joins = [
        pltpu.make_async_copy(block, rows.at[pl.ds(n * size, size)], sems.at[n])
        for n, block in enumerate(blocks)
    ]
    for join in joins:
        join.start()
    return joins


def forward_kernel(count, *refs):
    blocks, (w_in_hbm, down_hbm), (rows_t, preact, hidden), outs, scratch = (
        refs[:count],
        refs[count : count + 2],
        refs[count + 2 : count + 5],
        refs[count + 5 : 2 * count + 5],
        refs[2 * count + 5 :],
    )
    rows, w_in, down, block_sems, weight_sems, down_sem = scratch
    joins = join_copies(blocks, rows, block_sems)
    width, units = down.shape
    step = 256 if units % 256 == 0 else units
    loads = []
    for n in range(2 * units // step):
        begin = (n % 2) * units + n // 2 * step
        loads.append(
            pltpu.make_async_copy(
                w_in_hbm.at[:, pl.ds(begin, step)],
                w_in.at[:, pl.ds(begin, step)],
                weight_sems.at[n],
            )
        )
        loads[-1].start()
    load_down = pltpu.make_async_copy(down_hbm, down, down_sem)
    load_down.start()
    for join in joins:
        join.wait()
    for n in range(units // step):
        begin = n * step
        gate_at, up_at = slice(begin, begin + step), slice(units + begin, units + begin + step)
        loads[2 * n].wait()
        gate = jnp.dot(rows[...], w_in[:, gate_at], preferred_element_type=F32)
        loads[2 * n + 1].wait()
        up = jnp.dot(rows[...], w_in[:, up_at], preferred_element_type=F32)
        preact[:, gate_at] = gate
        preact[:, up_at] = up
        hidden[:, gate_at] = (gate / (1.0 + jnp.exp(-gate)) * up).astype(BF16)
    load_down.wait()
    for columns in column_steps(width):
        part = lax.dot_general(
            hidden[...], down[columns, :], (((1,), (1,)), ((), ())), preferred_element_type=F32
        )
        put_blocks(outs, part.astype(BF16), columns)
    transpose_into([rows], rows_t)


def forward(blocks, w_in, down):
    width, units = down.shape
    slots = sum(block.shape[0] for block in blocks)
    count = len(blocks)
    rows_t, preact, hidden, *outs = pl.pallas_call(
        functools.partial(forward_kernel, count),
        out_shape=(
            jax.ShapeDtypeStruct((width, slots), BF16),
            jax.ShapeDtypeStruct((slots, 2 * units), F32),
            jax.ShapeDtypeStruct((slots, units), BF16),
            *[jax.ShapeDtypeStruct(block.shape, BF16) for block in blocks],
        ),
        in_specs=anywhere(count) + in_hbm(2),
        out_specs=whole(3 + count),
        scratch_shapes=[
            pltpu.VMEM((slots, width), BF16),
            pltpu.VMEM(w_in.shape, BF16),
            pltpu.VMEM(down.shape, BF16),
            pltpu.SemaphoreType.DMA((count,)),
            pltpu.SemaphoreType.DMA((2 * units // min(units, 256),)),
            pltpu.SemaphoreType.DMA,
        ],
        compiler_params=pltpu.CompilerParams(vmem_limit_bytes=46 * 1024 * 1024),
        cost_estimate=BRIEF,
    )(*blocks, w_in, down)
    return rows_t, preact, hidden, outs


def backward_kernel(count, at, preact_hbm, w_in_hbm, rows_t, hidden, down, *refs):
    blocks, (pre_grad, grads_t, sent, w_in, *refs) = refs[:count], refs[count:]
    preact, load_sem, sem = refs
    fetch = pltpu.make_async_copy(preact_hbm, preact, sem)
    fetch.start()
    load = pltpu.make_async_copy(w_in_hbm, w_in, load_sem)
    load.start()
    units = down.shape[1]
    fetch.wait()
    grads = side_by_side(blocks, slice(0, down.shape[0]))
    step = 256 if units % 256 == 0 else units
    for begin in range(0, units, step):
        gate = preact[:, begin : begin + step]
        up = preact[:, units + begin : units + begin + step]
        hidden_grad = jnp.dot(grads, down[:, begin : begin + step], preferred_element_type=F32)
        sigmoid = 1.0 / (1.0 + jnp.exp(-gate))
        gate_grad = hidden_grad * up * sigmoid * (1.0 + gate * (1.0 - sigmoid))
        up_grad = hidden_grad * gate * sigmoid
        pre_grad[:, begin : begin + step] = gate_grad.astype(BF16)
        pre_grad[:, units + begin : units + begin + step] = up_grad.astype(BF16)
    transpose_into(blocks, grads_t)
    write_shares(at, rows_t, grads_t, pre_grad, hidden, sent)
    load.wait()


def return_kernel(count, alone, pre_grad, w_in, *refs):
    blocks, outs, sems = refs[:count], refs[count : 2 * count], refs[-1]
    size = blocks[0].shape[0]
    copies = [
        pltpu.make_async_copy(block, out.at[pl.ds(0, size)], sems.at[n])
        for n, (block, out) in enumerate(zip(blocks, outs))
        if n != alone
    ]
    for copy in copies:
        copy.start()
    for columns in column_steps(w_in.shape[0]):
        part = lax.dot_general(
            pre_grad[...], w_in[columns, :], (((1,), (1,)), ((), ())), preferred_element_type=F32
        ).astype(BF16)
        for n, out in enumerate(outs):
            out[out.shape[0] - size :, columns] = part[n * size : (n + 1) * size]
    for copy in copies:
        copy.wait()


def returns(pre_grad, w_in, produced, alone):
    count = len(produced)
    size, width = produced[0].shape
    return pl.pallas_call(
        functools.partial(return_kernel, count, alone),
        out_shape=[
            jax.ShapeDtypeStruct((size if n == alone else 2 * size, width), BF16)
            for n in range(count)
        ],
        in_specs=whole(2) + anywhere(count),
        out_specs=whole(count),
        scratch_shapes=[pltpu.SemaphoreType.DMA((count,))],
        compiler_params=ROOMY,
        cost_estimate=BRIEF,
    )(pre_grad, w_in, *produced)


def anywhere(count):
    return [pl.BlockSpec(memory_space=pl.ANY)] * count


def in_hbm(count):
    return [pl.BlockSpec(memory_space=pltpu.HBM)] * count


def backward(at, share, preact, w_in, rows_t, hidden, down, blocks):
    width, units = down.shape
    slots = preact.shape[0]
    count = len(blocks)
    return pl.pallas_call(
        functools.partial(backward_kernel, count),
        out_shape=(
            jax.ShapeDtypeStruct((slots, 2 * units), BF16),
            jax.ShapeDtypeStruct((width, slots), BF16),
            jax.ShapeDtypeStruct((at.shape[0], share, 3 * units // 2), BF16),
            jax.ShapeDtypeStruct(w_in.shape, BF16),
        ),
        in_specs=[pl.BlockSpec(memory_space=pltpu.SMEM)]
        + anywhere(2)
        + whole(3 + count),
        out_specs=whole(4),
        scratch_shapes=[
            pltpu.VMEM((slots, 2 * units), F32),
            pltpu.SemaphoreType.DMA,
            pltpu.SemaphoreType.DMA,
        ],
        compiler_params=BIG,
        cost_estimate=BRIEF,
    )(at, preact, w_in, rows_t, hidden, down, *blocks)


def shares(at, share, rows_t, grads_t, pre_grad, hidden, cost):
    units = hidden.shape[1]
    return pl.pallas_call(
        write_shares,
        out_shape=jax.ShapeDtypeStruct((at.shape[0], share, 3 * units // 2), BF16),
        in_specs=[pl.BlockSpec(memory_space=pltpu.SMEM)] + whole(4),
        out_specs=whole(1)[0],
        compiler_params=ROOMY,
        cost_estimate=cost,
    )(at, rows_t, grads_t, pre_grad, hidden)


def add_kernel(kept, got, left, right):
    half = left.shape[0]
    left[...] = add(kept[:half], got[:half]).astype(BF16)
    right[...] = add(kept[half:], got[half : 2 * half]).astype(BF16)


def next_kernel(kept, got, left_in, right_in, left_send, right_send):
    first = got.shape[0] // 2
    left_send[...] = (add(kept[1], got[first + 1]) + left_in[1].astype(F32)).astype(BF16)
    right_send[...] = (add(kept[3], got[first + 3]) + right_in[1].astype(F32)).astype(BF16)


def own_kernel(kept, got, left_in, right_in, left, right):
    first = got.shape[0] // 2
    left[...] = add(kept[0], got[first]) + left_in[0].astype(F32)
    right[...] = add(kept[2], got[first + 2]) + right_in[0].astype(F32)


def add(left, right):
    return left.astype(F32) + right.astype(F32)


CUBE_SEND = (3, 7, 5, 7, 1, 5, 1, 3)


def swap(block, bit):
    return lax.ppermute(block, "dp", [(at, at ^ bit) for at in range(lax.axis_size("dp"))])


def cube_sum(got, kept_first, kept_later):
    _, share, columns = got.shape

    def run(kernel, out_shape, inputs, cost=BRIEF):
        return pl.pallas_call(
            kernel,
            out_shape=out_shape,
            in_specs=whole(len(inputs)),
            out_specs=whole(len(out_shape)),
            compiler_params=ROOMY,
            cost_estimate=cost,
        )(*inputs)

    half = jax.ShapeDtypeStruct((2, share, columns), BF16)
    one = jax.ShapeDtypeStruct((share, columns), BF16)
    own = jax.ShapeDtypeStruct((share, columns), F32)
    left, right = run(add_kernel, (half, half), (kept_first, got))
    parts = (kept_later, got, swap(left, 2), swap(right, 4))
    left_send, right_send = run(next_kernel, (one, one), parts)
    left, right = run(own_kernel, (own, own), parts, COVER)
    return left, swap(left_send, 4), right, swap(right_send, 2)


def after(value, *others):
    return lax.optimization_barrier((value, *others))[0]


def partial_kernel(experts, capacity, alone, late, first, routes, scores, *refs):
    own, early, mixed, back, late_picker, scales = refs
    slots, toks = experts * capacity, mixed.shape[0]
    places = lax.broadcasted_iota(jnp.int32, (toks, slots), 1).astype(F32)
    hits = [
        places == to_column(row) for row in slot_rows(first[0], routes[...], experts, capacity)
    ]
    hits.append(functools.reduce(jnp.logical_or, hits))
    picker = jnp.concatenate([hit.astype(F32).astype(BF16) for hit in hits], axis=0)
    weights = weight_rows(scores[...])
    for k in range(scales.shape[0]):
        scales[k] = jnp.broadcast_to(to_column(weights[k : k + 1, :]), scales.shape[1:])

    def slots_of(blocks):
        parts = [picker[:, n * capacity : (n + 1) * capacity] for n in blocks]
        return jnp.concatenate(parts, axis=1)

    late_picker[...] = slots_of(late + [alone])
    now = slots_of((0, alone))
    for columns in column_steps(mixed.shape[1]):
        outputs = jnp.concatenate([own[:capacity, columns], early[:, columns]], axis=0)
        total, grad = sum_rows(now, scales, outputs, own[capacity:, columns])
        mixed[:, columns] = total
        back[:, columns] = grad


def sum_rows(picker, scales, outputs, gradients):
    tops, toks = scales.shape[:2]
    chosen = picker[: tops * toks, : outputs.shape[0]]
    picked = jnp.dot(chosen, outputs, preferred_element_type=F32)
    total = sum(scales[k, :, :1] * picked[k * toks : (k + 1) * toks] for k in range(tops))
    either = picker[tops * toks :, : gradients.shape[0]]
    return total, jnp.dot(either, gradients, preferred_element_type=F32)


def mean_kernel(count, left, left_last, right, right_last, wide, narrow):
    middle, edge = wide.shape[1] // 2, narrow.shape[1] // 2
    for at, (own, last) in enumerate(((left, left_last), (right, right_last))):
        total = (own[...] + last[...].astype(F32)) / count
        wide[:, at * middle : (at + 1) * middle] = total[:, :middle]
        narrow[:, at * edge : (at + 1) * edge] = total[:, middle:]


def means(count, sums):
    share, columns = sums[0].shape
    return pl.pallas_call(
        functools.partial(mean_kernel, count),
        out_shape=(
            jax.ShapeDtypeStruct((share, 4 * columns // 3), F32),
            jax.ShapeDtypeStruct((share, 2 * columns // 3), F32),
        ),
        in_specs=whole(4),
        out_specs=whole(2),
        compiler_params=ROOMY,
        cost_estimate=BRIEF,
    )(*sums)


def last_kernel(capacity, number, picker, scales, mixed_part, back_part, *refs):
    blocks, (mixed, back), (mixed_vmem, back_vmem, sems) = (
        refs[:number],
        refs[number : number + 2],
        refs[number + 2 :],
    )
    stores = []
    for c, columns in enumerate(column_steps(mixed.shape[1])):
        outputs = jnp.concatenate([block[:capacity, columns] for block in blocks[:-1]], axis=0)
        gradients = jnp.concatenate(
            [block[block.shape[0] - capacity :, columns] for block in blocks], axis=0
        )
        total, grad = sum_rows(picker[...], scales, outputs, gradients)
        mixed_vmem[:, columns] = (total + mixed_part[:, columns]).astype(BF16)
        back_vmem[:, columns] = (grad + back_part[:, columns]).astype(BF16)
        for n, (source, target) in enumerate(((mixed_vmem, mixed), (back_vmem, back))):
            stores.append(
                pltpu.make_async_copy(source.at[:, columns], target.at[:, columns], sems.at[c, n])
            )
            stores[-1].start()
    for stored in stores:
        stored.wait()


def last(capacity, parts, blocks):
    toks, width = parts[-1].shape
    out_shape = jax.ShapeDtypeStruct((toks, width), BF16)
    return pl.pallas_call(
        functools.partial(last_kernel, capacity, len(blocks)),
        out_shape=(out_shape, out_shape),
        in_specs=whole(4 + len(blocks)),
        out_specs=anywhere(2),
        scratch_shapes=[pltpu.VMEM((toks, width), BF16)] * 2
        + [pltpu.SemaphoreType.DMA((len(column_steps(width)), 2))],
        compiler_params=ROOMY,
        cost_estimate=BRIEF,
    )(*parts, *blocks)


def dispatch(experts, capacity, out_shape, first, *sources):
    weighted = len(sources) > 2
    return pl.pallas_call(
        functools.partial(dispatch_kernel, experts, capacity, weighted),
        out_shape=out_shape,
        in_specs=[pl.BlockSpec(memory_space=pltpu.SMEM)] + in_hbm(len(sources)),
        out_specs=anywhere(len(out_shape)),
        scratch_shapes=[pltpu.VMEM(out.shape, out.dtype) for out in out_shape]
        + [pltpu.VMEM(source.shape, source.dtype) for source in sources]
        + [
            pltpu.SemaphoreType.DMA((len(sources),)),
            pltpu.SemaphoreType.DMA((len(column_steps(out_shape[0].shape[1], 1024)), len(out_shape))),
        ],
        compiler_params=ALONE,
        cost_estimate=BRIEF,
    )(first, *sources)


def call(kernel, out_shape, inputs):
    return pl.pallas_call(
        kernel,
        out_shape=out_shape,
        in_specs=[pl.BlockSpec(memory_space=pltpu.SMEM)]
        + [pl.BlockSpec(memory_space=pltpu.VMEM)] * (len(inputs) - 1),
        compiler_params=ROOMY,
        cost_estimate=BRIEF,
    )(*inputs)


def body(tokens, routes, route_scores, out_grad, gate_up, down_weight):
    experts = lax.axis_size("expert")
    groups = lax.axis_size("dp")
    toks, width = tokens.shape
    tops = routes.shape[1]
    units = down_weight.shape[2]
    capacity = (toks * tops + experts - 1) // experts
    slots = experts * capacity
    share = width // groups
    direct = experts <= 8 and capacity % 16 == 0
    w_in, w_out = gate_up[0], down_weight[0]
    routes_t, scores_t = routes.T, route_scores.T
    me = lax.axis_index("expert") if direct else jnp.int32(0)
    first = me.astype(jnp.int32).reshape(1)
    sizes = [capacity] * experts if direct else [slots]
    block_shapes = [jax.ShapeDtypeStruct((size, width), BF16) for size in sizes]

    def travel(block, step, sign):
        pairs = [(at, (at + sign * step) % experts) for at in range(experts)]
        return lax.ppermute(block, "expert", pairs)

    def exchange(blocks, sign):
        if not direct:
            block = blocks[0].reshape(experts, capacity, width)
            moved = lax.all_to_all(block, "expert", split_axis=0, concat_axis=0, tiled=True)
            return [moved.reshape(slots, width)]
        steps = range(1, experts) if sign > 0 else range(experts - 1, 0, -1)
        moved = {step: travel(blocks[step], step, sign) for step in steps}
        return [blocks[0]] + [moved[step] for step in range(1, experts)]

    def joined(blocks):
        return blocks[0] if len(blocks) == 1 else jnp.concatenate(blocks, axis=0)

    def split(rows):
        return [rows[at : at + sizes[0]] for at in range(0, slots, sizes[0])]

    sent_rows = dispatch(experts, capacity, block_shapes, first, routes_t, tokens)
    got_rows = exchange(sent_rows, 1)
    sent_grads = dispatch(experts, capacity, block_shapes, first, routes_t, scores_t, out_grad)
    out_shape = jax.ShapeDtypeStruct((toks, width), BF16)
    cube = direct and experts == 4 and groups == 8 and share % 256 == 0
    if cube:
        sent_grads = after(sent_grads, got_rows[1])
        got_grads = exchange(sent_grads, 1)
        rows_t, preact, hidden, produced = forward(got_rows, w_in, w_out)
        got_grads = after(got_grads, hidden)
        own = lax.axis_index("dp")
        send_at = jnp.stack([jnp.bitwise_xor(own, j) for j in CUBE_SEND]).astype(jnp.int32)
        keep_at = jnp.bitwise_xor(send_at, 1)
        early = experts - 1
        early_out = travel(produced[early], early, -1)
        pre_grad, grads_t, sent, w_in_here = backward(
            send_at, share, preact, w_in, rows_t, hidden, w_out, got_grads
        )
        operands = (share, rows_t, grads_t, pre_grad, hidden)
        got = swap(sent, 1)
        blocks = returns(after(pre_grad, sent), w_in_here, produced, early)
        half = len(CUBE_SEND) // 2
        kept_first = shares(after(keep_at[:half], blocks[0]), *operands, COVER)
        returned = exchange(blocks, -1)
        kept_later = shares(after(keep_at[half:], kept_first, early_out, got), *operands, COVER)
        sums = cube_sum(got, kept_first, kept_later)
        late = [n for n in range(experts - 1, 0, -1) if n != early]
        mixed_part, back_part, picker, scales = call(
            functools.partial(partial_kernel, experts, capacity, early, late),
            (
                jax.ShapeDtypeStruct((toks, width), F32),
                jax.ShapeDtypeStruct((toks, width), F32),
                jax.ShapeDtypeStruct(((tops + 1) * toks, (len(late) + 1) * capacity), BF16),
                jax.ShapeDtypeStruct((tops, toks, 128), F32),
            ),
            (after(first, sums[0]), routes_t, scores_t, returned[0], early_out),
        )
        grad_in, grad_down = means(groups, sums)
        parts = (after(picker, grad_in), scales, mixed_part, back_part)
        mixed_out, token_grad = last(capacity, parts, [returned[n] for n in late + [early]])
    else:
        token_rows = joined(got_rows)
        grad_rows = joined(exchange(sent_grads, 1))
        preact = jnp.dot(token_rows, w_in, preferred_element_type=F32)
        gate, up = preact[:, :units], preact[:, units:]
        hidden = (jax.nn.silu(gate) * up).astype(BF16)
        produced = jnp.dot(hidden, w_out.T, preferred_element_type=F32).astype(BF16)
        returned = exchange(split(produced), -1)
        hidden_grad = jnp.dot(grad_rows, w_out, preferred_element_type=F32)
        sigmoid = jax.nn.sigmoid(gate)
        gate_grad = hidden_grad * up * sigmoid * (1.0 + gate * (1.0 - sigmoid))
        up_grad = hidden_grad * gate * sigmoid
        pre_grad = jnp.concatenate([gate_grad, up_grad], axis=1).astype(BF16)
        input_grad = jnp.dot(pre_grad, w_in.T, preferred_element_type=F32).astype(BF16)
        sent_back = exchange(split(input_grad), -1)

        def summed(left, right):
            part = contract(left, right).astype(BF16)
            total = lax.psum_scatter(part, "dp", scatter_dimension=0, tiled=True)
            return total.astype(F32) / groups

        grad_in = summed(token_rows, pre_grad)
        grad_down = summed(grad_rows, hidden)
        mixed_out = call(
            functools.partial(combine_kernel, experts, capacity, True),
            out_shape,
            (first, routes_t, scores_t, *returned),
        )
        token_grad = call(
            functools.partial(combine_kernel, experts, capacity, False),
            out_shape,
            (first, routes_t, *sent_back),
        )
    grad_in = grad_in.reshape(1, share, 2 * units)
    grad_down = grad_down.reshape(1, share, units)
    return (mixed_out, token_grad, grad_in, grad_down)


def solution(mesh):
    in_specs = (
        P(("dp", "expert"), None),
        P(("dp", "expert"), None),
        P(("dp", "expert"), None),
        P(("dp", "expert"), None),
        P("expert", None, None),
        P("expert", None, None),
    )
    out_specs = (
        P(("dp", "expert"), None),
        P(("dp", "expert"), None),
        P("expert", "dp", None),
        P("expert", "dp", None),
    )
    return jax.shard_map(body, mesh=mesh, in_specs=in_specs, out_specs=out_specs, check_vma=False)
```
